32 devices in a mesh: row: 4 (over x, core), span: 2 (over y), pitch: 4 (over z).
Axes of the slice: x: 2, y: 2, z: 4, core: 2. Of those that a mesh axis runs over, the one named last changes fastest.
Arguments:
- adjoint_start: float32 [5, 16, 64, 512], P(None, 'row', 'span', 'pitch'), may hold values from -8 to 8
- source: float32 [5, 16, 64, 512], P(None, 'row', 'span', 'pitch'), may hold values from -6 to 6
- couplings: float32 [6, 16, 64, 512], P(None, 'row', 'span', 'pitch'), may hold values from 0.2 to 1
- damping: float32 [16, 64, 512], P('row', 'span', 'pitch'), may hold values from 0.1 to 0.8
- jacobians: float32 [4, 6, 5, 5], P('row')
- giles_real: float32 [3, 64, 5, 5], replicated, may hold values from -6 to 6
- giles_imag: float32 [3, 64, 5, 5], replicated, may hold values from -6 to 6
- blades: int32 [4], replicated, may hold values from 16 to 79
- mode_orders: int32 [3, 64, 2], replicated, may hold values from -2 to 2
- cell_map: int32 [4, 512], P('row'), may hold values from 0 to 511
Outputs:
- adjoint: float32 [5, 16, 64, 512], P(None, 'row', 'span', 'pitch')
The draws below stay inside these ranges and needn't reach their ends.
All inputs are finite; a program needn't handle non-finite values.
Results may differ from the reference program's by a relative error of at most 0.0001.
Values sent between devices are 32-bit elements; how exact they have to be, the bound alone decides.
No kernel may reach another device: no remote copies, remote signals or barrier semaphores. Data moves between devices by JAX's collectives and lax.ppermute only.
A program may use at most 64 MiB of HBM per device.

```python
import math
import jax
import jax.numpy as jnp
from jax import lax

CA = 4
K = 64
ITERS = 5
ROWS = 4
NA = 16
NS = 64
NP = 512


def draw_jacobians(key, part):
    key_diagonal, key_rest = jax.random.split(key)
    diagonal = jax.random.uniform(key_diagonal, (ROWS, 6, 5, 1), jnp.float32, 0.6, 0.8)
    off_diagonal = jax.random.uniform(key_rest, (ROWS, 6, 5, 5), jnp.float32, -0.05, 0.05)
    identity = jnp.eye(5, dtype=jnp.float32)
    return off_diagonal * (1.0 - identity) + diagonal * identity


def touch_ends(drawn, own_key, least, high):
    shape = drawn.shape
    index_at = [jax.random.randint(jax.random.fold_in(own_key, axis), (), 0, shape[axis]) for axis in range(len(shape))]
    drawn = drawn.at[tuple(index_at)].set(least)
    longest = shape.index(max(shape))
    index_at[longest] = (index_at[longest] + 1) % shape[longest]
    return drawn.at[tuple(index_at)].set(high)


def block_levels(stream_key, extent, shards, low, top_value):
    def one(axis_at, shards_of):
        draws = jax.random.uniform(jax.random.fold_in(jax.random.fold_in(stream_key, 6), axis_at), (shards_of,), jnp.float32, low / len(shards), top_value / len(shards))
        return jnp.repeat(jnp.exp(draws), extent[axis_at] // shards_of).reshape((-1,) + (1,) * (len(extent) - axis_at - 1))

    loudness = one(*shards[0])
    for cut in shards[1:]:
        loudness = loudness * one(*cut)
    return loudness


def gaussian(rng, dims, spread, most, pieces=(), held_as=jnp.bfloat16):
    result = spread * jax.random.normal(rng, dims, jnp.float32)
    if pieces:
        result = result * block_levels(rng, dims, pieces, -0.22, 0.18)
    return jnp.clip(result, -most, most).astype(held_as)


def setup_inputs(seed: int = 0) -> dict:
    arg_keys = jax.random.split(jax.random.key(seed), 11)
    adjoint_start = gaussian(arg_keys[0], (5, NA, NS, NP), 2.0, 8.0, ((1, 4), (2, 2), (3, 4)), jnp.float32)
    source = gaussian(arg_keys[1], (5, NA, NS, NP), 1.0, 6.0, ((1, 4), (2, 2), (3, 4)), jnp.float32)
    couplings = jnp.clip(0.2 + 0.8 * jax.random.uniform(arg_keys[2], (6, NA, NS, NP), jnp.float32) ** block_levels(arg_keys[2], (6, NA, NS, NP), ((1, 4), (2, 2), (3, 4)), -0.2, 0.2), 0.2, 1.0)
    damping = jnp.clip(jnp.exp(math.log(0.8) - 2.0794415 * jax.random.uniform(arg_keys[3], (NA, NS, NP), jnp.float32) ** block_levels(arg_keys[3], (NA, NS, NP), ((0, 4), (1, 2), (2, 4)), -0.2, 0.2)), 0.1, 0.8)
    jacobians = draw_jacobians(jax.random.fold_in(arg_keys[10], 71), 0)
    giles_real = gaussian(arg_keys[5], (ROWS - 1, K, 5, 5), 1.0, 6.0, (), jnp.float32)
    giles_imag = gaussian(arg_keys[6], (ROWS - 1, K, 5, 5), 1.0, 6.0, (), jnp.float32)
    blades = touch_ends(jax.random.randint(arg_keys[7], (ROWS,), 16, 80), jax.random.fold_in(arg_keys[7], 1), 16, 79).astype(jnp.int32)
    mode_orders = touch_ends(jax.random.randint(arg_keys[8], (ROWS - 1, K, 2), -2, 3), jax.random.fold_in(arg_keys[8], 1), -2, 2).astype(jnp.int32)
    cell_map = touch_ends(jax.random.randint(arg_keys[9], (ROWS, NP), 0, NP), jax.random.fold_in(arg_keys[9], 1), 0, NP - 1).astype(jnp.int32)
    return {"adjoint_start": adjoint_start, "source": source, "couplings": couplings, "damping": damping, "jacobians": jacobians, "giles_real": giles_real, "giles_imag": giles_imag, "blades": blades, "mode_orders": mode_orders, "cell_map": cell_map}


PRECISE = lax.Precision.HIGHEST


def phase_table(numbers, positions, length):
    products = positions[..., :, None] * numbers[..., None, :]
    return jnp.mod(products, length).astype(jnp.float32) * (2.0 * math.pi / length)


def row_sweep(inputs):
    adjoint_row, source_row, coupling_row, diag_row, jacobian_row, boundary_row = inputs
    axial_zero = jnp.zeros_like(adjoint_row[:, :1])
    axial_next = jnp.concatenate([adjoint_row[:, 1:], axial_zero], 1)
    axial_prev = jnp.concatenate([axial_zero, adjoint_row[:, :-1]], 1)
    span_zero = jnp.zeros_like(adjoint_row[:, :, :1])
    span_next = jnp.concatenate([adjoint_row[:, :, 1:], span_zero], 2)
    span_prev = jnp.concatenate([span_zero, adjoint_row[:, :, :-1]], 2)
    pitch_next = jnp.roll(adjoint_row, -1, 3)
    pitch_prev = jnp.roll(adjoint_row, 1, 3)
    neighbours = jnp.stack([axial_next, axial_prev, span_next, span_prev, pitch_next, pitch_prev], 0)
    mixed_terms = jnp.einsum('dji,djasp->diasp', jacobian_row, neighbours, precision=PRECISE)
    coupled = jnp.sum(coupling_row[:, None] * mixed_terms, axis=0)
    right_side = source_row.at[:, CA - 1].add(boundary_row)
    return (right_side + coupled) / diag_row[None]


def to_rows(array):
    return jnp.swapaxes(array.reshape(array.shape[0], ROWS, CA, NS, NP), 0, 1)


def reference(adjoint_start, source, couplings, damping, jacobians, giles_real, giles_imag, blades, mode_orders, cell_map):
    adjoint = to_rows(adjoint_start)
    source_rows = to_rows(source)
    coupling_rows = to_rows(couplings)
    diag_sum = (damping + jnp.sum(couplings, 0)).reshape(ROWS, CA, NS, NP)
    mode_numbers = mode_orders[:, :, 0] * blades[:-1, None] + mode_orders[:, :, 1] * blades[1:, None]
    positions = jnp.broadcast_to(jnp.arange(NP, dtype=jnp.int32), (ROWS - 1, NP))
    forward_angles = phase_table(mode_numbers, positions, NP)
    forward_cos = jnp.cos(forward_angles) * (2.0 / NP)
    forward_sin = -jnp.sin(forward_angles) * (2.0 / NP)
    synth_angles = phase_table(mode_numbers, cell_map[:ROWS - 1], NP)
    synth_cos = jnp.cos(synth_angles)
    synth_sin = jnp.sin(synth_angles)
    for sweep in range(ITERS):
        strips = adjoint[1:, :, 0]
        real_part = jnp.einsum('icsp,ipk->icsk', strips, forward_cos, precision=PRECISE)
        imag_part = jnp.einsum('icsp,ipk->icsk', strips, forward_sin, precision=PRECISE)
        out_real = jnp.einsum('ikjc,ijsk->icsk', giles_real, real_part, precision=PRECISE) - jnp.einsum('ikjc,ijsk->icsk', giles_imag, imag_part, precision=PRECISE)
        out_imag = jnp.einsum('ikjc,ijsk->icsk', giles_real, imag_part, precision=PRECISE) + jnp.einsum('ikjc,ijsk->icsk', giles_imag, real_part, precision=PRECISE)
        boundary = jnp.einsum('icsk,ipk->icsp', out_real, synth_cos, precision=PRECISE) - jnp.einsum('icsk,ipk->icsp', out_imag, synth_sin, precision=PRECISE)
        boundary = jnp.concatenate([boundary, jnp.zeros((1, 5, NS, NP), jnp.float32)], 0)
        adjoint = lax.map(row_sweep, (adjoint, source_rows, coupling_rows, diag_sum, jacobians, boundary))
    return jnp.swapaxes(adjoint, 0, 1).reshape(5, NA, NS, NP)
```

```python
import math

import jax
import jax.numpy as jnp
from jax import lax
from jax.sharding import PartitionSpec as P

ITERS = 5


PRECISE = lax.Precision.HIGHEST


def shifted(x, axis, by):
    size = lax.axis_size(axis)
    pairs = [(i, i + by) for i in range(size) if 0 <= i + by < size]
    return lax.ppermute(x, axis, pairs)


def padded(cells, sides, width, closed):
    for axis, dim in sides:
        count = lax.axis_size(axis)
        ends = count if closed else count - 1
        head = lax.slice_in_dim(cells, 0, width, axis=dim)
        tail = lax.slice_in_dim(cells, cells.shape[dim] - width, cells.shape[dim], axis=dim)
        cells = jnp.concatenate(
            [
                lax.ppermute(tail, axis, [(i, (i + 1) % count) for i in range(ends)]),
                cells,
                lax.ppermute(head, axis, [((i + 1) % count, i) for i in range(ends)]),
            ],
            axis=dim,
        )
    return cells


def phase_table(numbers, positions, length):
    products = positions[:, None] * numbers[None, :]
    return jnp.mod(products, length).astype(jnp.float32) * (2.0 * math.pi / length)


def giles(real_part, imag_part, giles_re, giles_im):
    out_real = jnp.einsum("kjc,jsk->csk", giles_re, real_part, precision=PRECISE) - jnp.einsum(
        "kjc,jsk->csk", giles_im, imag_part, precision=PRECISE
    )
    out_imag = jnp.einsum("kjc,jsk->csk", giles_re, imag_part, precision=PRECISE) + jnp.einsum(
        "kjc,jsk->csk", giles_im, real_part, precision=PRECISE
    )
    return jnp.stack([out_real, out_imag], 2)


def send_upstream(amplitudes):
    return shifted(amplitudes, "row", -1)


def update(adjoint, source, couplings, diag_sum, jacobian_row, boundary):
    axial_cells = adjoint.shape[1]
    span_len = adjoint.shape[2]
    pitch_len = adjoint.shape[3]
    span_edges = jnp.concatenate([adjoint[:, :, :1], adjoint[:, :, -1:]], 2)
    span_got = padded(span_edges, (("span", 2),), 1, False)
    pitch_edges = jnp.concatenate([adjoint[:, :, :, :1], adjoint[:, :, :, -1:]], 3)
    pitch_got = padded(pitch_edges, (("pitch", 3),), 1, True)
    axial_index = lax.broadcasted_iota(jnp.int32, (1, axial_cells, 1, 1), 1)
    span_index = lax.broadcasted_iota(jnp.int32, (1, 1, span_len, 1), 2)
    pitch_index = lax.broadcasted_iota(jnp.int32, (1, 1, 1, pitch_len), 3)
    axial_next = jnp.where(axial_index == axial_cells - 1, 0.0, jnp.roll(adjoint, -1, 1))
    axial_prev = jnp.where(axial_index == 0, 0.0, jnp.roll(adjoint, 1, 1))
    span_next = jnp.where(span_index == span_len - 1, span_got[:, :, 3:4], jnp.roll(adjoint, -1, 2))
    span_prev = jnp.where(span_index == 0, span_got[:, :, 0:1], jnp.roll(adjoint, 1, 2))
    pitch_next = jnp.where(
        pitch_index == pitch_len - 1, pitch_got[:, :, :, 3:4], jnp.roll(adjoint, -1, 3)
    )
    pitch_prev = jnp.where(pitch_index == 0, pitch_got[:, :, :, 0:1], jnp.roll(adjoint, 1, 3))
    neighbours = (axial_next, axial_prev, span_next, span_prev, pitch_next, pitch_prev)
    total = source + jnp.where(axial_index == axial_cells - 1, boundary[:, None], 0.0)
    for direction in range(6):
        mixed = jacobian_row[direction, 0][:, None, None, None] * neighbours[direction][0][None]
        for entry in range(1, 5):
            mixed = (
                mixed
                + jacobian_row[direction, entry][:, None, None, None]
                * neighbours[direction][entry][None]
            )
        total = total + couplings[direction][None] * mixed
    return total / diag_sum[None]


def on_device(
    adjoint_start,
    source,
    couplings,
    damping,
    jacobians,
    giles_real,
    giles_imag,
    blades,
    mode_orders,
    cell_map,
):
    components, axial_cells, span_cells, pitch_cells = adjoint_start.shape
    rows_all = lax.axis_size("row")
    pitch_count = lax.axis_size("pitch")
    length = pitch_cells * pitch_count
    modes_count = mode_orders.shape[1]
    row_id = lax.axis_index("row")
    pitch_id = lax.axis_index("pitch")
    diag_sum = damping + jnp.sum(couplings, 0)
    jacobian_row = jacobians[0]
    sender_face = jnp.maximum(row_id - 1, 0)
    receiver_face = jnp.minimum(row_id, rows_all - 2)

    def mode_numbers(face):
        orders = lax.dynamic_index_in_dim(mode_orders, face, 0, keepdims=False)
        blades_low = lax.dynamic_index_in_dim(blades, face, 0, keepdims=False)
        blades_high = lax.dynamic_index_in_dim(blades, face + 1, 0, keepdims=False)
        return orders[:, 0] * blades_low + orders[:, 1] * blades_high

    send_modes = mode_numbers(sender_face)
    recv_modes = mode_numbers(receiver_face)
    giles_re = lax.dynamic_index_in_dim(giles_real, sender_face, 0, keepdims=False)
    giles_im = lax.dynamic_index_in_dim(giles_imag, sender_face, 0, keepdims=False)
    donor_cells = cell_map[0]
    own_cells = pitch_id * pitch_cells + jnp.arange(pitch_cells, dtype=jnp.int32)
    angles = phase_table(send_modes, own_cells, length)
    local_forward = jnp.concatenate([jnp.cos(angles), -jnp.sin(angles)], 1) * (2.0 / length)
    angles = phase_table(
        recv_modes,
        lax.dynamic_slice_in_dim(donor_cells, pitch_id * pitch_cells, pitch_cells),
        length,
    )
    local_synth = jnp.concatenate([jnp.cos(angles).T, -jnp.sin(angles).T], 0)
    share_count = modes_count // pitch_count
    mode_start = pitch_id * share_count
    giles_re_part = lax.dynamic_slice_in_dim(giles_re, mode_start, share_count, 0)
    giles_im_part = lax.dynamic_slice_in_dim(giles_im, mode_start, share_count, 0)
    adjoint = adjoint_start
    for sweep in range(ITERS):
        inlet_strip = adjoint[:, 0]
        partial_sum = jnp.dot(
            inlet_strip.reshape(components * span_cells, pitch_cells),
            local_forward,
            precision=PRECISE,
        )
        partial_sum = partial_sum.reshape(components, span_cells, 2, modes_count)
        pieces = partial_sum.reshape(components, span_cells, 2, pitch_count, share_count)
        pieces = jnp.moveaxis(pieces, 3, 0)
        owned = jnp.sum(lax.all_to_all(pieces, "pitch", 0, 0, tiled=True), 0)
        treated = giles(owned[:, :, 0], owned[:, :, 1], giles_re_part, giles_im_part)
        arrived = send_upstream(treated)
        copies = jnp.broadcast_to(arrived[None], (pitch_count, *arrived.shape))
        shares = lax.all_to_all(copies, "pitch", 0, 0, tiled=True)
        all_modes = jnp.moveaxis(shares, 0, 3)
        boundary_field = jnp.dot(
            all_modes.reshape(components * span_cells, 2 * modes_count),
            local_synth,
            precision=PRECISE,
        )
        boundary = boundary_field.reshape(components, span_cells, pitch_cells)
        adjoint = update(adjoint, source, couplings, diag_sum, jacobian_row, boundary)
    return adjoint


def solution(mesh):
    placed = (
        P(None, "row", "span", "pitch"),
        P(None, "row", "span", "pitch"),
        P(None, "row", "span", "pitch"),
        P("row", "span", "pitch"),
        P("row", None, None, None),
        P(),
        P(),
        P(),
        P(),
        P("row", None),
    )
    return jax.shard_map(
        on_device,
        mesh=mesh,
        in_specs=placed,
        out_specs=P(None, "row", "span", "pitch"),
        check_vma=False,
    )
```

```python
import functools
import math

import jax
import jax.numpy as jnp
from jax import lax
from jax.experimental import pallas as pl
from jax.experimental.pallas import tpu as pltpu
from jax.sharding import PartitionSpec as P

ITERS = 5
AXES = ("row", "span", "pitch")

ORDER_MAX = 2
BASE = 2 * ORDER_MAX + 1
COSINES = (BASE * BASE + 1) // 2
WAVES = 2 * COSINES - 1
COMPONENTS = 5
EDGE = 8
SEGMENT_LANES = 4 * EDGE
EXACT = lax.Precision.HIGHEST
PARAMS = pltpu.CompilerParams(vmem_limit_bytes=40 * 1024 * 1024)


def lanes(shape):
    return lax.broadcasted_iota(jnp.int32, shape, len(shape) - 1)


def rows(shape):
    return lax.broadcasted_iota(jnp.int32, shape, len(shape) - 2)


def column(j):
    component = (j * 41) >> 10
    wave = j - WAVES * component
    sine = wave >= COSINES
    return component, jnp.where(sine, wave - (COSINES - 1), wave), sine


def mode_number(mode, blades_ref, face):
    high = ((mode + ORDER_MAX) * 13) >> 6
    low = mode - BASE * high
    return high * blades_ref[face] + low * blades_ref[face + 1]


def waves(products, length):
    if length & (length - 1) == 0:
        phase = products & (length - 1)
    else:
        phase = jnp.mod(products, length)
    turn = phase.astype(jnp.float32) * (1.0 / length)
    quarter = jnp.floor(4.0 * turn + 0.5)
    x = (turn - 0.25 * quarter) * (2.0 * math.pi)
    y = x * x
    sine = x * (1.0 + y * (-1.0 / 6 + y * (1.0 / 120 + y * (-1.0 / 5040 + y * (1.0 / 362880)))))
    cosine = 1.0 + y * (-0.5 + y * (1.0 / 24 + y * (-1.0 / 720 + y * (1.0 / 40320 - y * (1.0 / 3628800)))))
    quarter = quarter.astype(jnp.int32) & 3
    odd = (quarter & 1) == 1
    cos_out = jnp.where(odd, sine, cosine)
    sin_out = jnp.where(odd, cosine, sine)
    cos_out = jnp.where((quarter == 1) | (quarter == 2), -cos_out, cos_out)
    sin_out = jnp.where(quarter >= 2, -sin_out, sin_out)
    return cos_out, sin_out


def to_edges(layers, pitch):
    lane = lanes(layers[0].shape)
    block = jnp.zeros_like(layers[0])
    for a, layer in enumerate(layers):
        if layer is None:
            continue
        start = a * SEGMENT_LANES
        first = pltpu.roll(layer, (start + EDGE) % pitch, layer.ndim - 1)
        last = pltpu.roll(layer, (start + 3 * EDGE) % pitch, layer.ndim - 1)
        block = jnp.where((lane >= start + EDGE) & (lane < start + 2 * EDGE), first, block)
        block = jnp.where((lane >= start + 2 * EDGE) & (lane < start + 3 * EDGE), last, block)
    return block


def pack_kernel(
    blades_ref, adjoint_ref, source_ref, couplings_ref, damping_ref,
    coef_ref, inv_ref, edges_ref, span_ref, right_ref, left_ref, dright_ref, dleft_ref,
    table_ref, modes_ref, modes_edge_ref, *, row_count, length,
):
    components, axial, span, pitch = adjoint_ref.shape
    row, side, place = (lax.axis_index(name) for name in AXES)
    tables = 1 + components
    diag = damping_ref[...]
    for d in range(6):
        diag = diag + couplings_ref[d]
    inverse = 1.0 / diag
    for c in range(components):
        coef_ref[c] = source_ref[c] * inverse
    for d in range(6):
        coef_ref[components + d] = couplings_ref[d] * inverse
    inv_ref[...] = inverse[axial - 1]

    fields = 2 * components + 6

    def field_layers(f):
        if f < components:
            return [adjoint_ref[f, a] for a in range(axial)]
        return [coef_ref[f - components, a] for a in range(axial)]

    for f in range(fields):
        edges_ref[f] = to_edges(field_layers(f), pitch)
    last = inv_ref[...]
    edges_ref[fields] = jnp.where(
        lanes(last.shape) >= (axial - 1) * SEGMENT_LANES,
        to_edges([jnp.zeros_like(last)] * (axial - 1) + [last], pitch), 0.0,
    )
    slot = (lanes((span, pitch)) // EDGE) % 4
    edge_row = pl.multiple_of(jnp.where(side == 0, span - EDGE, 0), EDGE)
    for out_ref, corner_ref, at in ((right_ref, dright_ref, 2), (left_ref, dleft_ref, 1)):
        for g in range(right_ref.shape[0]):
            packed = jnp.zeros((span, pitch), jnp.float32)
            for k in range(4):
                if 4 * g + k <= fields:
                    moved_field = pltpu.roll(edges_ref[4 * g + k], ((k - at) * EDGE) % pitch, 1)
                    packed = jnp.where(slot == k, moved_field, packed)
            out_ref[g] = packed
            corner_ref[g] = out_ref[g, pl.ds(edge_row, EDGE), :]
    for f in range(fields):
        ref, at = (adjoint_ref, f) if f < components else (coef_ref, f - components)
        for a in range(axial):
            span_ref[f * axial + a] = ref[at, a, pl.ds(edge_row, EDGE), :]
    span_ref[fields * axial] = inv_ref[pl.ds(edge_row, EDGE), :]

    j = lanes((pitch, pitch))
    component, mode, sine = column(j)
    number = mode_number(mode, blades_ref, jnp.maximum(row - 1, 0))
    cos_table, sin_table = waves(number * (place * pitch + rows((pitch, pitch))), length)
    table = jnp.where(component < components, jnp.where(sine, sin_table, cos_table), 0.0)
    table_ref[...] = table
    total = jnp.zeros((span, pitch), jnp.float32)
    for c in range(components):
        total += jnp.dot(
            adjoint_ref[c, 0], jnp.where(component == c, table, 0.0),
            precision=EXACT, preferred_element_type=jnp.float32,
        )
    modes_ref[...] = total
    modes_edge_ref[...] = modes_ref[pl.ds(edge_row, EDGE), :]


def synth_kernel(
    blades_ref, giles_re_ref, giles_im_ref, orders_ref, cells_ref, synth_ref,
    *, row_count, place_count, components, pitch, length, axial,
):
    row, place = lax.axis_index("row"), lax.axis_index("pitch")
    face = jnp.minimum(row, row_count - 2)
    modes = orders_ref.shape[2]
    orders = orders_ref[face]
    tag = BASE * orders[0:1] + orders[1:2]
    component, mode, _ = column(rows((pitch, modes)))
    same = (jnp.abs(tag) == mode) & (component < components)
    plain = jnp.where(same, 1.0, 0.0)
    signed = jnp.where(tag < 0, -plain, plain)
    dims = (((1,), (1,)), ((), ()))
    sums_re = lax.dot_general(giles_re_ref[...], plain, dims, precision=EXACT, preferred_element_type=jnp.float32)
    sums_im = lax.dot_general(giles_im_ref[...], signed, dims, precision=EXACT, preferred_element_type=jnp.float32)
    component, mode, sine = column(lanes(sums_re.shape))
    scale = 2.0 / length
    with_cos = jnp.where(sine, sums_im, sums_re) * scale
    with_sin = jnp.where(sine, sums_re, -sums_im) * scale
    component = component[0:1]

    def chunk(at):
        start = pl.multiple_of(lax.rem(place + at + place_count, place_count) * pitch, pitch)
        return cells_ref[:, pl.ds(start, pitch)]

    own = chunk(0)
    lane = lanes((1, pitch))
    first = (axial - 1) * SEGMENT_LANES
    edge = jnp.where(lane < first + EDGE, pltpu.roll(chunk(-1), (first + EDGE) % pitch, 1), pltpu.roll(own, (first + EDGE) % pitch, 1))
    edge = jnp.where(lane < first + 2 * EDGE, edge, pltpu.roll(own, (first + 3 * EDGE) % pitch, 1))
    edge = jnp.where(lane < first + 3 * EDGE, edge, pltpu.roll(chunk(1), (first + 3 * EDGE) % pitch, 1))

    def upright(cells):
        wide = jnp.broadcast_to(cells.astype(jnp.float32), (pitch, pitch))
        return jnp.transpose(wide).astype(jnp.int32)

    edge_cells = upright(edge)[first:first + SEGMENT_LANES]
    at_cells = jnp.concatenate([upright(own), edge_cells], 0)
    _, mode, _ = column(lanes(at_cells.shape))
    cos_table, sin_table = waves(mode_number(mode, blades_ref, face) * at_cells, length)
    for c in range(components):
        row_cos = jnp.zeros((1, pitch), jnp.float32)
        row_sin = jnp.zeros((1, pitch), jnp.float32)
        for b in range(components):
            at = b * components + c
            row_cos = jnp.where(component == b, with_cos[at:at + 1], row_cos)
            row_sin = jnp.where(component == b, with_sin[at:at + 1], row_sin)
        part = row_cos * cos_table + row_sin * sin_table
        synth_ref[pl.ds(c * pitch, pitch), :] = part[:pitch]
        synth_ref[pl.ds(components * pitch + c * SEGMENT_LANES, SEGMENT_LANES), :] = part[pitch:]
    used = components * (pitch + SEGMENT_LANES)
    rest = synth_ref.shape[0] - used
    if rest:
        synth_ref[pl.ds(used, rest), :] = jnp.zeros((rest, pitch), jnp.float32)


def mixed(jac_ref, source, couplings, neighbours):
    total = list(source)
    for d, neighbour in enumerate(neighbours):
        for c in range(len(total)):
            term = jac_ref[c, d] * neighbour[0]
            for b in range(1, len(total)):
                term = term + jac_ref[b * len(total) + c, d] * neighbour[b]
            total[c] = total[c] + couplings[d] * term
    return total


def layer_update(jac_ref, state_ref, edge_ref, coef_ref, t, a):
    components, wide, pitch = state_ref.shape[1], state_ref.shape[3], state_ref.shape[4]
    lane = lanes((wide, pitch))
    start = a * SEGMENT_LANES
    own = [state_ref[t, c, a + 1] for c in range(components)]
    above = [state_ref[t, c, a + 2] for c in range(components)]
    below = [state_ref[t, c, a] for c in range(components)]
    edge = [edge_ref[t, c] for c in range(components)]
    span_next = [pltpu.roll(x, wide - 1, 0) for x in own]
    span_prev = [pltpu.roll(x, 1, 0) for x in own]
    to_end = 2 * pitch - 1 - (start + 3 * EDGE)
    to_begin = 2 * pitch - (start + EDGE - 1)
    pitch_next = [
        jnp.where(lane == pitch - 1, pltpu.roll(e, lax.rem(to_end, pitch), 1), pltpu.roll(x, pitch - 1, 1))
        for e, x in zip(edge, own)
    ]
    pitch_prev = [
        jnp.where(lane == 0, pltpu.roll(e, lax.rem(to_begin, pitch), 1), pltpu.roll(x, 1, 1))
        for e, x in zip(edge, own)
    ]
    source = [coef_ref[c, a] for c in range(components)]
    couplings = [coef_ref[components + d, a] for d in range(6)]
    return mixed(jac_ref, source, couplings, (above, below, span_next, span_prev, pitch_next, pitch_prev))


def edge_update(jac_ref, edge_ref, edge_coef_ref, t, axial):
    components, wide, pitch = edge_ref.shape[1:]
    lane = lanes((wide, pitch))
    own = [edge_ref[t, c] for c in range(components)]
    above = [jnp.where(lane < (axial - 1) * SEGMENT_LANES, pltpu.roll(x, pitch - SEGMENT_LANES, 1), 0.0) for x in own]
    below = [jnp.where(lane >= SEGMENT_LANES, pltpu.roll(x, SEGMENT_LANES, 1), 0.0) for x in own]
    span_next = [pltpu.roll(x, wide - 1, 0) for x in own]
    span_prev = [pltpu.roll(x, 1, 0) for x in own]
    pitch_next = [pltpu.roll(x, pitch - 1, 1) for x in own]
    pitch_prev = [pltpu.roll(x, 1, 1) for x in own]
    source = [edge_coef_ref[c] for c in range(components)]
    couplings = [edge_coef_ref[components + d] for d in range(6)]
    return mixed(jac_ref, source, couplings, (above, below, span_next, span_prev, pitch_next, pitch_prev))


def edge_boundary(field, c, components, pitch, axial):
    at = components * pitch + c * SEGMENT_LANES
    tile = field[:, (at // pitch) * pitch:(at // pitch + 1) * pitch]
    return pltpu.roll(tile, ((axial - 1) * SEGMENT_LANES - at % pitch) % pitch, 1)


def first_kernel(
    jac_ref, adjoint_ref, coef_in_ref, inv_in_ref, edges_ref, span_ref,
    from_left_ref, from_right_ref, dleft_ref, dright_ref, table_ref, modes_a_ref, modes_b_ref, synth_ref,
    coef_ref, inv_ref, edge_coef_ref, front_ref, edge_front_ref, modes_ref,
    state_ref, edge_ref, *, fronts,
):
    components, axial, span, pitch = adjoint_ref.shape
    wide = span + EDGE
    side = lax.axis_index("span")
    fields = 2 * components + 6
    ghost_row = rows((EDGE, pitch))
    keep = ghost_row != jnp.where(side == 0, EDGE - 1, 0)

    def ghost(at):
        return jnp.where(keep, span_ref[at], 0.0)

    for f in range(fields):
        for a in range(axial):
            if f < components:
                state_ref[0, f, a + 1, :span] = adjoint_ref[f, a]
                state_ref[0, f, a + 1, span:] = ghost(f * axial + a)
            else:
                coef_ref[f - components, a, :span] = coef_in_ref[f - components, a]
                coef_ref[f - components, a, span:] = ghost(f * axial + a)
    inv_ref[:span] = inv_in_ref[...]
    inv_ref[span:] = ghost(fields * axial)
    for t in range(state_ref.shape[0]):
        for c in range(components):
            state_ref[t, c, 0] = jnp.zeros((wide, pitch), jnp.float32)
            state_ref[t, c, axial + 1] = jnp.zeros((wide, pitch), jnp.float32)

    for f in range(fields + 1):
        g, k = f // 4, f % 4
        target, at = (edge_ref.at[0], f) if f < components else (edge_coef_ref, f - components)
        to_first, to_last = (-k * EDGE) % pitch, ((3 - k) * EDGE) % pitch
        segment = (lanes((span, pitch)) // EDGE) % 4
        value = edges_ref[f]
        value = jnp.where(segment == 0, pltpu.roll(from_left_ref[g], to_first, 1), value)
        value = jnp.where(segment == 3, pltpu.roll(from_right_ref[g], to_last, 1), value)
        segment = (lanes((EDGE, pitch)) // EDGE) % 4
        if f < fields:
            layers = [span_ref[f * axial + a] for a in range(axial)]
        else:
            layers = [None] * (axial - 1) + [span_ref[fields * axial]]
            layers = [jnp.zeros((EDGE, pitch), jnp.float32) if x is None else x for x in layers]
        corner = to_edges(layers, pitch)
        corner = jnp.where(segment == 0, pltpu.roll(dleft_ref[g], to_first, 1), corner)
        corner = jnp.where(segment == 3, pltpu.roll(dright_ref[g], to_last, 1), corner)
        corner = jnp.where(keep, corner, 0.0)
        target[at, :span] = value
        target[at, span:] = corner

    field = lax.dot_general(
        modes_a_ref[...] + modes_b_ref[...], synth_ref[...], (((1,), (1,)), ((), ())),
        precision=EXACT, preferred_element_type=jnp.float32,
    )

    def step(t, count):
        def body(a, carry):
            new = layer_update(jac_ref, state_ref, edge_ref, coef_ref, t, a)
            for c in range(components):
                state_ref[t + 1, c, a + 1] = new[c]
            return carry

        lax.fori_loop(0, count, body, 0)

    def edge_step(t):
        new = edge_update(jac_ref, edge_ref, edge_coef_ref, t, axial)
        for c in range(components):
            edge_ref[t + 1, c] = new[c]

    step(0, axial)
    edge_step(0)
    for c in range(components):
        state_ref[1, c, axial] += inv_ref[...] * field[:, c * pitch:(c + 1) * pitch]
        edge_ref[1, c] += edge_coef_ref[components + 6] * edge_boundary(field, c, components, pitch, axial)

    def later(t, carry):
        step(t, jnp.where(t == 1, axial, axial - t))

        @pl.when(t < axial - 1)
        def _():
            edge_step(t)

        return carry

    lax.fori_loop(1, axial, later, 0)

    component, _, _ = column(lanes((pitch, pitch)))
    total = jnp.zeros((axial * wide, pitch), jnp.float32)
    for c in range(components):
        strips = jnp.concatenate([state_ref[t, c, 1] for t in range(1, axial + 1)], 0)
        total += jnp.dot(
            strips, jnp.where(component == c, table_ref[...], 0.0),
            precision=EXACT, preferred_element_type=jnp.float32,
        )
    modes_ref[...] = total
    for n, (t, a) in enumerate(fronts):
        front_ref[n] = state_ref[t, :, a + 1]
    edge_front_ref[...] = edge_ref[2]


def second_kernel(
    jac_ref, coef_ref, inv_ref, edge_coef_ref, front_ref, edge_front_ref, modes_a_ref, modes_b_ref, synth_ref,
    out_ref, state_ref, edge_ref, bound_ref, edge_bound_ref, *, fronts,
):
    components, axial, span, pitch = out_ref.shape
    wide = span + EDGE
    for t in range(state_ref.shape[0]):
        for c in range(components):
            state_ref[t, c, 0] = jnp.zeros((wide, pitch), jnp.float32)
            state_ref[t, c, axial + 1] = jnp.zeros((wide, pitch), jnp.float32)
    for n, (t, a) in enumerate(fronts):
        state_ref[t, :, a + 1] = front_ref[n]
    field = lax.dot_general(
        modes_a_ref[...] + modes_b_ref[...], synth_ref[...], (((1,), (1,)), ((), ())),
        precision=EXACT, preferred_element_type=jnp.float32,
    )
    for n in range(axial):
        part = field[n * wide:(n + 1) * wide]
        for c in range(components):
            bound_ref[n, c] = inv_ref[...] * part[:, c * pitch:(c + 1) * pitch]
            edge_bound_ref[n, c] = edge_coef_ref[components + 6] * edge_boundary(part, c, components, pitch, axial)
    for c in range(components):
        state_ref[2, c, axial] += bound_ref[0, c]
        edge_ref[2, c] = edge_front_ref[c] + edge_bound_ref[0, c]

    def later(t, carry):
        def body(a, inner):
            new = layer_update(jac_ref, state_ref, edge_ref, coef_ref, t, a)
            for c in range(components):
                state_ref[t + 1, c, a + 1] = new[c]
            return inner

        lax.fori_loop(axial - t, axial, body, 0)
        for c in range(components):
            state_ref[t + 1, c, axial] += bound_ref[t - 1, c]
        new = edge_update(jac_ref, edge_ref, edge_coef_ref, t, axial)
        for c in range(components):
            edge_ref[t + 1, c] = new[c] + edge_bound_ref[t - 1, c]
        return carry

    lax.fori_loop(2, axial, later, 0)

    def final(a, carry):
        new = layer_update(jac_ref, state_ref, edge_ref, coef_ref, axial, a)
        for c in range(components):
            out_ref[c, a] = new[c][:span]
        return carry

    lax.fori_loop(0, axial, final, 0)
    for c in range(components):
        out_ref[c, axial - 1] += bound_ref[axial - 1, c, :span]


def moved(x, to):
    sizes = [lax.axis_size(name) for name in AXES]
    pairs = []
    for r in range(sizes[0]):
        for s in range(sizes[1]):
            for p in range(sizes[2]):
                target = to(r, s, p)
                if all(0 <= at < size for at, size in zip(target, sizes)):
                    number = lambda at: (at[0] * sizes[1] + at[1]) * sizes[2] + at[2]
                    pairs.append((number((r, s, p)), number(target)))
    return lax.ppermute(x, AXES, pairs)


def struct(*shape):
    return jax.ShapeDtypeStruct(shape, jnp.float32)


def on_device(
    adjoint_start, source, couplings, damping, jacobians, giles_real, giles_imag, blades, mode_orders, cell_map,
):
    components, axial, span, pitch = adjoint_start.shape
    row_count, span_count, place_count = (lax.axis_size(name) for name in AXES)
    length = pitch * place_count
    assert components == COMPONENTS and components * WAVES <= pitch
    assert axial == ITERS - 1 and ITERS <= EDGE and axial * SEGMENT_LANES == pitch
    assert span_count == 2 and place_count & (place_count - 1) == 0
    wide = span + EDGE
    fields = 2 * components + 6
    groups = fields // 4 + 1
    smem = pl.BlockSpec(memory_space=pltpu.SMEM)
    vmem = pl.BlockSpec(memory_space=pltpu.VMEM)

    (coef, inv, edges, span_out, right, left, dright, dleft, table, modes, modes_edge) = pl.pallas_call(
        functools.partial(pack_kernel, row_count=row_count, length=length),
        out_shape=(
            struct(components + 6, axial, span, pitch), struct(span, pitch), struct(fields + 1, span, pitch),
            struct(fields * axial + 1, EDGE, pitch), struct(groups, span, pitch), struct(groups, span, pitch),
            struct(groups, EDGE, pitch), struct(groups, EDGE, pitch), struct(pitch, pitch),
            struct(span, pitch), struct(EDGE, pitch),
        ),
        in_specs=[smem] + [vmem] * 4,
        out_specs=[vmem] * 11,
        compiler_params=PARAMS,
        name="pack",
    )(blades, adjoint_start, source, couplings, damping)

    up_own = moved(modes, lambda r, s, p: (r - 1, s, p))
    up_other = moved(modes_edge, lambda r, s, p: (r - 1, 1 - s, p))
    from_span = moved(span_out, lambda r, s, p: (r, 1 - s, p))
    from_left = moved(right, lambda r, s, p: (r, s, (p + 1) % place_count))
    from_right = moved(left, lambda r, s, p: (r, s, (p - 1) % place_count))
    dleft_in = moved(dright, lambda r, s, p: (r, 1 - s, (p + 1) % place_count))
    dright_in = moved(dleft, lambda r, s, p: (r, 1 - s, (p - 1) % place_count))

    face = jnp.minimum(lax.axis_index("row"), row_count - 2)

    def of_face(giles):
        picked = lax.dynamic_index_in_dim(giles, face, 0, keepdims=False)
        return picked.transpose(1, 2, 0).reshape(components * components, -1)

    synth_rows = -(-components * (pitch + SEGMENT_LANES) // pitch) * pitch
    synth = pl.pallas_call(
        functools.partial(
            synth_kernel, row_count=row_count, place_count=place_count, components=components, pitch=pitch,
            length=length, axial=axial,
        ),
        out_shape=struct(synth_rows, pitch),
        in_specs=[smem] + [vmem] * 4,
        out_specs=vmem,
        compiler_params=PARAMS,
        name="synth",
    )(blades, of_face(giles_real), of_face(giles_imag), mode_orders.transpose(0, 2, 1), cell_map)

    def exchanged(x, bit):
        return moved(x, lambda r, s, p: (r, s, p ^ bit))

    total = jnp.concatenate([up_own, up_other], 0)
    other = jnp.zeros_like(total)
    bit = 1
    while bit < place_count:
        total = total + other if bit > 1 else total
        other = exchanged(total, bit)
        bit *= 2

    jac = jacobians[0].transpose(1, 2, 0).reshape(components * components, 6)
    fronts = [(t, a) for t in range(2, axial + 1) for a in range(max(axial - t - 1, 0), max(axial - t + 1, axial if t == 2 else 0))]
    coefx, invx, edge_coef, front, edge_front, modes = pl.pallas_call(
        functools.partial(first_kernel, fronts=fronts),
        out_shape=(
            struct(components + 6, axial, wide, pitch), struct(wide, pitch), struct(components + 7, wide, pitch),
            struct(len(fronts), components, wide, pitch), struct(components, wide, pitch), struct(axial * wide, pitch),
        ),
        in_specs=[smem] + [vmem] * 13,
        out_specs=[vmem] * 6,
        scratch_shapes=[
            pltpu.VMEM((axial + 1, components, axial + 2, wide, pitch), jnp.float32),
            pltpu.VMEM((axial + 1, components, wide, pitch), jnp.float32),
        ],
        compiler_params=PARAMS,
        name="first_sweeps",
    )(
        jac, adjoint_start, coef, inv, edges, from_span, from_left, from_right, dleft_in, dright_in, table,
        total, other, synth,
    )

    bit = 1
    while 2 * bit < place_count:
        modes = modes + exchanged(modes, bit)
        bit *= 2
    modes_a = moved(modes, lambda r, s, p: (r - 1, s, p))
    if bit < place_count:
        modes_b = moved(modes, lambda r, s, p: (r - 1, s, p ^ bit))
    else:
        modes_b = jnp.zeros_like(modes)
    return pl.pallas_call(
        functools.partial(second_kernel, fronts=fronts),
        out_shape=struct(components, axial, span, pitch),
        in_specs=[smem] + [vmem] * 8,
        out_specs=vmem,
        scratch_shapes=[
            pltpu.VMEM((axial + 1, components, axial + 2, wide, pitch), jnp.float32),
            pltpu.VMEM((axial + 1, components, wide, pitch), jnp.float32),
            pltpu.VMEM((axial, components, wide, pitch), jnp.float32),
            pltpu.VMEM((axial, components, wide, pitch), jnp.float32),
        ],
        compiler_params=PARAMS,
        name="second_sweeps",
    )(jac, coefx, invx, edge_coef, front, edge_front, modes_a, modes_b, synth)


def solution(mesh):
    placed = (
        P(None, "row", "span", "pitch"),
        P(None, "row", "span", "pitch"),
        P(None, "row", "span", "pitch"),
        P("row", "span", "pitch"),
        P("row", None, None, None),
        P(),
        P(),
        P(),
        P(),
        P("row", None),
    )
    return jax.shard_map(
        on_device,
        mesh=mesh,
        in_specs=placed,
        out_specs=P(None, "row", "span", "pitch"),
        check_vma=False,
    )
```

```python
import functools
import math

import jax
import jax.numpy as jnp
from jax import lax
from jax.experimental import pallas as pl
from jax.experimental.pallas import tpu as pltpu
from jax.sharding import PartitionSpec as P

ITERS = 5
AXES = ("row", "span", "pitch")

ORDER_MAX = 2
BASE = 2 * ORDER_MAX + 1
COSINES = (BASE * BASE + 1) // 2
WAVES = 2 * COSINES - 1
COMPONENTS = 5
EDGE = 8
HALF = EDGE // 2
SEGMENT_LANES = 4 * EDGE
EXACT = lax.Precision.HIGHEST
PARAMS = pltpu.CompilerParams(vmem_limit_bytes=40 * 1024 * 1024)


def lanes(shape):
    return lax.broadcasted_iota(jnp.int32, shape, len(shape) - 1)


def rows(shape):
    return lax.broadcasted_iota(jnp.int32, shape, len(shape) - 2)


def column(j):
    component = (j * 41) >> 10
    wave = j - WAVES * component
    sine = wave >= COSINES
    return component, jnp.where(sine, wave - (COSINES - 1), wave), sine


def mode_number(mode, blades_ref, face):
    high = ((mode + ORDER_MAX) * 13) >> 6
    low = mode - BASE * high
    return high * blades_ref[face] + low * blades_ref[face + 1]


def waves(products, length):
    if length & (length - 1) == 0:
        phase = products & (length - 1)
    else:
        phase = jnp.mod(products, length)
    turn = phase.astype(jnp.float32) * (1.0 / length)
    quarter = jnp.floor(4.0 * turn + 0.5)
    x = (turn - 0.25 * quarter) * (2.0 * math.pi)
    y = x * x
    sine = x * (1.0 + y * (-1.0 / 6 + y * (1.0 / 120 + y * (-1.0 / 5040 + y * (1.0 / 362880)))))
    cosine = 1.0 + y * (-0.5 + y * (1.0 / 24 + y * (-1.0 / 720 + y * (1.0 / 40320 - y * (1.0 / 3628800)))))
    quarter = quarter.astype(jnp.int32) & 3
    odd = (quarter & 1) == 1
    cos_out = jnp.where(odd, sine, cosine)
    sin_out = jnp.where(odd, cosine, sine)
    cos_out = jnp.where((quarter == 1) | (quarter == 2), -cos_out, cos_out)
    sin_out = jnp.where(quarter >= 2, -sin_out, sin_out)
    return cos_out, sin_out


def to_edges(layers, pitch):
    lane = lanes(layers[0].shape)
    block = jnp.zeros_like(layers[0])
    for a, layer in enumerate(layers):
        if layer is None:
            continue
        start = a * SEGMENT_LANES
        first = pltpu.roll(layer, (start + EDGE) % pitch, layer.ndim - 1)
        last = pltpu.roll(layer, (start + 3 * EDGE) % pitch, layer.ndim - 1)
        block = jnp.where((lane >= start + EDGE) & (lane < start + 2 * EDGE), first, block)
        block = jnp.where((lane >= start + 2 * EDGE) & (lane < start + 3 * EDGE), last, block)
    return block


def half_rows(side):
    return jnp.where(side == 0, EDGE // 2, 0), jnp.where(side == 0, 0, EDGE // 2)


def slots(fields, components):
    per_group = SEGMENT_LANES // HALF
    near = [(f // per_group, f % per_group * HALF) for f in range(fields)]
    group, lane = near[-1]
    far = [(group, lane + HALF + c) for c in range(components)]
    return near, far


def pack_kernel(
    blades_hbm, adjoint_hbm, source_hbm, couplings_hbm, damping_hbm,
    coef_ref, inv_ref, edges_ref, span_ref, corner_ref, right_ref, left_ref, table_ref,
    blades_ref, adjoint_ref, source_ref, couplings_ref, damping_ref, sems, *, length,
):
    components, axial, span, pitch = adjoint_ref.shape
    copies = [
        pltpu.make_async_copy(src, dst, sems.at[n])
        for n, (src, dst) in enumerate((
            (couplings_hbm, couplings_ref), (damping_hbm, damping_ref), (source_hbm, source_ref),
            (adjoint_hbm, adjoint_ref), (blades_hbm, blades_ref),
        ))
    ]
    for copy in copies:
        copy.start()
    row, side, place = (lax.axis_index(name) for name in AXES)
    copies[0].wait()
    copies[1].wait()
    diag = damping_ref[...]
    for d in range(6):
        diag = diag + couplings_ref[d]
    inverse = 1.0 / diag
    for d in range(6):
        coef_ref[components + d] = couplings_ref[d] * inverse
    inv_ref[...] = inverse[axial - 1]
    copies[2].wait()
    for c in range(components):
        coef_ref[c] = source_ref[c] * inverse
    copies[3].wait()

    fields = 2 * components + 6
    for f in range(fields):
        ref, at = (adjoint_ref, f) if f < components else (coef_ref, f - components)
        edges_ref[f] = to_edges([ref[at, a] for a in range(axial)], pitch)
    last = inv_ref[...]
    edges_ref[fields] = jnp.where(
        lanes(last.shape) >= (axial - 1) * SEGMENT_LANES,
        to_edges([jnp.zeros_like(last)] * (axial - 1) + [last], pitch), 0.0,
    )
    edge_row = pl.multiple_of(jnp.where(side == 0, span - EDGE, 0), EDGE)
    near, far = slots(fields + 1, components)
    groups = right_ref.shape[0]
    lane = lanes((span, pitch)) % SEGMENT_LANES
    for n, (out_ref, near_at, far_at) in enumerate((
        (right_ref, 3 * EDGE - HALF, 3 * EDGE - HALF - 1), (left_ref, EDGE, EDGE + HALF),
    )):
        packed = [jnp.zeros((span, pitch), jnp.float32) for _ in range(groups)]
        for f, (g, to) in enumerate(near):
            value = pltpu.roll(edges_ref[f], (to - near_at) % pitch, 1)
            packed[g] = jnp.where((lane >= to) & (lane < to + HALF), value, packed[g])
        for f, (g, to) in enumerate(far):
            packed[g] = jnp.where(lane == to, pltpu.roll(edges_ref[f], (to - far_at) % pitch, 1), packed[g])
        for g in range(groups):
            out_ref[g, :span] = packed[g]
            corner_ref[n * groups + g] = out_ref[g, pl.ds(edge_row, EDGE), :]

    to_low, to_high = half_rows(side)
    line = rows((EDGE, pitch))
    tiles = [(adjoint_ref, c, a) for c in range(components) for a in range(axial)]
    tiles += [(coef_ref, f, a) for f in range(components + 6) for a in range(axial)]
    tiles = [ref[f, a, pl.ds(edge_row, EDGE), :] for ref, f, a in tiles] + [inv_ref[pl.ds(edge_row, EDGE), :]]
    pairs = -(-len(tiles) // 2)
    for n in range(pairs):
        value = pltpu.roll(tiles[2 * n], to_low, 0)
        if 2 * n + 1 < len(tiles):
            value = jnp.where(line < HALF, value, pltpu.roll(tiles[2 * n + 1], to_high, 0))
        span_ref[n] = value
    fifth = jnp.where(side == 0, HALF - 1, HALF)
    for n in range(span_ref.shape[0] - pairs):
        value = jnp.zeros((EDGE, pitch), jnp.float32)
        for k in range(min(EDGE, components * axial - n * EDGE)):
            value = jnp.where(line == k, pltpu.roll(tiles[n * EDGE + k], lax.rem(k + EDGE - fifth, EDGE), 0), value)
        span_ref[pairs + n] = value

    copies[4].wait()
    component, mode, sine = column(lanes((pitch, pitch)))
    number = mode_number(mode, blades_ref, jnp.maximum(row - 1, 0))
    cos_table, sin_table = waves(number * (place * pitch + rows((pitch, pitch))), length)
    table_ref[...] = jnp.where(component < components, jnp.where(sine, sin_table, cos_table), 0.0)


def projected(strips, table):
    component, _, _ = column(lanes(table.shape))
    total = jnp.zeros((strips[0].shape[0], table.shape[1]), jnp.float32)
    for c, strip in enumerate(strips):
        total += jnp.dot(
            strip, jnp.where(component == c, table, 0.0), precision=EXACT, preferred_element_type=jnp.float32,
        )
    return total


def synthesised(modes, synth):
    return lax.dot_general(
        modes, synth, (((1,), (1,)), ((), ())), precision=EXACT, preferred_element_type=jnp.float32,
    )


def synth_kernel(
    blades_ref, giles_re_ref, giles_im_ref, orders_ref, cells_ref, after_ref, synth_ref,
    *, row_count, place_count, components, pitch, length, axial,
):
    row, place = lax.axis_index("row"), lax.axis_index("pitch")
    face = jnp.minimum(row, row_count - 2)
    modes = orders_ref.shape[2]
    orders = orders_ref[face]
    tag = BASE * orders[0:1] + orders[1:2]
    component, mode, _ = column(rows((pitch, modes)))
    same = (jnp.abs(tag) == mode) & (component < components)
    plain = jnp.where(same, 1.0, 0.0)
    signed = jnp.where(tag < 0, -plain, plain)
    dims = (((1,), (1,)), ((), ()))
    sums_re = lax.dot_general(giles_re_ref[...], plain, dims, precision=EXACT, preferred_element_type=jnp.float32)
    sums_im = lax.dot_general(giles_im_ref[...], signed, dims, precision=EXACT, preferred_element_type=jnp.float32)
    component, mode, sine = column(lanes(sums_re.shape))
    scale = 2.0 / length
    with_cos = jnp.where(sine, sums_im, sums_re) * scale
    with_sin = jnp.where(sine, sums_re, -sums_im) * scale
    component = component[0:1]

    def chunk(at):
        start = pl.multiple_of(lax.rem(place + at + place_count, place_count) * pitch, pitch)
        return cells_ref[:, pl.ds(start, pitch)]

    own = chunk(0)
    lane = lanes((1, pitch))
    first = (axial - 1) * SEGMENT_LANES
    edge = jnp.where(lane < first + EDGE, pltpu.roll(chunk(-1), (first + EDGE) % pitch, 1), pltpu.roll(own, (first + EDGE) % pitch, 1))
    edge = jnp.where(lane < first + 2 * EDGE, edge, pltpu.roll(own, (first + 3 * EDGE) % pitch, 1))
    edge = jnp.where(lane < first + 3 * EDGE, edge, pltpu.roll(chunk(1), (first + 3 * EDGE) % pitch, 1))

    def upright(cells):
        wide = jnp.broadcast_to(cells.astype(jnp.float32), (pitch, pitch))
        return jnp.transpose(wide).astype(jnp.int32)

    edge_cells = upright(edge)[first:first + SEGMENT_LANES]
    at_cells = jnp.concatenate([upright(own), edge_cells], 0)
    _, mode, _ = column(lanes(at_cells.shape))
    cos_table, sin_table = waves(mode_number(mode, blades_ref, face) * at_cells, length)
    for c in range(components):
        row_cos = jnp.zeros((1, pitch), jnp.float32)
        row_sin = jnp.zeros((1, pitch), jnp.float32)
        for b in range(components):
            at = b * components + c
            row_cos = jnp.where(component == b, with_cos[at:at + 1], row_cos)
            row_sin = jnp.where(component == b, with_sin[at:at + 1], row_sin)
        part = row_cos * cos_table + row_sin * sin_table
        synth_ref[pl.ds(c * pitch, pitch), :] = part[:pitch]
        synth_ref[pl.ds(components * pitch + c * SEGMENT_LANES, SEGMENT_LANES), :] = part[pitch:]
    used = components * (pitch + SEGMENT_LANES)
    rest = synth_ref.shape[0] - used
    if rest:
        synth_ref[pl.ds(used, rest), :] = jnp.zeros((rest, pitch), jnp.float32)


def mixed(jac_ref, source, couplings, neighbours):
    total = list(source)
    for d, neighbour in enumerate(neighbours):
        for c in range(len(total)):
            term = jac_ref[c, d] * neighbour[0]
            for b in range(1, len(total)):
                term = term + jac_ref[b * len(total) + c, d] * neighbour[b]
            total[c] = total[c] + couplings[d] * term
    return total


def layer_update(jac_ref, state_ref, edge_ref, coef_ref, t, a):
    components, wide, pitch = state_ref.shape[1], state_ref.shape[3], state_ref.shape[4]
    lane = lanes((wide, pitch))
    start = a * SEGMENT_LANES
    own = [state_ref[t, c, a + 1] for c in range(components)]
    above = [state_ref[t, c, a + 2] for c in range(components)]
    below = [state_ref[t, c, a] for c in range(components)]
    edge = [edge_ref[t, c] for c in range(components)]
    span_next = [pltpu.roll(x, wide - 1, 0) for x in own]
    span_prev = [pltpu.roll(x, 1, 0) for x in own]
    to_end = 2 * pitch - 1 - (start + 3 * EDGE)
    to_begin = 2 * pitch - (start + EDGE - 1)
    pitch_next = [
        jnp.where(lane == pitch - 1, pltpu.roll(e, lax.rem(to_end, pitch), 1), pltpu.roll(x, pitch - 1, 1))
        for e, x in zip(edge, own)
    ]
    pitch_prev = [
        jnp.where(lane == 0, pltpu.roll(e, lax.rem(to_begin, pitch), 1), pltpu.roll(x, 1, 1))
        for e, x in zip(edge, own)
    ]
    source = [coef_ref[c, a] for c in range(components)]
    couplings = [coef_ref[components + d, a] for d in range(6)]
    return mixed(jac_ref, source, couplings, (above, below, span_next, span_prev, pitch_next, pitch_prev))


def edge_update(jac_ref, edge_ref, edge_coef_ref, t, axial):
    components, wide, pitch = edge_ref.shape[1:]
    lane = lanes((wide, pitch))
    own = [edge_ref[t, c] for c in range(components)]
    above = [jnp.where(lane < (axial - 1) * SEGMENT_LANES, pltpu.roll(x, pitch - SEGMENT_LANES, 1), 0.0) for x in own]
    below = [jnp.where(lane >= SEGMENT_LANES, pltpu.roll(x, SEGMENT_LANES, 1), 0.0) for x in own]
    span_next = [pltpu.roll(x, wide - 1, 0) for x in own]
    span_prev = [pltpu.roll(x, 1, 0) for x in own]
    pitch_next = [pltpu.roll(x, pitch - 1, 1) for x in own]
    pitch_prev = [pltpu.roll(x, 1, 1) for x in own]
    source = [edge_coef_ref[c] for c in range(components)]
    couplings = [edge_coef_ref[components + d] for d in range(6)]
    return mixed(jac_ref, source, couplings, (above, below, span_next, span_prev, pitch_next, pitch_prev))


def edge_boundary(field, c, components, pitch, axial):
    at = components * pitch + c * SEGMENT_LANES
    tile = field[:, (at // pitch) * pitch:(at // pitch + 1) * pitch]
    return pltpu.roll(tile, ((axial - 1) * SEGMENT_LANES - at % pitch) % pitch, 1)


def advance(refs, t, a):
    state_ref = refs[1]
    for c, value in enumerate(layer_update(*refs, t, a)):
        state_ref[t + 1, c, a + 1] = value


def first_kernel(
    jac_ref, adjoint_ref, coef_in_ref, inv_in_ref, edges_ref, span_ref, from_left_ref, from_right_ref, table_ref,
    coef_ref, inv_ref, edge_coef_ref, state_ref, edge_ref, modes_ref,
):
    components, axial, span, pitch = adjoint_ref.shape
    wide = span + EDGE
    side = lax.axis_index("span")
    fields = 2 * components + 6
    line = rows((EDGE, pitch))
    keep_half = jnp.where(side == 0, line, EDGE - 1 - line) < HALF
    fifth = jnp.where(side == 0, HALF, HALF - 1)
    from_low, from_high = half_rows(1 - side)
    pairs = -(-(fields * axial + 1) // 2)

    def ghost(n):
        value = pltpu.roll(span_ref[n // 2], from_high if n % 2 else from_low, 0)
        value = jnp.where(keep_half, value, 0.0)
        if n < components * axial:
            extra = pltpu.roll(span_ref[pairs + n // EDGE], lax.rem(fifth + EDGE - n % EDGE, EDGE), 0)
            value = jnp.where(line == fifth, extra, value)
        return value

    near, far = slots(fields + 1, components)
    keep_five = keep_half | (line == fifth)
    for f in range(fields + 1):
        if f < fields:
            layers = [ghost(f * axial + a) for a in range(axial)]
        else:
            layers = [jnp.zeros((EDGE, pitch), jnp.float32)] * (axial - 1) + [ghost(fields * axial)]
        if f < components:
            for a in range(axial):
                state_ref[0, f, a + 1, :span] = adjoint_ref[f, a]
                state_ref[0, f, a + 1, span:] = layers[a]
        elif f < fields:
            for a in range(axial):
                coef_ref[f - components, a, :span] = coef_in_ref[f - components, a]
                coef_ref[f - components, a, span:] = layers[a]
        else:
            inv_ref[:span] = inv_in_ref[...]
            inv_ref[span:] = layers[-1]
        g, at = near[f]
        value = jnp.concatenate([edges_ref[f], to_edges(layers, pitch)], 0)
        lane = lanes((wide, pitch)) % SEGMENT_LANES
        value = jnp.where((lane >= HALF) & (lane < EDGE), pltpu.roll(from_left_ref[g], (HALF - at) % pitch, 1), value)
        value = jnp.where(
            (lane >= 3 * EDGE) & (lane < 3 * EDGE + HALF),
            pltpu.roll(from_right_ref[g], (3 * EDGE - at) % pitch, 1), value,
        )
        if f < components:
            g, at = far[f]
            value = jnp.where(lane == HALF - 1, pltpu.roll(from_left_ref[g], (HALF - 1 - at) % pitch, 1), value)
            value = jnp.where(
                lane == 3 * EDGE + HALF, pltpu.roll(from_right_ref[g], (3 * EDGE + HALF - at) % pitch, 1), value,
            )
        target, at = (edge_ref.at[0], f) if f < components else (edge_coef_ref, f - components)
        target[at, :span] = value[:span]
        target[at, span:] = jnp.where(keep_five if f < components else keep_half, value[span:], 0.0)
    for t in range(state_ref.shape[0]):
        for c in range(components):
            state_ref[t, c, 0] = jnp.zeros((wide, pitch), jnp.float32)
            state_ref[t, c, axial + 1] = jnp.zeros((wide, pitch), jnp.float32)

    refs = (jac_ref, state_ref, edge_ref, coef_ref)

    def sweep(t, carry):
        def body(a, inner):
            advance(refs, t, a)
            return inner

        lax.fori_loop(0, axial - 1 - t, body, 0)

        @pl.when(t < axial - 2)
        def _():
            for c, value in enumerate(edge_update(jac_ref, edge_ref, edge_coef_ref, t, axial)):
                edge_ref[t + 1, c] = value

        return carry

    lax.fori_loop(0, axial - 1, sweep, 0)
    strips = [jnp.concatenate([state_ref[t, c, 1] for t in range(axial)], 0) for c in range(components)]
    total = projected(strips, table_ref[...])
    to_low, to_high = half_rows(1 - side)
    for t in range(axial):
        modes_ref[pl.ds(t * span, span), :] = total[t * wide:t * wide + span]
    for n in range(axial // 2):
        low = total[2 * n * wide + span:2 * n * wide + wide]
        high = total[(2 * n + 1) * wide + span:(2 * n + 1) * wide + wide]
        both = jnp.where(line < HALF, pltpu.roll(low, to_low, 0), pltpu.roll(high, to_high, 0))
        modes_ref[pl.ds(axial * span + n * EDGE, EDGE), :] = both


def middle_kernel(
    jac_ref, coef_ref, edge_coef_ref, state_in_ref, edge_in_ref, table_ref, state_ref, edge_ref, modes_ref,
):
    components, axial, span = state_ref.shape[1], state_ref.shape[2] - 2, modes_ref.shape[0]
    refs = (jac_ref, state_ref, edge_ref, coef_ref)
    for c, value in enumerate(edge_update(jac_ref, edge_ref, edge_coef_ref, axial - 2, axial)):
        edge_ref[axial - 1, c] = value

    def body(t, carry):
        advance(refs, t, axial - 1 - t)
        return carry

    lax.fori_loop(0, axial, body, 0)
    modes_ref[...] = projected([state_ref[axial, c, 1, :span] for c in range(components)], table_ref[...])


def along_axis(jac_ref, coef_ref, delta, a, height):
    components = len(delta)
    out = []
    for c in range(components):
        term = jac_ref[c, 0] * delta[0]
        for b in range(1, components):
            term = term + jac_ref[b * components + c, 0] * delta[b]
        out.append(coef_ref[components, a, :height] * term)
    return out


def link_kernel(jac_ref, coef_ref, inv_ref, part_ref, modes_a_ref, modes_b_ref, synth_ref, table_ref, modes_ref):
    span, pitch = modes_ref.shape
    components, axial = coef_ref.shape[0] - 6, coef_ref.shape[1]
    modes = modes_a_ref[:span] + modes_b_ref[:span]
    field = synthesised(modes, synth_ref[:components * pitch])
    delta = [inv_ref[:span] * field[:, c * pitch:(c + 1) * pitch] for c in range(components)]
    for a in range(axial - 2, -1, -1):
        delta = along_axis(jac_ref, coef_ref, delta, a, span)
    modes_ref[...] = part_ref[...] + projected(delta, table_ref[...])


def second_kernel(
    jac_ref, coef_ref, inv_ref, edge_coef_ref, state_in_ref, edge_in_ref, modes_a_ref, modes_b_ref, synth_ref, after_ref,
    state_ref, edge_ref, bound_ref,
):
    components, axial = state_ref.shape[1], state_ref.shape[2] - 2
    wide, pitch = state_ref.shape[3:]
    span = wide - EDGE
    from_low, from_high = half_rows(1 - lax.axis_index("span"))
    packed = modes_a_ref[...] + modes_b_ref[...]
    parts = []
    for t in range(axial):
        ghost = packed[axial * span + t // 2 * EDGE:axial * span + (t // 2 + 1) * EDGE]
        parts += [packed[t * span:(t + 1) * span], pltpu.roll(ghost, from_high if t % 2 else from_low, 0)]
    field = synthesised(jnp.concatenate(parts, 0), synth_ref[...])
    edge_bound = []
    for n in range(axial):
        part = field[n * wide:(n + 1) * wide]
        edge_bound.append([])
        for c in range(components):
            bound_ref[n, c] = inv_ref[...] * part[:, c * pitch:(c + 1) * pitch]
            edge_bound[n].append(edge_coef_ref[components + 6] * edge_boundary(part, c, components, pitch, axial))
    delta = [bound_ref[0, c] for c in range(components)]
    for t in range(1, axial + 1):
        for c in range(components):
            state_ref[t, c, axial + 1 - t] += delta[c]
        if t < axial:
            delta = along_axis(jac_ref, coef_ref, delta, axial - 1 - t, wide)
    for c in range(components):
        edge_ref[1, c] += edge_bound[0][c]
    for t in range(1, axial):
        for c, value in enumerate(edge_update(jac_ref, edge_ref, edge_coef_ref, t, axial)):
            edge_ref[t + 1, c] = value + edge_bound[t][c]
    rest_of_sweeps(jac_ref, coef_ref, state_ref, edge_ref, bound_ref, 1, axial - 1)


def rest_of_sweeps(jac_ref, coef_ref, state_ref, edge_ref, bound_ref, first, last):
    components, axial = state_ref.shape[1], state_ref.shape[2] - 2
    refs = (jac_ref, state_ref, edge_ref, coef_ref)

    def sweep(t, carry):
        def body(a, inner):
            advance(refs, t, a)
            return inner

        lax.fori_loop(axial - t, axial, body, 0)
        for c in range(components):
            state_ref[t + 1, c, axial] += bound_ref[t, c]
        return carry

    lax.fori_loop(first, last, sweep, 0)


def third_kernel(jac_ref, coef_ref, state_in_ref, edge_ref, bound_ref, after_ref, state_ref, out_ref):
    components, axial, span, _ = out_ref.shape
    rest_of_sweeps(jac_ref, coef_ref, state_ref, edge_ref, bound_ref, axial - 1, axial)

    def final(a, carry):
        for c, value in enumerate(layer_update(jac_ref, state_ref, edge_ref, coef_ref, axial, a)):
            out_ref[c, a] = value[:span]
        return carry

    lax.fori_loop(0, axial, final, 0)


def last_kernel(inv_ref, modes_a_ref, modes_b_ref, synth_ref, swept_ref, out_ref):
    components, axial, span, pitch = out_ref.shape
    field = synthesised(modes_a_ref[...] + modes_b_ref[...], synth_ref[:components * pitch])
    for c in range(components):
        for a in range(axial - 1):
            out_ref[c, a] = swept_ref[c, a]
        out_ref[c, axial - 1] = swept_ref[c, axial - 1] + inv_ref[:span] * field[:, c * pitch:(c + 1) * pitch]


def moved(x, to):
    sizes = [lax.axis_size(name) for name in AXES]
    pairs = []
    for r in range(sizes[0]):
        for s in range(sizes[1]):
            for p in range(sizes[2]):
                target = to(r, s, p)
                if all(0 <= at < size for at, size in zip(target, sizes)):
                    number = lambda at: (at[0] * sizes[1] + at[1]) * sizes[2] + at[2]
                    pairs.append((number((r, s, p)), number(target)))
    return lax.ppermute(x, AXES, pairs)


def struct(*shape):
    return jax.ShapeDtypeStruct(shape, jnp.float32)


def on_device(
    adjoint_start, source, couplings, damping, jacobians, giles_real, giles_imag, blades, mode_orders, cell_map,
):
    components, axial, span, pitch = adjoint_start.shape
    row_count, span_count, place_count = (lax.axis_size(name) for name in AXES)
    length = pitch * place_count
    assert components == COMPONENTS and components * WAVES <= pitch
    assert axial == ITERS - 1 and ITERS <= EDGE and axial * SEGMENT_LANES == pitch
    assert span_count == 2 and place_count & (place_count - 1) == 0
    wide = span + EDGE
    fields = 2 * components + 6
    groups = slots(fields + 1, components)[1][-1][0] + 1
    pairs = -(-(fields * axial + 1) // 2)
    span_tiles = pairs + -(-components * axial // EDGE)
    smem = pl.BlockSpec(memory_space=pltpu.SMEM)
    vmem = pl.BlockSpec(memory_space=pltpu.VMEM)
    hbm = pl.BlockSpec(memory_space=pltpu.HBM)
    anywhere = pl.BlockSpec(memory_space=pl.ANY)

    def call(kernel, name, outs, ins, aliases=None, scratch=(), **fixed):
        specs = [spec for spec, _ in ins]
        return pl.pallas_call(
            functools.partial(kernel, **fixed),
            out_shape=outs,
            in_specs=specs,
            out_specs=jax.tree.map(lambda _: vmem, outs),
            scratch_shapes=scratch,
            input_output_aliases=aliases or {},
            compiler_params=PARAMS,
            name=name,
        )(*[value for _, value in ins])

    coef, inv, edges, span_out, corner, right, left, table = call(
        pack_kernel, "pack",
        (
            struct(components + 6, axial, span, pitch), struct(span, pitch), struct(fields + 1, span, pitch),
            struct(span_tiles, EDGE, pitch), struct(2 * groups, EDGE, pitch), struct(groups, wide, pitch),
            struct(groups, wide, pitch), struct(pitch, pitch),
        ),
        [(hbm, blades), (hbm, adjoint_start), (hbm, source), (hbm, couplings), (hbm, damping)],
        scratch=[
            pltpu.SMEM(blades.shape, jnp.int32), pltpu.VMEM(adjoint_start.shape, jnp.float32),
            pltpu.VMEM(source.shape, jnp.float32), pltpu.VMEM(couplings.shape, jnp.float32),
            pltpu.VMEM(damping.shape, jnp.float32), pltpu.SemaphoreType.DMA((5,)),
        ],
        length=length,
    )
    corner = moved(corner, lambda r, s, p: (r, 1 - s, p))
    from_span = moved(span_out, lambda r, s, p: (r, 1 - s, p))
    right = lax.dynamic_update_slice(right, corner[:groups], (0, span, 0))
    left = lax.dynamic_update_slice(left, corner[groups:], (0, span, 0))
    from_left = moved(right, lambda r, s, p: (r, s, (p + 1) % place_count))
    from_right = moved(left, lambda r, s, p: (r, s, (p - 1) % place_count))

    jac = jacobians[0].transpose(1, 2, 0).reshape(components * components, 6)
    state_shape = struct(axial + 1, components, axial + 2, wide, pitch)
    edge_shape = struct(axial + 1, components, wide, pitch)
    coef, inv, edge_coef, state, edge, modes = call(
        first_kernel, "first_sweeps",
        (
            struct(components + 6, axial, wide, pitch), struct(wide, pitch), struct(components + 7, wide, pitch),
            state_shape, edge_shape, struct(axial * span + axial // 2 * EDGE, pitch),
        ),
        [(smem, jac)] + [(vmem, x) for x in (adjoint_start, coef, inv, edges, from_span, from_left, from_right, table)],
    )

    def summed(x):
        bit = 1
        while 2 * bit < place_count:
            x = x + moved(x, lambda r, s, p: (r, s, p ^ bit))
            bit *= 2
        if bit < place_count:
            far = moved(x, lambda r, s, p: (r - 1, s, p ^ bit))
        else:
            far = jnp.zeros_like(x)
        return x, moved(x, lambda r, s, p: (r - 1, s, p)), far

    state, edge, part = call(
        middle_kernel, "middle_sweeps", (state_shape, edge_shape, struct(span, pitch)),
        [(smem, jac)] + [(vmem, x) for x in (coef, edge_coef, state, edge, table)],
        aliases={3: 0, 4: 1},
    )
    halfway, modes_a, modes_b = summed(modes)

    giles_real, giles_imag, halfway = lax.optimization_barrier((giles_real, giles_imag, halfway))
    face = jnp.minimum(lax.axis_index("row"), row_count - 2)

    def of_face(giles):
        picked = lax.dynamic_index_in_dim(giles, face, 0, keepdims=False)
        return picked.transpose(1, 2, 0).reshape(components * components, -1)

    synth = call(
        synth_kernel, "synth", struct(-(-components * (pitch + SEGMENT_LANES) // pitch) * pitch, pitch),
        [(smem, blades), (vmem, of_face(giles_real)), (vmem, of_face(giles_imag))]
        + [(vmem, mode_orders.transpose(0, 2, 1)), (vmem, cell_map), (anywhere, halfway)],
        row_count=row_count, place_count=place_count, components=components, pitch=pitch, length=length, axial=axial,
    )
    late = call(
        link_kernel, "late_modes", struct(span, pitch),
        [(smem, jac)] + [(vmem, x) for x in (coef, inv, part, modes_a, modes_b, synth, table)],
    )
    halfway, late_a, late_b = summed(late)
    state, edge, bound = call(
        second_kernel, "second_sweeps", (state_shape, edge_shape, struct(axial, components, wide, pitch)),
        [(smem, jac)] + [(vmem, x) for x in (coef, inv, edge_coef, state, edge, modes_a, modes_b, synth)]
        + [(anywhere, late)],
        aliases={4: 0, 5: 1},
    )
    state, swept = call(
        third_kernel, "third_sweeps", (state_shape, struct(components, axial, span, pitch)),
        [(smem, jac)] + [(vmem, x) for x in (coef, state, edge, bound)] + [(anywhere, halfway)],
        aliases={2: 0},
    )
    return call(
        last_kernel, "last_boundary", struct(components, axial, span, pitch),
        [(vmem, x) for x in (inv, late_a, late_b, synth, swept)],
    )


def solution(mesh):
    placed = (
        P(None, "row", "span", "pitch"),
        P(None, "row", "span", "pitch"),
        P(None, "row", "span", "pitch"),
        P("row", "span", "pitch"),
        P("row", None, None, None),
        P(),
        P(),
        P(),
        P(),
        P("row", None),
    )
    return jax.shard_map(
        on_device,
        mesh=mesh,
        in_specs=placed,
        out_specs=P(None, "row", "span", "pitch"),
        check_vma=False,
    )
```

```python
import functools
import math

import jax
import jax.numpy as jnp
from jax import lax
from jax.experimental import pallas as pl
from jax.experimental.pallas import tpu as pltpu
from jax.sharding import PartitionSpec as P

ITERS = 5
AXES = ("row", "span", "pitch")

ORDER_MAX = 2
BASE = 2 * ORDER_MAX + 1
COSINES = (BASE * BASE + 1) // 2
WAVES = 2 * COSINES - 1
COMPONENTS = 5
EDGE = 8
HALF = EDGE // 2
SEGMENT_LANES = 4 * EDGE
EXACT = lax.Precision.HIGHEST
MIB = 1024 * 1024


def params(limit):
    return pltpu.CompilerParams(vmem_limit_bytes=limit)


def lanes(shape):
    return lax.broadcasted_iota(jnp.int32, shape, len(shape) - 1)


def rows(shape):
    return lax.broadcasted_iota(jnp.int32, shape, len(shape) - 2)


def column(j):
    component = (j * 41) >> 10
    wave = j - WAVES * component
    sine = wave >= COSINES
    return component, jnp.where(sine, wave - (COSINES - 1), wave), sine


def mode_number(mode, blades):
    high = ((mode + ORDER_MAX) * 13) >> 6
    low = mode - BASE * high
    return high * blades[0] + low * blades[1]


def waves(products, length):
    if length & (length - 1) == 0:
        phase = products & (length - 1)
    else:
        phase = jnp.mod(products, length)
    turn = phase.astype(jnp.float32) * (1.0 / length)
    quarter = jnp.floor(4.0 * turn + 0.5)
    x = (turn - 0.25 * quarter) * (2.0 * math.pi)
    y = x * x
    sine = x * (1.0 + y * (-1.0 / 6 + y * (1.0 / 120 + y * (-1.0 / 5040 + y * (1.0 / 362880)))))
    cosine = 1.0 + y * (-0.5 + y * (1.0 / 24 + y * (-1.0 / 720 + y * (1.0 / 40320 - y * (1.0 / 3628800)))))
    quarter = quarter.astype(jnp.int32) & 3
    odd = (quarter & 1) == 1
    cos_out = jnp.where(odd, sine, cosine)
    sin_out = jnp.where(odd, cosine, sine)
    cos_out = jnp.where((quarter == 1) | (quarter == 2), -cos_out, cos_out)
    sin_out = jnp.where(quarter >= 2, -sin_out, sin_out)
    return cos_out, sin_out


def to_edges(layers, pitch):
    lane = lanes(layers[0].shape)
    block = jnp.zeros_like(layers[0])
    for a, layer in enumerate(layers):
        if layer is None:
            continue
        start = a * SEGMENT_LANES
        first = pltpu.roll(layer, (start + EDGE) % pitch, layer.ndim - 1)
        last = pltpu.roll(layer, (start + 3 * EDGE) % pitch, layer.ndim - 1)
        block = jnp.where((lane >= start + EDGE) & (lane < start + 2 * EDGE), first, block)
        block = jnp.where((lane >= start + 2 * EDGE) & (lane < start + 3 * EDGE), last, block)
    return block


def half_rows(side):
    return jnp.where(side == 0, EDGE // 2, 0), jnp.where(side == 0, 0, EDGE // 2)


def slots(fields, components):
    per_group = SEGMENT_LANES // HALF
    near = [(f // per_group, f % per_group * HALF) for f in range(fields)]
    group, lane = near[-1]
    far = [(group, lane + HALF + c) for c in range(components)]
    return near, far


def pack_kernel(
    blades_hbm, jacobians_hbm, adjoint_hbm, source_hbm, couplings_hbm, damping_hbm,
    adjoint_ref, coef_ref, inv_ref, edges_ref, span_ref, corner_ref, right_ref, left_ref, table_ref, rows_ref,
    blades_ref, jacobians_ref, source_ref, couplings_ref, damping_ref, sems, *, row_count, length,
):
    components, axial, span, pitch = adjoint_ref.shape
    copies = [
        pltpu.make_async_copy(src, dst, sems.at[n])
        for n, (src, dst) in enumerate((
            (couplings_hbm, couplings_ref), (damping_hbm, damping_ref), (source_hbm, source_ref),
            (adjoint_hbm, adjoint_ref), (blades_hbm, blades_ref), (jacobians_hbm, jacobians_ref),
        ))
    ]
    for copy in copies:
        copy.start()
    row, side, place = (lax.axis_index(name) for name in AXES)
    copies[0].wait()
    copies[1].wait()
    diag = damping_ref[...]
    for d in range(6):
        diag = diag + couplings_ref[d]
    inverse = 1.0 / diag
    for d in range(6):
        coef_ref[components + d] = couplings_ref[d] * inverse
    inv_ref[...] = inverse[axial - 1]
    copies[2].wait()
    for c in range(components):
        coef_ref[c] = source_ref[c] * inverse
    copies[3].wait()

    fields = 2 * components + 6
    for f in range(fields):
        ref, at = (adjoint_ref, f) if f < components else (coef_ref, f - components)
        edges_ref[f] = to_edges([ref[at, a] for a in range(axial)], pitch)
    last = inv_ref[...]
    edges_ref[fields] = jnp.where(
        lanes(last.shape) >= (axial - 1) * SEGMENT_LANES,
        to_edges([jnp.zeros_like(last)] * (axial - 1) + [last], pitch), 0.0,
    )
    edge_row = pl.multiple_of(jnp.where(side == 0, span - EDGE, 0), EDGE)
    near, far = slots(fields + 1, components)
    groups = right_ref.shape[0]
    lane = lanes((span, pitch)) % SEGMENT_LANES
    for n, (out_ref, near_at, far_at) in enumerate((
        (right_ref, 3 * EDGE - HALF, 3 * EDGE - HALF - 1), (left_ref, EDGE, EDGE + HALF),
    )):
        packed = [jnp.zeros((span, pitch), jnp.float32) for _ in range(groups)]
        for f, (g, to) in enumerate(near):
            value = pltpu.roll(edges_ref[f], (to - near_at) % pitch, 1)
            packed[g] = jnp.where((lane >= to) & (lane < to + HALF), value, packed[g])
        for f, (g, to) in enumerate(far):
            packed[g] = jnp.where(lane == to, pltpu.roll(edges_ref[f], (to - far_at) % pitch, 1), packed[g])
        for g in range(groups):
            out_ref[g, :span] = packed[g]
            corner_ref[n * groups + g] = out_ref[g, pl.ds(edge_row, EDGE), :]

    to_low, to_high = half_rows(side)
    line = rows((EDGE, pitch))
    tiles = [(adjoint_ref, c, a) for c in range(components) for a in range(axial)]
    tiles += [(coef_ref, f, a) for f in range(components + 6) for a in range(axial)]
    tiles = [ref[f, a, pl.ds(edge_row, EDGE), :] for ref, f, a in tiles] + [inv_ref[pl.ds(edge_row, EDGE), :]]
    pairs = -(-len(tiles) // 2)
    for n in range(pairs):
        value = pltpu.roll(tiles[2 * n], to_low, 0)
        if 2 * n + 1 < len(tiles):
            value = jnp.where(line < HALF, value, pltpu.roll(tiles[2 * n + 1], to_high, 0))
        span_ref[n] = value
    fifth = jnp.where(side == 0, HALF - 1, HALF)
    for n in range(span_ref.shape[0] - pairs):
        value = jnp.zeros((EDGE, pitch), jnp.float32)
        for k in range(min(EDGE, components * axial - n * EDGE)):
            value = jnp.where(line == k, pltpu.roll(tiles[n * EDGE + k], lax.rem(k + EDGE - fifth, EDGE), 0), value)
        span_ref[pairs + n] = value

    copies[4].wait()
    component, mode, sine = column(lanes((pitch, pitch)))
    face = jnp.maximum(row - 1, 0)
    number = mode_number(mode, (blades_ref[face], blades_ref[face + 1]))
    cos_table, sin_table = waves(number * (place * pitch + rows((pitch, pitch))), length)
    table_ref[...] = jnp.where(component < components, jnp.where(sine, sin_table, cos_table), 0.0)
    copies[5].wait()
    entries = 6 * components * components
    for b in range(components):
        for c in range(components):
            for d in range(6):
                entry = jnp.full((1, pitch), jacobians_ref[b, c, 0, d], jnp.float32)
                rows_ref[pl.ds((b * components + c) * 6 + d, 1), :] = entry
    face = jnp.minimum(row, row_count - 2)
    for n in range(2):
        rows_ref[pl.ds(entries + n, 1), :] = jnp.full((1, pitch), blades_ref[face + n].astype(jnp.float32), jnp.float32)


def projected(strips, table):
    component, _, _ = column(lanes(table.shape))
    total = jnp.zeros((strips[0].shape[0], table.shape[1]), jnp.float32)
    for c, strip in enumerate(strips):
        total += jnp.dot(
            strip, jnp.where(component == c, table, 0.0), precision=EXACT, preferred_element_type=jnp.float32,
        )
    return total


def synthesised(modes, synth):
    return lax.dot_general(
        modes, synth, (((1,), (1,)), ((), ())), precision=EXACT, preferred_element_type=jnp.float32,
    )


def synth_kernel(
    rows_ref, giles_re_ref, giles_im_ref, orders_ref, cells_ref, after_ref, synth_ref, sums_ref,
    *, row_count, place_count, components, pitch, length, axial,
):
    row, place = lax.axis_index("row"), lax.axis_index("pitch")
    face = jnp.minimum(row, row_count - 2)
    modes = orders_ref.shape[2]
    orders = orders_ref[face]
    tag = BASE * orders[0:1] + orders[1:2]
    component, mode, _ = column(rows((pitch, modes)))
    same = (jnp.abs(tag) == mode) & (component < components)
    plain = jnp.where(same, 1.0, 0.0)
    signed = jnp.where(tag < 0, -plain, plain)
    dims = (((1,), (1,)), ((), ()))
    for n, ref in enumerate((giles_re_ref, giles_im_ref)):
        for b in range(components):
            for c in range(components):
                sums_ref[n, pl.ds(b * components + c, 1), :] = ref[b, c, pl.ds(face, 1), :]
    sums_re = lax.dot_general(sums_ref[0], plain, dims, precision=EXACT, preferred_element_type=jnp.float32)
    sums_im = lax.dot_general(sums_ref[1], signed, dims, precision=EXACT, preferred_element_type=jnp.float32)
    component, mode, sine = column(lanes(sums_re.shape))
    scale = 2.0 / length
    with_cos = jnp.where(sine, sums_im, sums_re) * scale
    with_sin = jnp.where(sine, sums_re, -sums_im) * scale
    component = component[0:1]

    def chunk(at):
        start = pl.multiple_of(lax.rem(place + at + place_count, place_count) * pitch, pitch)
        return cells_ref[:, pl.ds(start, pitch)]

    own = chunk(0)
    lane = lanes((1, pitch))
    first = (axial - 1) * SEGMENT_LANES
    edge = jnp.where(lane < first + EDGE, pltpu.roll(chunk(-1), (first + EDGE) % pitch, 1), pltpu.roll(own, (first + EDGE) % pitch, 1))
    edge = jnp.where(lane < first + 2 * EDGE, edge, pltpu.roll(own, (first + 3 * EDGE) % pitch, 1))
    edge = jnp.where(lane < first + 3 * EDGE, edge, pltpu.roll(chunk(1), (first + 3 * EDGE) % pitch, 1))

    def upright(cells):
        wide = jnp.broadcast_to(cells.astype(jnp.float32), (pitch, pitch))
        return jnp.transpose(wide).astype(jnp.int32)

    edge_cells = upright(edge)[first:first + SEGMENT_LANES]
    at_cells = jnp.concatenate([upright(own), edge_cells], 0)
    _, mode, _ = column(lanes(at_cells.shape))
    entries = 6 * components * components
    blades = [rows_ref[pl.ds(entries + n, 1), :].astype(jnp.int32) for n in range(2)]
    cos_table, sin_table = waves(mode_number(mode, blades) * at_cells, length)
    for c in range(components):
        row_cos = jnp.zeros((1, pitch), jnp.float32)
        row_sin = jnp.zeros((1, pitch), jnp.float32)
        for b in range(components):
            at = b * components + c
            row_cos = jnp.where(component == b, with_cos[at:at + 1], row_cos)
            row_sin = jnp.where(component == b, with_sin[at:at + 1], row_sin)
        part = row_cos * cos_table + row_sin * sin_table
        synth_ref[pl.ds(c * pitch, pitch), :] = part[:pitch]
        synth_ref[pl.ds(components * pitch + c * SEGMENT_LANES, SEGMENT_LANES), :] = part[pitch:]
    used = components * (pitch + SEGMENT_LANES)
    rest = synth_ref.shape[0] - used
    if rest:
        synth_ref[pl.ds(used, rest), :] = jnp.zeros((rest, pitch), jnp.float32)


def jacobian(jac_ref, components, b, c, d):
    return jac_ref[pl.ds((b * components + c) * 6 + d, 1), :]


def mixed(jac_ref, source, couplings, neighbours):
    total = list(source)
    jac = functools.partial(jacobian, jac_ref, len(total))
    for d, neighbour in enumerate(neighbours):
        for c in range(len(total)):
            term = jac(0, c, d) * neighbour[0]
            for b in range(1, len(total)):
                term = term + jac(b, c, d) * neighbour[b]
            total[c] = total[c] + couplings[d] * term
    return total


def layer_update(jac_ref, state_ref, edge_ref, coef_ref, t, a):
    components, wide, pitch = state_ref.shape[1], state_ref.shape[3], state_ref.shape[4]
    lane = lanes((wide, pitch))
    start = a * SEGMENT_LANES
    own = [state_ref[t, c, a + 1] for c in range(components)]
    above = [state_ref[t, c, a + 2] for c in range(components)]
    below = [state_ref[t, c, a] for c in range(components)]
    edge = [edge_ref[t, c] for c in range(components)]
    span_next = [pltpu.roll(x, wide - 1, 0) for x in own]
    span_prev = [pltpu.roll(x, 1, 0) for x in own]
    to_end = 2 * pitch - 1 - (start + 3 * EDGE)
    to_begin = 2 * pitch - (start + EDGE - 1)
    pitch_next = [
        jnp.where(lane == pitch - 1, pltpu.roll(e, lax.rem(to_end, pitch), 1), pltpu.roll(x, pitch - 1, 1))
        for e, x in zip(edge, own)
    ]
    pitch_prev = [
        jnp.where(lane == 0, pltpu.roll(e, lax.rem(to_begin, pitch), 1), pltpu.roll(x, 1, 1))
        for e, x in zip(edge, own)
    ]
    source = [coef_ref[c, a] for c in range(components)]
    couplings = [coef_ref[components + d, a] for d in range(6)]
    return mixed(jac_ref, source, couplings, (above, below, span_next, span_prev, pitch_next, pitch_prev))


def edge_update(jac_ref, edge_ref, edge_coef_ref, t, axial):
    components, wide, pitch = edge_ref.shape[1:]
    lane = lanes((wide, pitch))
    own = [edge_ref[t, c] for c in range(components)]
    above = [jnp.where(lane < (axial - 1) * SEGMENT_LANES, pltpu.roll(x, pitch - SEGMENT_LANES, 1), 0.0) for x in own]
    below = [jnp.where(lane >= SEGMENT_LANES, pltpu.roll(x, SEGMENT_LANES, 1), 0.0) for x in own]
    span_next = [pltpu.roll(x, wide - 1, 0) for x in own]
    span_prev = [pltpu.roll(x, 1, 0) for x in own]
    pitch_next = [pltpu.roll(x, pitch - 1, 1) for x in own]
    pitch_prev = [pltpu.roll(x, 1, 1) for x in own]
    source = [edge_coef_ref[c] for c in range(components)]
    couplings = [edge_coef_ref[components + d] for d in range(6)]
    return mixed(jac_ref, source, couplings, (above, below, span_next, span_prev, pitch_next, pitch_prev))


def edge_boundary(field, c, components, pitch, axial):
    at = components * pitch + c * SEGMENT_LANES
    tile = field[:, (at // pitch) * pitch:(at // pitch + 1) * pitch]
    return pltpu.roll(tile, ((axial - 1) * SEGMENT_LANES - at % pitch) % pitch, 1)


def advance(refs, t, a):
    state_ref = refs[1]
    for c, value in enumerate(layer_update(*refs, t, a)):
        state_ref[t + 1, c, a + 1] = value


def first_kernel(
    jac_ref, adjoint_ref, coef_in_ref, inv_in_ref, edges_ref, span_ref, from_left_ref, from_right_ref, table_ref,
    coef_ref, inv_ref, edge_coef_ref, state_ref, edge_ref, modes_ref,
):
    components, axial, span, pitch = adjoint_ref.shape
    wide = span + EDGE
    side = lax.axis_index("span")
    fields = 2 * components + 6
    line = rows((EDGE, pitch))
    keep_half = jnp.where(side == 0, line, EDGE - 1 - line) < HALF
    fifth = jnp.where(side == 0, HALF, HALF - 1)
    from_low, from_high = half_rows(1 - side)
    pairs = -(-(fields * axial + 1) // 2)

    def ghost(n):
        value = pltpu.roll(span_ref[n // 2], from_high if n % 2 else from_low, 0)
        value = jnp.where(keep_half, value, 0.0)
        if n < components * axial:
            extra = pltpu.roll(span_ref[pairs + n // EDGE], lax.rem(fifth + EDGE - n % EDGE, EDGE), 0)
            value = jnp.where(line == fifth, extra, value)
        return value

    near, far = slots(fields + 1, components)
    keep_five = keep_half | (line == fifth)
    for f in range(fields + 1):
        if f < fields:
            layers = [ghost(f * axial + a) for a in range(axial)]
        else:
            layers = [jnp.zeros((EDGE, pitch), jnp.float32)] * (axial - 1) + [ghost(fields * axial)]
        if f < components:
            for a in range(axial):
                state_ref[0, f, a + 1, :span] = adjoint_ref[f, a]
                state_ref[0, f, a + 1, span:] = layers[a]
        elif f < fields:
            for a in range(axial):
                coef_ref[f - components, a, :span] = coef_in_ref[f - components, a]
                coef_ref[f - components, a, span:] = layers[a]
        else:
            inv_ref[:span] = inv_in_ref[...]
            inv_ref[span:] = layers[-1]
        g, at = near[f]
        value = jnp.concatenate([edges_ref[f], to_edges(layers, pitch)], 0)
        lane = lanes((wide, pitch)) % SEGMENT_LANES
        value = jnp.where((lane >= HALF) & (lane < EDGE), pltpu.roll(from_left_ref[g], (HALF - at) % pitch, 1), value)
        value = jnp.where(
            (lane >= 3 * EDGE) & (lane < 3 * EDGE + HALF),
            pltpu.roll(from_right_ref[g], (3 * EDGE - at) % pitch, 1), value,
        )
        if f < components:
            g, at = far[f]
            value = jnp.where(lane == HALF - 1, pltpu.roll(from_left_ref[g], (HALF - 1 - at) % pitch, 1), value)
            value = jnp.where(
                lane == 3 * EDGE + HALF, pltpu.roll(from_right_ref[g], (3 * EDGE + HALF - at) % pitch, 1), value,
            )
        target, at = (edge_ref.at[0], f) if f < components else (edge_coef_ref, f - components)
        target[at, :span] = value[:span]
        target[at, span:] = jnp.where(keep_five if f < components else keep_half, value[span:], 0.0)
    for t in range(state_ref.shape[0]):
        for c in range(components):
            state_ref[t, c, 0] = jnp.zeros((wide, pitch), jnp.float32)
            state_ref[t, c, axial + 1] = jnp.zeros((wide, pitch), jnp.float32)

    refs = (jac_ref, state_ref, edge_ref, coef_ref)

    def sweep(t, carry):
        def body(a, inner):
            advance(refs, t, a)
            return inner

        lax.fori_loop(0, axial - 1 - t, body, 0)

        @pl.when(t < axial - 2)
        def _():
            for c, value in enumerate(edge_update(jac_ref, edge_ref, edge_coef_ref, t, axial)):
                edge_ref[t + 1, c] = value

        return carry

    lax.fori_loop(0, axial - 1, sweep, 0)
    strips = [jnp.concatenate([state_ref[t, c, 1] for t in range(axial)], 0) for c in range(components)]
    total = projected(strips, table_ref[...])
    to_low, to_high = half_rows(1 - side)
    for t in range(axial):
        modes_ref[pl.ds(t * span, span), :] = total[t * wide:t * wide + span]
    for n in range(axial // 2):
        low = total[2 * n * wide + span:2 * n * wide + wide]
        high = total[(2 * n + 1) * wide + span:(2 * n + 1) * wide + wide]
        both = jnp.where(line < HALF, pltpu.roll(low, to_low, 0), pltpu.roll(high, to_high, 0))
        modes_ref[pl.ds(axial * span + n * EDGE, EDGE), :] = both


def middle_kernel(
    jac_ref, coef_ref, edge_coef_ref, state_in_ref, edge_in_ref, table_ref, state_ref, edge_ref, modes_ref,
):
    components, axial, span = state_ref.shape[1], state_ref.shape[2] - 2, modes_ref.shape[0]
    refs = (jac_ref, state_ref, edge_ref, coef_ref)
    for c, value in enumerate(edge_update(jac_ref, edge_ref, edge_coef_ref, axial - 2, axial)):
        edge_ref[axial - 1, c] = value

    def body(t, carry):
        advance(refs, t, axial - 1 - t)
        return carry

    lax.fori_loop(0, axial, body, 0)
    modes_ref[...] = projected([state_ref[axial, c, 1, :span] for c in range(components)], table_ref[...])


def along_axis(jac_ref, coef_ref, delta, a, height):
    components = len(delta)
    out = []
    for c in range(components):
        term = jacobian(jac_ref, components, 0, c, 0) * delta[0]
        for b in range(1, components):
            term = term + jacobian(jac_ref, components, b, c, 0) * delta[b]
        out.append(coef_ref[components, a, :height] * term)
    return out


def link_kernel(jac_ref, coef_ref, inv_ref, part_ref, modes_a_ref, modes_b_ref, synth_ref, table_ref, modes_ref):
    span, pitch = modes_ref.shape
    components, axial = coef_ref.shape[0] - 6, coef_ref.shape[1]
    modes = modes_a_ref[:span] + modes_b_ref[:span]
    field = synthesised(modes, synth_ref[:components * pitch])
    delta = [inv_ref[:span] * field[:, c * pitch:(c + 1) * pitch] for c in range(components)]
    for a in range(axial - 2, -1, -1):
        delta = along_axis(jac_ref, coef_ref, delta, a, span)
    modes_ref[...] = part_ref[...] + projected(delta, table_ref[...])


def second_kernel(
    jac_ref, coef_ref, inv_ref, edge_coef_ref, state_in_ref, edge_in_ref, modes_a_ref, modes_b_ref, synth_ref, after_ref,
    state_ref, edge_ref, bound_ref,
):
    components, axial = state_ref.shape[1], state_ref.shape[2] - 2
    wide, pitch = state_ref.shape[3:]
    span = wide - EDGE
    from_low, from_high = half_rows(1 - lax.axis_index("span"))
    packed = modes_a_ref[...] + modes_b_ref[...]
    parts = []
    for t in range(axial):
        ghost = packed[axial * span + t // 2 * EDGE:axial * span + (t // 2 + 1) * EDGE]
        parts += [packed[t * span:(t + 1) * span], pltpu.roll(ghost, from_high if t % 2 else from_low, 0)]
    field = synthesised(jnp.concatenate(parts, 0), synth_ref[...])
    edge_bound = []
    for n in range(axial):
        part = field[n * wide:(n + 1) * wide]
        edge_bound.append([])
        for c in range(components):
            bound_ref[n, c] = inv_ref[...] * part[:, c * pitch:(c + 1) * pitch]
            edge_bound[n].append(edge_coef_ref[components + 6] * edge_boundary(part, c, components, pitch, axial))
    delta = [bound_ref[0, c] for c in range(components)]
    for t in range(1, axial + 1):
        for c in range(components):
            state_ref[t, c, axial + 1 - t] += delta[c]
        if t < axial:
            delta = along_axis(jac_ref, coef_ref, delta, axial - 1 - t, wide)
    for c in range(components):
        edge_ref[1, c] += edge_bound[0][c]
    for t in range(1, axial):
        for c, value in enumerate(edge_update(jac_ref, edge_ref, edge_coef_ref, t, axial)):
            edge_ref[t + 1, c] = value + edge_bound[t][c]
    rest_of_sweeps(jac_ref, coef_ref, state_ref, edge_ref, bound_ref, 1, axial - 1)


def rest_of_sweeps(jac_ref, coef_ref, state_ref, edge_ref, bound_ref, first, last):
    components, axial = state_ref.shape[1], state_ref.shape[2] - 2
    refs = (jac_ref, state_ref, edge_ref, coef_ref)

    def sweep(t, carry):
        def body(a, inner):
            advance(refs, t, a)
            return inner

        lax.fori_loop(axial - t, axial, body, 0)
        for c in range(components):
            state_ref[t + 1, c, axial] += bound_ref[t, c]
        return carry

    lax.fori_loop(first, last, sweep, 0)


def third_kernel(jac_ref, coef_ref, state_in_ref, edge_ref, bound_ref, after_ref, state_ref, out_ref):
    components, axial, span, _ = out_ref.shape
    rest_of_sweeps(jac_ref, coef_ref, state_ref, edge_ref, bound_ref, axial - 1, axial)

    def final(a, carry):
        for c, value in enumerate(layer_update(jac_ref, state_ref, edge_ref, coef_ref, axial, a)):
            out_ref[c, a] = value[:span]
        return carry

    lax.fori_loop(0, axial, final, 0)


def last_kernel(inv_ref, modes_a_ref, modes_b_ref, synth_ref, swept_ref, out_ref):
    components, axial, span, pitch = out_ref.shape
    field = synthesised(modes_a_ref[...] + modes_b_ref[...], synth_ref[:components * pitch])
    for c in range(components):
        for a in range(axial - 1):
            out_ref[c, a] = swept_ref[c, a]
        out_ref[c, axial - 1] = swept_ref[c, axial - 1] + inv_ref[:span] * field[:, c * pitch:(c + 1) * pitch]


def moved(x, to):
    sizes = [lax.axis_size(name) for name in AXES]
    pairs = []
    for r in range(sizes[0]):
        for s in range(sizes[1]):
            for p in range(sizes[2]):
                target = to(r, s, p)
                if all(0 <= at < size for at, size in zip(target, sizes)):
                    number = lambda at: (at[0] * sizes[1] + at[1]) * sizes[2] + at[2]
                    pairs.append((number((r, s, p)), number(target)))
    return lax.ppermute(x, AXES, pairs)


def struct(*shape):
    return jax.ShapeDtypeStruct(shape, jnp.float32)


def on_device(
    adjoint_start, source, couplings, damping, jacobians, giles_real, giles_imag, blades, mode_orders, cell_map,
):
    components, axial, span, pitch = adjoint_start.shape
    row_count, span_count, place_count = (lax.axis_size(name) for name in AXES)
    length = pitch * place_count
    assert components == COMPONENTS and components * WAVES <= pitch
    assert axial == ITERS - 1 and ITERS <= EDGE and axial * SEGMENT_LANES == pitch
    assert span_count == 2 and place_count & (place_count - 1) == 0
    wide = span + EDGE
    fields = 2 * components + 6
    groups = slots(fields + 1, components)[1][-1][0] + 1
    pairs = -(-(fields * axial + 1) // 2)
    span_tiles = pairs + -(-components * axial // EDGE)
    vmem = pl.BlockSpec(memory_space=pltpu.VMEM)
    hbm = pl.BlockSpec(memory_space=pltpu.HBM)
    anywhere = pl.BlockSpec(memory_space=pl.ANY)

    def call(kernel, name, outs, ins, aliases=None, scratch=(), limit=40 * MIB, **fixed):
        specs = [spec for spec, _ in ins]
        return pl.pallas_call(
            functools.partial(kernel, **fixed),
            out_shape=outs,
            in_specs=specs,
            out_specs=jax.tree.map(lambda _: vmem, outs),
            scratch_shapes=scratch,
            input_output_aliases=aliases or {},
            compiler_params=params(limit),
            name=name,
        )(*[value for _, value in ins])

    adjoint, coef, inv, edges, span_out, corner, right, left, table, jac = call(
        pack_kernel, "pack",
        (
            struct(components, axial, span, pitch),
            struct(components + 6, axial, span, pitch), struct(span, pitch), struct(fields + 1, span, pitch),
            struct(span_tiles, EDGE, pitch), struct(2 * groups, EDGE, pitch), struct(groups, wide, pitch),
            struct(groups, wide, pitch), struct(pitch, pitch),
            struct(6 * components * components + 2, pitch),
        ),
        [(hbm, pltpu.with_memory_space_constraint(x, pltpu.HBM)) for x in (
            blades, jacobians.transpose(2, 3, 0, 1), adjoint_start, source, couplings, damping,
        )],
        scratch=[
            pltpu.SMEM(blades.shape, jnp.int32), pltpu.SMEM((components, components, 1, 6), jnp.float32),
            pltpu.VMEM(source.shape, jnp.float32), pltpu.VMEM(couplings.shape, jnp.float32),
            pltpu.VMEM(damping.shape, jnp.float32), pltpu.SemaphoreType.DMA((6,)),
        ],
        row_count=row_count, length=length,
    )
    corner = moved(corner, lambda r, s, p: (r, 1 - s, p))
    from_span = moved(span_out, lambda r, s, p: (r, 1 - s, p))
    right = lax.dynamic_update_slice(right, corner[:groups], (0, span, 0))
    left = lax.dynamic_update_slice(left, corner[groups:], (0, span, 0))
    from_left = moved(right, lambda r, s, p: (r, s, (p + 1) % place_count))
    from_right = moved(left, lambda r, s, p: (r, s, (p - 1) % place_count))

    state_shape = struct(axial + 1, components, axial + 2, wide, pitch)
    edge_shape = struct(axial + 1, components, wide, pitch)
    coef, inv, edge_coef, state, edge, modes = call(
        first_kernel, "first_sweeps",
        (
            struct(components + 6, axial, wide, pitch), struct(wide, pitch), struct(components + 7, wide, pitch),
            state_shape, edge_shape, struct(axial * span + axial // 2 * EDGE, pitch),
        ),
        [(vmem, jac)] + [(vmem, x) for x in (adjoint, coef, inv, edges, from_span, from_left, from_right, table)],
    )

    def summed(x):
        bit = 1
        while 2 * bit < place_count:
            x = x + moved(x, lambda r, s, p: (r, s, p ^ bit))
            bit *= 2
        if bit < place_count:
            far = moved(x, lambda r, s, p: (r - 1, s, p ^ bit))
        else:
            far = jnp.zeros_like(x)
        return x, moved(x, lambda r, s, p: (r - 1, s, p)), far

    state, edge, part = call(
        middle_kernel, "middle_sweeps", (state_shape, edge_shape, struct(span, pitch)),
        [(vmem, jac)] + [(vmem, x) for x in (coef, edge_coef, state, edge, table)],
        aliases={3: 0, 4: 1},
    )
    halfway, modes_a, modes_b = summed(modes)

    synth = call(
        synth_kernel, "synth", struct(-(-components * (pitch + SEGMENT_LANES) // pitch) * pitch, pitch),
        [(vmem, jac), (vmem, giles_real.transpose(2, 3, 0, 1)), (vmem, giles_imag.transpose(2, 3, 0, 1))]
        + [(vmem, mode_orders.transpose(0, 2, 1)), (vmem, cell_map), (anywhere, halfway)],
        scratch=[pltpu.VMEM((2, components * components, mode_orders.shape[1]), jnp.float32)],
        row_count=row_count, place_count=place_count, components=components, pitch=pitch, length=length, axial=axial,
    )
    late = call(
        link_kernel, "late_modes", struct(span, pitch),
        [(vmem, jac)] + [(vmem, x) for x in (coef, inv, part, modes_a, modes_b, synth, table)],
    )
    halfway, late_a, late_b = summed(late)
    state, edge, bound = call(
        second_kernel, "second_sweeps", (state_shape, edge_shape, struct(axial, components, wide, pitch)),
        [(vmem, jac)] + [(vmem, x) for x in (coef, inv, edge_coef, state, edge, modes_a, modes_b, synth)]
        + [(anywhere, late)],
        aliases={4: 0, 5: 1},
    )
    state, swept = call(
        third_kernel, "third_sweeps", (state_shape, struct(components, axial, span, pitch)),
        [(vmem, jac)] + [(vmem, x) for x in (coef, state, edge, bound)] + [(anywhere, halfway)],
        aliases={2: 0},
    )
    return call(
        last_kernel, "last_boundary", struct(components, axial, span, pitch),
        [(vmem, x) for x in (inv, late_a, late_b, synth, swept)],
    )


def solution(mesh):
    placed = (
        P(None, "row", "span", "pitch"),
        P(None, "row", "span", "pitch"),
        P(None, "row", "span", "pitch"),
        P("row", "span", "pitch"),
        P("row", None, None, None),
        P(),
        P(),
        P(),
        P(),
        P("row", None),
    )
    return jax.shard_map(
        on_device,
        mesh=mesh,
        in_specs=placed,
        out_specs=P(None, "row", "span", "pitch"),
        check_vma=False,
    )
```

```python
import functools
import math

import jax
import jax.numpy as jnp
from jax import lax
from jax.experimental import pallas as pl
from jax.experimental.pallas import tpu as pltpu
from jax.sharding import PartitionSpec as P

ITERS = 5
AXES = ("row", "span", "pitch")

ORDER_MAX = 2
BASE = 2 * ORDER_MAX + 1
COSINES = (BASE * BASE + 1) // 2
WAVES = 2 * COSINES - 1
COMPONENTS = 5
EDGE = 8
HALF = EDGE // 2
SEGMENT_LANES = 4 * EDGE
EXACT = lax.Precision.HIGHEST
MIB = 1024 * 1024


def params(limit):
    return pltpu.CompilerParams(vmem_limit_bytes=limit)


def lanes(shape):
    return lax.broadcasted_iota(jnp.int32, shape, len(shape) - 1)


def rows(shape):
    return lax.broadcasted_iota(jnp.int32, shape, len(shape) - 2)


def column(j):
    component = (j * 41) >> 10
    wave = j - WAVES * component
    sine = wave >= COSINES
    return component, jnp.where(sine, wave - (COSINES - 1), wave), sine


def mode_number(mode, blades):
    high = ((mode + ORDER_MAX) * 13) >> 6
    low = mode - BASE * high
    return high * blades[0] + low * blades[1]


def waves(products, length):
    if length & (length - 1) == 0:
        phase = products & (length - 1)
    else:
        phase = jnp.mod(products, length)
    turn = phase.astype(jnp.float32) * (1.0 / length)
    quarter = jnp.floor(4.0 * turn + 0.5)
    x = (turn - 0.25 * quarter) * (2.0 * math.pi)
    y = x * x
    sine = x * (1.0 + y * (-1.0 / 6 + y * (1.0 / 120 + y * (-1.0 / 5040 + y * (1.0 / 362880)))))
    cosine = 1.0 + y * (-0.5 + y * (1.0 / 24 + y * (-1.0 / 720 + y * (1.0 / 40320 - y * (1.0 / 3628800)))))
    quarter = quarter.astype(jnp.int32) & 3
    odd = (quarter & 1) == 1
    cos_out = jnp.where(odd, sine, cosine)
    sin_out = jnp.where(odd, cosine, sine)
    cos_out = jnp.where((quarter == 1) | (quarter == 2), -cos_out, cos_out)
    sin_out = jnp.where(quarter >= 2, -sin_out, sin_out)
    return cos_out, sin_out


def to_edges(layers, pitch):
    lane = lanes(layers[0].shape)
    block = jnp.zeros_like(layers[0])
    for a, layer in enumerate(layers):
        if layer is None:
            continue
        start = a * SEGMENT_LANES
        first = pltpu.roll(layer, (start + EDGE) % pitch, layer.ndim - 1)
        last = pltpu.roll(layer, (start + 3 * EDGE) % pitch, layer.ndim - 1)
        block = jnp.where((lane >= start + EDGE) & (lane < start + 2 * EDGE), first, block)
        block = jnp.where((lane >= start + 2 * EDGE) & (lane < start + 3 * EDGE), last, block)
    return block


def half_rows(side):
    return jnp.where(side == 0, EDGE // 2, 0), jnp.where(side == 0, 0, EDGE // 2)


def slots(fields, components):
    per_group = SEGMENT_LANES // HALF
    near = [(f // per_group, f % per_group * HALF) for f in range(fields)]
    group, lane = near[-1]
    far = [(group, lane + HALF + c) for c in range(components)]
    return near, far


def pack_kernel(
    adjoint_hbm, source_hbm, couplings_hbm, damping_hbm,
    adjoint_ref, coef_ref, inv_ref, edges_ref, span_ref, corner_ref, inner_ref, outer_ref,
    source_ref, couplings_ref, damping_ref, sems,
):
    components, axial, span, pitch = adjoint_ref.shape
    copies = [
        pltpu.make_async_copy(src, dst, sems.at[n])
        for n, (src, dst) in enumerate((
            (couplings_hbm, couplings_ref), (damping_hbm, damping_ref), (source_hbm, source_ref),
            (adjoint_hbm, adjoint_ref),
        ))
    ]
    for copy in copies:
        copy.start()
    side, place = lax.axis_index("span"), lax.axis_index("pitch")
    copies[0].wait()
    copies[1].wait()
    diag = damping_ref[...]
    for d in range(6):
        diag = diag + couplings_ref[d]
    inverse = 1.0 / diag
    for d in range(6):
        coef_ref[components + d] = couplings_ref[d] * inverse
    inv_ref[...] = inverse[axial - 1]
    copies[2].wait()
    for c in range(components):
        coef_ref[c] = source_ref[c] * inverse
    copies[3].wait()

    fields = 2 * components + 6
    for f in range(fields):
        ref, at = (adjoint_ref, f) if f < components else (coef_ref, f - components)
        edges_ref[f] = to_edges([ref[at, a] for a in range(axial)], pitch)
    last = inv_ref[...]
    edges_ref[fields] = jnp.where(
        lanes(last.shape) >= (axial - 1) * SEGMENT_LANES,
        to_edges([jnp.zeros_like(last)] * (axial - 1) + [last], pitch), 0.0,
    )
    edge_row = pl.multiple_of(jnp.where(side == 0, span - EDGE, 0), EDGE)
    near, far = slots(fields + 1, components)
    groups = inner_ref.shape[0]
    lane = lanes((span, pitch)) % SEGMENT_LANES
    sides = []
    for near_at, far_at in ((3 * EDGE - HALF, 3 * EDGE - HALF - 1), (EDGE, EDGE + HALF)):
        packed = [jnp.zeros((span, pitch), jnp.float32) for _ in range(groups)]
        for f, (g, to) in enumerate(near):
            value = pltpu.roll(edges_ref[f], (to - near_at) % pitch, 1)
            packed[g] = jnp.where((lane >= to) & (lane < to + HALF), value, packed[g])
        for f, (g, to) in enumerate(far):
            packed[g] = jnp.where(lane == to, pltpu.roll(edges_ref[f], (to - far_at) % pitch, 1), packed[g])
        sides.append(packed)
    even = lax.rem(place, 2) == 0
    for g in range(groups):
        inner_ref[g, :span] = jnp.where(even, sides[0][g], sides[1][g])
        outer_ref[g, :span] = jnp.where(even, sides[1][g], sides[0][g])
        corner_ref[g] = inner_ref[g, pl.ds(edge_row, EDGE), :]
        corner_ref[groups + g] = outer_ref[g, pl.ds(edge_row, EDGE), :]

    to_low, to_high = half_rows(side)
    line = rows((EDGE, pitch))
    tiles = [(adjoint_ref, c, a) for c in range(components) for a in range(axial)]
    tiles += [(coef_ref, f, a) for f in range(components + 6) for a in range(axial)]
    tiles = [ref[f, a, pl.ds(edge_row, EDGE), :] for ref, f, a in tiles] + [inv_ref[pl.ds(edge_row, EDGE), :]]
    pairs = -(-len(tiles) // 2)
    for n in range(pairs):
        value = pltpu.roll(tiles[2 * n], to_low, 0)
        if 2 * n + 1 < len(tiles):
            value = jnp.where(line < HALF, value, pltpu.roll(tiles[2 * n + 1], to_high, 0))
        span_ref[n] = value
    fifth = jnp.where(side == 0, HALF - 1, HALF)
    for n in range(span_ref.shape[0] - pairs):
        value = jnp.zeros((EDGE, pitch), jnp.float32)
        for k in range(min(EDGE, components * axial - n * EDGE)):
            value = jnp.where(line == k, pltpu.roll(tiles[n * EDGE + k], lax.rem(k + EDGE - fifth, EDGE), 0), value)
        span_ref[pairs + n] = value


def prepare_kernel(
    blades_hbm, jacobians_hbm, adjoint_ref, table_ref, rows_ref, modes_ref, blades_ref, jacobians_ref, sems,
    *, row_count, length,
):
    components, _, span, pitch = adjoint_ref.shape
    copies = [
        pltpu.make_async_copy(blades_hbm, blades_ref, sems.at[0]),
        pltpu.make_async_copy(jacobians_hbm, jacobians_ref, sems.at[1]),
    ]
    for copy in copies:
        copy.start()
    row, place = lax.axis_index("row"), lax.axis_index("pitch")
    copies[0].wait()
    component, mode, sine = column(lanes((pitch, pitch)))
    face = jnp.maximum(row - 1, 0)
    number = mode_number(mode, (blades_ref[face], blades_ref[face + 1]))
    cos_table, sin_table = waves(number * (place * pitch + rows((pitch, pitch))), length)
    table = jnp.where(component < components, jnp.where(sine, sin_table, cos_table), 0.0)
    table_ref[...] = table
    modes_ref[...] = projected([adjoint_ref[c, 0] for c in range(components)], table)
    copies[1].wait()
    entries = 6 * components * components
    for b in range(components):
        for c in range(components):
            for d in range(6):
                entry = jnp.full((1, pitch), jacobians_ref[b, c, 0, d], jnp.float32)
                rows_ref[pl.ds((b * components + c) * 6 + d, 1), :] = entry
    face = jnp.minimum(row, row_count - 2)
    for n in range(2):
        rows_ref[pl.ds(entries + n, 1), :] = jnp.full((1, pitch), blades_ref[face + n].astype(jnp.float32), jnp.float32)


def projected(strips, table):
    component, _, _ = column(lanes(table.shape))
    total = jnp.zeros((strips[0].shape[0], table.shape[1]), jnp.float32)
    for c, strip in enumerate(strips):
        total += jnp.dot(
            strip, jnp.where(component == c, table, 0.0), precision=EXACT, preferred_element_type=jnp.float32,
        )
    return total


def synthesised(modes, synth):
    return lax.dot_general(
        modes, synth, (((1,), (1,)), ((), ())), precision=EXACT, preferred_element_type=jnp.float32,
    )


def synth_kernel(
    rows_ref, giles_re_hbm, giles_im_hbm, orders_hbm, cells_hbm, synth_ref,
    giles_re_ref, giles_im_ref, orders_ref, cells_ref, sums_ref, sems,
    *, row_count, place_count, components, pitch, length, axial,
):
    copies = [
        pltpu.make_async_copy(src, dst, sems.at[n])
        for n, (src, dst) in enumerate((
            (orders_hbm, orders_ref), (giles_re_hbm, giles_re_ref), (giles_im_hbm, giles_im_ref), (cells_hbm, cells_ref),
        ))
    ]
    for copy in copies:
        copy.start()
    row, place = lax.axis_index("row"), lax.axis_index("pitch")
    face = jnp.minimum(row, row_count - 2)
    for copy in copies:
        copy.wait()
    modes = orders_ref.shape[2]
    orders = orders_ref[face]
    tag = BASE * orders[0:1] + orders[1:2]
    component, mode, _ = column(rows((pitch, modes)))
    same = (jnp.abs(tag) == mode) & (component < components)
    plain = jnp.where(same, 1.0, 0.0)
    signed = jnp.where(tag < 0, -plain, plain)
    dims = (((1,), (1,)), ((), ()))
    for n, ref in enumerate((giles_re_ref, giles_im_ref)):
        for b in range(components):
            for c in range(components):
                sums_ref[n, pl.ds(b * components + c, 1), :] = ref[b, c, pl.ds(face, 1), :]
    sums_re = lax.dot_general(sums_ref[0], plain, dims, precision=EXACT, preferred_element_type=jnp.float32)
    sums_im = lax.dot_general(sums_ref[1], signed, dims, precision=EXACT, preferred_element_type=jnp.float32)
    component, mode, sine = column(lanes(sums_re.shape))
    scale = 2.0 / length
    with_cos = jnp.where(sine, sums_im, sums_re) * scale
    with_sin = jnp.where(sine, sums_re, -sums_im) * scale
    component = component[0:1]

    def chunk(at):
        start = pl.multiple_of(lax.rem(place + at + place_count, place_count) * pitch, pitch)
        return cells_ref[:, pl.ds(start, pitch)]

    own = chunk(0)
    lane = lanes((1, pitch))
    first = (axial - 1) * SEGMENT_LANES
    edge = jnp.where(lane < first + EDGE, pltpu.roll(chunk(-1), (first + EDGE) % pitch, 1), pltpu.roll(own, (first + EDGE) % pitch, 1))
    edge = jnp.where(lane < first + 2 * EDGE, edge, pltpu.roll(own, (first + 3 * EDGE) % pitch, 1))
    edge = jnp.where(lane < first + 3 * EDGE, edge, pltpu.roll(chunk(1), (first + 3 * EDGE) % pitch, 1))

    def upright(cells):
        wide = jnp.broadcast_to(cells.astype(jnp.float32), (pitch, pitch))
        return jnp.transpose(wide).astype(jnp.int32)

    edge_cells = upright(edge)[first:first + SEGMENT_LANES]
    at_cells = jnp.concatenate([upright(own), edge_cells], 0)
    _, mode, _ = column(lanes(at_cells.shape))
    entries = 6 * components * components
    blades = [rows_ref[pl.ds(entries + n, 1), :].astype(jnp.int32) for n in range(2)]
    cos_table, sin_table = waves(mode_number(mode, blades) * at_cells, length)
    for c in range(components):
        row_cos = jnp.zeros((1, pitch), jnp.float32)
        row_sin = jnp.zeros((1, pitch), jnp.float32)
        for b in range(components):
            at = b * components + c
            row_cos = jnp.where(component == b, with_cos[at:at + 1], row_cos)
            row_sin = jnp.where(component == b, with_sin[at:at + 1], row_sin)
        part = row_cos * cos_table + row_sin * sin_table
        synth_ref[pl.ds(c * pitch, pitch), :] = part[:pitch]
        synth_ref[pl.ds(components * pitch + c * SEGMENT_LANES, SEGMENT_LANES), :] = part[pitch:]
    used = components * (pitch + SEGMENT_LANES)
    rest = synth_ref.shape[0] - used
    if rest:
        synth_ref[pl.ds(used, rest), :] = jnp.zeros((rest, pitch), jnp.float32)


def jacobian(jac_ref, components, b, c, d):
    return jac_ref[pl.ds((b * components + c) * 6 + d, 1), :]


def mixed(jac_ref, source, couplings, neighbours):
    total = list(source)
    jac = functools.partial(jacobian, jac_ref, len(total))
    for d, neighbour in enumerate(neighbours):
        for c in range(len(total)):
            term = jac(0, c, d) * neighbour[0]
            for b in range(1, len(total)):
                term = term + jac(b, c, d) * neighbour[b]
            total[c] = total[c] + couplings[d] * term
    return total


def layer_update(jac_ref, state_ref, edge_ref, coef_ref, t, a):
    components, wide, pitch = state_ref.shape[1], state_ref.shape[3], state_ref.shape[4]
    lane = lanes((wide, pitch))
    start = a * SEGMENT_LANES
    own = [state_ref[t, c, a + 1] for c in range(components)]
    above = [state_ref[t, c, a + 2] for c in range(components)]
    below = [state_ref[t, c, a] for c in range(components)]
    edge = [edge_ref[t, c] for c in range(components)]
    span_next = [pltpu.roll(x, wide - 1, 0) for x in own]
    span_prev = [pltpu.roll(x, 1, 0) for x in own]
    to_end = 2 * pitch - 1 - (start + 3 * EDGE)
    to_begin = 2 * pitch - (start + EDGE - 1)
    pitch_next = [
        jnp.where(lane == pitch - 1, pltpu.roll(e, lax.rem(to_end, pitch), 1), pltpu.roll(x, pitch - 1, 1))
        for e, x in zip(edge, own)
    ]
    pitch_prev = [
        jnp.where(lane == 0, pltpu.roll(e, lax.rem(to_begin, pitch), 1), pltpu.roll(x, 1, 1))
        for e, x in zip(edge, own)
    ]
    source = [coef_ref[c, a] for c in range(components)]
    couplings = [coef_ref[components + d, a] for d in range(6)]
    return mixed(jac_ref, source, couplings, (above, below, span_next, span_prev, pitch_next, pitch_prev))


def edge_update(jac_ref, edge_ref, edge_coef_ref, t, axial):
    components, wide, pitch = edge_ref.shape[1:]
    lane = lanes((wide, pitch))
    own = [edge_ref[t, c] for c in range(components)]
    above = [jnp.where(lane < (axial - 1) * SEGMENT_LANES, pltpu.roll(x, pitch - SEGMENT_LANES, 1), 0.0) for x in own]
    below = [jnp.where(lane >= SEGMENT_LANES, pltpu.roll(x, SEGMENT_LANES, 1), 0.0) for x in own]
    span_next = [pltpu.roll(x, wide - 1, 0) for x in own]
    span_prev = [pltpu.roll(x, 1, 0) for x in own]
    pitch_next = [pltpu.roll(x, pitch - 1, 1) for x in own]
    pitch_prev = [pltpu.roll(x, 1, 1) for x in own]
    source = [edge_coef_ref[c] for c in range(components)]
    couplings = [edge_coef_ref[components + d] for d in range(6)]
    return mixed(jac_ref, source, couplings, (above, below, span_next, span_prev, pitch_next, pitch_prev))


def edge_boundary(field, c, components, pitch, axial):
    at = components * pitch + c * SEGMENT_LANES
    tile = field[:, (at // pitch) * pitch:(at // pitch + 1) * pitch]
    return pltpu.roll(tile, ((axial - 1) * SEGMENT_LANES - at % pitch) % pitch, 1)


def advance(refs, t, a):
    state_ref = refs[1]
    for c, value in enumerate(layer_update(*refs, t, a)):
        state_ref[t + 1, c, a + 1] = value


def first_kernel(
    jac_ref, adjoint_ref, coef_in_ref, inv_in_ref, edges_ref, span_ref, inner_ref, outer_ref, table_ref,
    coef_ref, inv_ref, edge_coef_ref, state_ref, edge_ref, modes_ref, part_ref,
):
    components, axial, span, pitch = adjoint_ref.shape
    wide = span + EDGE
    side = lax.axis_index("span")
    fields = 2 * components + 6
    line = rows((EDGE, pitch))
    keep_half = jnp.where(side == 0, line, EDGE - 1 - line) < HALF
    fifth = jnp.where(side == 0, HALF, HALF - 1)
    from_low, from_high = half_rows(1 - side)
    pairs = -(-(fields * axial + 1) // 2)

    def ghost(n):
        value = pltpu.roll(span_ref[n // 2], from_high if n % 2 else from_low, 0)
        value = jnp.where(keep_half, value, 0.0)
        if n < components * axial:
            extra = pltpu.roll(span_ref[pairs + n // EDGE], lax.rem(fifth + EDGE - n % EDGE, EDGE), 0)
            value = jnp.where(line == fifth, extra, value)
        return value

    even = lax.rem(lax.axis_index("pitch"), 2) == 0
    from_left = [jnp.where(even, outer_ref[g], inner_ref[g]) for g in range(inner_ref.shape[0])]
    from_right = [jnp.where(even, inner_ref[g], outer_ref[g]) for g in range(inner_ref.shape[0])]
    near, far = slots(fields + 1, components)
    keep_five = keep_half | (line == fifth)
    for f in range(fields + 1):
        if f < fields:
            layers = [ghost(f * axial + a) for a in range(axial)]
        else:
            layers = [jnp.zeros((EDGE, pitch), jnp.float32)] * (axial - 1) + [ghost(fields * axial)]
        if f < components:
            for a in range(axial):
                state_ref[0, f, a + 1, :span] = adjoint_ref[f, a]
                state_ref[0, f, a + 1, span:] = layers[a]
        elif f < fields:
            for a in range(axial):
                coef_ref[f - components, a, :span] = coef_in_ref[f - components, a]
                coef_ref[f - components, a, span:] = layers[a]
        else:
            inv_ref[:span] = inv_in_ref[...]
            inv_ref[span:] = layers[-1]
        g, at = near[f]
        value = jnp.concatenate([edges_ref[f], to_edges(layers, pitch)], 0)
        lane = lanes((wide, pitch)) % SEGMENT_LANES
        value = jnp.where((lane >= HALF) & (lane < EDGE), pltpu.roll(from_left[g], (HALF - at) % pitch, 1), value)
        value = jnp.where(
            (lane >= 3 * EDGE) & (lane < 3 * EDGE + HALF),
            pltpu.roll(from_right[g], (3 * EDGE - at) % pitch, 1), value,
        )
        if f < components:
            g, at = far[f]
            value = jnp.where(lane == HALF - 1, pltpu.roll(from_left[g], (HALF - 1 - at) % pitch, 1), value)
            value = jnp.where(
                lane == 3 * EDGE + HALF, pltpu.roll(from_right[g], (3 * EDGE + HALF - at) % pitch, 1), value,
            )
        target, at = (edge_ref.at[0], f) if f < components else (edge_coef_ref, f - components)
        target[at, :span] = value[:span]
        target[at, span:] = jnp.where(keep_five if f < components else keep_half, value[span:], 0.0)
    for t in range(state_ref.shape[0]):
        for c in range(components):
            state_ref[t, c, 0] = jnp.zeros((wide, pitch), jnp.float32)
            state_ref[t, c, axial + 1] = jnp.zeros((wide, pitch), jnp.float32)

    refs = (jac_ref, state_ref, edge_ref, coef_ref)

    def sweep(t, carry):
        def body(a, inner):
            advance(refs, t, a)
            return inner

        lax.fori_loop(0, axial - t, body, 0)

        @pl.when(t < axial - 1)
        def _():
            for c, value in enumerate(edge_update(jac_ref, edge_ref, edge_coef_ref, t, axial)):
                edge_ref[t + 1, c] = value

        return carry

    lax.fori_loop(0, axial, sweep, 0)
    strips = [
        jnp.concatenate(
            [state_ref[t, c, 1] for t in range(1, axial)] + [state_ref[axial, c, 1, :span], state_ref[0, c, 1, span:]], 0,
        )
        for c in range(components)
    ]
    total = projected(strips, table_ref[...])
    to_low, to_high = half_rows(1 - side)
    for t in range(1, axial):
        modes_ref[pl.ds((t - 1) * span, span), :] = total[(t - 1) * wide:(t - 1) * wide + span]
    last = (axial - 1) * wide
    part_ref[...] = total[last:last + span]
    ghosts = [total[last + span:]] + [total[t * wide + span:(t + 1) * wide] for t in range(axial - 1)]
    for n in range(axial // 2):
        both = jnp.where(line < HALF, pltpu.roll(ghosts[2 * n], to_low, 0), pltpu.roll(ghosts[2 * n + 1], to_high, 0))
        modes_ref[pl.ds((axial - 1) * span + n * EDGE, EDGE), :] = both


def along_axis(jac_ref, coef_ref, delta, a, height):
    components = len(delta)
    out = []
    for c in range(components):
        term = jacobian(jac_ref, components, 0, c, 0) * delta[0]
        for b in range(1, components):
            term = term + jacobian(jac_ref, components, b, c, 0) * delta[b]
        out.append(coef_ref[components, a, :height] * term)
    return out


def late_kernel(
    jac_ref, coef_ref, inv_ref, part_ref, more_ref, modes_a_ref, modes_b_ref, synth_ref, table_ref, modes_ref,
):
    span, pitch = part_ref.shape
    components, axial = coef_ref.shape[0] - 6, coef_ref.shape[1]
    field = synthesised(modes_a_ref[...] + modes_b_ref[...], synth_ref[:components * pitch])
    delta = [inv_ref[:span] * field[:, c * pitch:(c + 1) * pitch] for c in range(components)]
    for a in range(axial - 2, -1, -1):
        delta = along_axis(jac_ref, coef_ref, delta, a, span)
    before = more_ref.shape[0]
    modes_ref[:before] = more_ref[...]
    modes_ref[before:] = part_ref[...] + projected(delta, table_ref[...])


def second_kernel(
    jac_ref, coef_ref, inv_ref, edge_coef_ref, state_in_ref, edge_in_ref, modes_a_ref, modes_b_ref, more_a_ref, more_b_ref,
    synth_ref, state_ref, edge_ref, out_ref, bound_ref,
):
    components, axial, span, pitch = out_ref.shape
    wide = span + EDGE
    from_low, from_high = half_rows(1 - lax.axis_index("span"))
    more = more_a_ref[...] + more_b_ref[...]
    own = [modes_a_ref[...] + modes_b_ref[...]] + [more[t * span:(t + 1) * span] for t in range(axial - 1)]
    start = (axial - 1) * span
    parts = []
    for t in range(axial):
        ghost = more[start + t // 2 * EDGE:start + (t // 2 + 1) * EDGE]
        parts += [own[t], pltpu.roll(ghost, from_high if t % 2 else from_low, 0)]
    field = synthesised(jnp.concatenate(parts + [more[start + axial // 2 * EDGE:]], 0), synth_ref[...])
    edge_bound = []
    for n in range(axial):
        part = field[n * wide:(n + 1) * wide]
        edge_bound.append([])
        for c in range(components):
            bound_ref[n, c] = inv_ref[...] * part[:, c * pitch:(c + 1) * pitch]
            edge_bound[n].append(edge_coef_ref[components + 6] * edge_boundary(part, c, components, pitch, axial))
    for c in range(components):
        bound_ref[axial, c, :span] = inv_ref[:span] * field[axial * wide:, c * pitch:(c + 1) * pitch]
    delta = [bound_ref[0, c] for c in range(components)]
    for t in range(1, axial + 1):
        for c in range(components):
            state_ref[t, c, axial + 1 - t] += delta[c]
        if t < axial:
            delta = along_axis(jac_ref, coef_ref, delta, axial - 1 - t, wide)
    for c in range(components):
        edge_ref[1, c] += edge_bound[0][c]
    for t in range(1, axial):
        for c, value in enumerate(edge_update(jac_ref, edge_ref, edge_coef_ref, t, axial)):
            edge_ref[t + 1, c] = value + edge_bound[t][c]
    refs = (jac_ref, state_ref, edge_ref, coef_ref)

    def sweep(t, carry):
        def body(a, inner):
            advance(refs, t, a)
            return inner

        lax.fori_loop(axial - t, axial, body, 0)
        for c in range(components):
            state_ref[t + 1, c, axial] += bound_ref[t, c]
        return carry

    lax.fori_loop(1, axial, sweep, 0)

    def final(a, carry):
        for c, value in enumerate(layer_update(*refs, axial, a)):
            out_ref[c, a] = value[:span]
        return carry

    lax.fori_loop(0, axial, final, 0)
    for c in range(components):
        out_ref[c, axial - 1] += bound_ref[axial, c, :span]


def moved(x, to):
    sizes = [lax.axis_size(name) for name in AXES]
    pairs = []
    for r in range(sizes[0]):
        for s in range(sizes[1]):
            for p in range(sizes[2]):
                target = to(r, s, p)
                if all(0 <= at < size for at, size in zip(target, sizes)):
                    number = lambda at: (at[0] * sizes[1] + at[1]) * sizes[2] + at[2]
                    pairs.append((number((r, s, p)), number(target)))
    return lax.ppermute(x, AXES, pairs)


def struct(*shape):
    return jax.ShapeDtypeStruct(shape, jnp.float32)


def on_device(
    adjoint_start, source, couplings, damping, jacobians, giles_real, giles_imag, blades, mode_orders, cell_map,
):
    components, axial, span, pitch = adjoint_start.shape
    row_count, span_count, place_count = (lax.axis_size(name) for name in AXES)
    length = pitch * place_count
    assert components == COMPONENTS and components * WAVES <= pitch
    assert axial == ITERS - 1 and ITERS <= EDGE and axial * SEGMENT_LANES == pitch
    assert span_count == 2 and place_count > 1 and place_count & (place_count - 1) == 0
    wide = span + EDGE
    fields = 2 * components + 6
    groups = slots(fields + 1, components)[1][-1][0] + 1
    pairs = -(-(fields * axial + 1) // 2)
    span_tiles = pairs + -(-components * axial // EDGE)
    vmem = pl.BlockSpec(memory_space=pltpu.VMEM)
    hbm = pl.BlockSpec(memory_space=pltpu.HBM)

    def in_hbm(x):
        return pltpu.with_memory_space_constraint(x, pltpu.HBM)

    def call(kernel, name, outs, ins, aliases=None, scratch=(), limit=40 * MIB, **fixed):
        specs = [spec for spec, _ in ins]
        return pl.pallas_call(
            functools.partial(kernel, **fixed),
            out_shape=outs,
            in_specs=specs,
            out_specs=jax.tree.map(lambda _: vmem, outs),
            scratch_shapes=scratch,
            input_output_aliases=aliases or {},
            compiler_params=params(limit),
            name=name,
        )(*[value for _, value in ins])

    adjoint, coef, inv, edges, span_out, corner, inner, outer = call(
        pack_kernel, "pack",
        (
            struct(components, axial, span, pitch),
            struct(components + 6, axial, span, pitch), struct(span, pitch), struct(fields + 1, span, pitch),
            struct(span_tiles, EDGE, pitch), struct(2 * groups, EDGE, pitch), struct(groups, wide, pitch),
            struct(groups, wide, pitch),
        ),
        [(hbm, in_hbm(x)) for x in (adjoint_start, source, couplings, damping)],
        scratch=[
            pltpu.VMEM(source.shape, jnp.float32), pltpu.VMEM(couplings.shape, jnp.float32),
            pltpu.VMEM(damping.shape, jnp.float32), pltpu.SemaphoreType.DMA((4,)),
        ],
    )
    table, jac, modes = call(
        prepare_kernel, "prepare",
        (struct(pitch, pitch), struct(6 * components * components + 2, pitch), struct(span, pitch)),
        [(hbm, in_hbm(blades)), (hbm, in_hbm(jacobians.transpose(2, 3, 0, 1))), (vmem, adjoint)],
        scratch=[
            pltpu.SMEM(blades.shape, jnp.int32), pltpu.SMEM((components, components, 1, 6), jnp.float32),
            pltpu.SemaphoreType.DMA((2,)),
        ],
        row_count=row_count, length=length,
    )
    steps = [1 << n for n in range(place_count.bit_length() - 2)]
    last_step = place_count // 2

    def near(x):
        return moved(x, lambda r, s, p: (r - 1, s, p))

    def far(x):
        return moved(x, lambda r, s, p: (r - 1, s, p ^ last_step))

    corner = moved(corner, lambda r, s, p: (r, 1 - s, p))
    from_span = moved(span_out, lambda r, s, p: (r, 1 - s, p))
    inner = lax.dynamic_update_slice(inner, corner[:groups], (0, span, 0))
    outer = lax.dynamic_update_slice(outer, corner[groups:], (0, span, 0))
    outer = moved(outer, lambda r, s, p: (r, s, (p - 1 + 2 * (p % 2)) % place_count))
    inner = moved(inner, lambda r, s, p: (r, s, p ^ 1))

    for step in steps:
        modes = modes + moved(modes, lambda r, s, p: (r, s, p ^ step))
    modes_b = far(modes)
    modes_a = near(modes)

    state_shape = struct(axial + 1, components, axial + 2, wide, pitch)
    edge_shape = struct(axial + 1, components, wide, pitch)
    coef, inv, edge_coef, state, edge, more, part = call(
        first_kernel, "first_sweeps",
        (
            struct(components + 6, axial, wide, pitch), struct(wide, pitch), struct(components + 7, wide, pitch),
            state_shape, edge_shape,
            struct((axial - 1) * span + axial // 2 * EDGE, pitch), struct(span, pitch),
        ),
        [(vmem, jac)] + [(vmem, x) for x in (adjoint, coef, inv, edges, from_span, inner, outer, table)],
    )

    tables = (
        giles_real.transpose(2, 3, 0, 1), giles_imag.transpose(2, 3, 0, 1), mode_orders.transpose(0, 2, 1), cell_map,
    )
    synth = call(
        synth_kernel, "synth", struct(-(-components * (pitch + SEGMENT_LANES) // pitch) * pitch, pitch),
        [(vmem, jac)] + [(hbm, in_hbm(x)) for x in tables],
        scratch=[pltpu.VMEM(x.shape, x.dtype) for x in tables] + [
            pltpu.VMEM((2, components * components, mode_orders.shape[1]), jnp.float32), pltpu.SemaphoreType.DMA((4,)),
        ],
        row_count=row_count, place_count=place_count, components=components, pitch=pitch, length=length, axial=axial,
    )
    more = call(
        late_kernel, "late_modes", struct(axial * span + axial // 2 * EDGE, pitch),
        [(vmem, x) for x in (jac, coef, inv, part, more, modes_a, modes_b, synth, table)],
    )
    for step in steps:
        more = more + moved(more, lambda r, s, p: (r, s, p ^ step))
    more_b = far(more)
    more_a = near(more)
    return call(
        second_kernel, "second_sweeps", (state_shape, edge_shape, struct(components, axial, span, pitch)),
        [(vmem, x) for x in (
            jac, coef, inv, edge_coef, state, edge, modes_a, modes_b, more_a, more_b, synth,
        )],
        aliases={4: 0, 5: 1},
        scratch=[pltpu.VMEM((axial + 1, components, wide, pitch), jnp.float32)],
    )[2]


def solution(mesh):
    placed = (
        P(None, "row", "span", "pitch"),
        P(None, "row", "span", "pitch"),
        P(None, "row", "span", "pitch"),
        P("row", "span", "pitch"),
        P("row", None, None, None),
        P(),
        P(),
        P(),
        P(),
        P("row", None),
    )
    return jax.shard_map(
        on_device,
        mesh=mesh,
        in_specs=placed,
        out_specs=P(None, "row", "span", "pitch"),
        check_vma=False,
    )
```

```python
import functools
import math

import jax
import jax.numpy as jnp
from jax import lax
from jax.experimental import pallas as pl
from jax.experimental.pallas import tpu as pltpu
from jax.sharding import PartitionSpec as P

ITERS = 5
AXES = ("row", "span", "pitch")

ORDER_MAX = 2
BASE = 2 * ORDER_MAX + 1
COSINES = (BASE * BASE + 1) // 2
WAVES = 2 * COSINES - 1
COMPONENTS = 5
EDGE = 8
HALF = EDGE // 2
SEGMENT_LANES = 4 * EDGE
EXACT = lax.Precision.HIGHEST
MIB = 1024 * 1024


def params(limit):
    return pltpu.CompilerParams(vmem_limit_bytes=limit)


def lanes(shape):
    return lax.broadcasted_iota(jnp.int32, shape, len(shape) - 1)


def rows(shape):
    return lax.broadcasted_iota(jnp.int32, shape, len(shape) - 2)


def column(j):
    component = (j * 41) >> 10
    wave = j - WAVES * component
    sine = wave >= COSINES
    return component, jnp.where(sine, wave - (COSINES - 1), wave), sine


def mode_number(mode, blades):
    high = ((mode + ORDER_MAX) * 13) >> 6
    low = mode - BASE * high
    return high * blades[0] + low * blades[1]


def waves(products, length):
    if length & (length - 1) == 0:
        phase = products & (length - 1)
    else:
        phase = jnp.mod(products, length)
    turn = phase.astype(jnp.float32) * (1.0 / length)
    quarter = jnp.floor(4.0 * turn + 0.5)
    x = (turn - 0.25 * quarter) * (2.0 * math.pi)
    y = x * x
    sine = x * (1.0 + y * (-1.0 / 6 + y * (1.0 / 120 + y * (-1.0 / 5040 + y * (1.0 / 362880)))))
    cosine = 1.0 + y * (-0.5 + y * (1.0 / 24 + y * (-1.0 / 720 + y * (1.0 / 40320 - y * (1.0 / 3628800)))))
    quarter = quarter.astype(jnp.int32) & 3
    odd = (quarter & 1) == 1
    cos_out = jnp.where(odd, sine, cosine)
    sin_out = jnp.where(odd, cosine, sine)
    cos_out = jnp.where((quarter == 1) | (quarter == 2), -cos_out, cos_out)
    sin_out = jnp.where(quarter >= 2, -sin_out, sin_out)
    return cos_out, sin_out


def to_edges(layers, pitch):
    lane = lanes(layers[0].shape)
    block = jnp.zeros_like(layers[0])
    for a, layer in enumerate(layers):
        if layer is None:
            continue
        start = a * SEGMENT_LANES
        first = pltpu.roll(layer, (start + EDGE) % pitch, layer.ndim - 1)
        last = pltpu.roll(layer, (start + 3 * EDGE) % pitch, layer.ndim - 1)
        block = jnp.where((lane >= start + EDGE) & (lane < start + 2 * EDGE), first, block)
        block = jnp.where((lane >= start + 2 * EDGE) & (lane < start + 3 * EDGE), last, block)
    return block


def half_rows(side):
    return jnp.where(side == 0, EDGE // 2, 0), jnp.where(side == 0, 0, EDGE // 2)


def slots(fields, components):
    per_group = SEGMENT_LANES // HALF
    near = [(f // per_group, f % per_group * HALF) for f in range(fields)]
    group, lane = near[-1]
    far = [(group, lane + HALF + c) for c in range(components)]
    return near, far


def pack_kernel(
    adjoint_hbm, source_hbm, couplings_hbm, damping_hbm, blades_hbm, *refs, groups, length,
):
    (adjoint_ref, coef_ref, inv_ref, edges_ref, span_ref, small_ref, inner_ref, outer_ref, table_ref, blades_ref) = refs[5:15]
    source_ref, couplings_ref, damping_ref, sems = refs[20:]
    components, axial, span, pitch = adjoint_ref.shape
    copies = [
        pltpu.make_async_copy(src, dst, sems.at[n])
        for n, (src, dst) in enumerate((
            (couplings_hbm, couplings_ref), (damping_hbm, damping_ref), (source_hbm, source_ref),
            (adjoint_hbm, adjoint_ref), (blades_hbm, blades_ref), *zip(refs[:5], refs[15:20]),
        ))
    ]
    for copy in copies:
        copy.start()
    row, side, place = (lax.axis_index(name) for name in AXES)
    copies[0].wait()
    copies[1].wait()
    diag = damping_ref[...]
    for d in range(6):
        diag = diag + couplings_ref[d]
    inverse = 1.0 / diag
    for d in range(6):
        coef_ref[components + d] = couplings_ref[d] * inverse
    inv_ref[...] = inverse[axial - 1]
    copies[2].wait()
    for c in range(components):
        coef_ref[c] = source_ref[c] * inverse
    copies[3].wait()

    fields = 2 * components + 6
    for f in range(fields):
        ref, at = (adjoint_ref, f) if f < components else (coef_ref, f - components)
        edges_ref[f] = to_edges([ref[at, a] for a in range(axial)], pitch)
    last = inv_ref[...]
    edges_ref[fields] = jnp.where(
        lanes(last.shape) >= (axial - 1) * SEGMENT_LANES,
        to_edges([jnp.zeros_like(last)] * (axial - 1) + [last], pitch), 0.0,
    )
    edge_row = pl.multiple_of(jnp.where(side == 0, span - EDGE, 0), EDGE)
    near, far = slots(fields + 1, components)
    lane = lanes((span, pitch)) % SEGMENT_LANES
    sides = []
    for near_at, far_at in ((3 * EDGE - HALF, 3 * EDGE - HALF - 1), (EDGE, EDGE + HALF)):
        packed = [jnp.zeros((span, pitch), jnp.float32) for _ in range(groups)]
        for f, (g, to) in enumerate(near):
            value = pltpu.roll(edges_ref[f], (to - near_at) % pitch, 1)
            packed[g] = jnp.where((lane >= to) & (lane < to + HALF), value, packed[g])
        for f, (g, to) in enumerate(far):
            packed[g] = jnp.where(lane == to, pltpu.roll(edges_ref[f], (to - far_at) % pitch, 1), packed[g])
        sides.append(packed)
    even = lax.rem(place, 2) == 0
    for g in range(groups):
        for n, (out_ref, value) in enumerate((
            (inner_ref, jnp.where(even, sides[0][g], sides[1][g])), (outer_ref, jnp.where(even, sides[1][g], sides[0][g])),
        )):
            out_ref[pl.ds(g * span, span), :] = value
            small_ref[pl.ds((n * (groups + 1) + g) * EDGE, EDGE), :] = out_ref[pl.ds(g * span + edge_row, EDGE), :]
    copies[4].wait()
    face = jnp.maximum(row - 1, 0)
    component, mode, sine = column(lanes((pitch, pitch)))
    number = mode_number(mode, [picked(blades_ref[...], face + n) for n in range(2)])
    cos_table, sin_table = waves(number * (place * pitch + rows((pitch, pitch))), length)
    table = jnp.where(component < components, jnp.where(sine, sin_table, cos_table), 0.0)
    table_ref[...] = table
    start = groups * span + (groups + 1) * EDGE
    inner_ref[pl.ds(start, span), :] = projected([adjoint_ref[c, 0] for c in range(components)], table)
    small_ref[pl.ds(groups * EDGE, EDGE), :] = inner_ref[pl.ds(start + edge_row, EDGE), :]

    to_low, to_high = half_rows(side)
    line = rows((EDGE, pitch))
    tiles = [(adjoint_ref, c, a) for c in range(components) for a in range(axial)]
    tiles += [(coef_ref, f, a) for f in range(components + 6) for a in range(axial)]
    tiles = [ref[f, a, pl.ds(edge_row, EDGE), :] for ref, f, a in tiles] + [inv_ref[pl.ds(edge_row, EDGE), :]]
    pairs = -(-len(tiles) // 2)
    for n in range(pairs):
        value = pltpu.roll(tiles[2 * n], to_low, 0)
        if 2 * n + 1 < len(tiles):
            value = jnp.where(line < HALF, value, pltpu.roll(tiles[2 * n + 1], to_high, 0))
        span_ref[n] = value
    fifth = jnp.where(side == 0, HALF - 1, HALF)
    for n in range(span_ref.shape[0] - pairs):
        value = jnp.zeros((EDGE, pitch), jnp.float32)
        for k in range(min(EDGE, components * axial - n * EDGE)):
            value = jnp.where(line == k, pltpu.roll(tiles[n * EDGE + k], lax.rem(k + EDGE - fifth, EDGE), 0), value)
        span_ref[pairs + n] = value
    for copy in copies[5:]:
        copy.wait()


def picked(values, at):
    chosen = jnp.where(lanes(values.shape) == at, values.astype(jnp.float32), 0.0)
    return jnp.sum(chosen, axis=1, keepdims=True).astype(jnp.int32)


def projected(strips, table):
    component, _, _ = column(lanes(table.shape))
    total = jnp.zeros((strips[0].shape[0], table.shape[1]), jnp.float32)
    for c, strip in enumerate(strips):
        total += jnp.dot(
            strip, jnp.where(component == c, table, 0.0), precision=EXACT, preferred_element_type=jnp.float32,
        )
    return total


def synthesised(modes, synth):
    return lax.dot_general(
        modes, synth, (((1,), (1,)), ((), ())), precision=EXACT, preferred_element_type=jnp.float32,
    )


def synth_kernel(
    blades_ref, jacobians_ref, giles_re_ref, giles_im_ref, orders_ref, cells_ref, synth_ref, rows_ref, sums_ref,
    *, row_count, place_count, components, pitch, length, axial,
):
    row, place = lax.axis_index("row"), lax.axis_index("pitch")
    face = jnp.minimum(row, row_count - 2)
    for b in range(components):
        for c in range(components):
            entries = jacobians_ref[b, c]
            for d in range(6):
                at = (b * components + c) * 6 + d
                rows_ref[pl.ds(at, 1), :] = jnp.broadcast_to(entries[:, d:d + 1], (1, pitch))
    modes = orders_ref.shape[2]
    orders = orders_ref[face]
    tag = BASE * orders[0:1] + orders[1:2]
    component, mode, _ = column(rows((pitch, modes)))
    same = (jnp.abs(tag) == mode) & (component < components)
    plain = jnp.where(same, 1.0, 0.0)
    signed = jnp.where(tag < 0, -plain, plain)
    dims = (((1,), (1,)), ((), ()))
    for n, ref in enumerate((giles_re_ref, giles_im_ref)):
        for b in range(components):
            for c in range(components):
                sums_ref[n, pl.ds(b * components + c, 1), :] = ref[b, c, pl.ds(face, 1), :]
    sums_re = lax.dot_general(sums_ref[0], plain, dims, precision=EXACT, preferred_element_type=jnp.float32)
    sums_im = lax.dot_general(sums_ref[1], signed, dims, precision=EXACT, preferred_element_type=jnp.float32)
    component, mode, sine = column(lanes(sums_re.shape))
    scale = 2.0 / length
    with_cos = jnp.where(sine, sums_im, sums_re) * scale
    with_sin = jnp.where(sine, sums_re, -sums_im) * scale
    component = component[0:1]

    def chunk(at):
        start = pl.multiple_of(lax.rem(place + at + place_count, place_count) * pitch, pitch)
        return cells_ref[:, pl.ds(start, pitch)]

    own = chunk(0)
    lane = lanes((1, pitch))
    first = (axial - 1) * SEGMENT_LANES
    edge = jnp.where(lane < first + EDGE, pltpu.roll(chunk(-1), (first + EDGE) % pitch, 1), pltpu.roll(own, (first + EDGE) % pitch, 1))
    edge = jnp.where(lane < first + 2 * EDGE, edge, pltpu.roll(own, (first + 3 * EDGE) % pitch, 1))
    edge = jnp.where(lane < first + 3 * EDGE, edge, pltpu.roll(chunk(1), (first + 3 * EDGE) % pitch, 1))

    def upright(cells):
        wide = jnp.broadcast_to(cells.astype(jnp.float32), (pitch, pitch))
        return jnp.transpose(wide).astype(jnp.int32)

    edge_cells = upright(edge)[first:first + SEGMENT_LANES]
    at_cells = jnp.concatenate([upright(own), edge_cells], 0)
    _, mode, _ = column(lanes(at_cells.shape))
    blades = [picked(blades_ref[...], face + n) for n in range(2)]
    cos_table, sin_table = waves(mode_number(mode, blades) * at_cells, length)
    for c in range(components):
        row_cos = jnp.zeros((1, pitch), jnp.float32)
        row_sin = jnp.zeros((1, pitch), jnp.float32)
        for b in range(components):
            at = b * components + c
            row_cos = jnp.where(component == b, with_cos[at:at + 1], row_cos)
            row_sin = jnp.where(component == b, with_sin[at:at + 1], row_sin)
        part = row_cos * cos_table + row_sin * sin_table
        synth_ref[pl.ds(c * pitch, pitch), :] = part[:pitch]
        synth_ref[pl.ds(components * pitch + c * SEGMENT_LANES, SEGMENT_LANES), :] = part[pitch:]
    used = components * (pitch + SEGMENT_LANES)
    rest = synth_ref.shape[0] - used
    if rest:
        synth_ref[pl.ds(used, rest), :] = jnp.zeros((rest, pitch), jnp.float32)


def jacobian(jac_ref, components, b, c, d):
    return jac_ref[pl.ds((b * components + c) * 6 + d, 1), :]


def mixed(jac_ref, source, couplings, neighbours):
    total = list(source)
    jac = functools.partial(jacobian, jac_ref, len(total))
    for d, neighbour in enumerate(neighbours):
        for c in range(len(total)):
            term = jac(0, c, d) * neighbour[0]
            for b in range(1, len(total)):
                term = term + jac(b, c, d) * neighbour[b]
            total[c] = total[c] + couplings[d] * term
    return total


def layer_update(jac_ref, state_ref, edge_ref, coef_ref, t, a):
    components, wide, pitch = state_ref.shape[1], state_ref.shape[3], state_ref.shape[4]
    lane = lanes((wide, pitch))
    start = a * SEGMENT_LANES
    own = [state_ref[t, c, a + 1] for c in range(components)]
    above = [state_ref[t, c, a + 2] for c in range(components)]
    below = [state_ref[t, c, a] for c in range(components)]
    edge = [edge_ref[t, c] for c in range(components)]
    span_next = [pltpu.roll(x, wide - 1, 0) for x in own]
    span_prev = [pltpu.roll(x, 1, 0) for x in own]
    to_end = 2 * pitch - 1 - (start + 3 * EDGE)
    to_begin = 2 * pitch - (start + EDGE - 1)
    pitch_next = [
        jnp.where(lane == pitch - 1, pltpu.roll(e, lax.rem(to_end, pitch), 1), pltpu.roll(x, pitch - 1, 1))
        for e, x in zip(edge, own)
    ]
    pitch_prev = [
        jnp.where(lane == 0, pltpu.roll(e, lax.rem(to_begin, pitch), 1), pltpu.roll(x, 1, 1))
        for e, x in zip(edge, own)
    ]
    source = [coef_ref[c, a] for c in range(components)]
    couplings = [coef_ref[components + d, a] for d in range(6)]
    return mixed(jac_ref, source, couplings, (above, below, span_next, span_prev, pitch_next, pitch_prev))


def edge_update(jac_ref, edge_ref, edge_coef_ref, t, axial):
    components, wide, pitch = edge_ref.shape[1:]
    lane = lanes((wide, pitch))
    own = [edge_ref[t, c] for c in range(components)]
    above = [jnp.where(lane < (axial - 1) * SEGMENT_LANES, pltpu.roll(x, pitch - SEGMENT_LANES, 1), 0.0) for x in own]
    below = [jnp.where(lane >= SEGMENT_LANES, pltpu.roll(x, SEGMENT_LANES, 1), 0.0) for x in own]
    span_next = [pltpu.roll(x, wide - 1, 0) for x in own]
    span_prev = [pltpu.roll(x, 1, 0) for x in own]
    pitch_next = [pltpu.roll(x, pitch - 1, 1) for x in own]
    pitch_prev = [pltpu.roll(x, 1, 1) for x in own]
    source = [edge_coef_ref[c] for c in range(components)]
    couplings = [edge_coef_ref[components + d] for d in range(6)]
    return mixed(jac_ref, source, couplings, (above, below, span_next, span_prev, pitch_next, pitch_prev))


def edge_boundary(field, c, components, pitch, axial):
    at = components * pitch + c * SEGMENT_LANES
    tile = field[:, (at // pitch) * pitch:(at // pitch + 1) * pitch]
    return pltpu.roll(tile, ((axial - 1) * SEGMENT_LANES - at % pitch) % pitch, 1)


def advance(refs, t, a):
    state_ref = refs[1]
    for c, value in enumerate(layer_update(*refs, t, a)):
        state_ref[t + 1, c, a + 1] = value


def first_kernel(
    jac_ref, adjoint_ref, coef_in_ref, inv_in_ref, edges_ref, span_ref, inner_ref, outer_ref, table_ref,
    coef_ref, inv_ref, edge_coef_ref, state_ref, edge_ref, modes_ref, part_ref, *, groups,
):
    components, axial, span, pitch = adjoint_ref.shape
    wide = span + EDGE
    side = lax.axis_index("span")
    fields = 2 * components + 6
    line = rows((EDGE, pitch))
    keep_half = jnp.where(side == 0, line, EDGE - 1 - line) < HALF
    fifth = jnp.where(side == 0, HALF, HALF - 1)
    from_low, from_high = half_rows(1 - side)
    pairs = -(-(fields * axial + 1) // 2)

    def ghost(n):
        value = pltpu.roll(span_ref[n // 2], from_high if n % 2 else from_low, 0)
        value = jnp.where(keep_half, value, 0.0)
        if n < components * axial:
            extra = pltpu.roll(span_ref[pairs + n // EDGE], lax.rem(fifth + EDGE - n % EDGE, EDGE), 0)
            value = jnp.where(line == fifth, extra, value)
        return value

    even = lax.rem(lax.axis_index("pitch"), 2) == 0

    def group(ref, g):
        corner = ref[pl.ds(groups * span + g * EDGE, EDGE), :]
        return jnp.concatenate([ref[pl.ds(g * span, span), :], corner], 0)

    halves = [(group(inner_ref, g), group(outer_ref, g)) for g in range(groups)]
    from_left = [jnp.where(even, outer, inner) for inner, outer in halves]
    from_right = [jnp.where(even, inner, outer) for inner, outer in halves]
    near, far = slots(fields + 1, components)
    keep_five = keep_half | (line == fifth)
    for f in range(fields + 1):
        if f < fields:
            layers = [ghost(f * axial + a) for a in range(axial)]
        else:
            layers = [jnp.zeros((EDGE, pitch), jnp.float32)] * (axial - 1) + [ghost(fields * axial)]
        if f < components:
            for a in range(axial):
                state_ref[0, f, a + 1, :span] = adjoint_ref[f, a]
                state_ref[0, f, a + 1, span:] = layers[a]
        elif f < fields:
            for a in range(axial):
                coef_ref[f - components, a, :span] = coef_in_ref[f - components, a]
                coef_ref[f - components, a, span:] = layers[a]
        else:
            inv_ref[:span] = inv_in_ref[...]
            inv_ref[span:] = layers[-1]
        g, at = near[f]
        value = jnp.concatenate([edges_ref[f], to_edges(layers, pitch)], 0)
        lane = lanes((wide, pitch)) % SEGMENT_LANES
        value = jnp.where((lane >= HALF) & (lane < EDGE), pltpu.roll(from_left[g], (HALF - at) % pitch, 1), value)
        value = jnp.where(
            (lane >= 3 * EDGE) & (lane < 3 * EDGE + HALF),
            pltpu.roll(from_right[g], (3 * EDGE - at) % pitch, 1), value,
        )
        if f < components:
            g, at = far[f]
            value = jnp.where(lane == HALF - 1, pltpu.roll(from_left[g], (HALF - 1 - at) % pitch, 1), value)
            value = jnp.where(
                lane == 3 * EDGE + HALF, pltpu.roll(from_right[g], (3 * EDGE + HALF - at) % pitch, 1), value,
            )
        target, at = (edge_ref.at[0], f) if f < components else (edge_coef_ref, f - components)
        target[at, :span] = value[:span]
        target[at, span:] = jnp.where(keep_five if f < components else keep_half, value[span:], 0.0)
    for t in range(state_ref.shape[0]):
        for c in range(components):
            state_ref[t, c, 0] = jnp.zeros((wide, pitch), jnp.float32)
            state_ref[t, c, axial + 1] = jnp.zeros((wide, pitch), jnp.float32)

    refs = (jac_ref, state_ref, edge_ref, coef_ref)

    def sweep(t, carry):
        def body(a, inner):
            advance(refs, t, a)
            return inner

        lax.fori_loop(0, axial - t, body, 0)

        @pl.when(t < axial - 1)
        def _():
            for c, value in enumerate(edge_update(jac_ref, edge_ref, edge_coef_ref, t, axial)):
                edge_ref[t + 1, c] = value

        return carry

    lax.fori_loop(0, axial, sweep, 0)
    strips = [
        jnp.concatenate([state_ref[t, c, 1] for t in range(1, axial)] + [state_ref[axial, c, 1, :span]], 0)
        for c in range(components)
    ]
    total = projected(strips, table_ref[...])
    ghosts = jnp.zeros((EDGE, pitch), jnp.float32)
    for t in range(1, axial):
        part = total[(t - 1) * wide:t * wide]
        modes_ref[pl.ds((t - 1) * span, span), :] = part[:span]
        keep, to_packed, _ = ghost_rows(side, t, axial)
        ghosts = jnp.where(keep, pltpu.roll(part[span:], to_packed, 0), ghosts)
    modes_ref[pl.ds((axial - 1) * span, EDGE), :] = ghosts
    part_ref[...] = total[(axial - 1) * wide:]


def ghost_rows(side, t, axial):
    line = rows((EDGE, 1))
    distance = jnp.where(side == 0, line, EDGE - 1 - line)
    start = sum(axial - n for n in range(1, t))
    to_packed = jnp.where(side == 0, start, (EDGE - start) % EDGE)
    from_packed = jnp.where(side == 0, (EDGE - start) % EDGE, start)
    return (distance >= start) & (distance < start + axial - t), to_packed, from_packed


def along_axis(jac_ref, coef_ref, delta, a, height):
    components = len(delta)
    out = []
    for c in range(components):
        term = jacobian(jac_ref, components, 0, c, 0) * delta[0]
        for b in range(1, components):
            term = term + jacobian(jac_ref, components, b, c, 0) * delta[b]
        out.append(coef_ref[components, a, :height] * term)
    return out


def late_kernel(
    jac_ref, coef_ref, inv_ref, part_ref, more_ref, modes_a_ref, modes_b_ref, synth_ref, table_ref, modes_ref,
):
    span, pitch = part_ref.shape
    components, axial = coef_ref.shape[0] - 6, coef_ref.shape[1]
    field = synthesised(modes_a_ref[EDGE:] + modes_b_ref[EDGE:], synth_ref[:components * pitch])
    delta = [inv_ref[:span] * field[:, c * pitch:(c + 1) * pitch] for c in range(components)]
    for a in range(axial - 2, -1, -1):
        delta = along_axis(jac_ref, coef_ref, delta, a, span)
    before = more_ref.shape[0]
    modes_ref[:before] = more_ref[...]
    modes_ref[before:] = part_ref[...] + projected(delta, table_ref[...])


def between_kernel(
    jac_ref, coef_ref, inv_ref, edge_coef_ref, state_in_ref, edge_in_ref, modes_a_ref, modes_b_ref, synth_ref, more_ref,
    state_ref, edge_ref, sent_ref,
):
    sent_ref[...] = more_ref[...]
    components, axial = state_ref.shape[1], state_ref.shape[2] - 2
    wide, pitch = state_ref.shape[3:]
    modes = modes_a_ref[...] + modes_b_ref[...]
    field = synthesised(jnp.concatenate([modes[EDGE:], modes[:EDGE]], 0), synth_ref[...])
    delta = [inv_ref[...] * field[:, c * pitch:(c + 1) * pitch] for c in range(components)]
    for t in range(1, axial + 1):
        for c in range(components):
            state_ref[t, c, axial + 1 - t] += delta[c]
        if t < axial:
            delta = along_axis(jac_ref, coef_ref, delta, axial - 1 - t, wide)
    for c in range(components):
        edge_ref[1, c] += edge_coef_ref[components + 6] * edge_boundary(field, c, components, pitch, axial)
    refs = (jac_ref, state_ref, edge_ref, coef_ref)

    def sweep(t, carry):
        advance(refs, t, axial - t)

        @pl.when(t < axial)
        def _():
            for c, value in enumerate(edge_update(jac_ref, edge_ref, edge_coef_ref, t, axial)):
                edge_ref[t + 1, c] = value

        return carry

    lax.fori_loop(1, axial + 1, sweep, 0)


def second_kernel(
    jac_ref, coef_ref, inv_ref, edge_coef_ref, state_in_ref, edge_in_ref, more_a_ref, more_b_ref, synth_ref,
    state_ref, edge_ref, out_ref, bound_ref,
):
    components, axial, span, pitch = out_ref.shape
    wide = span + EDGE
    side = lax.axis_index("span")
    more = more_a_ref[...] + more_b_ref[...]
    start = (axial - 1) * span
    parts = []
    for t in range(1, axial):
        _, _, from_packed = ghost_rows(side, t, axial)
        parts += [more[(t - 1) * span:t * span], pltpu.roll(more[start:start + EDGE], from_packed, 0)]
    field = synthesised(jnp.concatenate(parts + [more[start + EDGE:]], 0), synth_ref[...])
    for t in range(1, axial):
        part = field[(t - 1) * wide:t * wide]
        for c in range(components):
            bound_ref[t, c] = inv_ref[...] * part[:, c * pitch:(c + 1) * pitch]
    for c in range(components):
        bound_ref[axial, c, :span] = inv_ref[:span] * field[(axial - 1) * wide:, c * pitch:(c + 1) * pitch]
    delta = [bound_ref[1, c] for c in range(components)]
    for t in range(2, axial + 2):
        for c in range(components):
            state_ref[t, c, axial + 2 - t] += delta[c]
        if t < axial + 1:
            delta = along_axis(jac_ref, coef_ref, delta, axial - t, wide)
    for t in range(1, axial):
        if t > 1:
            for c, value in enumerate(edge_update(jac_ref, edge_ref, edge_coef_ref, t, axial)):
                edge_ref[t + 1, c] = value
        part = field[(t - 1) * wide:t * wide]
        for c in range(components):
            edge_ref[t + 1, c] += edge_coef_ref[components + 6] * edge_boundary(part, c, components, pitch, axial)
    refs = (jac_ref, state_ref, edge_ref, coef_ref)

    def sweep(t, carry):
        def body(a, inner):
            advance(refs, t, a)
            return inner

        lax.fori_loop(axial + 1 - t, axial, body, 0)
        for c in range(components):
            state_ref[t + 1, c, axial] += bound_ref[t, c]
        return carry

    lax.fori_loop(2, axial, sweep, 0)

    def final(a, carry):
        for c, value in enumerate(layer_update(*refs, axial, a)):
            out_ref[c, a] = value[:span]
        return carry

    lax.fori_loop(1, axial, final, 0)
    for c in range(components):
        out_ref[c, 0] = state_ref[axial + 1, c, 1, :span]
        out_ref[c, axial - 1] += bound_ref[axial, c, :span]


def moved(x, to):
    sizes = [lax.axis_size(name) for name in AXES]
    pairs = []
    for r in range(sizes[0]):
        for s in range(sizes[1]):
            for p in range(sizes[2]):
                target = to(r, s, p)
                if all(0 <= at < size for at, size in zip(target, sizes)):
                    number = lambda at: (at[0] * sizes[1] + at[1]) * sizes[2] + at[2]
                    pairs.append((number((r, s, p)), number(target)))
    return lax.ppermute(x, AXES, pairs)


def struct(*shape):
    return jax.ShapeDtypeStruct(shape, jnp.float32)


def on_device(
    adjoint_start, source, couplings, damping, jacobians, giles_real, giles_imag, blades, mode_orders, cell_map,
):
    components, axial, span, pitch = adjoint_start.shape
    row_count, span_count, place_count = (lax.axis_size(name) for name in AXES)
    length = pitch * place_count
    assert sum(axial - t for t in range(1, axial)) <= EDGE
    assert components == COMPONENTS and components * WAVES <= pitch
    assert axial == ITERS - 1 and ITERS <= EDGE and axial * SEGMENT_LANES == pitch
    assert span_count == 2 and place_count > 1 and place_count & (place_count - 1) == 0
    wide = span + EDGE
    fields = 2 * components + 6
    groups = slots(fields + 1, components)[1][-1][0] + 1
    pairs = -(-(fields * axial + 1) // 2)
    span_tiles = pairs + -(-components * axial // EDGE)
    vmem = pl.BlockSpec(memory_space=pltpu.VMEM)
    hbm = pl.BlockSpec(memory_space=pltpu.HBM)

    def in_hbm(x):
        return pltpu.with_memory_space_constraint(x, pltpu.HBM)

    def call(kernel, name, outs, ins, aliases=None, scratch=(), limit=40 * MIB, **fixed):
        specs = [spec for spec, _ in ins]
        return pl.pallas_call(
            functools.partial(kernel, **fixed),
            out_shape=outs,
            in_specs=specs,
            out_specs=jax.tree.map(lambda _: vmem, outs),
            scratch_shapes=scratch,
            input_output_aliases=aliases or {},
            compiler_params=params(limit),
            name=name,
        )(*[value for _, value in ins])

    tables = (
        jacobians.transpose(2, 3, 0, 1), giles_real.transpose(2, 3, 0, 1), giles_imag.transpose(2, 3, 0, 1),
        mode_orders.transpose(0, 2, 1), cell_map,
    )
    blades = blades.reshape(1, -1)
    corner_rows = groups * EDGE
    adjoint, coef, inv, edges, span_out, small, inner, outer, table, blades, *tables = call(
        pack_kernel, "pack",
        (
            struct(components, axial, span, pitch), struct(components + 6, axial, span, pitch), struct(span, pitch),
            struct(fields + 1, span, pitch), struct(span_tiles, EDGE, pitch), struct(2 * corner_rows + EDGE, pitch),
            struct(groups * span + corner_rows + EDGE + span, pitch), struct(groups * span + corner_rows, pitch),
            struct(pitch, pitch), *(jax.ShapeDtypeStruct(x.shape, x.dtype) for x in (blades, *tables)),
        ),
        [(hbm, in_hbm(x)) for x in (adjoint_start, source, couplings, damping, blades, *tables)],
        scratch=[
            pltpu.VMEM(source.shape, jnp.float32), pltpu.VMEM(couplings.shape, jnp.float32),
            pltpu.VMEM(damping.shape, jnp.float32), pltpu.SemaphoreType.DMA((5 + len(tables),)),
        ],
        groups=groups, length=length,
    )
    steps = [1 << n for n in range(place_count.bit_length() - 2)]
    last_step = place_count // 2

    def near(x):
        return moved(x, lambda r, s, p: (r - 1, s, p))

    def far(x):
        return moved(x, lambda r, s, p: (r - 1, s, p ^ last_step))

    small = moved(small, lambda r, s, p: (r, 1 - s, p))
    from_span = moved(span_out, lambda r, s, p: (r, 1 - s, p))
    inner = lax.dynamic_update_slice(inner, small[:corner_rows + EDGE], (groups * span, 0))
    outer = lax.dynamic_update_slice(outer, small[corner_rows + EDGE:], (groups * span, 0))
    modes = inner[groups * span + corner_rows:]
    outer = moved(outer, lambda r, s, p: (r, s, (p - 1 + 2 * (p % 2)) % place_count))
    inner = moved(inner, lambda r, s, p: (r, s, p ^ 1))

    modes = modes + inner[groups * span + corner_rows:] if steps else modes
    for step in steps[1:]:
        modes = modes + moved(modes, lambda r, s, p: (r, s, p ^ step))
    modes_b = far(modes)
    modes_a = near(modes)

    synth, jac = call(
        synth_kernel, "synth",
        (
            struct(-(-components * (pitch + SEGMENT_LANES) // pitch) * pitch, pitch),
            struct(-(-6 * components * components // EDGE) * EDGE, pitch),
        ),
        [(vmem, x) for x in (blades, *tables)],
        scratch=[pltpu.VMEM((2, components * components, mode_orders.shape[1]), jnp.float32)],
        row_count=row_count, place_count=place_count, components=components, pitch=pitch, length=length, axial=axial,
    )
    state_shape = struct(axial + 2, components, axial + 2, wide, pitch)
    edge_shape = struct(axial + 1, components, wide, pitch)
    coef, inv, edge_coef, state, edge, more, part = call(
        first_kernel, "first_sweeps",
        (
            struct(components + 6, axial, wide, pitch), struct(wide, pitch), struct(components + 7, wide, pitch),
            state_shape, edge_shape,
            struct((axial - 1) * span + EDGE, pitch), struct(span, pitch),
        ),
        [(vmem, jac)] + [(vmem, x) for x in (adjoint, coef, inv, edges, from_span, inner, outer, table)],
        groups=groups,
    )

    more_shape = struct(axial * span + EDGE, pitch)
    more = call(
        late_kernel, "late_modes", more_shape,
        [(vmem, x) for x in (jac, coef, inv, part, more, modes_a, modes_b, synth, table)],
    )
    state, edge, sent = call(
        between_kernel, "between_sweeps", (state_shape, edge_shape, more_shape),
        [(vmem, x) for x in (jac, coef, inv, edge_coef, state, edge, modes_a, modes_b, synth, more)],
        aliases={4: 0, 5: 1},
    )
    for step in steps:
        got = moved(more, lambda r, s, p: (r, s, p ^ step))
        more, sent = sent + got, sent + got
    more_b = far(more)
    more_a = near(more)
    return call(
        second_kernel, "second_sweeps", (state_shape, edge_shape, struct(components, axial, span, pitch)),
        [(vmem, x) for x in (jac, coef, inv, edge_coef, state, edge, more_a, more_b, synth)],
        aliases={4: 0, 5: 1},
        scratch=[pltpu.VMEM((axial + 1, components, wide, pitch), jnp.float32)],
    )[2]


def solution(mesh):
    placed = (
        P(None, "row", "span", "pitch"),
        P(None, "row", "span", "pitch"),
        P(None, "row", "span", "pitch"),
        P("row", "span", "pitch"),
        P("row", None, None, None),
        P(),
        P(),
        P(),
        P(),
        P("row", None),
    )
    return jax.shard_map(
        on_device,
        mesh=mesh,
        in_specs=placed,
        out_specs=P(None, "row", "span", "pitch"),
        check_vma=False,
    )
```

```python
import functools
import math

import jax
import jax.numpy as jnp
from jax import lax
from jax.experimental import pallas as pl
from jax.experimental.pallas import tpu as pltpu
from jax.sharding import PartitionSpec as P

ITERS = 5
AXES = ("row", "span", "pitch")

ORDER_MAX = 2
BASE = 2 * ORDER_MAX + 1
COSINES = (BASE * BASE + 1) // 2
WAVES = 2 * COSINES - 1
COMPONENTS = 5
EDGE = 8
HALF = EDGE // 2
SEGMENT_LANES = 4 * EDGE
EXACT = lax.Precision.HIGHEST
MIB = 1024 * 1024


def params(limit):
    return pltpu.CompilerParams(vmem_limit_bytes=limit)


def lanes(shape):
    return lax.broadcasted_iota(jnp.int32, shape, len(shape) - 1)


def rows(shape):
    return lax.broadcasted_iota(jnp.int32, shape, len(shape) - 2)


def column(j):
    component = (j * 41) >> 10
    wave = j - WAVES * component
    sine = wave >= COSINES
    return component, jnp.where(sine, wave - (COSINES - 1), wave), sine


def mode_number(mode, blades):
    high = ((mode + ORDER_MAX) * 13) >> 6
    low = mode - BASE * high
    return high * blades[0] + low * blades[1]


def waves(products, length):
    if length & (length - 1) == 0:
        phase = products & (length - 1)
    else:
        phase = jnp.mod(products, length)
    turn = phase.astype(jnp.float32) * (1.0 / length)
    quarter = jnp.floor(4.0 * turn + 0.5)
    x = (turn - 0.25 * quarter) * (2.0 * math.pi)
    y = x * x
    sine = x * (1.0 + y * (-1.0 / 6 + y * (1.0 / 120 + y * (-1.0 / 5040 + y * (1.0 / 362880)))))
    cosine = 1.0 + y * (-0.5 + y * (1.0 / 24 + y * (-1.0 / 720 + y * (1.0 / 40320 - y * (1.0 / 3628800)))))
    quarter = quarter.astype(jnp.int32) & 3
    odd = (quarter & 1) == 1
    cos_out = jnp.where(odd, sine, cosine)
    sin_out = jnp.where(odd, cosine, sine)
    cos_out = jnp.where((quarter == 1) | (quarter == 2), -cos_out, cos_out)
    sin_out = jnp.where(quarter >= 2, -sin_out, sin_out)
    return cos_out, sin_out


def to_edges(layers, pitch):
    lane = lanes(layers[0].shape)
    block = jnp.zeros_like(layers[0])
    for a, layer in enumerate(layers):
        if layer is None:
            continue
        start = a * SEGMENT_LANES
        first = pltpu.roll(layer, (start + EDGE) % pitch, layer.ndim - 1)
        last = pltpu.roll(layer, (start + 3 * EDGE) % pitch, layer.ndim - 1)
        block = jnp.where((lane >= start + EDGE) & (lane < start + 2 * EDGE), first, block)
        block = jnp.where((lane >= start + 2 * EDGE) & (lane < start + 3 * EDGE), last, block)
    return block


def half_rows(side):
    return jnp.where(side == 0, EDGE // 2, 0), jnp.where(side == 0, 0, EDGE // 2)


def slots(fields, components):
    per_group = SEGMENT_LANES // HALF
    near = [(f // per_group, f % per_group * HALF) for f in range(fields)]
    group, lane = near[-1]
    far = [(group, lane + HALF + c) for c in range(components)]
    return near, far


def pack_kernel(
    adjoint_hbm, source_hbm, couplings_hbm, damping_hbm, blades_hbm, *refs, groups, length,
):
    (adjoint_ref, coef_ref, inv_ref, edges_ref, span_ref, small_ref, inner_ref, outer_ref, table_ref, modes_ref, blades_ref) = refs[5:16]
    source_ref, couplings_ref, damping_ref, sems = refs[21:]
    components, axial, span, pitch = adjoint_ref.shape
    copies = [
        pltpu.make_async_copy(src, dst, sems.at[n])
        for n, (src, dst) in enumerate((
            (couplings_hbm, couplings_ref), (damping_hbm, damping_ref), (source_hbm, source_ref),
            (adjoint_hbm, adjoint_ref), (blades_hbm, blades_ref), *zip(refs[:5], refs[16:21]),
        ))
    ]
    for copy in copies:
        copy.start()
    row, side, place = (lax.axis_index(name) for name in AXES)
    copies[0].wait()
    copies[1].wait()
    diag = damping_ref[...]
    for d in range(6):
        diag = diag + couplings_ref[d]
    inverse = 1.0 / diag
    for d in range(6):
        coef_ref[components + d] = couplings_ref[d] * inverse
    inv_ref[...] = inverse[axial - 1]
    copies[2].wait()
    for c in range(components):
        coef_ref[c] = source_ref[c] * inverse
    copies[3].wait()

    fields = 2 * components + 6
    for f in range(fields):
        ref, at = (adjoint_ref, f) if f < components else (coef_ref, f - components)
        edges_ref[f] = to_edges([ref[at, a] for a in range(axial)], pitch)
    last = inv_ref[...]
    edges_ref[fields] = jnp.where(
        lanes(last.shape) >= (axial - 1) * SEGMENT_LANES,
        to_edges([jnp.zeros_like(last)] * (axial - 1) + [last], pitch), 0.0,
    )
    edge_row = pl.multiple_of(jnp.where(side == 0, span - EDGE, 0), EDGE)
    near, far = slots(fields + 1, components)
    lane = lanes((span, pitch)) % SEGMENT_LANES
    sides = []
    for near_at, far_at in ((3 * EDGE - HALF, 3 * EDGE - HALF - 1), (EDGE, EDGE + HALF)):
        packed = [jnp.zeros((span, pitch), jnp.float32) for _ in range(groups)]
        for f, (g, to) in enumerate(near):
            value = pltpu.roll(edges_ref[f], (to - near_at) % pitch, 1)
            packed[g] = jnp.where((lane >= to) & (lane < to + HALF), value, packed[g])
        for f, (g, to) in enumerate(far):
            packed[g] = jnp.where(lane == to, pltpu.roll(edges_ref[f], (to - far_at) % pitch, 1), packed[g])
        sides.append(packed)
    even = lax.rem(place, 2) == 0
    for g in range(groups):
        for n, (out_ref, value) in enumerate((
            (inner_ref, jnp.where(even, sides[0][g], sides[1][g])), (outer_ref, jnp.where(even, sides[1][g], sides[0][g])),
        )):
            out_ref[pl.ds(g * span, span), :] = value
            small_ref[pl.ds((n * groups + g) * EDGE, EDGE), :] = out_ref[pl.ds(g * span + edge_row, EDGE), :]
    copies[4].wait()
    face = jnp.maximum(row - 1, 0)
    component, mode, sine = column(lanes((pitch, pitch)))
    number = mode_number(mode, [picked(blades_ref[...], face + n) for n in range(2)])
    cos_table, sin_table = waves(number * (place * pitch + rows((pitch, pitch))), length)
    table = jnp.where(component < components, jnp.where(sine, sin_table, cos_table), 0.0)
    table_ref[...] = table
    modes_ref[:span] = projected([adjoint_ref[c, 0] for c in range(components)], table)
    small_ref[pl.ds(2 * groups * EDGE, EDGE), :] = modes_ref[pl.ds(edge_row, EDGE), :]

    to_low, to_high = half_rows(side)
    line = rows((EDGE, pitch))
    tiles = [(adjoint_ref, c, a) for c in range(components) for a in range(axial)]
    tiles += [(coef_ref, f, a) for f in range(components + 6) for a in range(axial)]
    tiles = [ref[f, a, pl.ds(edge_row, EDGE), :] for ref, f, a in tiles] + [inv_ref[pl.ds(edge_row, EDGE), :]]
    pairs = -(-len(tiles) // 2)
    for n in range(pairs):
        value = pltpu.roll(tiles[2 * n], to_low, 0)
        if 2 * n + 1 < len(tiles):
            value = jnp.where(line < HALF, value, pltpu.roll(tiles[2 * n + 1], to_high, 0))
        span_ref[n] = value
    fifth = jnp.where(side == 0, HALF - 1, HALF)
    for n in range(span_ref.shape[0] - pairs):
        value = jnp.zeros((EDGE, pitch), jnp.float32)
        for k in range(min(EDGE, components * axial - n * EDGE)):
            value = jnp.where(line == k, pltpu.roll(tiles[n * EDGE + k], lax.rem(k + EDGE - fifth, EDGE), 0), value)
        span_ref[pairs + n] = value
    for copy in copies[5:]:
        copy.wait()


def picked(values, at):
    chosen = jnp.where(lanes(values.shape) == at, values.astype(jnp.float32), 0.0)
    return jnp.sum(chosen, axis=1, keepdims=True).astype(jnp.int32)


def projected(strips, table):
    component, _, _ = column(lanes(table.shape))
    total = jnp.zeros((strips[0].shape[0], table.shape[1]), jnp.float32)
    for c, strip in enumerate(strips):
        total += jnp.dot(
            strip, jnp.where(component == c, table, 0.0), precision=EXACT, preferred_element_type=jnp.float32,
        )
    return total


def synthesised(modes, synth):
    return lax.dot_general(
        modes, synth, (((1,), (1,)), ((), ())), precision=EXACT, preferred_element_type=jnp.float32,
    )


def synth_kernel(
    blades_ref, jacobians_ref, giles_re_ref, giles_im_ref, orders_ref, cells_ref, synth_ref, rows_ref, sums_ref,
    *, row_count, place_count, components, pitch, length, axial,
):
    row, place = lax.axis_index("row"), lax.axis_index("pitch")
    face = jnp.minimum(row, row_count - 2)
    for b in range(components):
        for c in range(components):
            entries = jacobians_ref[b, c]
            for d in range(6):
                at = (b * components + c) * 6 + d
                rows_ref[pl.ds(at, 1), :] = jnp.broadcast_to(entries[:, d:d + 1], (1, pitch))
    modes = orders_ref.shape[2]
    orders = orders_ref[face]
    tag = BASE * orders[0:1] + orders[1:2]
    component, mode, _ = column(rows((pitch, modes)))
    same = (jnp.abs(tag) == mode) & (component < components)
    plain = jnp.where(same, 1.0, 0.0)
    signed = jnp.where(tag < 0, -plain, plain)
    dims = (((1,), (1,)), ((), ()))
    for n, ref in enumerate((giles_re_ref, giles_im_ref)):
        for b in range(components):
            for c in range(components):
                sums_ref[n, pl.ds(b * components + c, 1), :] = ref[b, c, pl.ds(face, 1), :]
    sums_re = lax.dot_general(sums_ref[0], plain, dims, precision=EXACT, preferred_element_type=jnp.float32)
    sums_im = lax.dot_general(sums_ref[1], signed, dims, precision=EXACT, preferred_element_type=jnp.float32)
    component, mode, sine = column(lanes(sums_re.shape))
    scale = 2.0 / length
    with_cos = jnp.where(sine, sums_im, sums_re) * scale
    with_sin = jnp.where(sine, sums_re, -sums_im) * scale
    component = component[0:1]

    def chunk(at):
        start = pl.multiple_of(lax.rem(place + at + place_count, place_count) * pitch, pitch)
        return cells_ref[:, pl.ds(start, pitch)]

    own = chunk(0)
    lane = lanes((1, pitch))
    first = (axial - 1) * SEGMENT_LANES
    edge = jnp.where(lane < first + EDGE, pltpu.roll(chunk(-1), (first + EDGE) % pitch, 1), pltpu.roll(own, (first + EDGE) % pitch, 1))
    edge = jnp.where(lane < first + 2 * EDGE, edge, pltpu.roll(own, (first + 3 * EDGE) % pitch, 1))
    edge = jnp.where(lane < first + 3 * EDGE, edge, pltpu.roll(chunk(1), (first + 3 * EDGE) % pitch, 1))

    def upright(cells):
        wide = jnp.broadcast_to(cells.astype(jnp.float32), (pitch, pitch))
        return jnp.transpose(wide).astype(jnp.int32)

    edge_cells = upright(edge)[first:first + SEGMENT_LANES]
    at_cells = jnp.concatenate([upright(own), edge_cells], 0)
    _, mode, _ = column(lanes(at_cells.shape))
    blades = [picked(blades_ref[...], face + n) for n in range(2)]
    cos_table, sin_table = waves(mode_number(mode, blades) * at_cells, length)
    for c in range(components):
        row_cos = jnp.zeros((1, pitch), jnp.float32)
        row_sin = jnp.zeros((1, pitch), jnp.float32)
        for b in range(components):
            at = b * components + c
            row_cos = jnp.where(component == b, with_cos[at:at + 1], row_cos)
            row_sin = jnp.where(component == b, with_sin[at:at + 1], row_sin)
        part = row_cos * cos_table + row_sin * sin_table
        synth_ref[pl.ds(c * pitch, pitch), :] = part[:pitch]
        synth_ref[pl.ds(components * pitch + c * SEGMENT_LANES, SEGMENT_LANES), :] = part[pitch:]
    used = components * (pitch + SEGMENT_LANES)
    rest = synth_ref.shape[0] - used
    if rest:
        synth_ref[pl.ds(used, rest), :] = jnp.zeros((rest, pitch), jnp.float32)


def jacobian(jac_ref, components, b, c, d):
    return jac_ref[pl.ds((b * components + c) * 6 + d, 1), :]


def mixed(jac_ref, source, couplings, neighbours):
    total = list(source)
    jac = functools.partial(jacobian, jac_ref, len(total))
    for d, neighbour in enumerate(neighbours):
        for c in range(len(total)):
            term = jac(0, c, d) * neighbour[0]
            for b in range(1, len(total)):
                term = term + jac(b, c, d) * neighbour[b]
            total[c] = total[c] + couplings[d] * term
    return total


def layer_update(jac_ref, state_ref, edge_ref, coef_ref, t, a):
    components, wide, pitch = state_ref.shape[1], state_ref.shape[3], state_ref.shape[4]
    lane = lanes((wide, pitch))
    start = a * SEGMENT_LANES
    own = [state_ref[t, c, a + 1] for c in range(components)]
    above = [state_ref[t, c, a + 2] for c in range(components)]
    below = [state_ref[t, c, a] for c in range(components)]
    edge = [edge_ref[t, c] for c in range(components)]
    span_next = [pltpu.roll(x, wide - 1, 0) for x in own]
    span_prev = [pltpu.roll(x, 1, 0) for x in own]
    to_end = 2 * pitch - 1 - (start + 3 * EDGE)
    to_begin = 2 * pitch - (start + EDGE - 1)
    pitch_next = [
        jnp.where(lane == pitch - 1, pltpu.roll(e, lax.rem(to_end, pitch), 1), pltpu.roll(x, pitch - 1, 1))
        for e, x in zip(edge, own)
    ]
    pitch_prev = [
        jnp.where(lane == 0, pltpu.roll(e, lax.rem(to_begin, pitch), 1), pltpu.roll(x, 1, 1))
        for e, x in zip(edge, own)
    ]
    source = [coef_ref[c, a] for c in range(components)]
    couplings = [coef_ref[components + d, a] for d in range(6)]
    return mixed(jac_ref, source, couplings, (above, below, span_next, span_prev, pitch_next, pitch_prev))


def edge_update(jac_ref, edge_ref, edge_coef_ref, t, axial):
    components, wide, pitch = edge_ref.shape[1:]
    lane = lanes((wide, pitch))
    own = [edge_ref[t, c] for c in range(components)]
    above = [jnp.where(lane < (axial - 1) * SEGMENT_LANES, pltpu.roll(x, pitch - SEGMENT_LANES, 1), 0.0) for x in own]
    below = [jnp.where(lane >= SEGMENT_LANES, pltpu.roll(x, SEGMENT_LANES, 1), 0.0) for x in own]
    span_next = [pltpu.roll(x, wide - 1, 0) for x in own]
    span_prev = [pltpu.roll(x, 1, 0) for x in own]
    pitch_next = [pltpu.roll(x, pitch - 1, 1) for x in own]
    pitch_prev = [pltpu.roll(x, 1, 1) for x in own]
    source = [edge_coef_ref[c] for c in range(components)]
    couplings = [edge_coef_ref[components + d] for d in range(6)]
    return mixed(jac_ref, source, couplings, (above, below, span_next, span_prev, pitch_next, pitch_prev))


def edge_boundary(field, c, components, pitch, axial):
    at = components * pitch + c * SEGMENT_LANES
    tile = field[:, (at // pitch) * pitch:(at // pitch + 1) * pitch]
    return pltpu.roll(tile, ((axial - 1) * SEGMENT_LANES - at % pitch) % pitch, 1)


def advance(refs, t, a):
    state_ref = refs[1]
    for c, value in enumerate(layer_update(*refs, t, a)):
        state_ref[t + 1, c, a + 1] = value


def first_kernel(
    jac_ref, adjoint_ref, coef_in_ref, inv_in_ref, edges_ref, inner_ref, outer_ref, span_ref,
    coef_ref, inv_ref, edge_coef_ref, state_ref, edge_ref, *, groups,
):
    components, axial, span, pitch = adjoint_ref.shape
    wide = span + EDGE
    side = lax.axis_index("span")
    fields = 2 * components + 6
    line = rows((EDGE, pitch))
    keep_half = jnp.where(side == 0, line, EDGE - 1 - line) < HALF
    fifth = jnp.where(side == 0, HALF, HALF - 1)
    from_low, from_high = half_rows(1 - side)
    pairs = -(-(fields * axial + 1) // 2)

    def ghost(n):
        value = pltpu.roll(span_ref[n // 2], from_high if n % 2 else from_low, 0)
        value = jnp.where(keep_half, value, 0.0)
        if n < components * axial:
            extra = pltpu.roll(span_ref[pairs + n // EDGE], lax.rem(fifth + EDGE - n % EDGE, EDGE), 0)
            value = jnp.where(line == fifth, extra, value)
        return value

    even = lax.rem(lax.axis_index("pitch"), 2) == 0

    def group(ref, g):
        corner = ref[pl.ds(groups * span + g * EDGE, EDGE), :]
        return jnp.concatenate([ref[pl.ds(g * span, span), :], corner], 0)

    halves = [(group(inner_ref, g), group(outer_ref, g)) for g in range(groups)]
    from_left = [jnp.where(even, outer, inner) for inner, outer in halves]
    from_right = [jnp.where(even, inner, outer) for inner, outer in halves]
    near, far = slots(fields + 1, components)
    keep_five = keep_half | (line == fifth)
    for f in range(fields + 1):
        if f < fields:
            layers = [ghost(f * axial + a) for a in range(axial)]
        else:
            layers = [jnp.zeros((EDGE, pitch), jnp.float32)] * (axial - 1) + [ghost(fields * axial)]
        if f < components:
            for a in range(axial):
                state_ref[0, f, a + 1, :span] = adjoint_ref[f, a]
                state_ref[0, f, a + 1, span:] = layers[a]
        elif f < fields:
            for a in range(axial):
                coef_ref[f - components, a, :span] = coef_in_ref[f - components, a]
                coef_ref[f - components, a, span:] = layers[a]
        else:
            inv_ref[:span] = inv_in_ref[...]
            inv_ref[span:] = layers[-1]
        g, at = near[f]
        value = jnp.concatenate([edges_ref[f], to_edges(layers, pitch)], 0)
        lane = lanes((wide, pitch)) % SEGMENT_LANES
        value = jnp.where((lane >= HALF) & (lane < EDGE), pltpu.roll(from_left[g], (HALF - at) % pitch, 1), value)
        value = jnp.where(
            (lane >= 3 * EDGE) & (lane < 3 * EDGE + HALF),
            pltpu.roll(from_right[g], (3 * EDGE - at) % pitch, 1), value,
        )
        if f < components:
            g, at = far[f]
            value = jnp.where(lane == HALF - 1, pltpu.roll(from_left[g], (HALF - 1 - at) % pitch, 1), value)
            value = jnp.where(
                lane == 3 * EDGE + HALF, pltpu.roll(from_right[g], (3 * EDGE + HALF - at) % pitch, 1), value,
            )
        target, at = (edge_ref.at[0], f) if f < components else (edge_coef_ref, f - components)
        target[at, :span] = value[:span]
        target[at, span:] = jnp.where(keep_five if f < components else keep_half, value[span:], 0.0)
    for t in range(state_ref.shape[0]):
        for c in range(components):
            state_ref[t, c, 0] = jnp.zeros((wide, pitch), jnp.float32)
            state_ref[t, c, axial + 1] = jnp.zeros((wide, pitch), jnp.float32)

    sweeps_without_boundaries(jac_ref, state_ref, edge_ref, coef_ref, edge_coef_ref, 0, 1)


def sweeps_without_boundaries(jac_ref, state_ref, edge_ref, coef_ref, edge_coef_ref, first, last):
    axial = state_ref.shape[2] - 2
    refs = (jac_ref, state_ref, edge_ref, coef_ref)

    def sweep(t, carry):
        def body(a, inner):
            advance(refs, t, a)
            return inner

        lax.fori_loop(0, axial - t, body, 0)

        @pl.when(t < axial - 1)
        def _():
            for c, value in enumerate(edge_update(jac_ref, edge_ref, edge_coef_ref, t, axial)):
                edge_ref[t + 1, c] = value

        return carry

    lax.fori_loop(first, last, sweep, 0)


def more_kernel(
    jac_ref, coef_ref, edge_coef_ref, state_in_ref, edge_in_ref, table_ref, state_ref, edge_ref, modes_ref, part_ref,
):
    components, axial = state_ref.shape[1], state_ref.shape[2] - 2
    wide, pitch = state_ref.shape[3:]
    span = wide - EDGE
    side = lax.axis_index("span")
    sweeps_without_boundaries(jac_ref, state_ref, edge_ref, coef_ref, edge_coef_ref, 1, axial)
    strips = [
        jnp.concatenate([state_ref[t, c, 1] for t in range(1, axial)] + [state_ref[axial, c, 1, :span]], 0)
        for c in range(components)
    ]
    total = projected(strips, table_ref[...])
    ghosts = jnp.zeros((EDGE, pitch), jnp.float32)
    for t in range(1, axial):
        part = total[(t - 1) * wide:t * wide]
        modes_ref[pl.ds((t - 1) * span, span), :] = part[:span]
        keep, to_packed, _ = ghost_rows(side, t, axial)
        ghosts = jnp.where(keep, pltpu.roll(part[span:], to_packed, 0), ghosts)
    modes_ref[pl.ds((axial - 1) * span, EDGE), :] = ghosts
    part_ref[...] = total[(axial - 1) * wide:]


def ghost_rows(side, t, axial):
    line = rows((EDGE, 1))
    distance = jnp.where(side == 0, line, EDGE - 1 - line)
    start = sum(axial - n for n in range(1, t))
    to_packed = jnp.where(side == 0, start, (EDGE - start) % EDGE)
    from_packed = jnp.where(side == 0, (EDGE - start) % EDGE, start)
    return (distance >= start) & (distance < start + axial - t), to_packed, from_packed


def along_axis(jac_ref, coef_ref, delta, a, height):
    components = len(delta)
    out = []
    for c in range(components):
        term = jacobian(jac_ref, components, 0, c, 0) * delta[0]
        for b in range(1, components):
            term = term + jacobian(jac_ref, components, b, c, 0) * delta[b]
        out.append(coef_ref[components, a, :height] * term)
    return out


def late_kernel(
    jac_ref, coef_ref, inv_ref, part_ref, more_ref, modes_a_ref, modes_b_ref, synth_ref, table_ref, modes_ref,
):
    span, pitch = part_ref.shape
    components, axial = coef_ref.shape[0] - 6, coef_ref.shape[1]
    field = synthesised(modes_a_ref[:span] + modes_b_ref[:span], synth_ref[:components * pitch])
    delta = [inv_ref[:span] * field[:, c * pitch:(c + 1) * pitch] for c in range(components)]
    for a in range(axial - 2, -1, -1):
        delta = along_axis(jac_ref, coef_ref, delta, a, span)
    before = more_ref.shape[0]
    modes_ref[:before] = more_ref[...]
    modes_ref[before:] = part_ref[...] + projected(delta, table_ref[...])


def between_kernel(
    jac_ref, coef_ref, inv_ref, edge_coef_ref, state_in_ref, edge_in_ref, modes_a_ref, modes_b_ref, synth_ref, more_ref,
    state_ref, edge_ref, sent_ref,
):
    sent_ref[...] = more_ref[...]
    components, axial = state_ref.shape[1], state_ref.shape[2] - 2
    wide, pitch = state_ref.shape[3:]
    field = synthesised(modes_a_ref[...] + modes_b_ref[...], synth_ref[...])
    delta = [inv_ref[...] * field[:, c * pitch:(c + 1) * pitch] for c in range(components)]
    for t in range(1, axial + 1):
        for c in range(components):
            state_ref[t, c, axial + 1 - t] += delta[c]
        if t < axial:
            delta = along_axis(jac_ref, coef_ref, delta, axial - 1 - t, wide)
    for c in range(components):
        edge_ref[1, c] += edge_coef_ref[components + 6] * edge_boundary(field, c, components, pitch, axial)
    refs = (jac_ref, state_ref, edge_ref, coef_ref)

    def sweep(t, carry):
        advance(refs, t, axial - t)

        @pl.when(t < axial)
        def _():
            for c, value in enumerate(edge_update(jac_ref, edge_ref, edge_coef_ref, t, axial)):
                edge_ref[t + 1, c] = value

        return carry

    lax.fori_loop(1, axial + 1, sweep, 0)


def second_kernel(
    jac_ref, coef_ref, inv_ref, edge_coef_ref, state_in_ref, edge_in_ref, more_a_ref, more_b_ref, synth_ref,
    state_ref, edge_ref, out_ref, bound_ref,
):
    components, axial, span, pitch = out_ref.shape
    wide = span + EDGE
    side = lax.axis_index("span")
    more = more_a_ref[...] + more_b_ref[...]
    start = (axial - 1) * span
    parts = []
    for t in range(1, axial):
        _, _, from_packed = ghost_rows(side, t, axial)
        parts += [more[(t - 1) * span:t * span], pltpu.roll(more[start:start + EDGE], from_packed, 0)]
    field = synthesised(jnp.concatenate(parts + [more[start + EDGE:]], 0), synth_ref[...])
    for t in range(1, axial):
        part = field[(t - 1) * wide:t * wide]
        for c in range(components):
            bound_ref[t, c] = inv_ref[...] * part[:, c * pitch:(c + 1) * pitch]
    for c in range(components):
        bound_ref[axial, c, :span] = inv_ref[:span] * field[(axial - 1) * wide:, c * pitch:(c + 1) * pitch]
    delta = [bound_ref[1, c] for c in range(components)]
    for t in range(2, axial + 2):
        for c in range(components):
            state_ref[t, c, axial + 2 - t] += delta[c]
        if t < axial + 1:
            delta = along_axis(jac_ref, coef_ref, delta, axial - t, wide)
    for t in range(1, axial):
        if t > 1:
            for c, value in enumerate(edge_update(jac_ref, edge_ref, edge_coef_ref, t, axial)):
                edge_ref[t + 1, c] = value
        part = field[(t - 1) * wide:t * wide]
        for c in range(components):
            edge_ref[t + 1, c] += edge_coef_ref[components + 6] * edge_boundary(part, c, components, pitch, axial)
    refs = (jac_ref, state_ref, edge_ref, coef_ref)

    def sweep(t, carry):
        def body(a, inner):
            advance(refs, t, a)
            return inner

        lax.fori_loop(axial + 1 - t, axial, body, 0)
        for c in range(components):
            state_ref[t + 1, c, axial] += bound_ref[t, c]
        return carry

    lax.fori_loop(2, axial, sweep, 0)

    def final(a, carry):
        for c, value in enumerate(layer_update(*refs, axial, a)):
            out_ref[c, a] = value[:span]
        return carry

    lax.fori_loop(1, axial, final, 0)
    for c in range(components):
        out_ref[c, 0] = state_ref[axial + 1, c, 1, :span]
        out_ref[c, axial - 1] += bound_ref[axial, c, :span]


def moved(x, to):
    sizes = [lax.axis_size(name) for name in AXES]
    pairs = []
    for r in range(sizes[0]):
        for s in range(sizes[1]):
            for p in range(sizes[2]):
                target = to(r, s, p)
                if all(0 <= at < size for at, size in zip(target, sizes)):
                    number = lambda at: (at[0] * sizes[1] + at[1]) * sizes[2] + at[2]
                    pairs.append((number((r, s, p)), number(target)))
    return lax.ppermute(x, AXES, pairs)


def struct(*shape):
    return jax.ShapeDtypeStruct(shape, jnp.float32)


def on_device(
    adjoint_start, source, couplings, damping, jacobians, giles_real, giles_imag, blades, mode_orders, cell_map,
):
    components, axial, span, pitch = adjoint_start.shape
    row_count, span_count, place_count = (lax.axis_size(name) for name in AXES)
    length = pitch * place_count
    assert sum(axial - t for t in range(1, axial)) <= EDGE
    assert components == COMPONENTS and components * WAVES <= pitch
    assert axial == ITERS - 1 and ITERS <= EDGE and axial * SEGMENT_LANES == pitch
    assert span_count == 2 and place_count > 1 and place_count & (place_count - 1) == 0
    wide = span + EDGE
    fields = 2 * components + 6
    groups = slots(fields + 1, components)[1][-1][0] + 1
    pairs = -(-(fields * axial + 1) // 2)
    span_tiles = pairs + -(-components * axial // EDGE)
    vmem = pl.BlockSpec(memory_space=pltpu.VMEM)
    hbm = pl.BlockSpec(memory_space=pltpu.HBM)

    def in_hbm(x):
        return pltpu.with_memory_space_constraint(x, pltpu.HBM)

    def call(kernel, name, outs, ins, aliases=None, scratch=(), limit=40 * MIB, **fixed):
        specs = [spec for spec, _ in ins]
        return pl.pallas_call(
            functools.partial(kernel, **fixed),
            out_shape=outs,
            in_specs=specs,
            out_specs=jax.tree.map(lambda _: vmem, outs),
            scratch_shapes=scratch,
            input_output_aliases=aliases or {},
            compiler_params=params(limit),
            name=name,
        )(*[value for _, value in ins])

    tables = (
        jacobians.transpose(2, 3, 0, 1), giles_real.transpose(2, 3, 0, 1), giles_imag.transpose(2, 3, 0, 1),
        mode_orders.transpose(0, 2, 1), cell_map,
    )
    blades = blades.reshape(1, -1)
    corner_rows = groups * EDGE
    adjoint, coef, inv, edges, span_out, small, inner, outer, table, modes, blades, *tables = call(
        pack_kernel, "pack",
        (
            struct(components, axial, span, pitch), struct(components + 6, axial, span, pitch), struct(span, pitch),
            struct(fields + 1, span, pitch), struct(span_tiles, EDGE, pitch), struct(2 * corner_rows + EDGE, pitch),
            struct(groups * wide, pitch), struct(groups * wide, pitch),
            struct(pitch, pitch), struct(wide, pitch), *(jax.ShapeDtypeStruct(x.shape, x.dtype) for x in (blades, *tables)),
        ),
        [(hbm, in_hbm(x)) for x in (adjoint_start, source, couplings, damping, blades, *tables)],
        scratch=[
            pltpu.VMEM(source.shape, jnp.float32), pltpu.VMEM(couplings.shape, jnp.float32),
            pltpu.VMEM(damping.shape, jnp.float32), pltpu.SemaphoreType.DMA((5 + len(tables),)),
        ],
        groups=groups, length=length,
    )
    steps = [1 << n for n in range(place_count.bit_length() - 2)]
    last_step = place_count // 2

    def near(x):
        return moved(x, lambda r, s, p: (r - 1, s, p))

    def far(x):
        return moved(x, lambda r, s, p: (r - 1, s, p ^ last_step))

    small = moved(small, lambda r, s, p: (r, 1 - s, p))
    small, span_out = lax.optimization_barrier((small, span_out))
    from_span = moved(span_out, lambda r, s, p: (r, 1 - s, p))
    inner = lax.dynamic_update_slice(inner, small[:corner_rows], (groups * span, 0))
    outer = lax.dynamic_update_slice(outer, small[corner_rows:2 * corner_rows], (groups * span, 0))
    modes = lax.dynamic_update_slice(modes, small[2 * corner_rows:], (span, 0))
    outer = moved(outer, lambda r, s, p: (r, s, (p - 1 + 2 * (p % 2)) % place_count))
    inner = moved(inner, lambda r, s, p: (r, s, p ^ 1))
    for step in steps:
        modes = modes + moved(modes, lambda r, s, p: (r, s, p ^ step))

    synth, jac = call(
        synth_kernel, "synth",
        (
            struct(-(-components * (pitch + SEGMENT_LANES) // pitch) * pitch, pitch),
            struct(-(-6 * components * components // EDGE) * EDGE, pitch),
        ),
        [(vmem, x) for x in (blades, *tables)],
        scratch=[pltpu.VMEM((2, components * components, mode_orders.shape[1]), jnp.float32)],
        row_count=row_count, place_count=place_count, components=components, pitch=pitch, length=length, axial=axial,
    )
    state_shape = struct(axial + 2, components, axial + 2, wide, pitch)
    edge_shape = struct(axial + 1, components, wide, pitch)
    coef, inv, edge_coef, state, edge = call(
        first_kernel, "first_sweep",
        (
            struct(components + 6, axial, wide, pitch), struct(wide, pitch), struct(components + 7, wide, pitch),
            state_shape, edge_shape,
        ),
        [(vmem, x) for x in (jac, adjoint, coef, inv, edges, inner, outer, from_span)],
        groups=groups,
    )
    inv, modes = lax.optimization_barrier((inv, modes))
    modes_b = far(modes)
    modes_a = near(modes)
    state, edge, more, part = call(
        more_kernel, "more_sweeps",
        (state_shape, edge_shape, struct((axial - 1) * span + EDGE, pitch), struct(span, pitch)),
        [(vmem, x) for x in (jac, coef, edge_coef, state, edge, table)],
        aliases={3: 0, 4: 1},
    )
    more_shape = struct(axial * span + EDGE, pitch)
    more = call(
        late_kernel, "late_modes", more_shape,
        [(vmem, x) for x in (jac, coef, inv, part, more, modes_a, modes_b, synth, table)],
    )
    state, edge, sent = call(
        between_kernel, "between_sweeps", (state_shape, edge_shape, more_shape),
        [(vmem, x) for x in (jac, coef, inv, edge_coef, state, edge, modes_a, modes_b, synth, more)],
        aliases={4: 0, 5: 1},
    )
    for step in steps:
        got = moved(more, lambda r, s, p: (r, s, p ^ step))
        more, sent = sent + got, sent + got
    more_b = far(more)
    more_a = near(more)
    return call(
        second_kernel, "second_sweeps", (state_shape, edge_shape, struct(components, axial, span, pitch)),
        [(vmem, x) for x in (jac, coef, inv, edge_coef, state, edge, more_a, more_b, synth)],
        aliases={4: 0, 5: 1},
        scratch=[pltpu.VMEM((axial + 1, components, wide, pitch), jnp.float32)],
    )[2]


def solution(mesh):
    placed = (
        P(None, "row", "span", "pitch"),
        P(None, "row", "span", "pitch"),
        P(None, "row", "span", "pitch"),
        P("row", "span", "pitch"),
        P("row", None, None, None),
        P(),
        P(),
        P(),
        P(),
        P("row", None),
    )
    return jax.shard_map(
        on_device,
        mesh=mesh,
        in_specs=placed,
        out_specs=P(None, "row", "span", "pitch"),
        check_vma=False,
    )
```

```python
import functools
import math

import jax
import jax.numpy as jnp
from jax import lax
from jax.experimental import pallas as pl
from jax.experimental.pallas import tpu as pltpu
from jax.sharding import PartitionSpec as P

ITERS = 5
AXES = ("row", "span", "pitch")

ORDER_MAX = 2
BASE = 2 * ORDER_MAX + 1
COSINES = (BASE * BASE + 1) // 2
WAVES = 2 * COSINES - 1
COMPONENTS = 5
EDGE = 8
HALF = EDGE // 2
SEGMENT_LANES = 4 * EDGE
EXACT = lax.Precision.HIGHEST
MIB = 1024 * 1024


def params(limit):
    return pltpu.CompilerParams(vmem_limit_bytes=limit)


def lanes(shape):
    return lax.broadcasted_iota(jnp.int32, shape, len(shape) - 1)


def rows(shape):
    return lax.broadcasted_iota(jnp.int32, shape, len(shape) - 2)


def column(j):
    component = (j * 41) >> 10
    wave = j - WAVES * component
    sine = wave >= COSINES
    return component, jnp.where(sine, wave - (COSINES - 1), wave), sine


def mode_number(mode, blades):
    high = ((mode + ORDER_MAX) * 13) >> 6
    low = mode - BASE * high
    return high * blades[0] + low * blades[1]


def waves(products, length):
    if length & (length - 1) == 0:
        phase = products & (length - 1)
    else:
        phase = jnp.mod(products, length)
    turn = phase.astype(jnp.float32) * (1.0 / length)
    quarter = jnp.floor(4.0 * turn + 0.5)
    x = (turn - 0.25 * quarter) * (2.0 * math.pi)
    y = x * x
    sine = x * (1.0 + y * (-1.0 / 6 + y * (1.0 / 120 + y * (-1.0 / 5040 + y * (1.0 / 362880)))))
    cosine = 1.0 + y * (-0.5 + y * (1.0 / 24 + y * (-1.0 / 720 + y * (1.0 / 40320 - y * (1.0 / 3628800)))))
    quarter = quarter.astype(jnp.int32) & 3
    odd = (quarter & 1) == 1
    cos_out = jnp.where(odd, sine, cosine)
    sin_out = jnp.where(odd, cosine, sine)
    cos_out = jnp.where((quarter == 1) | (quarter == 2), -cos_out, cos_out)
    sin_out = jnp.where(quarter >= 2, -sin_out, sin_out)
    return cos_out, sin_out


def to_edges(layers, pitch):
    lane = lanes(layers[0].shape)
    block = jnp.zeros_like(layers[0])
    for a, layer in enumerate(layers):
        if layer is None:
            continue
        start = a * SEGMENT_LANES
        first = pltpu.roll(layer, (start + EDGE) % pitch, layer.ndim - 1)
        last = pltpu.roll(layer, (start + 3 * EDGE) % pitch, layer.ndim - 1)
        block = jnp.where((lane >= start + EDGE) & (lane < start + 2 * EDGE), first, block)
        block = jnp.where((lane >= start + 2 * EDGE) & (lane < start + 3 * EDGE), last, block)
    return block


def half_rows(side):
    return jnp.where(side == 0, EDGE // 2, 0), jnp.where(side == 0, 0, EDGE // 2)


def slots(fields, components):
    per_group = SEGMENT_LANES // HALF
    near = [(f // per_group, f % per_group * HALF) for f in range(fields)]
    group, lane = near[-1]
    far = [(group, lane + HALF + c) for c in range(components)]
    return near, far


def pack_kernel(
    adjoint_hbm, source_hbm, couplings_hbm, damping_hbm, blades_hbm, *refs, groups, length,
):
    (adjoint_ref, coef_ref, inv_ref, edges_ref, span_ref, small_ref, inner_ref, outer_ref, table_ref, blades_ref) = refs[5:15]
    source_ref, couplings_ref, damping_ref, sems = refs[20:]
    components, axial, span, pitch = adjoint_ref.shape
    copies = [
        pltpu.make_async_copy(src, dst, sems.at[n])
        for n, (src, dst) in enumerate((
            (couplings_hbm, couplings_ref), (damping_hbm, damping_ref), (source_hbm, source_ref),
            (adjoint_hbm, adjoint_ref), (blades_hbm, blades_ref), *zip(refs[:5], refs[15:20]),
        ))
    ]
    for copy in copies:
        copy.start()
    row, side, place = (lax.axis_index(name) for name in AXES)
    copies[0].wait()
    copies[1].wait()
    diag = damping_ref[...]
    for d in range(6):
        diag = diag + couplings_ref[d]
    inverse = 1.0 / diag
    for d in range(6):
        coef_ref[components + d] = couplings_ref[d] * inverse
    inv_ref[...] = inverse[axial - 1]
    copies[2].wait()
    for c in range(components):
        coef_ref[c] = source_ref[c] * inverse
    copies[3].wait()

    fields = 2 * components + 6
    for f in range(fields):
        ref, at = (adjoint_ref, f) if f < components else (coef_ref, f - components)
        edges_ref[f] = to_edges([ref[at, a] for a in range(axial)], pitch)
    last = inv_ref[...]
    edges_ref[fields] = jnp.where(
        lanes(last.shape) >= (axial - 1) * SEGMENT_LANES,
        to_edges([jnp.zeros_like(last)] * (axial - 1) + [last], pitch), 0.0,
    )
    edge_row = pl.multiple_of(jnp.where(side == 0, span - EDGE, 0), EDGE)
    near, far = slots(fields + 1, components)
    lane = lanes((span, pitch)) % SEGMENT_LANES
    sides = []
    for near_at, far_at in ((3 * EDGE - HALF, 3 * EDGE - HALF - 1), (EDGE, EDGE + HALF)):
        packed = [jnp.zeros((span, pitch), jnp.float32) for _ in range(groups)]
        for f, (g, to) in enumerate(near):
            value = pltpu.roll(edges_ref[f], (to - near_at) % pitch, 1)
            packed[g] = jnp.where((lane >= to) & (lane < to + HALF), value, packed[g])
        for f, (g, to) in enumerate(far):
            packed[g] = jnp.where(lane == to, pltpu.roll(edges_ref[f], (to - far_at) % pitch, 1), packed[g])
        sides.append(packed)
    even = lax.rem(place, 2) == 0
    for g in range(groups):
        for n, (out_ref, value) in enumerate((
            (inner_ref, jnp.where(even, sides[0][g], sides[1][g])), (outer_ref, jnp.where(even, sides[1][g], sides[0][g])),
        )):
            out_ref[pl.ds(g * span, span), :] = value
            small_ref[pl.ds((n * (groups + 1) + g) * EDGE, EDGE), :] = out_ref[pl.ds(g * span + edge_row, EDGE), :]
    copies[4].wait()
    face = jnp.maximum(row - 1, 0)
    component, mode, sine = column(lanes((pitch, pitch)))
    number = mode_number(mode, [picked(blades_ref[...], face + n) for n in range(2)])
    cos_table, sin_table = waves(number * (place * pitch + rows((pitch, pitch))), length)
    table = jnp.where(component < components, jnp.where(sine, sin_table, cos_table), 0.0)
    table_ref[...] = table
    start = groups * span + (groups + 1) * EDGE
    inner_ref[pl.ds(start, span), :] = projected([adjoint_ref[c, 0] for c in range(components)], table)
    small_ref[pl.ds(groups * EDGE, EDGE), :] = inner_ref[pl.ds(start + edge_row, EDGE), :]

    to_low, to_high = half_rows(side)
    line = rows((EDGE, pitch))
    tiles = [(adjoint_ref, c, a) for c in range(components) for a in range(axial)]
    tiles += [(coef_ref, f, a) for f in range(components + 6) for a in range(axial)]
    tiles = [ref[f, a, pl.ds(edge_row, EDGE), :] for ref, f, a in tiles] + [inv_ref[pl.ds(edge_row, EDGE), :]]
    pairs = -(-len(tiles) // 2)
    for n in range(pairs):
        value = pltpu.roll(tiles[2 * n], to_low, 0)
        if 2 * n + 1 < len(tiles):
            value = jnp.where(line < HALF, value, pltpu.roll(tiles[2 * n + 1], to_high, 0))
        span_ref[n] = value
    fifth = jnp.where(side == 0, HALF - 1, HALF)
    for n in range(span_ref.shape[0] - pairs):
        value = jnp.zeros((EDGE, pitch), jnp.float32)
        for k in range(min(EDGE, components * axial - n * EDGE)):
            value = jnp.where(line == k, pltpu.roll(tiles[n * EDGE + k], lax.rem(k + EDGE - fifth, EDGE), 0), value)
        span_ref[pairs + n] = value
    for copy in copies[5:]:
        copy.wait()


def picked(values, at):
    chosen = jnp.where(lanes(values.shape) == at, values.astype(jnp.float32), 0.0)
    return jnp.sum(chosen, axis=1, keepdims=True).astype(jnp.int32)


def projected(strips, table):
    component, _, _ = column(lanes(table.shape))
    total = jnp.zeros((strips[0].shape[0], table.shape[1]), jnp.float32)
    for c, strip in enumerate(strips):
        total += jnp.dot(
            strip, jnp.where(component == c, table, 0.0), precision=EXACT, preferred_element_type=jnp.float32,
        )
    return total


def synthesised(modes, synth):
    return lax.dot_general(
        modes, synth, (((1,), (1,)), ((), ())), precision=EXACT, preferred_element_type=jnp.float32,
    )


def synth_kernel(
    blades_ref, jacobians_ref, giles_re_ref, giles_im_ref, orders_ref, cells_ref, synth_ref, rows_ref, sums_ref,
    *, row_count, place_count, components, pitch, length, axial,
):
    row, place = lax.axis_index("row"), lax.axis_index("pitch")
    face = jnp.minimum(row, row_count - 2)
    for b in range(components):
        for c in range(components):
            entries = jacobians_ref[b, c]
            for d in range(6):
                at = (b * components + c) * 6 + d
                rows_ref[pl.ds(at, 1), :] = jnp.broadcast_to(entries[:, d:d + 1], (1, pitch))
    modes = orders_ref.shape[2]
    orders = orders_ref[face]
    tag = BASE * orders[0:1] + orders[1:2]
    component, mode, _ = column(rows((pitch, modes)))
    same = (jnp.abs(tag) == mode) & (component < components)
    plain = jnp.where(same, 1.0, 0.0)
    signed = jnp.where(tag < 0, -plain, plain)
    dims = (((1,), (1,)), ((), ()))
    for n, ref in enumerate((giles_re_ref, giles_im_ref)):
        for b in range(components):
            for c in range(components):
                sums_ref[n, pl.ds(b * components + c, 1), :] = ref[b, c, pl.ds(face, 1), :]
    sums_re = lax.dot_general(sums_ref[0], plain, dims, precision=EXACT, preferred_element_type=jnp.float32)
    sums_im = lax.dot_general(sums_ref[1], signed, dims, precision=EXACT, preferred_element_type=jnp.float32)
    component, mode, sine = column(lanes(sums_re.shape))
    scale = 2.0 / length
    with_cos = jnp.where(sine, sums_im, sums_re) * scale
    with_sin = jnp.where(sine, sums_re, -sums_im) * scale
    component = component[0:1]

    def chunk(at):
        start = pl.multiple_of(lax.rem(place + at + place_count, place_count) * pitch, pitch)
        return cells_ref[:, pl.ds(start, pitch)]

    own = chunk(0)
    lane = lanes((1, pitch))
    first = (axial - 1) * SEGMENT_LANES
    edge = jnp.where(lane < first + EDGE, pltpu.roll(chunk(-1), (first + EDGE) % pitch, 1), pltpu.roll(own, (first + EDGE) % pitch, 1))
    edge = jnp.where(lane < first + 2 * EDGE, edge, pltpu.roll(own, (first + 3 * EDGE) % pitch, 1))
    edge = jnp.where(lane < first + 3 * EDGE, edge, pltpu.roll(chunk(1), (first + 3 * EDGE) % pitch, 1))

    def upright(cells):
        wide = jnp.broadcast_to(cells.astype(jnp.float32), (pitch, pitch))
        return jnp.transpose(wide).astype(jnp.int32)

    edge_cells = upright(edge)[first:first + SEGMENT_LANES]
    at_cells = jnp.concatenate([upright(own), edge_cells], 0)
    _, mode, _ = column(lanes(at_cells.shape))
    blades = [picked(blades_ref[...], face + n) for n in range(2)]
    cos_table, sin_table = waves(mode_number(mode, blades) * at_cells, length)
    for c in range(components):
        row_cos = jnp.zeros((1, pitch), jnp.float32)
        row_sin = jnp.zeros((1, pitch), jnp.float32)
        for b in range(components):
            at = b * components + c
            row_cos = jnp.where(component == b, with_cos[at:at + 1], row_cos)
            row_sin = jnp.where(component == b, with_sin[at:at + 1], row_sin)
        part = row_cos * cos_table + row_sin * sin_table
        synth_ref[pl.ds(c * pitch, pitch), :] = part[:pitch]
        synth_ref[pl.ds(components * pitch + c * SEGMENT_LANES, SEGMENT_LANES), :] = part[pitch:]
    used = components * (pitch + SEGMENT_LANES)
    rest = synth_ref.shape[0] - used
    if rest:
        synth_ref[pl.ds(used, rest), :] = jnp.zeros((rest, pitch), jnp.float32)


def jacobian(jac_ref, components, b, c, d):
    return jac_ref[pl.ds((b * components + c) * 6 + d, 1), :]


def mixed(jac_ref, source, couplings, neighbours):
    total = list(source)
    jac = functools.partial(jacobian, jac_ref, len(total))
    for d, neighbour in enumerate(neighbours):
        for c in range(len(total)):
            term = jac(0, c, d) * neighbour[0]
            for b in range(1, len(total)):
                term = term + jac(b, c, d) * neighbour[b]
            total[c] = total[c] + couplings[d] * term
    return total


def layer_update(jac_ref, state_ref, edge_ref, coef_ref, t, a):
    components, wide, pitch = state_ref.shape[1], state_ref.shape[3], state_ref.shape[4]
    lane = lanes((wide, pitch))
    start = a * SEGMENT_LANES
    own = [state_ref[t, c, a + 1] for c in range(components)]
    above = [state_ref[t, c, a + 2] for c in range(components)]
    below = [state_ref[t, c, a] for c in range(components)]
    edge = [edge_ref[t, c] for c in range(components)]
    span_next = [pltpu.roll(x, wide - 1, 0) for x in own]
    span_prev = [pltpu.roll(x, 1, 0) for x in own]
    to_end = 2 * pitch - 1 - (start + 3 * EDGE)
    to_begin = 2 * pitch - (start + EDGE - 1)
    pitch_next = [
        jnp.where(lane == pitch - 1, pltpu.roll(e, lax.rem(to_end, pitch), 1), pltpu.roll(x, pitch - 1, 1))
        for e, x in zip(edge, own)
    ]
    pitch_prev = [
        jnp.where(lane == 0, pltpu.roll(e, lax.rem(to_begin, pitch), 1), pltpu.roll(x, 1, 1))
        for e, x in zip(edge, own)
    ]
    source = [coef_ref[c, a] for c in range(components)]
    couplings = [coef_ref[components + d, a] for d in range(6)]
    return mixed(jac_ref, source, couplings, (above, below, span_next, span_prev, pitch_next, pitch_prev))


def edge_update(jac_ref, edge_ref, edge_coef_ref, t, axial):
    components, wide, pitch = edge_ref.shape[1:]
    lane = lanes((wide, pitch))
    own = [edge_ref[t, c] for c in range(components)]
    above = [jnp.where(lane < (axial - 1) * SEGMENT_LANES, pltpu.roll(x, pitch - SEGMENT_LANES, 1), 0.0) for x in own]
    below = [jnp.where(lane >= SEGMENT_LANES, pltpu.roll(x, SEGMENT_LANES, 1), 0.0) for x in own]
    span_next = [pltpu.roll(x, wide - 1, 0) for x in own]
    span_prev = [pltpu.roll(x, 1, 0) for x in own]
    pitch_next = [pltpu.roll(x, pitch - 1, 1) for x in own]
    pitch_prev = [pltpu.roll(x, 1, 1) for x in own]
    source = [edge_coef_ref[c] for c in range(components)]
    couplings = [edge_coef_ref[components + d] for d in range(6)]
    return mixed(jac_ref, source, couplings, (above, below, span_next, span_prev, pitch_next, pitch_prev))


def edge_boundary(field, c, components, pitch, axial):
    at = components * pitch + c * SEGMENT_LANES
    tile = field[:, (at // pitch) * pitch:(at // pitch + 1) * pitch]
    return pltpu.roll(tile, ((axial - 1) * SEGMENT_LANES - at % pitch) % pitch, 1)


def advance(refs, t, a):
    state_ref = refs[1]
    for c, value in enumerate(layer_update(*refs, t, a)):
        state_ref[t + 1, c, a + 1] = value


def first_kernel(
    jac_ref, adjoint_ref, coef_in_ref, inv_in_ref, edges_ref, span_ref, inner_ref, outer_ref, table_ref,
    coef_ref, inv_ref, edge_coef_ref, state_ref, edge_ref, modes_ref, part_ref, *, groups,
):
    components, axial, span, pitch = adjoint_ref.shape
    wide = span + EDGE
    side = lax.axis_index("span")
    fields = 2 * components + 6
    line = rows((EDGE, pitch))
    keep_half = jnp.where(side == 0, line, EDGE - 1 - line) < HALF
    fifth = jnp.where(side == 0, HALF, HALF - 1)
    from_low, from_high = half_rows(1 - side)
    pairs = -(-(fields * axial + 1) // 2)

    def ghost(n):
        value = pltpu.roll(span_ref[n // 2], from_high if n % 2 else from_low, 0)
        value = jnp.where(keep_half, value, 0.0)
        if n < components * axial:
            extra = pltpu.roll(span_ref[pairs + n // EDGE], lax.rem(fifth + EDGE - n % EDGE, EDGE), 0)
            value = jnp.where(line == fifth, extra, value)
        return value

    even = lax.rem(lax.axis_index("pitch"), 2) == 0

    def group(ref, g):
        corner = ref[pl.ds(groups * span + g * EDGE, EDGE), :]
        return jnp.concatenate([ref[pl.ds(g * span, span), :], corner], 0)

    halves = [(group(inner_ref, g), group(outer_ref, g)) for g in range(groups)]
    from_left = [jnp.where(even, outer, inner) for inner, outer in halves]
    from_right = [jnp.where(even, inner, outer) for inner, outer in halves]
    near, far = slots(fields + 1, components)
    keep_five = keep_half | (line == fifth)
    for f in range(fields + 1):
        if f < fields:
            layers = [ghost(f * axial + a) for a in range(axial)]
        else:
            layers = [jnp.zeros((EDGE, pitch), jnp.float32)] * (axial - 1) + [ghost(fields * axial)]
        if f < components:
            for a in range(axial):
                state_ref[0, f, a + 1, :span] = adjoint_ref[f, a]
                state_ref[0, f, a + 1, span:] = layers[a]
        elif f < fields:
            for a in range(axial):
                coef_ref[f - components, a, :span] = coef_in_ref[f - components, a]
                coef_ref[f - components, a, span:] = layers[a]
        else:
            inv_ref[:span] = inv_in_ref[...]
            inv_ref[span:] = layers[-1]
        g, at = near[f]
        value = jnp.concatenate([edges_ref[f], to_edges(layers, pitch)], 0)
        lane = lanes((wide, pitch)) % SEGMENT_LANES
        value = jnp.where((lane >= HALF) & (lane < EDGE), pltpu.roll(from_left[g], (HALF - at) % pitch, 1), value)
        value = jnp.where(
            (lane >= 3 * EDGE) & (lane < 3 * EDGE + HALF),
            pltpu.roll(from_right[g], (3 * EDGE - at) % pitch, 1), value,
        )
        if f < components:
            g, at = far[f]
            value = jnp.where(lane == HALF - 1, pltpu.roll(from_left[g], (HALF - 1 - at) % pitch, 1), value)
            value = jnp.where(
                lane == 3 * EDGE + HALF, pltpu.roll(from_right[g], (3 * EDGE + HALF - at) % pitch, 1), value,
            )
        target, at = (edge_ref.at[0], f) if f < components else (edge_coef_ref, f - components)
        target[at, :span] = value[:span]
        target[at, span:] = jnp.where(keep_five if f < components else keep_half, value[span:], 0.0)
    for t in range(state_ref.shape[0]):
        for c in range(components):
            state_ref[t, c, 0] = jnp.zeros((wide, pitch), jnp.float32)
            state_ref[t, c, axial + 1] = jnp.zeros((wide, pitch), jnp.float32)

    refs = (jac_ref, state_ref, edge_ref, coef_ref)

    def sweep(t, carry):
        def body(a, inner):
            advance(refs, t, a)
            return inner

        lax.fori_loop(0, axial - t, body, 0)

        @pl.when(t < axial - 1)
        def _():
            for c, value in enumerate(edge_update(jac_ref, edge_ref, edge_coef_ref, t, axial)):
                edge_ref[t + 1, c] = value

        return carry

    lax.fori_loop(0, axial, sweep, 0)
    strips = [
        jnp.concatenate([state_ref[t, c, 1] for t in range(1, axial)] + [state_ref[axial, c, 1, :span]], 0)
        for c in range(components)
    ]
    total = projected(strips, table_ref[...])
    ghosts = jnp.zeros((EDGE, pitch), jnp.float32)
    for t in range(1, axial):
        part = total[(t - 1) * wide:t * wide]
        modes_ref[pl.ds((t - 1) * span, span), :] = part[:span]
        keep, to_packed, _ = ghost_rows(side, t, axial)
        ghosts = jnp.where(keep, pltpu.roll(part[span:], to_packed, 0), ghosts)
    modes_ref[pl.ds((axial - 1) * span, EDGE), :] = ghosts
    part_ref[...] = total[(axial - 1) * wide:]


def ghost_rows(side, t, axial):
    line = rows((EDGE, 1))
    distance = jnp.where(side == 0, line, EDGE - 1 - line)
    start = sum(axial - n for n in range(1, t))
    to_packed = jnp.where(side == 0, start, (EDGE - start) % EDGE)
    from_packed = jnp.where(side == 0, (EDGE - start) % EDGE, start)
    return (distance >= start) & (distance < start + axial - t), to_packed, from_packed


def along_axis(jac_ref, coef_ref, delta, a, height):
    components = len(delta)
    out = []
    for c in range(components):
        term = jacobian(jac_ref, components, 0, c, 0) * delta[0]
        for b in range(1, components):
            term = term + jacobian(jac_ref, components, b, c, 0) * delta[b]
        out.append(coef_ref[components, a, :height] * term)
    return out


def late_kernel(
    jac_ref, coef_ref, inv_ref, part_ref, more_ref, first_ref, synth_ref, table_ref, modes_ref,
):
    span, pitch = part_ref.shape
    components, axial = coef_ref.shape[0] - 6, coef_ref.shape[1]
    field = synthesised(first_ref[EDGE:], synth_ref[:components * pitch])
    delta = [inv_ref[:span] * field[:, c * pitch:(c + 1) * pitch] for c in range(components)]
    for a in range(axial - 2, -1, -1):
        delta = along_axis(jac_ref, coef_ref, delta, a, span)
    before = more_ref.shape[0]
    modes_ref[:before] = more_ref[...]
    modes_ref[before:] = part_ref[...] + projected(delta, table_ref[...])


def between_kernel(
    jac_ref, coef_ref, inv_ref, edge_coef_ref, state_in_ref, edge_in_ref, modes_ref, synth_ref, more_ref,
    state_ref, edge_ref, sent_ref,
):
    sent_ref[...] = more_ref[...]
    components, axial = state_ref.shape[1], state_ref.shape[2] - 2
    wide, pitch = state_ref.shape[3:]
    modes = modes_ref[...]
    field = synthesised(jnp.concatenate([modes[EDGE:], modes[:EDGE]], 0), synth_ref[...])
    delta = [inv_ref[...] * field[:, c * pitch:(c + 1) * pitch] for c in range(components)]
    for t in range(1, axial + 1):
        for c in range(components):
            state_ref[t, c, axial + 1 - t] += delta[c]
        if t < axial:
            delta = along_axis(jac_ref, coef_ref, delta, axial - 1 - t, wide)
    for c in range(components):
        edge_ref[1, c] += edge_coef_ref[components + 6] * edge_boundary(field, c, components, pitch, axial)
    refs = (jac_ref, state_ref, edge_ref, coef_ref)

    def sweep(t, carry):
        advance(refs, t, axial - t)

        @pl.when(t < axial)
        def _():
            for c, value in enumerate(edge_update(jac_ref, edge_ref, edge_coef_ref, t, axial)):
                edge_ref[t + 1, c] = value

        return carry

    lax.fori_loop(1, axial + 1, sweep, 0)


def second_kernel(
    jac_ref, coef_ref, inv_ref, edge_coef_ref, state_in_ref, edge_in_ref, more_a_ref, more_b_ref, synth_ref,
    state_ref, edge_ref, out_ref, bound_ref,
):
    components, axial, span, pitch = out_ref.shape
    wide = span + EDGE
    side = lax.axis_index("span")
    more = more_a_ref[...] + more_b_ref[...]
    start = (axial - 1) * span
    parts = []
    for t in range(1, axial):
        _, _, from_packed = ghost_rows(side, t, axial)
        parts += [more[(t - 1) * span:t * span], pltpu.roll(more[start:start + EDGE], from_packed, 0)]
    field = synthesised(jnp.concatenate(parts + [more[start + EDGE:]], 0), synth_ref[...])
    for t in range(1, axial):
        part = field[(t - 1) * wide:t * wide]
        for c in range(components):
            bound_ref[t, c] = inv_ref[...] * part[:, c * pitch:(c + 1) * pitch]
    for c in range(components):
        bound_ref[axial, c, :span] = inv_ref[:span] * field[(axial - 1) * wide:, c * pitch:(c + 1) * pitch]
    delta = [bound_ref[1, c] for c in range(components)]
    for t in range(2, axial + 2):
        for c in range(components):
            state_ref[t, c, axial + 2 - t] += delta[c]
        if t < axial + 1:
            delta = along_axis(jac_ref, coef_ref, delta, axial - t, wide)
    for t in range(1, axial):
        if t > 1:
            for c, value in enumerate(edge_update(jac_ref, edge_ref, edge_coef_ref, t, axial)):
                edge_ref[t + 1, c] = value
        part = field[(t - 1) * wide:t * wide]
        for c in range(components):
            edge_ref[t + 1, c] += edge_coef_ref[components + 6] * edge_boundary(part, c, components, pitch, axial)
    refs = (jac_ref, state_ref, edge_ref, coef_ref)

    def sweep(t, carry):
        def body(a, inner):
            advance(refs, t, a)
            return inner

        lax.fori_loop(axial + 1 - t, axial, body, 0)
        for c in range(components):
            state_ref[t + 1, c, axial] += bound_ref[t, c]
        return carry

    lax.fori_loop(2, axial, sweep, 0)

    def final(a, carry):
        for c, value in enumerate(layer_update(*refs, axial, a)):
            out_ref[c, a] = value[:span]
        return carry

    lax.fori_loop(1, axial, final, 0)
    for c in range(components):
        out_ref[c, 0] = state_ref[axial + 1, c, 1, :span]
        out_ref[c, axial - 1] += bound_ref[axial, c, :span]


def moved(x, to):
    sizes = [lax.axis_size(name) for name in AXES]
    pairs = []
    for r in range(sizes[0]):
        for s in range(sizes[1]):
            for p in range(sizes[2]):
                target = to(r, s, p)
                if all(0 <= at < size for at, size in zip(target, sizes)):
                    number = lambda at: (at[0] * sizes[1] + at[1]) * sizes[2] + at[2]
                    pairs.append((number((r, s, p)), number(target)))
    return lax.ppermute(x, AXES, pairs)


def struct(*shape):
    return jax.ShapeDtypeStruct(shape, jnp.float32)


def on_device(
    adjoint_start, source, couplings, damping, jacobians, giles_real, giles_imag, blades, mode_orders, cell_map,
):
    components, axial, span, pitch = adjoint_start.shape
    row_count, span_count, place_count = (lax.axis_size(name) for name in AXES)
    length = pitch * place_count
    assert sum(axial - t for t in range(1, axial)) <= EDGE
    assert components == COMPONENTS and components * WAVES <= pitch
    assert axial == ITERS - 1 and ITERS <= EDGE and axial * SEGMENT_LANES == pitch
    assert span_count == 2 and place_count > 1 and place_count & (place_count - 1) == 0
    wide = span + EDGE
    fields = 2 * components + 6
    groups = slots(fields + 1, components)[1][-1][0] + 1
    pairs = -(-(fields * axial + 1) // 2)
    span_tiles = pairs + -(-components * axial // EDGE)
    vmem = pl.BlockSpec(memory_space=pltpu.VMEM)
    hbm = pl.BlockSpec(memory_space=pltpu.HBM)

    def in_hbm(x):
        return pltpu.with_memory_space_constraint(x, pltpu.HBM)

    def call(kernel, name, outs, ins, aliases=None, scratch=(), limit=40 * MIB, **fixed):
        specs = [spec for spec, _ in ins]
        return pl.pallas_call(
            functools.partial(kernel, **fixed),
            out_shape=outs,
            in_specs=specs,
            out_specs=jax.tree.map(lambda _: vmem, outs),
            scratch_shapes=scratch,
            input_output_aliases=aliases or {},
            compiler_params=params(limit),
            name=name,
        )(*[value for _, value in ins])

    tables = (
        jacobians.transpose(2, 3, 0, 1), giles_real.transpose(2, 3, 0, 1), giles_imag.transpose(2, 3, 0, 1),
        mode_orders.transpose(0, 2, 1), cell_map,
    )
    blades = blades.reshape(1, -1)
    corner_rows = groups * EDGE
    adjoint, coef, inv, edges, span_out, small, inner, outer, table, blades, *tables = call(
        pack_kernel, "pack",
        (
            struct(components, axial, span, pitch), struct(components + 6, axial, span, pitch), struct(span, pitch),
            struct(fields + 1, span, pitch), struct(span_tiles, EDGE, pitch), struct(2 * corner_rows + EDGE, pitch),
            struct(groups * span + corner_rows + EDGE + span, pitch), struct(groups * span + corner_rows, pitch),
            struct(pitch, pitch), *(jax.ShapeDtypeStruct(x.shape, x.dtype) for x in (blades, *tables)),
        ),
        [(hbm, in_hbm(x)) for x in (adjoint_start, source, couplings, damping, blades, *tables)],
        scratch=[
            pltpu.VMEM(source.shape, jnp.float32), pltpu.VMEM(couplings.shape, jnp.float32),
            pltpu.VMEM(damping.shape, jnp.float32), pltpu.SemaphoreType.DMA((5 + len(tables),)),
        ],
        groups=groups, length=length,
    )
    steps = [1 << n for n in range(place_count.bit_length() - 2)]
    last_step = place_count // 2

    def near(x):
        return moved(x, lambda r, s, p: (r - 1, s, p))

    def far(x):
        return moved(x, lambda r, s, p: (r - 1, s, p ^ last_step))

    small = moved(small, lambda r, s, p: (r, 1 - s, p))
    from_span = moved(span_out, lambda r, s, p: (r, 1 - s, p))
    inner = lax.dynamic_update_slice(inner, small[:corner_rows + EDGE], (groups * span, 0))
    outer = lax.dynamic_update_slice(outer, small[corner_rows + EDGE:], (groups * span, 0))
    modes = inner[groups * span + corner_rows:]
    outer = moved(outer, lambda r, s, p: (r, s, (p - 1 + 2 * (p % 2)) % place_count))
    inner = moved(inner, lambda r, s, p: (r, s, p ^ 1))

    modes = modes + inner[groups * span + corner_rows:]
    for step in [1 << n for n in range(1, place_count.bit_length() - 1)]:
        modes = modes + moved(modes, lambda r, s, p: (r, s, p ^ step))
    modes = near(modes)

    synth, jac = call(
        synth_kernel, "synth",
        (
            struct(-(-components * (pitch + SEGMENT_LANES) // pitch) * pitch, pitch),
            struct(-(-6 * components * components // EDGE) * EDGE, pitch),
        ),
        [(vmem, x) for x in (blades, *tables)],
        scratch=[pltpu.VMEM((2, components * components, mode_orders.shape[1]), jnp.float32)],
        row_count=row_count, place_count=place_count, components=components, pitch=pitch, length=length, axial=axial,
    )
    state_shape = struct(axial + 2, components, axial + 2, wide, pitch)
    edge_shape = struct(axial + 1, components, wide, pitch)
    coef, inv, edge_coef, state, edge, more, part = call(
        first_kernel, "first_sweeps",
        (
            struct(components + 6, axial, wide, pitch), struct(wide, pitch), struct(components + 7, wide, pitch),
            state_shape, edge_shape,
            struct((axial - 1) * span + EDGE, pitch), struct(span, pitch),
        ),
        [(vmem, jac)] + [(vmem, x) for x in (adjoint, coef, inv, edges, from_span, inner, outer, table)],
        groups=groups,
    )

    more_shape = struct(axial * span + EDGE, pitch)
    more = call(
        late_kernel, "late_modes", more_shape,
        [(vmem, x) for x in (jac, coef, inv, part, more, modes, synth, table)],
    )
    state, edge, sent = call(
        between_kernel, "between_sweeps", (state_shape, edge_shape, more_shape),
        [(vmem, x) for x in (jac, coef, inv, edge_coef, state, edge, modes, synth, more)],
        aliases={4: 0, 5: 1},
    )
    for step in steps:
        got = moved(more, lambda r, s, p: (r, s, p ^ step))
        more, sent = sent + got, sent + got
    more_b = far(more)
    more_a = near(more)
    return call(
        second_kernel, "second_sweeps", (state_shape, edge_shape, struct(components, axial, span, pitch)),
        [(vmem, x) for x in (jac, coef, inv, edge_coef, state, edge, more_a, more_b, synth)],
        aliases={4: 0, 5: 1},
        scratch=[pltpu.VMEM((axial + 1, components, wide, pitch), jnp.float32)],
    )[2]


def solution(mesh):
    placed = (
        P(None, "row", "span", "pitch"),
        P(None, "row", "span", "pitch"),
        P(None, "row", "span", "pitch"),
        P("row", "span", "pitch"),
        P("row", None, None, None),
        P(),
        P(),
        P(),
        P(),
        P("row", None),
    )
    return jax.shard_map(
        on_device,
        mesh=mesh,
        in_specs=placed,
        out_specs=P(None, "row", "span", "pitch"),
        check_vma=False,
    )
```

```python
import functools
import math

import jax
import jax.numpy as jnp
from jax import lax
from jax.experimental import pallas as pl
from jax.experimental.pallas import tpu as pltpu
from jax.sharding import PartitionSpec as P

ITERS = 5
AXES = ("row", "span", "pitch")

ORDER_MAX = 2
BASE = 2 * ORDER_MAX + 1
COSINES = (BASE * BASE + 1) // 2
WAVES = 2 * COSINES - 1
COMPONENTS = 5
EDGE = 8
HALF = EDGE // 2
SEGMENT_LANES = 4 * EDGE
EXACT = lax.Precision.HIGHEST
MIB = 1024 * 1024


def params(limit):
    return pltpu.CompilerParams(vmem_limit_bytes=limit)


def lanes(shape):
    return lax.broadcasted_iota(jnp.int32, shape, len(shape) - 1)


def rows(shape):
    return lax.broadcasted_iota(jnp.int32, shape, len(shape) - 2)


def column(j):
    component = (j * 41) >> 10
    wave = j - WAVES * component
    sine = wave >= COSINES
    return component, jnp.where(sine, wave - (COSINES - 1), wave), sine


def mode_number(mode, blades):
    high = ((mode + ORDER_MAX) * 13) >> 6
    low = mode - BASE * high
    return high * blades[0] + low * blades[1]


def waves(products, length):
    if length & (length - 1) == 0:
        phase = products & (length - 1)
    else:
        phase = jnp.mod(products, length)
    turn = phase.astype(jnp.float32) * (1.0 / length)
    quarter = jnp.floor(4.0 * turn + 0.5)
    x = (turn - 0.25 * quarter) * (2.0 * math.pi)
    y = x * x
    sine = x * (1.0 + y * (-1.0 / 6 + y * (1.0 / 120 + y * (-1.0 / 5040 + y * (1.0 / 362880)))))
    cosine = 1.0 + y * (-0.5 + y * (1.0 / 24 + y * (-1.0 / 720 + y * (1.0 / 40320 - y * (1.0 / 3628800)))))
    quarter = quarter.astype(jnp.int32) & 3
    odd = (quarter & 1) == 1
    cos_out = jnp.where(odd, sine, cosine)
    sin_out = jnp.where(odd, cosine, sine)
    cos_out = jnp.where((quarter == 1) | (quarter == 2), -cos_out, cos_out)
    sin_out = jnp.where(quarter >= 2, -sin_out, sin_out)
    return cos_out, sin_out


def to_edges(layers, pitch):
    lane = lanes(layers[0].shape)
    block = jnp.zeros_like(layers[0])
    for a, layer in enumerate(layers):
        if layer is None:
            continue
        start = a * SEGMENT_LANES
        first = pltpu.roll(layer, (start + EDGE) % pitch, layer.ndim - 1)
        last = pltpu.roll(layer, (start + 3 * EDGE) % pitch, layer.ndim - 1)
        block = jnp.where((lane >= start + EDGE) & (lane < start + 2 * EDGE), first, block)
        block = jnp.where((lane >= start + 2 * EDGE) & (lane < start + 3 * EDGE), last, block)
    return block


def half_rows(side):
    return jnp.where(side == 0, EDGE // 2, 0), jnp.where(side == 0, 0, EDGE // 2)


def slots(fields, components):
    per_group = SEGMENT_LANES // HALF
    near = [(f // per_group, f % per_group * HALF) for f in range(fields)]
    group, lane = near[-1]
    far = [(group, lane + HALF + c) for c in range(components)]
    return near, far


def pack_kernel(
    adjoint_hbm, source_hbm, couplings_hbm, damping_hbm, blades_hbm, *refs, groups, length,
):
    (adjoint_ref, coef_ref, inv_ref, edges_ref, span_ref, small_ref, inner_ref, outer_ref, table_ref, blades_ref) = refs[5:15]
    source_ref, couplings_ref, damping_ref, sems = refs[20:]
    components, axial, span, pitch = adjoint_ref.shape
    copies = [
        pltpu.make_async_copy(src, dst, sems.at[n])
        for n, (src, dst) in enumerate((
            (couplings_hbm, couplings_ref), (damping_hbm, damping_ref), (source_hbm, source_ref),
            (adjoint_hbm, adjoint_ref), (blades_hbm, blades_ref), *zip(refs[:5], refs[15:20]),
        ))
    ]
    for copy in copies:
        copy.start()
    row, side, place = (lax.axis_index(name) for name in AXES)
    copies[0].wait()
    copies[1].wait()
    diag = damping_ref[...]
    for d in range(6):
        diag = diag + couplings_ref[d]
    inverse = 1.0 / diag
    for d in range(6):
        coef_ref[components + d] = couplings_ref[d] * inverse
    inv_ref[...] = inverse[axial - 1]
    copies[2].wait()
    for c in range(components):
        coef_ref[c] = source_ref[c] * inverse
    copies[3].wait()

    fields = 2 * components + 6
    for f in range(fields):
        ref, at = (adjoint_ref, f) if f < components else (coef_ref, f - components)
        edges_ref[f] = to_edges([ref[at, a] for a in range(axial)], pitch)
    last = inv_ref[...]
    edges_ref[fields] = jnp.where(
        lanes(last.shape) >= (axial - 1) * SEGMENT_LANES,
        to_edges([jnp.zeros_like(last)] * (axial - 1) + [last], pitch), 0.0,
    )
    edge_row = pl.multiple_of(jnp.where(side == 0, span - EDGE, 0), EDGE)
    near, far = slots(fields + 1, components)
    lane = lanes((span, pitch)) % SEGMENT_LANES
    sides = []
    for near_at, far_at in ((3 * EDGE - HALF, 3 * EDGE - HALF - 1), (EDGE, EDGE + HALF)):
        packed = [jnp.zeros((span, pitch), jnp.float32) for _ in range(groups)]
        for f, (g, to) in enumerate(near):
            value = pltpu.roll(edges_ref[f], (to - near_at) % pitch, 1)
            packed[g] = jnp.where((lane >= to) & (lane < to + HALF), value, packed[g])
        for f, (g, to) in enumerate(far):
            packed[g] = jnp.where(lane == to, pltpu.roll(edges_ref[f], (to - far_at) % pitch, 1), packed[g])
        sides.append(packed)
    even = lax.rem(place, 2) == 0
    for g in range(groups):
        for n, (out_ref, value) in enumerate((
            (inner_ref, jnp.where(even, sides[0][g], sides[1][g])), (outer_ref, jnp.where(even, sides[1][g], sides[0][g])),
        )):
            out_ref[pl.ds(g * span, span), :] = value
            small_ref[pl.ds((n * (groups + 1) + g) * EDGE, EDGE), :] = out_ref[pl.ds(g * span + edge_row, EDGE), :]
    copies[4].wait()
    face = jnp.maximum(row - 1, 0)
    component, mode, sine = column(lanes((pitch, pitch)))
    number = mode_number(mode, [picked(blades_ref[...], face + n) for n in range(2)])
    cos_table, sin_table = waves(number * (place * pitch + rows((pitch, pitch))), length)
    table = jnp.where(component < components, jnp.where(sine, sin_table, cos_table), 0.0)
    for c in range(components):
        for n, value in enumerate(split(jnp.where(component == c, table, 0.0))):
            table_ref[n, pl.ds(c * pitch, pitch), :] = value
    start = groups * span + (groups + 1) * EDGE
    inner_ref[pl.ds(start, span), :] = projected([adjoint_ref[c, 0] for c in range(components)], table_ref)
    small_ref[pl.ds(groups * EDGE, EDGE), :] = inner_ref[pl.ds(start + edge_row, EDGE), :]

    to_low, to_high = half_rows(side)
    line = rows((EDGE, pitch))
    tiles = [(adjoint_ref, c, a) for c in range(components) for a in range(axial)]
    tiles += [(coef_ref, f, a) for f in range(components + 6) for a in range(axial)]
    tiles = [ref[f, a, pl.ds(edge_row, EDGE), :] for ref, f, a in tiles] + [inv_ref[pl.ds(edge_row, EDGE), :]]
    pairs = -(-len(tiles) // 2)
    for n in range(pairs):
        value = pltpu.roll(tiles[2 * n], to_low, 0)
        if 2 * n + 1 < len(tiles):
            value = jnp.where(line < HALF, value, pltpu.roll(tiles[2 * n + 1], to_high, 0))
        span_ref[n] = value
    fifth = jnp.where(side == 0, HALF - 1, HALF)
    for n in range(span_ref.shape[0] - pairs):
        value = jnp.zeros((EDGE, pitch), jnp.float32)
        for k in range(min(EDGE, components * axial - n * EDGE)):
            value = jnp.where(line == k, pltpu.roll(tiles[n * EDGE + k], lax.rem(k + EDGE - fifth, EDGE), 0), value)
        span_ref[pairs + n] = value
    for copy in copies[5:]:
        copy.wait()


def picked(values, at):
    chosen = jnp.where(lanes(values.shape) == at, values.astype(jnp.float32), 0.0)
    return jnp.sum(chosen, axis=1, keepdims=True).astype(jnp.int32)


def split(x):
    high = x.astype(jnp.bfloat16)
    return high, (x - high.astype(jnp.float32)).astype(jnp.bfloat16)


def product(x, table, dims):
    x_high, x_low = split(x)
    table_high, table_low = table
    dot = functools.partial(lax.dot_general, dimension_numbers=(dims, ((), ())), preferred_element_type=jnp.float32)
    return dot(x_high, table_high) + (dot(x_low, table_high) + dot(x_high, table_low))


def projected(strips, table_ref):
    return product(jnp.concatenate(strips, 1), (table_ref[0], table_ref[1]), ((1,), (0,)))


def synthesised(modes, synth_ref, count):
    return product(modes, (synth_ref[0, :count], synth_ref[1, :count]), ((1,), (1,)))


def synth_kernel(
    blades_ref, jacobians_ref, giles_re_ref, giles_im_ref, orders_ref, cells_ref, synth_ref, rows_ref, sums_ref,
    *, row_count, place_count, components, pitch, length, axial,
):
    row, place = lax.axis_index("row"), lax.axis_index("pitch")
    face = jnp.minimum(row, row_count - 2)
    for b in range(components):
        for c in range(components):
            entries = jacobians_ref[b, c]
            for d in range(6):
                at = (b * components + c) * 6 + d
                rows_ref[pl.ds(at, 1), :] = jnp.broadcast_to(entries[:, d:d + 1], (1, pitch))
    modes = orders_ref.shape[2]
    orders = orders_ref[face]
    tag = BASE * orders[0:1] + orders[1:2]
    component, mode, _ = column(rows((pitch, modes)))
    same = (jnp.abs(tag) == mode) & (component < components)
    plain = jnp.where(same, 1.0, 0.0)
    signed = jnp.where(tag < 0, -plain, plain)
    dims = (((1,), (1,)), ((), ()))
    for n, ref in enumerate((giles_re_ref, giles_im_ref)):
        for b in range(components):
            for c in range(components):
                sums_ref[n, pl.ds(b * components + c, 1), :] = ref[b, c, pl.ds(face, 1), :]
    sums_re = lax.dot_general(sums_ref[0], plain, dims, precision=EXACT, preferred_element_type=jnp.float32)
    sums_im = lax.dot_general(sums_ref[1], signed, dims, precision=EXACT, preferred_element_type=jnp.float32)
    component, mode, sine = column(lanes(sums_re.shape))
    scale = 2.0 / length
    with_cos = jnp.where(sine, sums_im, sums_re) * scale
    with_sin = jnp.where(sine, sums_re, -sums_im) * scale
    component = component[0:1]

    def chunk(at):
        start = pl.multiple_of(lax.rem(place + at + place_count, place_count) * pitch, pitch)
        return cells_ref[:, pl.ds(start, pitch)]

    own = chunk(0)
    lane = lanes((1, pitch))
    first = (axial - 1) * SEGMENT_LANES
    edge = jnp.where(lane < first + EDGE, pltpu.roll(chunk(-1), (first + EDGE) % pitch, 1), pltpu.roll(own, (first + EDGE) % pitch, 1))
    edge = jnp.where(lane < first + 2 * EDGE, edge, pltpu.roll(own, (first + 3 * EDGE) % pitch, 1))
    edge = jnp.where(lane < first + 3 * EDGE, edge, pltpu.roll(chunk(1), (first + 3 * EDGE) % pitch, 1))

    def upright(cells):
        wide = jnp.broadcast_to(cells.astype(jnp.float32), (pitch, pitch))
        return jnp.transpose(wide).astype(jnp.int32)

    edge_cells = upright(edge)[first:first + SEGMENT_LANES]
    at_cells = jnp.concatenate([upright(own), edge_cells], 0)
    _, mode, _ = column(lanes(at_cells.shape))
    blades = [picked(blades_ref[...], face + n) for n in range(2)]
    cos_table, sin_table = waves(mode_number(mode, blades) * at_cells, length)
    for c in range(components):
        row_cos = jnp.zeros((1, pitch), jnp.float32)
        row_sin = jnp.zeros((1, pitch), jnp.float32)
        for b in range(components):
            at = b * components + c
            row_cos = jnp.where(component == b, with_cos[at:at + 1], row_cos)
            row_sin = jnp.where(component == b, with_sin[at:at + 1], row_sin)
        part = row_cos * cos_table + row_sin * sin_table
        for n, value in enumerate(split(part)):
            synth_ref[n, pl.ds(c * pitch, pitch), :] = value[:pitch]
            synth_ref[n, pl.ds(components * pitch + c * SEGMENT_LANES, SEGMENT_LANES), :] = value[pitch:]
    used = components * (pitch + SEGMENT_LANES)
    rest = synth_ref.shape[1] - used
    if rest:
        synth_ref[:, pl.ds(used, rest), :] = jnp.zeros((2, rest, pitch), jnp.bfloat16)


def jacobian(jac_ref, components, b, c, d):
    return jac_ref[pl.ds((b * components + c) * 6 + d, 1), :]


def mixed(jac_ref, source, couplings, neighbours):
    total = list(source)
    jac = functools.partial(jacobian, jac_ref, len(total))
    for d, neighbour in enumerate(neighbours):
        for c in range(len(total)):
            term = jac(0, c, d) * neighbour[0]
            for b in range(1, len(total)):
                term = term + jac(b, c, d) * neighbour[b]
            total[c] = total[c] + couplings[d] * term
    return total


def layer_update(jac_ref, state_ref, edge_ref, coef_ref, t, a, height):
    components, wide, pitch = state_ref.shape[1], state_ref.shape[3], state_ref.shape[4]
    lane = lanes((height, pitch))
    start = a * SEGMENT_LANES
    own = [state_ref[t, c, a + 1] for c in range(components)]
    above = [state_ref[t, c, a + 2, :height] for c in range(components)]
    below = [state_ref[t, c, a, :height] for c in range(components)]
    edge = [edge_ref[t, c, :height] for c in range(components)]
    span_next = [pltpu.roll(x, wide - 1, 0)[:height] for x in own]
    span_prev = [pltpu.roll(x, 1, 0)[:height] for x in own]
    own = [x[:height] for x in own]
    to_end = 2 * pitch - 1 - (start + 3 * EDGE)
    to_begin = 2 * pitch - (start + EDGE - 1)
    pitch_next = [
        jnp.where(lane == pitch - 1, pltpu.roll(e, lax.rem(to_end, pitch), 1), pltpu.roll(x, pitch - 1, 1))
        for e, x in zip(edge, own)
    ]
    pitch_prev = [
        jnp.where(lane == 0, pltpu.roll(e, lax.rem(to_begin, pitch), 1), pltpu.roll(x, 1, 1))
        for e, x in zip(edge, own)
    ]
    source = [coef_ref[c, a, :height] for c in range(components)]
    couplings = [coef_ref[components + d, a, :height] for d in range(6)]
    return mixed(jac_ref, source, couplings, (above, below, span_next, span_prev, pitch_next, pitch_prev))


def edge_update(jac_ref, edge_ref, edge_coef_ref, t, axial):
    components, wide, pitch = edge_ref.shape[1:]
    lane = lanes((wide, pitch))
    own = [edge_ref[t, c] for c in range(components)]
    above = [jnp.where(lane < (axial - 1) * SEGMENT_LANES, pltpu.roll(x, pitch - SEGMENT_LANES, 1), 0.0) for x in own]
    below = [jnp.where(lane >= SEGMENT_LANES, pltpu.roll(x, SEGMENT_LANES, 1), 0.0) for x in own]
    span_next = [pltpu.roll(x, wide - 1, 0) for x in own]
    span_prev = [pltpu.roll(x, 1, 0) for x in own]
    pitch_next = [pltpu.roll(x, pitch - 1, 1) for x in own]
    pitch_prev = [pltpu.roll(x, 1, 1) for x in own]
    source = [edge_coef_ref[c] for c in range(components)]
    couplings = [edge_coef_ref[components + d] for d in range(6)]
    return mixed(jac_ref, source, couplings, (above, below, span_next, span_prev, pitch_next, pitch_prev))


def edge_boundary(field, c, components, pitch, axial):
    at = components * pitch + c * SEGMENT_LANES
    tile = field[:, (at // pitch) * pitch:(at // pitch + 1) * pitch]
    return pltpu.roll(tile, ((axial - 1) * SEGMENT_LANES - at % pitch) % pitch, 1)


def advance(refs, t, a, height=None):
    state_ref = refs[1]
    height = height or state_ref.shape[3]
    for c, value in enumerate(layer_update(*refs, t, a, height)):
        state_ref[t + 1, c, a + 1, :height] = value


def first_kernel(
    jac_ref, adjoint_ref, coef_in_ref, inv_in_ref, edges_ref, span_ref, inner_ref, outer_ref, table_ref,
    coef_ref, inv_ref, edge_coef_ref, state_ref, edge_ref, modes_ref, part_ref, *, groups,
):
    components, axial, span, pitch = adjoint_ref.shape
    wide = span + EDGE
    side = lax.axis_index("span")
    fields = 2 * components + 6
    line = rows((EDGE, pitch))
    keep_half = jnp.where(side == 0, line, EDGE - 1 - line) < HALF
    fifth = jnp.where(side == 0, HALF, HALF - 1)
    from_low, from_high = half_rows(1 - side)
    pairs = -(-(fields * axial + 1) // 2)

    def ghost(n):
        value = pltpu.roll(span_ref[n // 2], from_high if n % 2 else from_low, 0)
        value = jnp.where(keep_half, value, 0.0)
        if n < components * axial:
            extra = pltpu.roll(span_ref[pairs + n // EDGE], lax.rem(fifth + EDGE - n % EDGE, EDGE), 0)
            value = jnp.where(line == fifth, extra, value)
        return value

    even = lax.rem(lax.axis_index("pitch"), 2) == 0

    def group(ref, g):
        corner = ref[pl.ds(groups * span + g * EDGE, EDGE), :]
        return jnp.concatenate([ref[pl.ds(g * span, span), :], corner], 0)

    halves = [(group(inner_ref, g), group(outer_ref, g)) for g in range(groups)]
    from_left = [jnp.where(even, outer, inner) for inner, outer in halves]
    from_right = [jnp.where(even, inner, outer) for inner, outer in halves]
    near, far = slots(fields + 1, components)
    keep_five = keep_half | (line == fifth)
    for f in range(fields + 1):
        if f < fields:
            layers = [ghost(f * axial + a) for a in range(axial)]
        else:
            layers = [jnp.zeros((EDGE, pitch), jnp.float32)] * (axial - 1) + [ghost(fields * axial)]
        if f < components:
            for a in range(axial):
                state_ref[0, f, a + 1, :span] = adjoint_ref[f, a]
                state_ref[0, f, a + 1, span:] = layers[a]
        elif f < fields:
            for a in range(axial):
                coef_ref[f - components, a, :span] = coef_in_ref[f - components, a]
                coef_ref[f - components, a, span:] = layers[a]
        else:
            inv_ref[:span] = inv_in_ref[...]
            inv_ref[span:] = layers[-1]
        g, at = near[f]
        value = jnp.concatenate([edges_ref[f], to_edges(layers, pitch)], 0)
        lane = lanes((wide, pitch)) % SEGMENT_LANES
        value = jnp.where((lane >= HALF) & (lane < EDGE), pltpu.roll(from_left[g], (HALF - at) % pitch, 1), value)
        value = jnp.where(
            (lane >= 3 * EDGE) & (lane < 3 * EDGE + HALF),
            pltpu.roll(from_right[g], (3 * EDGE - at) % pitch, 1), value,
        )
        if f < components:
            g, at = far[f]
            value = jnp.where(lane == HALF - 1, pltpu.roll(from_left[g], (HALF - 1 - at) % pitch, 1), value)
            value = jnp.where(
                lane == 3 * EDGE + HALF, pltpu.roll(from_right[g], (3 * EDGE + HALF - at) % pitch, 1), value,
            )
        target, at = (edge_ref.at[0], f) if f < components else (edge_coef_ref, f - components)
        target[at, :span] = value[:span]
        target[at, span:] = jnp.where(keep_five if f < components else keep_half, value[span:], 0.0)
    for t in range(state_ref.shape[0]):
        for c in range(components):
            state_ref[t, c, 0] = jnp.zeros((wide, pitch), jnp.float32)
            state_ref[t, c, axial + 1] = jnp.zeros((wide, pitch), jnp.float32)

    refs = (jac_ref, state_ref, edge_ref, coef_ref)

    def sweep(t, carry):
        def body(a, inner):
            advance(refs, t, a)
            return inner

        lax.fori_loop(0, axial - t, body, 0)

        for c, value in enumerate(edge_update(jac_ref, edge_ref, edge_coef_ref, t, axial)):
            edge_ref[t + 1, c] = value
        return carry

    lax.fori_loop(0, axial - 1, sweep, 0)
    advance(refs, axial - 1, 0)
    strips = [
        jnp.concatenate([state_ref[t, c, 1] for t in range(1, axial)] + [state_ref[axial, c, 1, :span]], 0)
        for c in range(components)
    ]
    total = projected(strips, table_ref)
    ghosts = jnp.zeros((EDGE, pitch), jnp.float32)
    for t in range(1, axial):
        part = total[(t - 1) * wide:t * wide]
        modes_ref[pl.ds((t - 1) * span, span), :] = part[:span]
        keep, to_packed, _ = ghost_rows(side, t, axial)
        ghosts = jnp.where(keep, pltpu.roll(part[span:], to_packed, 0), ghosts)
    modes_ref[pl.ds((axial - 1) * span, EDGE), :] = ghosts
    part_ref[...] = total[(axial - 1) * wide:]


def ghost_rows(side, t, axial):
    line = rows((EDGE, 1))
    distance = jnp.where(side == 0, line, EDGE - 1 - line)
    start = sum(axial - n for n in range(1, t))
    to_packed = jnp.where(side == 0, start, (EDGE - start) % EDGE)
    from_packed = jnp.where(side == 0, (EDGE - start) % EDGE, start)
    return (distance >= start) & (distance < start + axial - t), to_packed, from_packed


def along_axis(jac_ref, coef_ref, delta, a, height):
    components = len(delta)
    out = []
    for c in range(components):
        term = jacobian(jac_ref, components, 0, c, 0) * delta[0]
        for b in range(1, components):
            term = term + jacobian(jac_ref, components, b, c, 0) * delta[b]
        out.append(coef_ref[components, a, :height] * term)
    return out


def late_kernel(
    jac_ref, coef_ref, inv_ref, part_ref, more_ref, modes_a_ref, modes_b_ref, synth_ref, table_ref, modes_ref,
):
    span, pitch = part_ref.shape
    components, axial = coef_ref.shape[0] - 6, coef_ref.shape[1]
    field = synthesised(modes_a_ref[EDGE:] + modes_b_ref[EDGE:], synth_ref, components * pitch)
    delta = [inv_ref[:span] * field[:, c * pitch:(c + 1) * pitch] for c in range(components)]
    for a in range(axial - 2, -1, -1):
        delta = along_axis(jac_ref, coef_ref, delta, a, span)
    before = more_ref.shape[0]
    modes_ref[:before] = more_ref[...]
    modes_ref[before:] = part_ref[...] + projected(delta, table_ref)


def between_kernel(
    jac_ref, coef_ref, inv_ref, edge_coef_ref, state_in_ref, edge_in_ref, modes_a_ref, modes_b_ref, synth_ref, more_ref,
    state_ref, edge_ref, sent_ref,
):
    sent_ref[...] = more_ref[...]
    components, axial = state_ref.shape[1], state_ref.shape[2] - 2
    wide, pitch = state_ref.shape[3:]
    modes = modes_a_ref[...] + modes_b_ref[...]
    field = synthesised(jnp.concatenate([modes[EDGE:], modes[:EDGE]], 0), synth_ref, synth_ref.shape[1])
    delta = [inv_ref[...] * field[:, c * pitch:(c + 1) * pitch] for c in range(components)]
    for t in range(1, axial + 1):
        for c in range(components):
            state_ref[t, c, axial + 1 - t] += delta[c]
        if t < axial:
            delta = along_axis(jac_ref, coef_ref, delta, axial - 1 - t, wide)
    for c in range(components):
        edge_ref[1, c] += edge_coef_ref[components + 6] * edge_boundary(field, c, components, pitch, axial)
    diagonal_sweeps(jac_ref, state_ref, edge_ref, coef_ref, edge_coef_ref, 1, axial // 2 + 1)


def beside_kernel(jac_ref, coef_ref, edge_coef_ref, state_in_ref, edge_in_ref, state_ref, edge_ref):
    axial, span = state_ref.shape[2] - 2, state_ref.shape[3] - EDGE
    diagonal_sweeps(jac_ref, state_ref, edge_ref, coef_ref, edge_coef_ref, axial // 2 + 1, axial)
    advance((jac_ref, state_ref, edge_ref, coef_ref), axial, 0, span)


def diagonal_sweeps(jac_ref, state_ref, edge_ref, coef_ref, edge_coef_ref, first, last):
    axial = state_ref.shape[2] - 2

    def sweep(t, carry):
        advance((jac_ref, state_ref, edge_ref, coef_ref), t, axial - t)
        for c, value in enumerate(edge_update(jac_ref, edge_ref, edge_coef_ref, t, axial)):
            edge_ref[t + 1, c] = value
        return carry

    lax.fori_loop(first, last, sweep, 0)


def second_kernel(
    jac_ref, coef_ref, inv_ref, edge_coef_ref, state_in_ref, edge_in_ref, more_a_ref, more_b_ref, synth_ref,
    state_ref, edge_ref, out_ref, bound_ref,
):
    components, axial, span, pitch = out_ref.shape
    wide = span + EDGE
    side = lax.axis_index("span")
    more = more_a_ref[...] + more_b_ref[...]
    start = (axial - 1) * span
    parts = []
    for t in range(1, axial):
        _, _, from_packed = ghost_rows(side, t, axial)
        parts += [more[(t - 1) * span:t * span], pltpu.roll(more[start:start + EDGE], from_packed, 0)]
    field = synthesised(jnp.concatenate(parts + [more[start + EDGE:]], 0), synth_ref, synth_ref.shape[1])
    for t in range(1, axial):
        part = field[(t - 1) * wide:t * wide]
        for c in range(components):
            bound_ref[t, c] = inv_ref[...] * part[:, c * pitch:(c + 1) * pitch]
    for c in range(components):
        bound_ref[axial, c, :span] = inv_ref[:span] * field[(axial - 1) * wide:, c * pitch:(c + 1) * pitch]
    delta = [bound_ref[1, c] for c in range(components)]
    for t in range(2, axial + 2):
        height = wide if t <= axial else span
        for c in range(components):
            state_ref[t, c, axial + 2 - t, :height] += delta[c][:height]
        if t < axial + 1:
            delta = along_axis(jac_ref, coef_ref, delta, axial - t, wide)
    for t in range(1, axial):
        if t > 1:
            for c, value in enumerate(edge_update(jac_ref, edge_ref, edge_coef_ref, t, axial)):
                edge_ref[t + 1, c] = value
        part = field[(t - 1) * wide:t * wide]
        for c in range(components):
            edge_ref[t + 1, c] += edge_coef_ref[components + 6] * edge_boundary(part, c, components, pitch, axial)
    refs = (jac_ref, state_ref, edge_ref, coef_ref)

    def sweep(t, carry):
        def body(a, inner):
            advance(refs, t, a)
            return inner

        lax.fori_loop(axial + 1 - t, axial, body, 0)
        for c in range(components):
            state_ref[t + 1, c, axial] += bound_ref[t, c]
        return carry

    lax.fori_loop(2, axial, sweep, 0)

    def final(a, carry):
        for c, value in enumerate(layer_update(*refs, axial, a, span)):
            out_ref[c, a] = value
        return carry

    lax.fori_loop(1, axial, final, 0)
    for c in range(components):
        out_ref[c, 0] = state_ref[axial + 1, c, 1, :span]
        out_ref[c, axial - 1] += bound_ref[axial, c, :span]


def moved(x, to):
    sizes = [lax.axis_size(name) for name in AXES]
    pairs = []
    for r in range(sizes[0]):
        for s in range(sizes[1]):
            for p in range(sizes[2]):
                target = to(r, s, p)
                if all(0 <= at < size for at, size in zip(target, sizes)):
                    number = lambda at: (at[0] * sizes[1] + at[1]) * sizes[2] + at[2]
                    pairs.append((number((r, s, p)), number(target)))
    return lax.ppermute(x, AXES, pairs)


def struct(*shape):
    return jax.ShapeDtypeStruct(shape, jnp.float32)


def on_device(
    adjoint_start, source, couplings, damping, jacobians, giles_real, giles_imag, blades, mode_orders, cell_map,
):
    components, axial, span, pitch = adjoint_start.shape
    row_count, span_count, place_count = (lax.axis_size(name) for name in AXES)
    length = pitch * place_count
    assert sum(axial - t for t in range(1, axial)) <= EDGE
    assert components == COMPONENTS and components * WAVES <= pitch
    assert axial == ITERS - 1 and ITERS <= EDGE and axial * SEGMENT_LANES == pitch
    assert span_count == 2 and place_count > 1 and place_count & (place_count - 1) == 0
    wide = span + EDGE
    fields = 2 * components + 6
    groups = slots(fields + 1, components)[1][-1][0] + 1
    pairs = -(-(fields * axial + 1) // 2)
    span_tiles = pairs + -(-components * axial // EDGE)
    vmem = pl.BlockSpec(memory_space=pltpu.VMEM)
    hbm = pl.BlockSpec(memory_space=pltpu.HBM)

    def in_hbm(x):
        return pltpu.with_memory_space_constraint(x, pltpu.HBM)

    def call(kernel, name, outs, ins, aliases=None, scratch=(), limit=40 * MIB, **fixed):
        specs = [spec for spec, _ in ins]
        return pl.pallas_call(
            functools.partial(kernel, **fixed),
            out_shape=outs,
            in_specs=specs,
            out_specs=jax.tree.map(lambda _: vmem, outs),
            scratch_shapes=scratch,
            input_output_aliases=aliases or {},
            compiler_params=params(limit),
            name=name,
        )(*[value for _, value in ins])

    tables = (
        jacobians.transpose(2, 3, 0, 1), giles_real.transpose(2, 3, 0, 1), giles_imag.transpose(2, 3, 0, 1),
        mode_orders.transpose(0, 2, 1), cell_map,
    )
    blades = blades.reshape(1, -1)
    corner_rows = groups * EDGE
    adjoint, coef, inv, edges, span_out, small, inner, outer, table, blades, *tables = call(
        pack_kernel, "pack",
        (
            struct(components, axial, span, pitch), struct(components + 6, axial, span, pitch), struct(span, pitch),
            struct(fields + 1, span, pitch), struct(span_tiles, EDGE, pitch), struct(2 * corner_rows + EDGE, pitch),
            struct(groups * span + corner_rows + EDGE + span, pitch), struct(groups * span + corner_rows, pitch),
            jax.ShapeDtypeStruct((2, components * pitch, pitch), jnp.bfloat16), *(jax.ShapeDtypeStruct(x.shape, x.dtype) for x in (blades, *tables)),
        ),
        [(hbm, in_hbm(x)) for x in (adjoint_start, source, couplings, damping, blades, *tables)],
        scratch=[
            pltpu.VMEM(source.shape, jnp.float32), pltpu.VMEM(couplings.shape, jnp.float32),
            pltpu.VMEM(damping.shape, jnp.float32), pltpu.SemaphoreType.DMA((5 + len(tables),)),
        ],
        groups=groups, length=length,
    )
    steps = [1 << n for n in range(place_count.bit_length() - 2)]
    last_step = place_count // 2

    def near(x):
        return moved(x, lambda r, s, p: (r - 1, s, p))

    def far(x):
        return moved(x, lambda r, s, p: (r - 1, s, p ^ last_step))

    small = moved(small, lambda r, s, p: (r, 1 - s, p))
    from_span = moved(span_out, lambda r, s, p: (r, 1 - s, p))
    inner = lax.dynamic_update_slice(inner, small[:corner_rows + EDGE], (groups * span, 0))
    outer = lax.dynamic_update_slice(outer, small[corner_rows + EDGE:], (groups * span, 0))
    modes = inner[groups * span + corner_rows:]
    outer = moved(outer, lambda r, s, p: (r, s, (p - 1 + 2 * (p % 2)) % place_count))
    inner = moved(inner, lambda r, s, p: (r, s, p ^ 1))

    modes = modes + inner[groups * span + corner_rows:] if steps else modes
    for step in steps[1:]:
        modes = modes + moved(modes, lambda r, s, p: (r, s, p ^ step))
    modes_b = far(modes)
    modes_a = near(modes)

    synth, jac = call(
        synth_kernel, "synth",
        (
            jax.ShapeDtypeStruct(
                (2, -(-components * (pitch + SEGMENT_LANES) // pitch) * pitch, pitch), jnp.bfloat16
            ),
            struct(-(-6 * components * components // EDGE) * EDGE, pitch),
        ),
        [(vmem, x) for x in (blades, *tables)],
        scratch=[pltpu.VMEM((2, components * components, mode_orders.shape[1]), jnp.float32)],
        row_count=row_count, place_count=place_count, components=components, pitch=pitch, length=length, axial=axial,
    )
    state_shape = struct(axial + 2, components, axial + 2, wide, pitch)
    edge_shape = struct(axial + 1, components, wide, pitch)
    coef, inv, edge_coef, state, edge, more, part = call(
        first_kernel, "first_sweeps",
        (
            struct(components + 6, axial, wide, pitch), struct(wide, pitch), struct(components + 7, wide, pitch),
            state_shape, edge_shape,
            struct((axial - 1) * span + EDGE, pitch), struct(span, pitch),
        ),
        [(vmem, jac)] + [(vmem, x) for x in (adjoint, coef, inv, edges, from_span, inner, outer, table)],
        groups=groups,
    )

    more_shape = struct(axial * span + EDGE, pitch)
    more = call(
        late_kernel, "late_modes", more_shape,
        [(vmem, x) for x in (jac, coef, inv, part, more, modes_a, modes_b, synth, table)],
    )
    state, edge, sent = call(
        between_kernel, "between_sweeps", (state_shape, edge_shape, more_shape),
        [(vmem, x) for x in (jac, coef, inv, edge_coef, state, edge, modes_a, modes_b, synth, more)],
        aliases={4: 0, 5: 1},
    )
    state, edge = call(
        beside_kernel, "beside_sweeps", (state_shape, edge_shape),
        [(vmem, x) for x in (jac, coef, edge_coef, state, edge)],
        aliases={3: 0, 4: 1},
    )
    for step in steps:
        got = moved(more, lambda r, s, p: (r, s, p ^ step))
        more, sent = sent + got, sent + got
    more_b = far(more)
    more_a = near(more)
    return call(
        second_kernel, "second_sweeps", (state_shape, edge_shape, struct(components, axial, span, pitch)),
        [(vmem, x) for x in (jac, coef, inv, edge_coef, state, edge, more_a, more_b, synth)],
        aliases={4: 0, 5: 1},
        scratch=[pltpu.VMEM((axial + 1, components, wide, pitch), jnp.float32)],
    )[2]


def solution(mesh):
    placed = (
        P(None, "row", "span", "pitch"),
        P(None, "row", "span", "pitch"),
        P(None, "row", "span", "pitch"),
        P("row", "span", "pitch"),
        P("row", None, None, None),
        P(),
        P(),
        P(),
        P(),
        P("row", None),
    )
    return jax.shard_map(
        on_device,
        mesh=mesh,
        in_specs=placed,
        out_specs=P(None, "row", "span", "pitch"),
        check_vma=False,
    )
```

```python
import functools
import math

import jax
import jax.numpy as jnp
from jax import lax
from jax.experimental import pallas as pl
from jax.experimental.pallas import tpu as pltpu
from jax.sharding import PartitionSpec as P

ITERS = 5
AXES = ("row", "span", "pitch")

ORDER_MAX = 2
BASE = 2 * ORDER_MAX + 1
COSINES = (BASE * BASE + 1) // 2
WAVES = 2 * COSINES - 1
COMPONENTS = 5
EDGE = 8
HALF = EDGE // 2
SEGMENT_LANES = 4 * EDGE
EXACT = lax.Precision.HIGHEST
MIB = 1024 * 1024


def params(limit):
    return pltpu.CompilerParams(vmem_limit_bytes=limit)


def lanes(shape):
    return lax.broadcasted_iota(jnp.int32, shape, len(shape) - 1)


def rows(shape):
    return lax.broadcasted_iota(jnp.int32, shape, len(shape) - 2)


def column(j):
    component = (j * 41) >> 10
    wave = j - WAVES * component
    sine = wave >= COSINES
    return component, jnp.where(sine, wave - (COSINES - 1), wave), sine


def mode_number(mode, blades):
    high = ((mode + ORDER_MAX) * 13) >> 6
    low = mode - BASE * high
    return high * blades[0] + low * blades[1]


def waves(products, length):
    if length & (length - 1) == 0:
        phase = products & (length - 1)
    else:
        phase = jnp.mod(products, length)
    turn = phase.astype(jnp.float32) * (1.0 / length)
    quarter = jnp.floor(4.0 * turn + 0.5)
    x = (turn - 0.25 * quarter) * (2.0 * math.pi)
    y = x * x
    sine = x * (1.0 + y * (-1.0 / 6 + y * (1.0 / 120 + y * (-1.0 / 5040 + y * (1.0 / 362880)))))
    cosine = 1.0 + y * (-0.5 + y * (1.0 / 24 + y * (-1.0 / 720 + y * (1.0 / 40320 - y * (1.0 / 3628800)))))
    quarter = quarter.astype(jnp.int32) & 3
    odd = (quarter & 1) == 1
    cos_out = jnp.where(odd, sine, cosine)
    sin_out = jnp.where(odd, cosine, sine)
    cos_out = jnp.where((quarter == 1) | (quarter == 2), -cos_out, cos_out)
    sin_out = jnp.where(quarter >= 2, -sin_out, sin_out)
    return cos_out, sin_out


def to_edges(layers, pitch):
    lane = lanes(layers[0].shape)
    block = jnp.zeros_like(layers[0])
    for a, layer in enumerate(layers):
        if layer is None:
            continue
        start = a * SEGMENT_LANES
        first = pltpu.roll(layer, (start + EDGE) % pitch, layer.ndim - 1)
        last = pltpu.roll(layer, (start + 3 * EDGE) % pitch, layer.ndim - 1)
        block = jnp.where((lane >= start + EDGE) & (lane < start + 2 * EDGE), first, block)
        block = jnp.where((lane >= start + 2 * EDGE) & (lane < start + 3 * EDGE), last, block)
    return block


def half_rows(side):
    return jnp.where(side == 0, EDGE // 2, 0), jnp.where(side == 0, 0, EDGE // 2)


def slots(fields, components):
    per_group = SEGMENT_LANES // HALF
    near = [(f // per_group, f % per_group * HALF) for f in range(fields)]
    group, lane = near[-1]
    far = [(group, lane + HALF + c) for c in range(components)]
    return near, far


def pack_kernel(
    adjoint_hbm, source_hbm, couplings_hbm, damping_hbm, blades_hbm, *refs, groups, length,
):
    (state_ref, coef_ref, inv_ref, edges_ref, span_ref, small_ref, inner_ref, outer_ref, table_ref, blades_ref) = refs[5:15]
    source_ref, couplings_ref, damping_ref, sems = refs[20:]
    components, axial, span, pitch = source_ref.shape
    adjoint_ref = state_ref.at[0, :, :, pl.ds(0, span), :]
    copies = [
        pltpu.make_async_copy(src, dst, sems.at[n])
        for n, (src, dst) in enumerate((
            (couplings_hbm, couplings_ref), (damping_hbm, damping_ref), (source_hbm, source_ref),
            (adjoint_hbm, adjoint_ref), (blades_hbm, blades_ref), *zip(refs[:5], refs[15:20]),
        ))
    ]
    for copy in copies:
        copy.start()
    row, side, place = (lax.axis_index(name) for name in AXES)
    copies[0].wait()
    copies[1].wait()
    diag = damping_ref[...]
    for d in range(6):
        diag = diag + couplings_ref[d]
    inverse = 1.0 / diag
    for d in range(6):
        coef_ref[components + d, :, :span] = couplings_ref[d] * inverse
    inv_ref[:span] = inverse[axial - 1]
    copies[2].wait()
    for c in range(components):
        coef_ref[c, :, :span] = source_ref[c] * inverse
    copies[3].wait()

    fields = 2 * components + 6
    for f in range(fields):
        ref, at = (adjoint_ref, f) if f < components else (coef_ref, f - components)
        edges_ref[f] = to_edges([ref[at, a, :span] for a in range(axial)], pitch)
    last = inv_ref[:span]
    edges_ref[fields] = jnp.where(
        lanes(last.shape) >= (axial - 1) * SEGMENT_LANES,
        to_edges([jnp.zeros_like(last)] * (axial - 1) + [last], pitch), 0.0,
    )
    edge_row = pl.multiple_of(jnp.where(side == 0, span - EDGE, 0), EDGE)
    near, far = slots(fields + 1, components)
    lane = lanes((span, pitch)) % SEGMENT_LANES
    sides = []
    for near_at, far_at in ((3 * EDGE - HALF, 3 * EDGE - HALF - 1), (EDGE, EDGE + HALF)):
        packed = [jnp.zeros((span, pitch), jnp.float32) for _ in range(groups)]
        for f, (g, to) in enumerate(near):
            value = pltpu.roll(edges_ref[f], (to - near_at) % pitch, 1)
            packed[g] = jnp.where((lane >= to) & (lane < to + HALF), value, packed[g])
        for f, (g, to) in enumerate(far):
            packed[g] = jnp.where(lane == to, pltpu.roll(edges_ref[f], (to - far_at) % pitch, 1), packed[g])
        sides.append(packed)
    even = lax.rem(place, 2) == 0
    for g in range(groups):
        for n, (out_ref, value) in enumerate((
            (inner_ref, jnp.where(even, sides[0][g], sides[1][g])), (outer_ref, jnp.where(even, sides[1][g], sides[0][g])),
        )):
            out_ref[pl.ds(g * span, span), :] = value
            small_ref[pl.ds((n * (groups + 1) + g) * EDGE, EDGE), :] = out_ref[pl.ds(g * span + edge_row, EDGE), :]
    copies[4].wait()
    face = jnp.maximum(row - 1, 0)
    component, mode, sine = column(lanes((pitch, pitch)))
    number = mode_number(mode, [picked(blades_ref[...], face + n) for n in range(2)])
    cos_table, sin_table = waves(number * (place * pitch + rows((pitch, pitch))), length)
    table = jnp.where(component < components, jnp.where(sine, sin_table, cos_table), 0.0)
    for c in range(components):
        for n, value in enumerate(split(jnp.where(component == c, table, 0.0))):
            table_ref[n, pl.ds(c * pitch, pitch), :] = value
    start = groups * span + (groups + 1) * EDGE
    inner_ref[pl.ds(start, span), :] = projected([adjoint_ref[c, 0] for c in range(components)], table_ref)
    small_ref[pl.ds(groups * EDGE, EDGE), :] = inner_ref[pl.ds(start + edge_row, EDGE), :]

    to_low, to_high = half_rows(side)
    line = rows((EDGE, pitch))
    tiles = [(adjoint_ref, c, a) for c in range(components) for a in range(axial)]
    tiles += [(coef_ref, f, a) for f in range(components + 6) for a in range(axial)]
    tiles = [ref[f, a, pl.ds(edge_row, EDGE), :] for ref, f, a in tiles] + [inv_ref[pl.ds(edge_row, EDGE), :]]
    pairs = -(-len(tiles) // 2)
    for n in range(pairs):
        value = pltpu.roll(tiles[2 * n], to_low, 0)
        if 2 * n + 1 < len(tiles):
            value = jnp.where(line < HALF, value, pltpu.roll(tiles[2 * n + 1], to_high, 0))
        span_ref[n] = value
    fifth = jnp.where(side == 0, HALF - 1, HALF)
    for n in range(span_ref.shape[0] - pairs):
        value = jnp.zeros((EDGE, pitch), jnp.float32)
        for k in range(min(EDGE, components * axial - n * EDGE)):
            value = jnp.where(line == k, pltpu.roll(tiles[n * EDGE + k], lax.rem(k + EDGE - fifth, EDGE), 0), value)
        span_ref[pairs + n] = value
    for copy in copies[5:]:
        copy.wait()


def picked(values, at):
    chosen = jnp.where(lanes(values.shape) == at, values.astype(jnp.float32), 0.0)
    return jnp.sum(chosen, axis=1, keepdims=True).astype(jnp.int32)


def split(x):
    high = x.astype(jnp.bfloat16)
    return high, (x - high.astype(jnp.float32)).astype(jnp.bfloat16)


def product(x, table, dims):
    x_high, x_low = split(x)
    table_high, table_low = table
    dot = functools.partial(lax.dot_general, dimension_numbers=(dims, ((), ())), preferred_element_type=jnp.float32)
    return dot(x_high, table_high) + (dot(x_low, table_high) + dot(x_high, table_low))


def projected(strips, table_ref):
    return product(jnp.concatenate(strips, 1), (table_ref[0], table_ref[1]), ((1,), (0,)))


def synthesised(modes, synth_ref, count):
    return product(modes, (synth_ref[0, :count], synth_ref[1, :count]), ((1,), (1,)))


def synth_kernel(
    blades_ref, jacobians_ref, giles_re_ref, giles_im_ref, orders_ref, cells_ref, synth_ref, rows_ref, sums_ref,
    *, row_count, place_count, components, pitch, length, axial,
):
    row, place = lax.axis_index("row"), lax.axis_index("pitch")
    face = jnp.minimum(row, row_count - 2)
    for b in range(components):
        for c in range(components):
            entries = jacobians_ref[b, c]
            for d in range(6):
                at = (b * components + c) * 6 + d
                rows_ref[pl.ds(at, 1), :] = jnp.broadcast_to(entries[:, d:d + 1], (1, pitch))
    modes = orders_ref.shape[2]
    orders = orders_ref[face]
    tag = BASE * orders[0:1] + orders[1:2]
    component, mode, _ = column(rows((pitch, modes)))
    same = (jnp.abs(tag) == mode) & (component < components)
    plain = jnp.where(same, 1.0, 0.0)
    signed = jnp.where(tag < 0, -plain, plain)
    dims = (((1,), (1,)), ((), ()))
    for n, ref in enumerate((giles_re_ref, giles_im_ref)):
        for b in range(components):
            for c in range(components):
                sums_ref[n, pl.ds(b * components + c, 1), :] = ref[b, c, pl.ds(face, 1), :]
    sums_re = lax.dot_general(sums_ref[0], plain, dims, precision=EXACT, preferred_element_type=jnp.float32)
    sums_im = lax.dot_general(sums_ref[1], signed, dims, precision=EXACT, preferred_element_type=jnp.float32)
    component, mode, sine = column(lanes(sums_re.shape))
    scale = 2.0 / length
    with_cos = jnp.where(sine, sums_im, sums_re) * scale
    with_sin = jnp.where(sine, sums_re, -sums_im) * scale
    component = component[0:1]

    def chunk(at):
        start = pl.multiple_of(lax.rem(place + at + place_count, place_count) * pitch, pitch)
        return cells_ref[:, pl.ds(start, pitch)]

    own = chunk(0)
    lane = lanes((1, pitch))
    first = (axial - 1) * SEGMENT_LANES
    edge = jnp.where(lane < first + EDGE, pltpu.roll(chunk(-1), (first + EDGE) % pitch, 1), pltpu.roll(own, (first + EDGE) % pitch, 1))
    edge = jnp.where(lane < first + 2 * EDGE, edge, pltpu.roll(own, (first + 3 * EDGE) % pitch, 1))
    edge = jnp.where(lane < first + 3 * EDGE, edge, pltpu.roll(chunk(1), (first + 3 * EDGE) % pitch, 1))

    def upright(cells):
        wide = jnp.broadcast_to(cells.astype(jnp.float32), (pitch, pitch))
        return jnp.transpose(wide).astype(jnp.int32)

    edge_cells = upright(edge)[first:first + SEGMENT_LANES]
    at_cells = jnp.concatenate([upright(own), edge_cells], 0)
    _, mode, _ = column(lanes(at_cells.shape))
    blades = [picked(blades_ref[...], face + n) for n in range(2)]
    cos_table, sin_table = waves(mode_number(mode, blades) * at_cells, length)
    for c in range(components):
        row_cos = jnp.zeros((1, pitch), jnp.float32)
        row_sin = jnp.zeros((1, pitch), jnp.float32)
        for b in range(components):
            at = b * components + c
            row_cos = jnp.where(component == b, with_cos[at:at + 1], row_cos)
            row_sin = jnp.where(component == b, with_sin[at:at + 1], row_sin)
        part = row_cos * cos_table + row_sin * sin_table
        for n, value in enumerate(split(part)):
            synth_ref[n, pl.ds(c * pitch, pitch), :] = value[:pitch]
            synth_ref[n, pl.ds(components * pitch + c * SEGMENT_LANES, SEGMENT_LANES), :] = value[pitch:]
    used = components * (pitch + SEGMENT_LANES)
    rest = synth_ref.shape[1] - used
    if rest:
        synth_ref[:, pl.ds(used, rest), :] = jnp.zeros((2, rest, pitch), jnp.bfloat16)


def jacobian(jac_ref, components, b, c, d):
    return jac_ref[pl.ds((b * components + c) * 6 + d, 1), :]


def mixed(jac_ref, source, couplings, neighbours):
    total = list(source)
    jac = functools.partial(jacobian, jac_ref, len(total))
    for d, neighbour in enumerate(neighbours):
        if neighbour is None:
            continue
        for c in range(len(total)):
            term = jac(0, c, d) * neighbour[0]
            for b in range(1, len(total)):
                term = term + jac(b, c, d) * neighbour[b]
            total[c] = total[c] + couplings[d] * term
    return total


def layer_update(jac_ref, state_ref, edge_ref, coef_ref, t, a, height):
    _, components, axial, wide, pitch = state_ref.shape
    lane = lanes((height, pitch))
    start = a * SEGMENT_LANES
    own = [state_ref[t, c, a] for c in range(components)]
    above = [state_ref[t, c, a + 1, :height] for c in range(components)] if a < axial - 1 else None
    below = [state_ref[t, c, a - 1, :height] for c in range(components)] if a else None
    edge = [edge_ref[t, c, :height] for c in range(components)]
    span_next = [pltpu.roll(x, wide - 1, 0)[:height] for x in own]
    span_prev = [pltpu.roll(x, 1, 0)[:height] for x in own]
    own = [x[:height] for x in own]
    to_end = (pitch - 1 - (start + 3 * EDGE)) % pitch
    to_begin = (pitch - (start + EDGE - 1)) % pitch
    pitch_next = [
        jnp.where(lane == pitch - 1, pltpu.roll(e, to_end, 1), pltpu.roll(x, pitch - 1, 1))
        for e, x in zip(edge, own)
    ]
    pitch_prev = [
        jnp.where(lane == 0, pltpu.roll(e, to_begin, 1), pltpu.roll(x, 1, 1))
        for e, x in zip(edge, own)
    ]
    source = [coef_ref[c, a, :height] for c in range(components)]
    couplings = [coef_ref[components + d, a, :height] for d in range(6)]
    return mixed(jac_ref, source, couplings, (above, below, span_next, span_prev, pitch_next, pitch_prev))


def edge_update(jac_ref, edge_ref, edge_coef_ref, t, axial):
    components, wide, pitch = edge_ref.shape[1:]
    lane = lanes((wide, pitch))
    own = [edge_ref[t, c] for c in range(components)]
    above = [jnp.where(lane < (axial - 1) * SEGMENT_LANES, pltpu.roll(x, pitch - SEGMENT_LANES, 1), 0.0) for x in own]
    below = [jnp.where(lane >= SEGMENT_LANES, pltpu.roll(x, SEGMENT_LANES, 1), 0.0) for x in own]
    span_next = [pltpu.roll(x, wide - 1, 0) for x in own]
    span_prev = [pltpu.roll(x, 1, 0) for x in own]
    pitch_next = [pltpu.roll(x, pitch - 1, 1) for x in own]
    pitch_prev = [pltpu.roll(x, 1, 1) for x in own]
    source = [edge_coef_ref[c] for c in range(components)]
    couplings = [edge_coef_ref[components + d] for d in range(6)]
    return mixed(jac_ref, source, couplings, (above, below, span_next, span_prev, pitch_next, pitch_prev))


def edge_boundary(field, c, components, pitch, axial):
    at = components * pitch + c * SEGMENT_LANES
    tile = field[:, (at // pitch) * pitch:(at // pitch + 1) * pitch]
    return pltpu.roll(tile, ((axial - 1) * SEGMENT_LANES - at % pitch) % pitch, 1)


def advance(refs, t, a, height=None):
    state_ref = refs[1]
    height = height or state_ref.shape[3]
    for c, value in enumerate(layer_update(*refs, t, a, height)):
        state_ref[t + 1, c, a, :height] = value


def first_kernel(
    jac_ref, state_in_ref, coef_in_ref, inv_in_ref, edges_ref, span_ref, inner_ref, outer_ref, table_ref,
    coef_ref, inv_ref, edge_coef_ref, state_ref, edge_ref, modes_ref, part_ref, *, groups,
):
    _, components, axial, wide, pitch = state_ref.shape
    span = wide - EDGE
    side = lax.axis_index("span")
    fields = 2 * components + 6
    line = rows((EDGE, pitch))
    keep_half = jnp.where(side == 0, line, EDGE - 1 - line) < HALF
    fifth = jnp.where(side == 0, HALF, HALF - 1)
    from_low, from_high = half_rows(1 - side)
    pairs = -(-(fields * axial + 1) // 2)

    def ghost(n):
        value = pltpu.roll(span_ref[n // 2], from_high if n % 2 else from_low, 0)
        value = jnp.where(keep_half, value, 0.0)
        if n < components * axial:
            extra = pltpu.roll(span_ref[pairs + n // EDGE], lax.rem(fifth + EDGE - n % EDGE, EDGE), 0)
            value = jnp.where(line == fifth, extra, value)
        return value

    even = lax.rem(lax.axis_index("pitch"), 2) == 0

    def group(ref, g):
        corner = ref[pl.ds(groups * span + g * EDGE, EDGE), :]
        return jnp.concatenate([ref[pl.ds(g * span, span), :], corner], 0)

    halves = [(group(inner_ref, g), group(outer_ref, g)) for g in range(groups)]
    from_left = [jnp.where(even, outer, inner) for inner, outer in halves]
    from_right = [jnp.where(even, inner, outer) for inner, outer in halves]
    near, far = slots(fields + 1, components)
    keep_five = keep_half | (line == fifth)
    for f in range(fields + 1):
        if f < fields:
            layers = [ghost(f * axial + a) for a in range(axial)]
        else:
            layers = [jnp.zeros((EDGE, pitch), jnp.float32)] * (axial - 1) + [ghost(fields * axial)]
        if f < components:
            for a in range(axial):
                state_ref[0, f, a, span:] = layers[a]
        elif f < fields:
            for a in range(axial):
                coef_ref[f - components, a, span:] = layers[a]
        else:
            inv_ref[span:] = layers[-1]
        g, at = near[f]
        value = jnp.concatenate([edges_ref[f], to_edges(layers, pitch)], 0)
        lane = lanes((wide, pitch)) % SEGMENT_LANES
        value = jnp.where((lane >= HALF) & (lane < EDGE), pltpu.roll(from_left[g], (HALF - at) % pitch, 1), value)
        value = jnp.where(
            (lane >= 3 * EDGE) & (lane < 3 * EDGE + HALF),
            pltpu.roll(from_right[g], (3 * EDGE - at) % pitch, 1), value,
        )
        if f < components:
            g, at = far[f]
            value = jnp.where(lane == HALF - 1, pltpu.roll(from_left[g], (HALF - 1 - at) % pitch, 1), value)
            value = jnp.where(
                lane == 3 * EDGE + HALF, pltpu.roll(from_right[g], (3 * EDGE + HALF - at) % pitch, 1), value,
            )
        target, at = (edge_ref.at[0], f) if f < components else (edge_coef_ref, f - components)
        target[at, :span] = value[:span]
        target[at, span:] = jnp.where(keep_five if f < components else keep_half, value[span:], 0.0)
    refs = (jac_ref, state_ref, edge_ref, coef_ref)
    for t in range(axial):
        for a in range(axial - t):
            advance(refs, t, a)
        if t < axial - 1:
            for c, value in enumerate(edge_update(jac_ref, edge_ref, edge_coef_ref, t, axial)):
                edge_ref[t + 1, c] = value
    strips = [
        jnp.concatenate([state_ref[t, c, 0] for t in range(1, axial)] + [state_ref[axial, c, 0, :span]], 0)
        for c in range(components)
    ]
    total = projected(strips, table_ref)
    ghosts = jnp.zeros((EDGE, pitch), jnp.float32)
    for t in range(1, axial):
        part = total[(t - 1) * wide:t * wide]
        modes_ref[pl.ds((t - 1) * span, span), :] = part[:span]
        keep, to_packed, _ = ghost_rows(side, t, axial)
        ghosts = jnp.where(keep, pltpu.roll(part[span:], to_packed, 0), ghosts)
    modes_ref[pl.ds((axial - 1) * span, EDGE), :] = ghosts
    part_ref[...] = total[(axial - 1) * wide:]


def ghost_rows(side, t, axial):
    line = rows((EDGE, 1))
    distance = jnp.where(side == 0, line, EDGE - 1 - line)
    start = sum(axial - n for n in range(1, t))
    to_packed = jnp.where(side == 0, start, (EDGE - start) % EDGE)
    from_packed = jnp.where(side == 0, (EDGE - start) % EDGE, start)
    return (distance >= start) & (distance < start + axial - t), to_packed, from_packed


def along_axis(jac_ref, coef_ref, delta, a, height):
    components = len(delta)
    out = []
    for c in range(components):
        term = jacobian(jac_ref, components, 0, c, 0) * delta[0]
        for b in range(1, components):
            term = term + jacobian(jac_ref, components, b, c, 0) * delta[b]
        out.append(coef_ref[components, a, :height] * term)
    return out


def late_kernel(
    jac_ref, coef_ref, inv_ref, part_ref, more_ref, modes_a_ref, modes_b_ref, synth_ref, table_ref, modes_ref,
):
    span, pitch = part_ref.shape
    components, axial = coef_ref.shape[0] - 6, coef_ref.shape[1]
    field = synthesised(modes_a_ref[EDGE:] + modes_b_ref[EDGE:], synth_ref, components * pitch)
    delta = [inv_ref[:span] * field[:, c * pitch:(c + 1) * pitch] for c in range(components)]
    for a in range(axial - 2, -1, -1):
        delta = along_axis(jac_ref, coef_ref, delta, a, span)
    before = more_ref.shape[0]
    modes_ref[:before] = more_ref[...]
    modes_ref[before:] = part_ref[...] + projected(delta, table_ref)


def between_kernel(
    jac_ref, coef_ref, inv_ref, edge_coef_ref, state_in_ref, edge_in_ref, modes_a_ref, modes_b_ref, synth_ref, more_ref,
    state_ref, edge_ref, sent_ref,
):
    sent_ref[...] = more_ref[...]
    components, axial = state_ref.shape[1], state_ref.shape[2]
    wide, pitch = state_ref.shape[3:]
    modes = modes_a_ref[...] + modes_b_ref[...]
    field = synthesised(jnp.concatenate([modes[EDGE:], modes[:EDGE]], 0), synth_ref, synth_ref.shape[1])
    delta = [inv_ref[...] * field[:, c * pitch:(c + 1) * pitch] for c in range(components)]
    for t in range(1, axial + 1):
        for c in range(components):
            state_ref[t, c, axial - t] += delta[c]
        if t < axial:
            delta = along_axis(jac_ref, coef_ref, delta, axial - 1 - t, wide)
    for c in range(components):
        edge_ref[1, c] += edge_coef_ref[components + 6] * edge_boundary(field, c, components, pitch, axial)
    diagonal_sweeps(jac_ref, state_ref, edge_ref, coef_ref, edge_coef_ref, 1, axial // 2 + 1)


def beside_kernel(jac_ref, coef_ref, edge_coef_ref, state_in_ref, edge_in_ref, state_ref, edge_ref):
    axial, span = state_ref.shape[2], state_ref.shape[3] - EDGE
    diagonal_sweeps(jac_ref, state_ref, edge_ref, coef_ref, edge_coef_ref, axial // 2 + 1, axial)
    advance((jac_ref, state_ref, edge_ref, coef_ref), axial, 0, span)


def diagonal_sweeps(jac_ref, state_ref, edge_ref, coef_ref, edge_coef_ref, first, last):
    axial = state_ref.shape[2]
    for t in range(first, last):
        advance((jac_ref, state_ref, edge_ref, coef_ref), t, axial - t)
        for c, value in enumerate(edge_update(jac_ref, edge_ref, edge_coef_ref, t, axial)):
            edge_ref[t + 1, c] = value


def second_kernel(
    jac_ref, coef_ref, inv_ref, edge_coef_ref, state_in_ref, edge_in_ref, more_a_ref, more_b_ref, synth_ref,
    state_ref, edge_ref, out_ref, bound_ref,
):
    components, axial, span, pitch = out_ref.shape
    wide = span + EDGE
    side = lax.axis_index("span")
    more = more_a_ref[...] + more_b_ref[...]
    start = (axial - 1) * span
    parts = []
    for t in range(1, axial):
        _, _, from_packed = ghost_rows(side, t, axial)
        parts += [more[(t - 1) * span:t * span], pltpu.roll(more[start:start + EDGE], from_packed, 0)]
    field = synthesised(jnp.concatenate(parts + [more[start + EDGE:]], 0), synth_ref, synth_ref.shape[1])
    for t in range(1, axial):
        part = field[(t - 1) * wide:t * wide]
        for c in range(components):
            bound_ref[t, c] = inv_ref[...] * part[:, c * pitch:(c + 1) * pitch]
    for c in range(components):
        bound_ref[axial, c, :span] = inv_ref[:span] * field[(axial - 1) * wide:, c * pitch:(c + 1) * pitch]
    delta = [bound_ref[1, c] for c in range(components)]
    for t in range(2, axial + 2):
        height = wide if t <= axial else span
        for c in range(components):
            state_ref[t, c, axial + 1 - t, :height] += delta[c][:height]
        if t < axial + 1:
            delta = along_axis(jac_ref, coef_ref, delta, axial - t, wide)
    for t in range(1, axial):
        if t > 1:
            for c, value in enumerate(edge_update(jac_ref, edge_ref, edge_coef_ref, t, axial)):
                edge_ref[t + 1, c] = value
        part = field[(t - 1) * wide:t * wide]
        for c in range(components):
            edge_ref[t + 1, c] += edge_coef_ref[components + 6] * edge_boundary(part, c, components, pitch, axial)
    refs = (jac_ref, state_ref, edge_ref, coef_ref)

    for t in range(2, axial):
        for a in range(axial + 1 - t, axial):
            advance(refs, t, a)
        for c in range(components):
            state_ref[t + 1, c, axial - 1] += bound_ref[t, c]
    for a in range(1, axial):
        for c, value in enumerate(layer_update(*refs, axial, a, span)):
            out_ref[c, a] = value + bound_ref[axial, c, :span] if a == axial - 1 else value
    for c in range(components):
        out_ref[c, 0] = state_ref[axial + 1, c, 0, :span]


def moved(x, to):
    sizes = [lax.axis_size(name) for name in AXES]
    pairs = []
    for r in range(sizes[0]):
        for s in range(sizes[1]):
            for p in range(sizes[2]):
                target = to(r, s, p)
                if all(0 <= at < size for at, size in zip(target, sizes)):
                    number = lambda at: (at[0] * sizes[1] + at[1]) * sizes[2] + at[2]
                    pairs.append((number((r, s, p)), number(target)))
    return lax.ppermute(x, AXES, pairs)


def struct(*shape):
    return jax.ShapeDtypeStruct(shape, jnp.float32)


def on_device(
    adjoint_start, source, couplings, damping, jacobians, giles_real, giles_imag, blades, mode_orders, cell_map,
):
    components, axial, span, pitch = adjoint_start.shape
    row_count, span_count, place_count = (lax.axis_size(name) for name in AXES)
    length = pitch * place_count
    assert sum(axial - t for t in range(1, axial)) <= EDGE
    assert components == COMPONENTS and components * WAVES <= pitch
    assert axial == ITERS - 1 and ITERS <= EDGE and axial * SEGMENT_LANES == pitch
    assert span_count == 2 and place_count > 1 and place_count & (place_count - 1) == 0
    wide = span + EDGE
    fields = 2 * components + 6
    groups = slots(fields + 1, components)[1][-1][0] + 1
    pairs = -(-(fields * axial + 1) // 2)
    span_tiles = pairs + -(-components * axial // EDGE)
    vmem = pl.BlockSpec(memory_space=pltpu.VMEM)
    hbm = pl.BlockSpec(memory_space=pltpu.HBM)

    def in_hbm(x):
        return pltpu.with_memory_space_constraint(x, pltpu.HBM)

    def call(kernel, name, outs, ins, aliases=None, scratch=(), limit=40 * MIB, **fixed):
        specs = [spec for spec, _ in ins]
        return pl.pallas_call(
            functools.partial(kernel, **fixed),
            out_shape=outs,
            in_specs=specs,
            out_specs=jax.tree.map(lambda _: vmem, outs),
            scratch_shapes=scratch,
            input_output_aliases=aliases or {},
            compiler_params=params(limit),
            name=name,
        )(*[value for _, value in ins])

    tables = (
        jacobians.transpose(2, 3, 0, 1), giles_real.transpose(2, 3, 0, 1), giles_imag.transpose(2, 3, 0, 1),
        mode_orders.transpose(0, 2, 1), cell_map,
    )
    blades = blades.reshape(1, -1)
    corner_rows = groups * EDGE
    state_shape = struct(axial + 2, components, axial, wide, pitch)
    state, coef, inv, edges, span_out, small, inner, outer, table, blades, *tables = call(
        pack_kernel, "pack",
        (
            state_shape, struct(components + 6, axial, wide, pitch), struct(wide, pitch),
            struct(fields + 1, span, pitch), struct(span_tiles, EDGE, pitch), struct(2 * corner_rows + EDGE, pitch),
            struct(groups * span + corner_rows + EDGE + span, pitch), struct(groups * span + corner_rows, pitch),
            jax.ShapeDtypeStruct((2, components * pitch, pitch), jnp.bfloat16), *(jax.ShapeDtypeStruct(x.shape, x.dtype) for x in (blades, *tables)),
        ),
        [(hbm, in_hbm(x)) for x in (adjoint_start, source, couplings, damping, blades, *tables)],
        scratch=[
            pltpu.VMEM(source.shape, jnp.float32), pltpu.VMEM(couplings.shape, jnp.float32),
            pltpu.VMEM(damping.shape, jnp.float32), pltpu.SemaphoreType.DMA((5 + len(tables),)),
        ],
        groups=groups, length=length,
    )
    steps = [1 << n for n in range(place_count.bit_length() - 2)]
    last_step = place_count // 2

    def near(x):
        return moved(x, lambda r, s, p: (r - 1, s, p))

    def far(x):
        return moved(x, lambda r, s, p: (r - 1, s, p ^ last_step))

    small = moved(small, lambda r, s, p: (r, 1 - s, p))
    from_span = moved(span_out, lambda r, s, p: (r, 1 - s, p))
    inner = lax.dynamic_update_slice(inner, small[:corner_rows + EDGE], (groups * span, 0))
    outer = lax.dynamic_update_slice(outer, small[corner_rows + EDGE:], (groups * span, 0))
    modes = inner[groups * span + corner_rows:]
    outer = moved(outer, lambda r, s, p: (r, s, (p - 1 + 2 * (p % 2)) % place_count))
    inner = moved(inner, lambda r, s, p: (r, s, p ^ 1))

    modes = modes + inner[groups * span + corner_rows:] if steps else modes
    for step in steps[1:]:
        modes = modes + moved(modes, lambda r, s, p: (r, s, p ^ step))
    modes_b = far(modes)
    modes_a = near(modes)

    synth, jac = call(
        synth_kernel, "synth",
        (
            jax.ShapeDtypeStruct(
                (2, -(-components * (pitch + SEGMENT_LANES) // pitch) * pitch, pitch), jnp.bfloat16
            ),
            struct(-(-6 * components * components // EDGE) * EDGE, pitch),
        ),
        [(vmem, x) for x in (blades, *tables)],
        scratch=[pltpu.VMEM((2, components * components, mode_orders.shape[1]), jnp.float32)],
        row_count=row_count, place_count=place_count, components=components, pitch=pitch, length=length, axial=axial,
    )
    edge_shape = struct(axial + 1, components, wide, pitch)
    coef, inv, edge_coef, state, edge, more, part = call(
        first_kernel, "first_sweeps",
        (
            struct(components + 6, axial, wide, pitch), struct(wide, pitch), struct(components + 7, wide, pitch),
            state_shape, edge_shape,
            struct((axial - 1) * span + EDGE, pitch), struct(span, pitch),
        ),
        [(vmem, jac)] + [(vmem, x) for x in (state, coef, inv, edges, from_span, inner, outer, table)],
        aliases={1: 3, 2: 0, 3: 1},
        groups=groups,
    )

    more_shape = struct(axial * span + EDGE, pitch)
    more = call(
        late_kernel, "late_modes", more_shape,
        [(vmem, x) for x in (jac, coef, inv, part, more, modes_a, modes_b, synth, table)],
    )
    state, edge, sent = call(
        between_kernel, "between_sweeps", (state_shape, edge_shape, more_shape),
        [(vmem, x) for x in (jac, coef, inv, edge_coef, state, edge, modes_a, modes_b, synth, more)],
        aliases={4: 0, 5: 1},
    )
    state, edge = call(
        beside_kernel, "beside_sweeps", (state_shape, edge_shape),
        [(vmem, x) for x in (jac, coef, edge_coef, state, edge)],
        aliases={3: 0, 4: 1},
    )
    for step in steps:
        got = moved(more, lambda r, s, p: (r, s, p ^ step))
        more, sent = sent + got, sent + got
    more_b = far(more)
    more_a = near(more)
    return call(
        second_kernel, "second_sweeps", (state_shape, edge_shape, struct(components, axial, span, pitch)),
        [(vmem, x) for x in (jac, coef, inv, edge_coef, state, edge, more_a, more_b, synth)],
        aliases={4: 0, 5: 1},
        scratch=[pltpu.VMEM((axial + 1, components, wide, pitch), jnp.float32)],
    )[2]


def solution(mesh):
    placed = (
        P(None, "row", "span", "pitch"),
        P(None, "row", "span", "pitch"),
        P(None, "row", "span", "pitch"),
        P("row", "span", "pitch"),
        P("row", None, None, None),
        P(),
        P(),
        P(),
        P(),
        P("row", None),
    )
    return jax.shard_map(
        on_device,
        mesh=mesh,
        in_specs=placed,
        out_specs=P(None, "row", "span", "pitch"),
        check_vma=False,
    )
```

```python
import functools
import math

import jax
import jax.numpy as jnp
from jax import lax
from jax.experimental import pallas as pl
from jax.experimental.pallas import tpu as pltpu
from jax.sharding import PartitionSpec as P

ITERS = 5
AXES = ("row", "span", "pitch")

ORDER_MAX = 2
BASE = 2 * ORDER_MAX + 1
COSINES = (BASE * BASE + 1) // 2
WAVES = 2 * COSINES - 1
COMPONENTS = 5
EDGE = 8
HALF = EDGE // 2
SEGMENT_LANES = 4 * EDGE
EXACT = lax.Precision.HIGHEST
MIB = 1024 * 1024


def params(limit):
    return pltpu.CompilerParams(vmem_limit_bytes=limit)


def lanes(shape):
    return lax.broadcasted_iota(jnp.int32, shape, len(shape) - 1)


def rows(shape):
    return lax.broadcasted_iota(jnp.int32, shape, len(shape) - 2)


def column(j):
    component = (j * 41) >> 10
    wave = j - WAVES * component
    sine = wave >= COSINES
    return component, jnp.where(sine, wave - (COSINES - 1), wave), sine


def mode_number(mode, blades):
    high = ((mode + ORDER_MAX) * 13) >> 6
    low = mode - BASE * high
    return high * blades[0] + low * blades[1]


def waves(products, length):
    if length & (length - 1) == 0:
        phase = products & (length - 1)
    else:
        phase = jnp.mod(products, length)
    turn = phase.astype(jnp.float32) * (1.0 / length)
    quarter = jnp.floor(4.0 * turn + 0.5)
    x = (turn - 0.25 * quarter) * (2.0 * math.pi)
    y = x * x
    sine = x * (1.0 + y * (-1.0 / 6 + y * (1.0 / 120 + y * (-1.0 / 5040 + y * (1.0 / 362880)))))
    cosine = 1.0 + y * (-0.5 + y * (1.0 / 24 + y * (-1.0 / 720 + y * (1.0 / 40320 - y * (1.0 / 3628800)))))
    quarter = quarter.astype(jnp.int32) & 3
    odd = (quarter & 1) == 1
    cos_out = jnp.where(odd, sine, cosine)
    sin_out = jnp.where(odd, cosine, sine)
    cos_out = jnp.where((quarter == 1) | (quarter == 2), -cos_out, cos_out)
    sin_out = jnp.where(quarter >= 2, -sin_out, sin_out)
    return cos_out, sin_out


def to_edges(layers, pitch):
    lane = lanes(layers[-1].shape)
    block = jnp.zeros_like(layers[-1])
    for a, layer in enumerate(layers):
        if layer is None:
            continue
        start = a * SEGMENT_LANES
        first = pltpu.roll(layer, (start + EDGE) % pitch, layer.ndim - 1)
        last = pltpu.roll(layer, (start + 3 * EDGE) % pitch, layer.ndim - 1)
        block = jnp.where((lane >= start + EDGE) & (lane < start + 2 * EDGE), first, block)
        block = jnp.where((lane >= start + 2 * EDGE) & (lane < start + 3 * EDGE), last, block)
    return block


def half_rows(side):
    return jnp.where(side == 0, EDGE // 2, 0), jnp.where(side == 0, 0, EDGE // 2)


def slots(fields, components):
    per_group = SEGMENT_LANES // HALF
    near = [(f // per_group, f % per_group * HALF) for f in range(fields)]
    group, lane = near[-1]
    far = [(group, lane + HALF + c) for c in range(components)]
    return near, far


def packed_edges(blocks, place, components):
    near, far = slots(len(blocks), components)
    pitch = blocks[0].shape[1]
    lane = lanes(blocks[0].shape) % SEGMENT_LANES
    sides = []
    for near_at, far_at in ((3 * EDGE - HALF, 3 * EDGE - HALF - 1), (EDGE, EDGE + HALF)):
        packed = [jnp.zeros_like(blocks[0]) for _ in range(far[-1][0] + 1)]
        for f, (g, to) in enumerate(near):
            value = pltpu.roll(blocks[f], (to - near_at) % pitch, 1)
            packed[g] = jnp.where((lane >= to) & (lane < to + HALF), value, packed[g])
        for f, (g, to) in enumerate(far):
            packed[g] = jnp.where(lane == to, pltpu.roll(blocks[f], (to - far_at) % pitch, 1), packed[g])
        sides.append(packed)
    even = lax.rem(place, 2) == 0
    inner = [jnp.where(even, right, left) for right, left in zip(*sides)]
    outer = [jnp.where(even, left, right) for right, left in zip(*sides)]
    return inner, outer


def edge_blocks(state_ref, coef_ref, inv_ref, at):
    components, axial, pitch = state_ref.shape[1], state_ref.shape[2], state_ref.shape[4]
    blocks = [to_edges([state_ref[0, c, a, at, :] for a in range(axial)], pitch) for c in range(components)]
    blocks += [to_edges([coef_ref[f, a, at, :] for a in range(axial)], pitch) for f in range(components + 6)]
    return blocks + [to_edges([None] * (axial - 1) + [inv_ref[at, :]], pitch)]


def start_kernel(
    adjoint_hbm, source_hbm, couplings_hbm, damping_hbm, blades_hbm, *refs, groups, length,
):
    state_ref, coef_ref, inv_ref, small_ref, modes_ref, table_ref, blades_ref = refs[5:12]
    source_ref, couplings_ref, damping_ref, sems = refs[17:]
    components, axial, span, pitch = source_ref.shape
    adjoint_ref = state_ref.at[0, :, :, pl.ds(0, span), :]
    copies = [
        pltpu.make_async_copy(src, dst, sems.at[n])
        for n, (src, dst) in enumerate((
            (couplings_hbm, couplings_ref), (damping_hbm, damping_ref), (source_hbm, source_ref),
            (adjoint_hbm, adjoint_ref), (blades_hbm, blades_ref), *zip(refs[:5], refs[12:17]),
        ))
    ]
    for copy in copies:
        copy.start()
    row, side, place = (lax.axis_index(name) for name in AXES)
    copies[4].wait()
    face = jnp.maximum(row - 1, 0)
    component, mode, sine = column(lanes((pitch, pitch)))
    number = mode_number(mode, [picked(blades_ref[...], face + n) for n in range(2)])
    cos_table, sin_table = waves(number * (place * pitch + rows((pitch, pitch))), length)
    table = jnp.where(component < components, jnp.where(sine, sin_table, cos_table), 0.0)
    for c in range(components):
        for n, value in enumerate(split(jnp.where(component == c, table, 0.0))):
            table_ref[n, pl.ds(c * pitch, pitch), :] = value
    copies[0].wait()
    copies[1].wait()
    diag = damping_ref[...]
    for d in range(6):
        diag = diag + couplings_ref[d]
    inverse = 1.0 / diag
    for d in range(6):
        coef_ref[components + d, :, :span] = couplings_ref[d] * inverse
    inv_ref[:span] = inverse[axial - 1]
    copies[2].wait()
    for c in range(components):
        coef_ref[c, :, :span] = source_ref[c] * inverse
    copies[3].wait()
    edge_row = pl.multiple_of(jnp.where(side == 0, span - EDGE, 0), EDGE)
    blocks = edge_blocks(state_ref, coef_ref, inv_ref, pl.ds(edge_row, EDGE))
    for n, packed in enumerate(packed_edges(blocks, place, components)):
        for g, value in enumerate(packed):
            small_ref[pl.ds((n * groups + g) * EDGE, EDGE), :] = value
    modes_ref[:span] = projected([adjoint_ref[c, 0] for c in range(components)], table_ref)
    small_ref[pl.ds(2 * groups * EDGE, EDGE), :] = modes_ref[pl.ds(edge_row, EDGE), :]
    for copy in copies[5:]:
        copy.wait()


def pack_kernel(state_ref, coef_ref, inv_ref, edges_ref, span_ref, inner_ref, outer_ref):
    _, components, axial, wide, pitch = state_ref.shape
    span = wide - EDGE
    side, place = lax.axis_index("span"), lax.axis_index("pitch")
    blocks = edge_blocks(state_ref, coef_ref, inv_ref, pl.ds(0, span))
    for f, block in enumerate(blocks):
        edges_ref[f] = block
    for out_ref, packed in zip((inner_ref, outer_ref), packed_edges(blocks, place, components)):
        for g, value in enumerate(packed):
            out_ref[pl.ds(g * span, span), :] = value

    edge_row = pl.multiple_of(jnp.where(side == 0, span - EDGE, 0), EDGE)
    to_low, to_high = half_rows(side)
    line = rows((EDGE, pitch))
    tiles = [state_ref[0, c, a, pl.ds(edge_row, EDGE), :] for c in range(components) for a in range(axial)]
    tiles += [coef_ref[f, a, pl.ds(edge_row, EDGE), :] for f in range(components + 6) for a in range(axial)]
    tiles += [inv_ref[pl.ds(edge_row, EDGE), :]]
    pairs = -(-len(tiles) // 2)
    for n in range(pairs):
        value = pltpu.roll(tiles[2 * n], to_low, 0)
        if 2 * n + 1 < len(tiles):
            value = jnp.where(line < HALF, value, pltpu.roll(tiles[2 * n + 1], to_high, 0))
        span_ref[n] = value
    fifth = jnp.where(side == 0, HALF - 1, HALF)
    for n in range(span_ref.shape[0] - pairs):
        value = jnp.zeros((EDGE, pitch), jnp.float32)
        for k in range(min(EDGE, components * axial - n * EDGE)):
            value = jnp.where(line == k, pltpu.roll(tiles[n * EDGE + k], lax.rem(k + EDGE - fifth, EDGE), 0), value)
        span_ref[pairs + n] = value


def picked(values, at):
    chosen = jnp.where(lanes(values.shape) == at, values.astype(jnp.float32), 0.0)
    return jnp.sum(chosen, axis=1, keepdims=True).astype(jnp.int32)


def split(x):
    high = x.astype(jnp.bfloat16)
    return high, (x - high.astype(jnp.float32)).astype(jnp.bfloat16)


def product(x, table, dims):
    x_high, x_low = split(x)
    table_high, table_low = table
    dot = functools.partial(lax.dot_general, dimension_numbers=(dims, ((), ())), preferred_element_type=jnp.float32)
    return dot(x_high, table_high) + (dot(x_low, table_high) + dot(x_high, table_low))


def projected(strips, table_ref):
    return product(jnp.concatenate(strips, 1), (table_ref[0], table_ref[1]), ((1,), (0,)))


def synthesised(modes, synth_ref, count):
    return product(modes, (synth_ref[0, :count], synth_ref[1, :count]), ((1,), (1,)))


def synth_kernel(
    blades_ref, jacobians_ref, giles_re_ref, giles_im_ref, orders_ref, cells_ref, synth_ref, rows_ref, sums_ref,
    *, row_count, place_count, components, pitch, length, axial,
):
    row, place = lax.axis_index("row"), lax.axis_index("pitch")
    face = jnp.minimum(row, row_count - 2)
    for b in range(components):
        for c in range(components):
            entries = jacobians_ref[b, c]
            for d in range(6):
                at = (b * components + c) * 6 + d
                rows_ref[pl.ds(at, 1), :] = jnp.broadcast_to(entries[:, d:d + 1], (1, pitch))
    modes = orders_ref.shape[2]
    orders = orders_ref[face]
    tag = BASE * orders[0:1] + orders[1:2]
    component, mode, _ = column(rows((pitch, modes)))
    same = (jnp.abs(tag) == mode) & (component < components)
    plain = jnp.where(same, 1.0, 0.0)
    signed = jnp.where(tag < 0, -plain, plain)
    dims = (((1,), (1,)), ((), ()))
    for n, ref in enumerate((giles_re_ref, giles_im_ref)):
        for b in range(components):
            for c in range(components):
                sums_ref[n, pl.ds(b * components + c, 1), :] = ref[b, c, pl.ds(face, 1), :]
    sums_re = lax.dot_general(sums_ref[0], plain, dims, precision=EXACT, preferred_element_type=jnp.float32)
    sums_im = lax.dot_general(sums_ref[1], signed, dims, precision=EXACT, preferred_element_type=jnp.float32)
    component, mode, sine = column(lanes(sums_re.shape))
    scale = 2.0 / length
    with_cos = jnp.where(sine, sums_im, sums_re) * scale
    with_sin = jnp.where(sine, sums_re, -sums_im) * scale
    component = component[0:1]

    def chunk(at):
        start = pl.multiple_of(lax.rem(place + at + place_count, place_count) * pitch, pitch)
        return cells_ref[:, pl.ds(start, pitch)]

    own = chunk(0)
    lane = lanes((1, pitch))
    first = (axial - 1) * SEGMENT_LANES
    edge = jnp.where(lane < first + EDGE, pltpu.roll(chunk(-1), (first + EDGE) % pitch, 1), pltpu.roll(own, (first + EDGE) % pitch, 1))
    edge = jnp.where(lane < first + 2 * EDGE, edge, pltpu.roll(own, (first + 3 * EDGE) % pitch, 1))
    edge = jnp.where(lane < first + 3 * EDGE, edge, pltpu.roll(chunk(1), (first + 3 * EDGE) % pitch, 1))

    def upright(cells):
        wide = jnp.broadcast_to(cells.astype(jnp.float32), (pitch, pitch))
        return jnp.transpose(wide).astype(jnp.int32)

    edge_cells = upright(edge)[first:first + SEGMENT_LANES]
    at_cells = jnp.concatenate([upright(own), edge_cells], 0)
    _, mode, _ = column(lanes(at_cells.shape))
    blades = [picked(blades_ref[...], face + n) for n in range(2)]
    cos_table, sin_table = waves(mode_number(mode, blades) * at_cells, length)
    for c in range(components):
        row_cos = jnp.zeros((1, pitch), jnp.float32)
        row_sin = jnp.zeros((1, pitch), jnp.float32)
        for b in range(components):
            at = b * components + c
            row_cos = jnp.where(component == b, with_cos[at:at + 1], row_cos)
            row_sin = jnp.where(component == b, with_sin[at:at + 1], row_sin)
        part = row_cos * cos_table + row_sin * sin_table
        for n, value in enumerate(split(part)):
            synth_ref[n, pl.ds(c * pitch, pitch), :] = value[:pitch]
            synth_ref[n, pl.ds(components * pitch + c * SEGMENT_LANES, SEGMENT_LANES), :] = value[pitch:]
    used = components * (pitch + SEGMENT_LANES)
    rest = synth_ref.shape[1] - used
    if rest:
        synth_ref[:, pl.ds(used, rest), :] = jnp.zeros((2, rest, pitch), jnp.bfloat16)


def jacobian(jac_ref, components, b, c, d):
    return jac_ref[pl.ds((b * components + c) * 6 + d, 1), :]


def mixed(jac_ref, source, couplings, neighbours):
    total = list(source)
    jac = functools.partial(jacobian, jac_ref, len(total))
    for d, neighbour in enumerate(neighbours):
        if neighbour is None:
            continue
        for c in range(len(total)):
            term = jac(0, c, d) * neighbour[0]
            for b in range(1, len(total)):
                term = term + jac(b, c, d) * neighbour[b]
            total[c] = total[c] + couplings[d] * term
    return total


def layer_update(jac_ref, state_ref, edge_ref, coef_ref, t, a, height):
    _, components, axial, wide, pitch = state_ref.shape
    lane = lanes((height, pitch))
    start = a * SEGMENT_LANES
    own = [state_ref[t, c, a] for c in range(components)]
    above = [state_ref[t, c, a + 1, :height] for c in range(components)] if a < axial - 1 else None
    below = [state_ref[t, c, a - 1, :height] for c in range(components)] if a else None
    edge = [edge_ref[t, c, :height] for c in range(components)]
    span_next = [pltpu.roll(x, wide - 1, 0)[:height] for x in own]
    span_prev = [pltpu.roll(x, 1, 0)[:height] for x in own]
    own = [x[:height] for x in own]
    to_end = (pitch - 1 - (start + 3 * EDGE)) % pitch
    to_begin = (pitch - (start + EDGE - 1)) % pitch
    pitch_next = [
        jnp.where(lane == pitch - 1, pltpu.roll(e, to_end, 1), pltpu.roll(x, pitch - 1, 1))
        for e, x in zip(edge, own)
    ]
    pitch_prev = [
        jnp.where(lane == 0, pltpu.roll(e, to_begin, 1), pltpu.roll(x, 1, 1))
        for e, x in zip(edge, own)
    ]
    source = [coef_ref[c, a, :height] for c in range(components)]
    couplings = [coef_ref[components + d, a, :height] for d in range(6)]
    return mixed(jac_ref, source, couplings, (above, below, span_next, span_prev, pitch_next, pitch_prev))


def edge_update(jac_ref, edge_ref, edge_coef_ref, t, axial):
    components, wide, pitch = edge_ref.shape[1:]
    lane = lanes((wide, pitch))
    own = [edge_ref[t, c] for c in range(components)]
    above = [jnp.where(lane < (axial - 1) * SEGMENT_LANES, pltpu.roll(x, pitch - SEGMENT_LANES, 1), 0.0) for x in own]
    below = [jnp.where(lane >= SEGMENT_LANES, pltpu.roll(x, SEGMENT_LANES, 1), 0.0) for x in own]
    span_next = [pltpu.roll(x, wide - 1, 0) for x in own]
    span_prev = [pltpu.roll(x, 1, 0) for x in own]
    pitch_next = [pltpu.roll(x, pitch - 1, 1) for x in own]
    pitch_prev = [pltpu.roll(x, 1, 1) for x in own]
    source = [edge_coef_ref[c] for c in range(components)]
    couplings = [edge_coef_ref[components + d] for d in range(6)]
    return mixed(jac_ref, source, couplings, (above, below, span_next, span_prev, pitch_next, pitch_prev))


def edge_boundary(field, c, components, pitch, axial):
    at = components * pitch + c * SEGMENT_LANES
    tile = field[:, (at // pitch) * pitch:(at // pitch + 1) * pitch]
    return pltpu.roll(tile, ((axial - 1) * SEGMENT_LANES - at % pitch) % pitch, 1)


def advance(refs, t, a, height=None):
    state_ref = refs[1]
    height = height or state_ref.shape[3]
    for c, value in enumerate(layer_update(*refs, t, a, height)):
        state_ref[t + 1, c, a, :height] = value


def first_kernel(
    jac_ref, state_in_ref, coef_in_ref, inv_in_ref, edges_ref, span_ref, inner_ref, outer_ref, table_ref,
    coef_ref, inv_ref, edge_coef_ref, state_ref, edge_ref, modes_ref, part_ref, *, groups,
):
    _, components, axial, wide, pitch = state_ref.shape
    span = wide - EDGE
    side = lax.axis_index("span")
    fields = 2 * components + 6
    line = rows((EDGE, pitch))
    keep_half = jnp.where(side == 0, line, EDGE - 1 - line) < HALF
    fifth = jnp.where(side == 0, HALF, HALF - 1)
    from_low, from_high = half_rows(1 - side)
    pairs = -(-(fields * axial + 1) // 2)

    def ghost(n):
        value = pltpu.roll(span_ref[n // 2], from_high if n % 2 else from_low, 0)
        value = jnp.where(keep_half, value, 0.0)
        if n < components * axial:
            extra = pltpu.roll(span_ref[pairs + n // EDGE], lax.rem(fifth + EDGE - n % EDGE, EDGE), 0)
            value = jnp.where(line == fifth, extra, value)
        return value

    even = lax.rem(lax.axis_index("pitch"), 2) == 0

    def group(ref, g):
        corner = ref[pl.ds(groups * span + g * EDGE, EDGE), :]
        return jnp.concatenate([ref[pl.ds(g * span, span), :], corner], 0)

    halves = [(group(inner_ref, g), group(outer_ref, g)) for g in range(groups)]
    from_left = [jnp.where(even, outer, inner) for inner, outer in halves]
    from_right = [jnp.where(even, inner, outer) for inner, outer in halves]
    near, far = slots(fields + 1, components)
    keep_five = keep_half | (line == fifth)
    for f in range(fields + 1):
        if f < fields:
            layers = [ghost(f * axial + a) for a in range(axial)]
        else:
            layers = [jnp.zeros((EDGE, pitch), jnp.float32)] * (axial - 1) + [ghost(fields * axial)]
        if f < components:
            for a in range(axial):
                state_ref[0, f, a, span:] = layers[a]
        elif f < fields:
            for a in range(axial):
                coef_ref[f - components, a, span:] = layers[a]
        else:
            inv_ref[span:] = layers[-1]
        g, at = near[f]
        value = jnp.concatenate([edges_ref[f], to_edges(layers, pitch)], 0)
        lane = lanes((wide, pitch)) % SEGMENT_LANES
        value = jnp.where((lane >= HALF) & (lane < EDGE), pltpu.roll(from_left[g], (HALF - at) % pitch, 1), value)
        value = jnp.where(
            (lane >= 3 * EDGE) & (lane < 3 * EDGE + HALF),
            pltpu.roll(from_right[g], (3 * EDGE - at) % pitch, 1), value,
        )
        if f < components:
            g, at = far[f]
            value = jnp.where(lane == HALF - 1, pltpu.roll(from_left[g], (HALF - 1 - at) % pitch, 1), value)
            value = jnp.where(
                lane == 3 * EDGE + HALF, pltpu.roll(from_right[g], (3 * EDGE + HALF - at) % pitch, 1), value,
            )
        target, at = (edge_ref.at[0], f) if f < components else (edge_coef_ref, f - components)
        target[at, :span] = value[:span]
        target[at, span:] = jnp.where(keep_five if f < components else keep_half, value[span:], 0.0)
    refs = (jac_ref, state_ref, edge_ref, coef_ref)
    for t in range(axial):
        for a in range(axial - t):
            advance(refs, t, a)
        if t < axial - 1:
            for c, value in enumerate(edge_update(jac_ref, edge_ref, edge_coef_ref, t, axial)):
                edge_ref[t + 1, c] = value
    strips = [
        jnp.concatenate([state_ref[t, c, 0] for t in range(1, axial)] + [state_ref[axial, c, 0, :span]], 0)
        for c in range(components)
    ]
    total = projected(strips, table_ref)
    ghosts = jnp.zeros((EDGE, pitch), jnp.float32)
    for t in range(1, axial):
        part = total[(t - 1) * wide:t * wide]
        modes_ref[pl.ds((t - 1) * span, span), :] = part[:span]
        keep, to_packed, _ = ghost_rows(side, t, axial)
        ghosts = jnp.where(keep, pltpu.roll(part[span:], to_packed, 0), ghosts)
    modes_ref[pl.ds((axial - 1) * span, EDGE), :] = ghosts
    part_ref[...] = total[(axial - 1) * wide:]


def ghost_rows(side, t, axial):
    line = rows((EDGE, 1))
    distance = jnp.where(side == 0, line, EDGE - 1 - line)
    start = sum(axial - n for n in range(1, t))
    to_packed = jnp.where(side == 0, start, (EDGE - start) % EDGE)
    from_packed = jnp.where(side == 0, (EDGE - start) % EDGE, start)
    return (distance >= start) & (distance < start + axial - t), to_packed, from_packed


def along_axis(jac_ref, coef_ref, delta, a, height):
    components = len(delta)
    out = []
    for c in range(components):
        term = jacobian(jac_ref, components, 0, c, 0) * delta[0]
        for b in range(1, components):
            term = term + jacobian(jac_ref, components, b, c, 0) * delta[b]
        out.append(coef_ref[components, a, :height] * term)
    return out


def late_kernel(
    jac_ref, coef_ref, inv_ref, part_ref, more_ref, modes_a_ref, modes_b_ref, synth_ref, table_ref, modes_ref,
):
    span, pitch = part_ref.shape
    components, axial = coef_ref.shape[0] - 6, coef_ref.shape[1]
    field = synthesised(modes_a_ref[:span] + modes_b_ref[:span], synth_ref, components * pitch)
    delta = [inv_ref[:span] * field[:, c * pitch:(c + 1) * pitch] for c in range(components)]
    for a in range(axial - 2, -1, -1):
        delta = along_axis(jac_ref, coef_ref, delta, a, span)
    before = more_ref.shape[0]
    modes_ref[:before] = more_ref[...]
    modes_ref[before:] = part_ref[...] + projected(delta, table_ref)


def between_kernel(
    jac_ref, coef_ref, inv_ref, edge_coef_ref, state_in_ref, edge_in_ref, modes_a_ref, modes_b_ref, synth_ref, more_ref,
    state_ref, edge_ref, sent_ref,
):
    sent_ref[...] = more_ref[...]
    components, axial = state_ref.shape[1], state_ref.shape[2]
    wide, pitch = state_ref.shape[3:]
    field = synthesised(modes_a_ref[...] + modes_b_ref[...], synth_ref, synth_ref.shape[1])
    delta = [inv_ref[...] * field[:, c * pitch:(c + 1) * pitch] for c in range(components)]
    for t in range(1, axial + 1):
        for c in range(components):
            state_ref[t, c, axial - t] += delta[c]
        if t < axial:
            delta = along_axis(jac_ref, coef_ref, delta, axial - 1 - t, wide)
    for c in range(components):
        edge_ref[1, c] += edge_coef_ref[components + 6] * edge_boundary(field, c, components, pitch, axial)
    diagonal_sweeps(jac_ref, state_ref, edge_ref, coef_ref, edge_coef_ref, 1, axial // 2 + 1)


def beside_kernel(jac_ref, coef_ref, edge_coef_ref, state_in_ref, edge_in_ref, state_ref, edge_ref):
    axial, span = state_ref.shape[2], state_ref.shape[3] - EDGE
    diagonal_sweeps(jac_ref, state_ref, edge_ref, coef_ref, edge_coef_ref, axial // 2 + 1, axial)
    advance((jac_ref, state_ref, edge_ref, coef_ref), axial, 0, span)


def diagonal_sweeps(jac_ref, state_ref, edge_ref, coef_ref, edge_coef_ref, first, last):
    axial = state_ref.shape[2]
    for t in range(first, last):
        advance((jac_ref, state_ref, edge_ref, coef_ref), t, axial - t)
        for c, value in enumerate(edge_update(jac_ref, edge_ref, edge_coef_ref, t, axial)):
            edge_ref[t + 1, c] = value


def second_kernel(
    jac_ref, coef_ref, inv_ref, edge_coef_ref, state_in_ref, edge_in_ref, more_a_ref, more_b_ref, synth_ref,
    state_ref, edge_ref, out_ref, bound_ref,
):
    components, axial, span, pitch = out_ref.shape
    wide = span + EDGE
    side = lax.axis_index("span")
    more = more_a_ref[...] + more_b_ref[...]
    start = (axial - 1) * span
    parts = []
    for t in range(1, axial):
        _, _, from_packed = ghost_rows(side, t, axial)
        parts += [more[(t - 1) * span:t * span], pltpu.roll(more[start:start + EDGE], from_packed, 0)]
    field = synthesised(jnp.concatenate(parts + [more[start + EDGE:]], 0), synth_ref, synth_ref.shape[1])
    for t in range(1, axial):
        part = field[(t - 1) * wide:t * wide]
        for c in range(components):
            bound_ref[t, c] = inv_ref[...] * part[:, c * pitch:(c + 1) * pitch]
    for c in range(components):
        bound_ref[axial, c, :span] = inv_ref[:span] * field[(axial - 1) * wide:, c * pitch:(c + 1) * pitch]
    delta = [bound_ref[1, c] for c in range(components)]
    for t in range(2, axial + 2):
        height = wide if t <= axial else span
        for c in range(components):
            state_ref[t, c, axial + 1 - t, :height] += delta[c][:height]
        if t < axial + 1:
            delta = along_axis(jac_ref, coef_ref, delta, axial - t, wide)
    for t in range(1, axial):
        if t > 1:
            for c, value in enumerate(edge_update(jac_ref, edge_ref, edge_coef_ref, t, axial)):
                edge_ref[t + 1, c] = value
        part = field[(t - 1) * wide:t * wide]
        for c in range(components):
            edge_ref[t + 1, c] += edge_coef_ref[components + 6] * edge_boundary(part, c, components, pitch, axial)
    refs = (jac_ref, state_ref, edge_ref, coef_ref)

    for t in range(2, axial):
        for a in range(axial + 1 - t, axial):
            advance(refs, t, a)
        for c in range(components):
            state_ref[t + 1, c, axial - 1] += bound_ref[t, c]
    for a in range(1, axial):
        for c, value in enumerate(layer_update(*refs, axial, a, span)):
            out_ref[c, a] = value + bound_ref[axial, c, :span] if a == axial - 1 else value
    for c in range(components):
        out_ref[c, 0] = state_ref[axial + 1, c, 0, :span]


def moved(x, to):
    sizes = [lax.axis_size(name) for name in AXES]
    pairs = []
    for r in range(sizes[0]):
        for s in range(sizes[1]):
            for p in range(sizes[2]):
                target = to(r, s, p)
                if all(0 <= at < size for at, size in zip(target, sizes)):
                    number = lambda at: (at[0] * sizes[1] + at[1]) * sizes[2] + at[2]
                    pairs.append((number((r, s, p)), number(target)))
    return lax.ppermute(x, AXES, pairs)


def struct(*shape):
    return jax.ShapeDtypeStruct(shape, jnp.float32)


def on_device(
    adjoint_start, source, couplings, damping, jacobians, giles_real, giles_imag, blades, mode_orders, cell_map,
):
    components, axial, span, pitch = adjoint_start.shape
    row_count, span_count, place_count = (lax.axis_size(name) for name in AXES)
    length = pitch * place_count
    assert sum(axial - t for t in range(1, axial)) <= EDGE
    assert components == COMPONENTS and components * WAVES <= pitch
    assert axial == ITERS - 1 and ITERS <= EDGE and axial * SEGMENT_LANES == pitch
    assert span_count == 2 and place_count > 1 and place_count & (place_count - 1) == 0
    wide = span + EDGE
    fields = 2 * components + 6
    groups = slots(fields + 1, components)[1][-1][0] + 1
    pairs = -(-(fields * axial + 1) // 2)
    span_tiles = pairs + -(-components * axial // EDGE)
    vmem = pl.BlockSpec(memory_space=pltpu.VMEM)
    hbm = pl.BlockSpec(memory_space=pltpu.HBM)

    def in_hbm(x):
        return pltpu.with_memory_space_constraint(x, pltpu.HBM)

    def call(kernel, name, outs, ins, aliases=None, scratch=(), limit=40 * MIB, **fixed):
        specs = [spec for spec, _ in ins]
        return pl.pallas_call(
            functools.partial(kernel, **fixed),
            out_shape=outs,
            in_specs=specs,
            out_specs=jax.tree.map(lambda _: vmem, outs),
            scratch_shapes=scratch,
            input_output_aliases=aliases or {},
            compiler_params=params(limit),
            name=name,
        )(*[value for _, value in ins])

    tables = (
        jacobians.transpose(2, 3, 0, 1), giles_real.transpose(2, 3, 0, 1), giles_imag.transpose(2, 3, 0, 1),
        mode_orders.transpose(0, 2, 1), cell_map,
    )
    blades = blades.reshape(1, -1)
    corner_rows = groups * EDGE
    state_shape = struct(axial + 2, components, axial, wide, pitch)
    state, coef, inv, small, modes, table, blades, *tables = call(
        start_kernel, "start",
        (
            state_shape, struct(components + 6, axial, wide, pitch), struct(wide, pitch),
            struct(2 * corner_rows + EDGE, pitch), struct(wide, pitch),
            jax.ShapeDtypeStruct((2, components * pitch, pitch), jnp.bfloat16),
            *(jax.ShapeDtypeStruct(x.shape, x.dtype) for x in (blades, *tables)),
        ),
        [(hbm, in_hbm(x)) for x in (adjoint_start, source, couplings, damping, blades, *tables)],
        scratch=[
            pltpu.VMEM(source.shape, jnp.float32), pltpu.VMEM(couplings.shape, jnp.float32),
            pltpu.VMEM(damping.shape, jnp.float32), pltpu.SemaphoreType.DMA((5 + len(tables),)),
        ],
        groups=groups, length=length,
    )
    edges, span_out, inner, outer = call(
        pack_kernel, "pack",
        (
            struct(fields + 1, span, pitch), struct(span_tiles, EDGE, pitch), struct(groups * wide, pitch),
            struct(groups * wide, pitch),
        ),
        [(vmem, x) for x in (state, coef, inv)],
    )
    steps = [1 << n for n in range(place_count.bit_length() - 2)]
    last_step = place_count // 2

    def near(x):
        return moved(x, lambda r, s, p: (r - 1, s, p))

    def far(x):
        return moved(x, lambda r, s, p: (r - 1, s, p ^ last_step))

    small, edges = lax.optimization_barrier((moved(small, lambda r, s, p: (r, 1 - s, p)), edges))
    from_span = moved(span_out, lambda r, s, p: (r, 1 - s, p))
    synth, jac = call(
        synth_kernel, "synth",
        (
            jax.ShapeDtypeStruct(
                (2, -(-components * (pitch + SEGMENT_LANES) // pitch) * pitch, pitch), jnp.bfloat16
            ),
            struct(-(-6 * components * components // EDGE) * EDGE, pitch),
        ),
        [(vmem, x) for x in (blades, *tables)],
        scratch=[pltpu.VMEM((2, components * components, mode_orders.shape[1]), jnp.float32)],
        row_count=row_count, place_count=place_count, components=components, pitch=pitch, length=length, axial=axial,
    )
    edge_shape = struct(axial + 1, components, wide, pitch)
    modes = lax.dynamic_update_slice(modes, small[2 * corner_rows:], (span, 0))
    for n, step in enumerate(steps):
        got = moved(modes, lambda r, s, p: (r, s, p ^ step))
        if n == 0:
            got, jac, inner, outer = lax.optimization_barrier((got, jac, inner, outer))
        modes = modes + got
    modes_b = far(modes)
    modes_a = near(modes)
    inner = lax.dynamic_update_slice(inner, small[:corner_rows], (groups * span, 0))
    outer = lax.dynamic_update_slice(outer, small[corner_rows:2 * corner_rows], (groups * span, 0))
    outer = moved(outer, lambda r, s, p: (r, s, (p - 1 + 2 * (p % 2)) % place_count))
    inner = moved(inner, lambda r, s, p: (r, s, p ^ 1))

    coef, inv, edge_coef, state, edge, more, part = call(
        first_kernel, "first_sweeps",
        (
            struct(components + 6, axial, wide, pitch), struct(wide, pitch), struct(components + 7, wide, pitch),
            state_shape, edge_shape,
            struct((axial - 1) * span + EDGE, pitch), struct(span, pitch),
        ),
        [(vmem, jac)] + [(vmem, x) for x in (state, coef, inv, edges, from_span, inner, outer, table)],
        aliases={1: 3, 2: 0, 3: 1},
        groups=groups,
    )

    more_shape = struct(axial * span + EDGE, pitch)
    more = call(
        late_kernel, "late_modes", more_shape,
        [(vmem, x) for x in (jac, coef, inv, part, more, modes_a, modes_b, synth, table)],
    )
    state, edge, sent = call(
        between_kernel, "between_sweeps", (state_shape, edge_shape, more_shape),
        [(vmem, x) for x in (jac, coef, inv, edge_coef, state, edge, modes_a, modes_b, synth, more)],
        aliases={4: 0, 5: 1},
    )
    state, edge = call(
        beside_kernel, "beside_sweeps", (state_shape, edge_shape),
        [(vmem, x) for x in (jac, coef, edge_coef, state, edge)],
        aliases={3: 0, 4: 1},
    )
    for step in steps:
        got = moved(more, lambda r, s, p: (r, s, p ^ step))
        more, sent = sent + got, sent + got
    more_b = far(more)
    more_a = near(more)
    return call(
        second_kernel, "second_sweeps", (state_shape, edge_shape, struct(components, axial, span, pitch)),
        [(vmem, x) for x in (jac, coef, inv, edge_coef, state, edge, more_a, more_b, synth)],
        aliases={4: 0, 5: 1},
        scratch=[pltpu.VMEM((axial + 1, components, wide, pitch), jnp.float32)],
    )[2]


def solution(mesh):
    placed = (
        P(None, "row", "span", "pitch"),
        P(None, "row", "span", "pitch"),
        P(None, "row", "span", "pitch"),
        P("row", "span", "pitch"),
        P("row", None, None, None),
        P(),
        P(),
        P(),
        P(),
        P("row", None),
    )
    return jax.shard_map(
        on_device,
        mesh=mesh,
        in_specs=placed,
        out_specs=P(None, "row", "span", "pitch"),
        check_vma=False,
    )
```

```python
import functools
import math

import jax
import jax.numpy as jnp
from jax import lax
from jax.experimental import pallas as pl
from jax.experimental.pallas import tpu as pltpu
from jax.sharding import PartitionSpec as P

ITERS = 5
AXES = ("row", "span", "pitch")

ORDER_MAX = 2
BASE = 2 * ORDER_MAX + 1
COSINES = (BASE * BASE + 1) // 2
WAVES = 2 * COSINES - 1
COMPONENTS = 5
EDGE = 8
HALF = EDGE // 2
SEGMENT_LANES = 4 * EDGE
EXACT = lax.Precision.HIGHEST
MIB = 1024 * 1024


def params(limit):
    return pltpu.CompilerParams(vmem_limit_bytes=limit)


def lanes(shape):
    return lax.broadcasted_iota(jnp.int32, shape, len(shape) - 1)


def rows(shape):
    return lax.broadcasted_iota(jnp.int32, shape, len(shape) - 2)


def column(j):
    component = (j * 41) >> 10
    wave = j - WAVES * component
    sine = wave >= COSINES
    return component, jnp.where(sine, wave - (COSINES - 1), wave), sine


def mode_number(mode, blades):
    high = ((mode + ORDER_MAX) * 13) >> 6
    low = mode - BASE * high
    return high * blades[0] + low * blades[1]


def waves(products, length):
    if length & (length - 1) == 0:
        phase = products & (length - 1)
    else:
        phase = jnp.mod(products, length)
    turn = phase.astype(jnp.float32) * (1.0 / length)
    quarter = jnp.floor(4.0 * turn + 0.5)
    x = (turn - 0.25 * quarter) * (2.0 * math.pi)
    y = x * x
    sine = x * (1.0 + y * (-1.0 / 6 + y * (1.0 / 120 + y * (-1.0 / 5040 + y * (1.0 / 362880)))))
    cosine = 1.0 + y * (-0.5 + y * (1.0 / 24 + y * (-1.0 / 720 + y * (1.0 / 40320 - y * (1.0 / 3628800)))))
    quarter = quarter.astype(jnp.int32) & 3
    odd = (quarter & 1) == 1
    cos_out = jnp.where(odd, sine, cosine)
    sin_out = jnp.where(odd, cosine, sine)
    cos_out = jnp.where((quarter == 1) | (quarter == 2), -cos_out, cos_out)
    sin_out = jnp.where(quarter >= 2, -sin_out, sin_out)
    return cos_out, sin_out


def to_edges(layers, pitch):
    lane = lanes(layers[-1].shape)
    block = jnp.zeros_like(layers[-1])
    for a, layer in enumerate(layers):
        if layer is None:
            continue
        start = a * SEGMENT_LANES
        first = pltpu.roll(layer, (start + EDGE) % pitch, layer.ndim - 1)
        last = pltpu.roll(layer, (start + 3 * EDGE) % pitch, layer.ndim - 1)
        block = jnp.where((lane >= start + EDGE) & (lane < start + 2 * EDGE), first, block)
        block = jnp.where((lane >= start + 2 * EDGE) & (lane < start + 3 * EDGE), last, block)
    return block


def half_rows(side):
    return jnp.where(side == 0, EDGE // 2, 0), jnp.where(side == 0, 0, EDGE // 2)


def slots(fields, components):
    per_group = SEGMENT_LANES // HALF
    near = [(f // per_group, f % per_group * HALF) for f in range(fields)]
    group, lane = near[-1]
    far = [(group, lane + HALF + c) for c in range(components)]
    return near, far


def packed_edges(blocks, place, components):
    near, far = slots(len(blocks), components)
    pitch = blocks[0].shape[1]
    lane = lanes(blocks[0].shape) % SEGMENT_LANES
    sides = []
    for near_at, far_at in ((3 * EDGE - HALF, 3 * EDGE - HALF - 1), (EDGE, EDGE + HALF)):
        packed = [jnp.zeros_like(blocks[0]) for _ in range(far[-1][0] + 1)]
        for f, (g, to) in enumerate(near):
            value = pltpu.roll(blocks[f], (to - near_at) % pitch, 1)
            packed[g] = jnp.where((lane >= to) & (lane < to + HALF), value, packed[g])
        for f, (g, to) in enumerate(far):
            packed[g] = jnp.where(lane == to, pltpu.roll(blocks[f], (to - far_at) % pitch, 1), packed[g])
        sides.append(packed)
    even = lax.rem(place, 2) == 0
    inner = [jnp.where(even, right, left) for right, left in zip(*sides)]
    outer = [jnp.where(even, left, right) for right, left in zip(*sides)]
    return inner, outer


def edge_blocks(state_ref, coef_ref, inv_ref, at):
    components, axial, pitch = state_ref.shape[1], state_ref.shape[2], state_ref.shape[4]
    blocks = [to_edges([state_ref[0, c, a, at, :] for a in range(axial)], pitch) for c in range(components)]
    blocks += [to_edges([coef_ref[f, a, at, :] for a in range(axial)], pitch) for f in range(components + 6)]
    return blocks + [to_edges([None] * (axial - 1) + [inv_ref[at, :]], pitch)]


def start_kernel(
    adjoint_hbm, source_hbm, couplings_hbm, damping_hbm, blades_hbm, *refs, groups, length,
):
    state_ref, coef_ref, inv_ref, span_ref, small_ref, modes_ref, table_ref, blades_ref = refs[5:13]
    source_ref, couplings_ref, damping_ref, sems = refs[18:]
    components, axial, span, pitch = source_ref.shape
    adjoint_ref = state_ref.at[0, :, :, pl.ds(0, span), :]
    copies = [
        pltpu.make_async_copy(src, dst, sems.at[n])
        for n, (src, dst) in enumerate((
            (couplings_hbm, couplings_ref), (damping_hbm, damping_ref), (source_hbm, source_ref),
            (adjoint_hbm, adjoint_ref), (blades_hbm, blades_ref), *zip(refs[:5], refs[13:18]),
        ))
    ]
    for copy in copies:
        copy.start()
    row, side, place = (lax.axis_index(name) for name in AXES)
    copies[4].wait()
    face = jnp.maximum(row - 1, 0)
    component, mode, sine = column(lanes((pitch, pitch)))
    number = mode_number(mode, [picked(blades_ref[...], face + n) for n in range(2)])
    cos_table, sin_table = waves(number * (place * pitch + rows((pitch, pitch))), length)
    table = jnp.where(component < components, jnp.where(sine, sin_table, cos_table), 0.0)
    for c in range(components):
        for n, value in enumerate(split(jnp.where(component == c, table, 0.0))):
            table_ref[n, pl.ds(c * pitch, pitch), :] = value
    copies[0].wait()
    copies[1].wait()
    diag = damping_ref[...]
    for d in range(6):
        diag = diag + couplings_ref[d]
    inverse = 1.0 / diag
    for d in range(6):
        coef_ref[components + d, :, :span] = couplings_ref[d] * inverse
    inv_ref[:span] = inverse[axial - 1]
    copies[2].wait()
    for c in range(components):
        coef_ref[c, :, :span] = source_ref[c] * inverse
    copies[3].wait()
    edge_row = pl.multiple_of(jnp.where(side == 0, span - EDGE, 0), EDGE)
    blocks = edge_blocks(state_ref, coef_ref, inv_ref, pl.ds(edge_row, EDGE))
    for n, packed in enumerate(packed_edges(blocks, place, components)):
        for g, value in enumerate(packed):
            small_ref[pl.ds((n * (groups + 1) + g) * EDGE, EDGE), :] = value
    modes_ref[...] = projected([adjoint_ref[c, 0] for c in range(components)], table_ref)
    small_ref[pl.ds(groups * EDGE, EDGE), :] = modes_ref[pl.ds(edge_row, EDGE), :]

    to_low, to_high = half_rows(side)
    line = rows((EDGE, pitch))
    tiles = [state_ref[0, c, a, pl.ds(edge_row, EDGE), :] for c in range(components) for a in range(axial)]
    tiles += [coef_ref[f, a, pl.ds(edge_row, EDGE), :] for f in range(components + 6) for a in range(axial)]
    tiles += [inv_ref[pl.ds(edge_row, EDGE), :]]
    pairs = -(-len(tiles) // 2)
    for n in range(pairs):
        value = pltpu.roll(tiles[2 * n], to_low, 0)
        if 2 * n + 1 < len(tiles):
            value = jnp.where(line < HALF, value, pltpu.roll(tiles[2 * n + 1], to_high, 0))
        span_ref[n] = value
    fifth = jnp.where(side == 0, HALF - 1, HALF)
    for n in range(span_ref.shape[0] - pairs):
        value = jnp.zeros((EDGE, pitch), jnp.float32)
        for k in range(min(EDGE, components * axial - n * EDGE)):
            value = jnp.where(line == k, pltpu.roll(tiles[n * EDGE + k], lax.rem(k + EDGE - fifth, EDGE), 0), value)
        span_ref[pairs + n] = value
    for copy in copies[5:]:
        copy.wait()


def pack_kernel(state_ref, coef_ref, inv_ref, modes_ref, edges_ref, inner_ref, outer_ref, *, groups):
    _, components, axial, wide, pitch = state_ref.shape
    span = wide - EDGE
    place = lax.axis_index("pitch")
    blocks = edge_blocks(state_ref, coef_ref, inv_ref, pl.ds(0, span))
    for f, block in enumerate(blocks):
        edges_ref[f] = block
    for out_ref, packed in zip((inner_ref, outer_ref), packed_edges(blocks, place, components)):
        for g, value in enumerate(packed):
            out_ref[pl.ds(g * span, span), :] = value
    start = groups * span + (groups + 1) * EDGE
    inner_ref[pl.ds(start, span), :] = modes_ref[...]


def picked(values, at):
    chosen = jnp.where(lanes(values.shape) == at, values.astype(jnp.float32), 0.0)
    return jnp.sum(chosen, axis=1, keepdims=True).astype(jnp.int32)


def split(x):
    high = x.astype(jnp.bfloat16)
    return high, (x - high.astype(jnp.float32)).astype(jnp.bfloat16)


def product(x, table, dims):
    x_high, x_low = split(x)
    table_high, table_low = table
    dot = functools.partial(lax.dot_general, dimension_numbers=(dims, ((), ())), preferred_element_type=jnp.float32)
    return dot(x_high, table_high) + (dot(x_low, table_high) + dot(x_high, table_low))


def projected(strips, table_ref):
    return product(jnp.concatenate(strips, 1), (table_ref[0], table_ref[1]), ((1,), (0,)))


def synthesised(modes, synth_ref, count):
    return product(modes, (synth_ref[0, :count], synth_ref[1, :count]), ((1,), (1,)))


def synth_kernel(
    blades_ref, jacobians_ref, giles_re_ref, giles_im_ref, orders_ref, cells_ref, synth_ref, rows_ref, sums_ref,
    *, row_count, place_count, components, pitch, length, axial,
):
    row, place = lax.axis_index("row"), lax.axis_index("pitch")
    face = jnp.minimum(row, row_count - 2)
    for b in range(components):
        for c in range(components):
            entries = jacobians_ref[b, c]
            for d in range(6):
                at = (b * components + c) * 6 + d
                rows_ref[pl.ds(at, 1), :] = jnp.broadcast_to(entries[:, d:d + 1], (1, pitch))
    modes = orders_ref.shape[2]
    orders = orders_ref[face]
    tag = BASE * orders[0:1] + orders[1:2]
    component, mode, _ = column(rows((pitch, modes)))
    same = (jnp.abs(tag) == mode) & (component < components)
    plain = jnp.where(same, 1.0, 0.0)
    signed = jnp.where(tag < 0, -plain, plain)
    dims = (((1,), (1,)), ((), ()))
    for n, ref in enumerate((giles_re_ref, giles_im_ref)):
        for b in range(components):
            for c in range(components):
                sums_ref[n, pl.ds(b * components + c, 1), :] = ref[b, c, pl.ds(face, 1), :]
    sums_re = lax.dot_general(sums_ref[0], plain, dims, precision=EXACT, preferred_element_type=jnp.float32)
    sums_im = lax.dot_general(sums_ref[1], signed, dims, precision=EXACT, preferred_element_type=jnp.float32)
    component, mode, sine = column(lanes(sums_re.shape))
    scale = 2.0 / length
    with_cos = jnp.where(sine, sums_im, sums_re) * scale
    with_sin = jnp.where(sine, sums_re, -sums_im) * scale
    component = component[0:1]

    def chunk(at):
        start = pl.multiple_of(lax.rem(place + at + place_count, place_count) * pitch, pitch)
        return cells_ref[:, pl.ds(start, pitch)]

    own = chunk(0)
    lane = lanes((1, pitch))
    first = (axial - 1) * SEGMENT_LANES
    edge = jnp.where(lane < first + EDGE, pltpu.roll(chunk(-1), (first + EDGE) % pitch, 1), pltpu.roll(own, (first + EDGE) % pitch, 1))
    edge = jnp.where(lane < first + 2 * EDGE, edge, pltpu.roll(own, (first + 3 * EDGE) % pitch, 1))
    edge = jnp.where(lane < first + 3 * EDGE, edge, pltpu.roll(chunk(1), (first + 3 * EDGE) % pitch, 1))

    def upright(cells):
        wide = jnp.broadcast_to(cells.astype(jnp.float32), (pitch, pitch))
        return jnp.transpose(wide).astype(jnp.int32)

    edge_cells = upright(edge)[first:first + SEGMENT_LANES]
    at_cells = jnp.concatenate([upright(own), edge_cells], 0)
    _, mode, _ = column(lanes(at_cells.shape))
    blades = [picked(blades_ref[...], face + n) for n in range(2)]
    cos_table, sin_table = waves(mode_number(mode, blades) * at_cells, length)
    for c in range(components):
        row_cos = jnp.zeros((1, pitch), jnp.float32)
        row_sin = jnp.zeros((1, pitch), jnp.float32)
        for b in range(components):
            at = b * components + c
            row_cos = jnp.where(component == b, with_cos[at:at + 1], row_cos)
            row_sin = jnp.where(component == b, with_sin[at:at + 1], row_sin)
        part = row_cos * cos_table + row_sin * sin_table
        for n, value in enumerate(split(part)):
            synth_ref[n, pl.ds(c * pitch, pitch), :] = value[:pitch]
            synth_ref[n, pl.ds(components * pitch + c * SEGMENT_LANES, SEGMENT_LANES), :] = value[pitch:]
    used = components * (pitch + SEGMENT_LANES)
    rest = synth_ref.shape[1] - used
    if rest:
        synth_ref[:, pl.ds(used, rest), :] = jnp.zeros((2, rest, pitch), jnp.bfloat16)


def jacobian(jac_ref, components, b, c, d):
    return jac_ref[pl.ds((b * components + c) * 6 + d, 1), :]


def mixed(jac_ref, source, couplings, neighbours):
    total = list(source)
    jac = functools.partial(jacobian, jac_ref, len(total))
    for d, neighbour in enumerate(neighbours):
        if neighbour is None:
            continue
        for c in range(len(total)):
            term = jac(0, c, d) * neighbour[0]
            for b in range(1, len(total)):
                term = term + jac(b, c, d) * neighbour[b]
            total[c] = total[c] + couplings[d] * term
    return total


def layer_update(jac_ref, state_ref, edge_ref, coef_ref, t, a, height):
    _, components, axial, wide, pitch = state_ref.shape
    lane = lanes((height, pitch))
    start = a * SEGMENT_LANES
    own = [state_ref[t, c, a] for c in range(components)]
    above = [state_ref[t, c, a + 1, :height] for c in range(components)] if a < axial - 1 else None
    below = [state_ref[t, c, a - 1, :height] for c in range(components)] if a else None
    edge = [edge_ref[t, c, :height] for c in range(components)]
    span_next = [pltpu.roll(x, wide - 1, 0)[:height] for x in own]
    span_prev = [pltpu.roll(x, 1, 0)[:height] for x in own]
    own = [x[:height] for x in own]
    to_end = (pitch - 1 - (start + 3 * EDGE)) % pitch
    to_begin = (pitch - (start + EDGE - 1)) % pitch
    pitch_next = [
        jnp.where(lane == pitch - 1, pltpu.roll(e, to_end, 1), pltpu.roll(x, pitch - 1, 1))
        for e, x in zip(edge, own)
    ]
    pitch_prev = [
        jnp.where(lane == 0, pltpu.roll(e, to_begin, 1), pltpu.roll(x, 1, 1))
        for e, x in zip(edge, own)
    ]
    source = [coef_ref[c, a, :height] for c in range(components)]
    couplings = [coef_ref[components + d, a, :height] for d in range(6)]
    return mixed(jac_ref, source, couplings, (above, below, span_next, span_prev, pitch_next, pitch_prev))


def edge_update(jac_ref, edge_ref, edge_coef_ref, t, axial):
    components, wide, pitch = edge_ref.shape[1:]
    lane = lanes((wide, pitch))
    own = [edge_ref[t, c] for c in range(components)]
    above = [jnp.where(lane < (axial - 1) * SEGMENT_LANES, pltpu.roll(x, pitch - SEGMENT_LANES, 1), 0.0) for x in own]
    below = [jnp.where(lane >= SEGMENT_LANES, pltpu.roll(x, SEGMENT_LANES, 1), 0.0) for x in own]
    span_next = [pltpu.roll(x, wide - 1, 0) for x in own]
    span_prev = [pltpu.roll(x, 1, 0) for x in own]
    pitch_next = [pltpu.roll(x, pitch - 1, 1) for x in own]
    pitch_prev = [pltpu.roll(x, 1, 1) for x in own]
    source = [edge_coef_ref[c] for c in range(components)]
    couplings = [edge_coef_ref[components + d] for d in range(6)]
    return mixed(jac_ref, source, couplings, (above, below, span_next, span_prev, pitch_next, pitch_prev))


def edge_boundary(field, c, components, pitch, axial):
    at = components * pitch + c * SEGMENT_LANES
    tile = field[:, (at // pitch) * pitch:(at // pitch + 1) * pitch]
    return pltpu.roll(tile, ((axial - 1) * SEGMENT_LANES - at % pitch) % pitch, 1)


def advance(refs, t, a, height=None):
    state_ref = refs[1]
    height = height or state_ref.shape[3]
    for c, value in enumerate(layer_update(*refs, t, a, height)):
        state_ref[t + 1, c, a, :height] = value


def first_kernel(
    jac_ref, state_in_ref, coef_in_ref, inv_in_ref, edges_ref, span_ref, inner_ref, outer_ref, table_ref,
    coef_ref, inv_ref, edge_coef_ref, state_ref, edge_ref, modes_ref, part_ref, *, groups,
):
    _, components, axial, wide, pitch = state_ref.shape
    span = wide - EDGE
    side = lax.axis_index("span")
    fields = 2 * components + 6
    line = rows((EDGE, pitch))
    keep_half = jnp.where(side == 0, line, EDGE - 1 - line) < HALF
    fifth = jnp.where(side == 0, HALF, HALF - 1)
    from_low, from_high = half_rows(1 - side)
    pairs = -(-(fields * axial + 1) // 2)

    def ghost(n):
        value = pltpu.roll(span_ref[n // 2], from_high if n % 2 else from_low, 0)
        value = jnp.where(keep_half, value, 0.0)
        if n < components * axial:
            extra = pltpu.roll(span_ref[pairs + n // EDGE], lax.rem(fifth + EDGE - n % EDGE, EDGE), 0)
            value = jnp.where(line == fifth, extra, value)
        return value

    even = lax.rem(lax.axis_index("pitch"), 2) == 0

    def group(ref, g):
        corner = ref[pl.ds(groups * span + g * EDGE, EDGE), :]
        return jnp.concatenate([ref[pl.ds(g * span, span), :], corner], 0)

    halves = [(group(inner_ref, g), group(outer_ref, g)) for g in range(groups)]
    from_left = [jnp.where(even, outer, inner) for inner, outer in halves]
    from_right = [jnp.where(even, inner, outer) for inner, outer in halves]
    near, far = slots(fields + 1, components)
    keep_five = keep_half | (line == fifth)
    for f in range(fields + 1):
        if f < fields:
            layers = [ghost(f * axial + a) for a in range(axial)]
        else:
            layers = [jnp.zeros((EDGE, pitch), jnp.float32)] * (axial - 1) + [ghost(fields * axial)]
        if f < components:
            for a in range(axial):
                state_ref[0, f, a, span:] = layers[a]
        elif f < fields:
            for a in range(axial):
                coef_ref[f - components, a, span:] = layers[a]
        else:
            inv_ref[span:] = layers[-1]
        g, at = near[f]
        value = jnp.concatenate([edges_ref[f], to_edges(layers, pitch)], 0)
        lane = lanes((wide, pitch)) % SEGMENT_LANES
        value = jnp.where((lane >= HALF) & (lane < EDGE), pltpu.roll(from_left[g], (HALF - at) % pitch, 1), value)
        value = jnp.where(
            (lane >= 3 * EDGE) & (lane < 3 * EDGE + HALF),
            pltpu.roll(from_right[g], (3 * EDGE - at) % pitch, 1), value,
        )
        if f < components:
            g, at = far[f]
            value = jnp.where(lane == HALF - 1, pltpu.roll(from_left[g], (HALF - 1 - at) % pitch, 1), value)
            value = jnp.where(
                lane == 3 * EDGE + HALF, pltpu.roll(from_right[g], (3 * EDGE + HALF - at) % pitch, 1), value,
            )
        target, at = (edge_ref.at[0], f) if f < components else (edge_coef_ref, f - components)
        target[at, :span] = value[:span]
        target[at, span:] = jnp.where(keep_five if f < components else keep_half, value[span:], 0.0)
    refs = (jac_ref, state_ref, edge_ref, coef_ref)
    for t in range(axial):
        for a in range(axial - t):
            advance(refs, t, a)
        if t < axial - 1:
            for c, value in enumerate(edge_update(jac_ref, edge_ref, edge_coef_ref, t, axial)):
                edge_ref[t + 1, c] = value
    strips = [
        jnp.concatenate([state_ref[t, c, 0] for t in range(1, axial)] + [state_ref[axial, c, 0, :span]], 0)
        for c in range(components)
    ]
    total = projected(strips, table_ref)
    ghosts = jnp.zeros((EDGE, pitch), jnp.float32)
    for t in range(1, axial):
        part = total[(t - 1) * wide:t * wide]
        modes_ref[pl.ds((t - 1) * span, span), :] = part[:span]
        keep, to_packed, _ = ghost_rows(side, t, axial)
        ghosts = jnp.where(keep, pltpu.roll(part[span:], to_packed, 0), ghosts)
    modes_ref[pl.ds((axial - 1) * span, EDGE), :] = ghosts
    part_ref[...] = total[(axial - 1) * wide:]


def ghost_rows(side, t, axial):
    line = rows((EDGE, 1))
    distance = jnp.where(side == 0, line, EDGE - 1 - line)
    start = sum(axial - n for n in range(1, t))
    to_packed = jnp.where(side == 0, start, (EDGE - start) % EDGE)
    from_packed = jnp.where(side == 0, (EDGE - start) % EDGE, start)
    return (distance >= start) & (distance < start + axial - t), to_packed, from_packed


def along_axis(jac_ref, coef_ref, delta, a, height):
    components = len(delta)
    out = []
    for c in range(components):
        term = jacobian(jac_ref, components, 0, c, 0) * delta[0]
        for b in range(1, components):
            term = term + jacobian(jac_ref, components, b, c, 0) * delta[b]
        out.append(coef_ref[components, a, :height] * term)
    return out


def late_kernel(
    jac_ref, coef_ref, inv_ref, part_ref, more_ref, modes_b_ref, modes_a_ref, synth_ref, table_ref, modes_ref,
):
    span, pitch = part_ref.shape
    components, axial = coef_ref.shape[0] - 6, coef_ref.shape[1]
    field = synthesised(modes_a_ref[EDGE:] + modes_b_ref[EDGE:], synth_ref, components * pitch)
    delta = [inv_ref[:span] * field[:, c * pitch:(c + 1) * pitch] for c in range(components)]
    for a in range(axial - 2, -1, -1):
        delta = along_axis(jac_ref, coef_ref, delta, a, span)
    before = more_ref.shape[0]
    modes_ref[:before] = more_ref[...]
    modes_ref[before:] = part_ref[...] + projected(delta, table_ref)


def between_kernel(
    jac_ref, coef_ref, inv_ref, edge_coef_ref, state_in_ref, edge_in_ref, modes_b_ref, modes_a_ref, synth_ref, more_ref,
    state_ref, edge_ref, sent_ref,
):
    sent_ref[...] = more_ref[...]
    components, axial = state_ref.shape[1], state_ref.shape[2]
    wide, pitch = state_ref.shape[3:]
    modes = modes_a_ref[...] + modes_b_ref[...]
    field = synthesised(jnp.concatenate([modes[EDGE:], modes[:EDGE]], 0), synth_ref, synth_ref.shape[1])
    delta = [inv_ref[...] * field[:, c * pitch:(c + 1) * pitch] for c in range(components)]
    for t in range(1, axial + 1):
        for c in range(components):
            state_ref[t, c, axial - t] += delta[c]
        if t < axial:
            delta = along_axis(jac_ref, coef_ref, delta, axial - 1 - t, wide)
    for c in range(components):
        edge_ref[1, c] += edge_coef_ref[components + 6] * edge_boundary(field, c, components, pitch, axial)
    diagonal_sweeps(jac_ref, state_ref, edge_ref, coef_ref, edge_coef_ref, 1, axial // 2 + 1)


def beside_kernel(jac_ref, coef_ref, edge_coef_ref, state_in_ref, edge_in_ref, state_ref, edge_ref):
    axial, span = state_ref.shape[2], state_ref.shape[3] - EDGE
    diagonal_sweeps(jac_ref, state_ref, edge_ref, coef_ref, edge_coef_ref, axial // 2 + 1, axial)
    advance((jac_ref, state_ref, edge_ref, coef_ref), axial, 0, span)


def diagonal_sweeps(jac_ref, state_ref, edge_ref, coef_ref, edge_coef_ref, first, last):
    axial = state_ref.shape[2]
    for t in range(first, last):
        advance((jac_ref, state_ref, edge_ref, coef_ref), t, axial - t)
        for c, value in enumerate(edge_update(jac_ref, edge_ref, edge_coef_ref, t, axial)):
            edge_ref[t + 1, c] = value


def second_kernel(
    jac_ref, coef_ref, inv_ref, edge_coef_ref, state_in_ref, edge_in_ref, more_a_ref, more_b_ref, synth_ref,
    state_ref, edge_ref, out_ref, bound_ref,
):
    components, axial, span, pitch = out_ref.shape
    wide = span + EDGE
    side = lax.axis_index("span")
    more = more_a_ref[...] + more_b_ref[...]
    start = (axial - 1) * span
    parts = []
    for t in range(1, axial):
        _, _, from_packed = ghost_rows(side, t, axial)
        parts += [more[(t - 1) * span:t * span], pltpu.roll(more[start:start + EDGE], from_packed, 0)]
    field = synthesised(jnp.concatenate(parts + [more[start + EDGE:]], 0), synth_ref, synth_ref.shape[1])
    for t in range(1, axial):
        part = field[(t - 1) * wide:t * wide]
        for c in range(components):
            bound_ref[t, c] = inv_ref[...] * part[:, c * pitch:(c + 1) * pitch]
    for c in range(components):
        bound_ref[axial, c, :span] = inv_ref[:span] * field[(axial - 1) * wide:, c * pitch:(c + 1) * pitch]
    delta = [bound_ref[1, c] for c in range(components)]
    for t in range(2, axial + 2):
        height = wide if t <= axial else span
        for c in range(components):
            state_ref[t, c, axial + 1 - t, :height] += delta[c][:height]
        if t < axial + 1:
            delta = along_axis(jac_ref, coef_ref, delta, axial - t, wide)
    for t in range(1, axial):
        if t > 1:
            for c, value in enumerate(edge_update(jac_ref, edge_ref, edge_coef_ref, t, axial)):
                edge_ref[t + 1, c] = value
        part = field[(t - 1) * wide:t * wide]
        for c in range(components):
            edge_ref[t + 1, c] += edge_coef_ref[components + 6] * edge_boundary(part, c, components, pitch, axial)
    refs = (jac_ref, state_ref, edge_ref, coef_ref)

    for t in range(2, axial):
        for a in range(axial + 1 - t, axial):
            advance(refs, t, a)
        for c in range(components):
            state_ref[t + 1, c, axial - 1] += bound_ref[t, c]
    for a in range(1, axial):
        for c, value in enumerate(layer_update(*refs, axial, a, span)):
            out_ref[c, a] = value + bound_ref[axial, c, :span] if a == axial - 1 else value
    for c in range(components):
        out_ref[c, 0] = state_ref[axial + 1, c, 0, :span]


def moved(x, to):
    sizes = [lax.axis_size(name) for name in AXES]
    pairs = []
    for r in range(sizes[0]):
        for s in range(sizes[1]):
            for p in range(sizes[2]):
                target = to(r, s, p)
                if all(0 <= at < size for at, size in zip(target, sizes)):
                    number = lambda at: (at[0] * sizes[1] + at[1]) * sizes[2] + at[2]
                    pairs.append((number((r, s, p)), number(target)))
    return lax.ppermute(x, AXES, pairs)


def struct(*shape):
    return jax.ShapeDtypeStruct(shape, jnp.float32)


def on_device(
    adjoint_start, source, couplings, damping, jacobians, giles_real, giles_imag, blades, mode_orders, cell_map,
):
    components, axial, span, pitch = adjoint_start.shape
    row_count, span_count, place_count = (lax.axis_size(name) for name in AXES)
    length = pitch * place_count
    assert sum(axial - t for t in range(1, axial)) <= EDGE
    assert components == COMPONENTS and components * WAVES <= pitch
    assert axial == ITERS - 1 and ITERS <= EDGE and axial * SEGMENT_LANES == pitch
    assert span_count == 2 and place_count > 2 and place_count & (place_count - 1) == 0
    wide = span + EDGE
    fields = 2 * components + 6
    groups = slots(fields + 1, components)[1][-1][0] + 1
    pairs = -(-(fields * axial + 1) // 2)
    span_tiles = pairs + -(-components * axial // EDGE)
    vmem = pl.BlockSpec(memory_space=pltpu.VMEM)
    hbm = pl.BlockSpec(memory_space=pltpu.HBM)

    def in_hbm(x):
        return pltpu.with_memory_space_constraint(x, pltpu.HBM)

    def call(kernel, name, outs, ins, aliases=None, scratch=(), limit=40 * MIB, **fixed):
        specs = [spec for spec, _ in ins]
        return pl.pallas_call(
            functools.partial(kernel, **fixed),
            out_shape=outs,
            in_specs=specs,
            out_specs=jax.tree.map(lambda _: vmem, outs),
            scratch_shapes=scratch,
            input_output_aliases=aliases or {},
            compiler_params=params(limit),
            name=name,
        )(*[value for _, value in ins])

    tables = (
        jacobians.transpose(2, 3, 0, 1), giles_real.transpose(2, 3, 0, 1), giles_imag.transpose(2, 3, 0, 1),
        mode_orders.transpose(0, 2, 1), cell_map,
    )
    blades = blades.reshape(1, -1)
    corner_rows = groups * EDGE
    state_shape = struct(axial + 2, components, axial, wide, pitch)
    state, coef, inv, span_out, small, modes, table, blades, *tables = call(
        start_kernel, "start",
        (
            state_shape, struct(components + 6, axial, wide, pitch), struct(wide, pitch),
            struct(span_tiles, EDGE, pitch), struct(2 * corner_rows + EDGE, pitch), struct(span, pitch),
            jax.ShapeDtypeStruct((2, components * pitch, pitch), jnp.bfloat16),
            *(jax.ShapeDtypeStruct(x.shape, x.dtype) for x in (blades, *tables)),
        ),
        [(hbm, in_hbm(x)) for x in (adjoint_start, source, couplings, damping, blades, *tables)],
        scratch=[
            pltpu.VMEM(source.shape, jnp.float32), pltpu.VMEM(couplings.shape, jnp.float32),
            pltpu.VMEM(damping.shape, jnp.float32), pltpu.SemaphoreType.DMA((5 + len(tables),)),
        ],
        groups=groups, length=length,
    )
    edges, inner, outer = call(
        pack_kernel, "pack",
        (struct(fields + 1, span, pitch), struct((groups + 1) * wide, pitch), struct(groups * wide, pitch)),
        [(vmem, x) for x in (state, coef, inv, modes)],
        groups=groups,
    )
    steps = [1 << n for n in range(place_count.bit_length() - 2)]
    last_step = place_count // 2

    def near(x):
        return moved(x, lambda r, s, p: (r - 1, s, p))

    def far(x):
        return moved(x, lambda r, s, p: (r - 1, s, p ^ last_step))

    small, edges = lax.optimization_barrier((moved(small, lambda r, s, p: (r, 1 - s, p)), edges))
    from_span = moved(span_out, lambda r, s, p: (r, 1 - s, p))
    synth, jac = call(
        synth_kernel, "synth",
        (
            jax.ShapeDtypeStruct(
                (2, -(-components * (pitch + SEGMENT_LANES) // pitch) * pitch, pitch), jnp.bfloat16
            ),
            struct(-(-6 * components * components // EDGE) * EDGE, pitch),
        ),
        [(vmem, x) for x in (blades, *tables)],
        scratch=[pltpu.VMEM((2, components * components, mode_orders.shape[1]), jnp.float32)],
        row_count=row_count, place_count=place_count, components=components, pitch=pitch, length=length, axial=axial,
    )
    edge_shape = struct(axial + 1, components, wide, pitch)
    inner = lax.dynamic_update_slice(inner, small[:corner_rows + EDGE], (groups * span, 0))
    outer = lax.dynamic_update_slice(outer, small[corner_rows + EDGE:], (groups * span, 0))
    modes = inner[groups * span + corner_rows:]
    outer = moved(outer, lambda r, s, p: (r, s, (p - 1 + 2 * (p % 2)) % place_count))
    inner = moved(inner, lambda r, s, p: (r, s, p ^ 1))
    modes = modes + inner[groups * span + corner_rows:]
    for step in steps[1:]:
        modes = modes + moved(modes, lambda r, s, p: (r, s, p ^ step))
    modes_b = far(modes)
    modes_a = near(modes)

    coef, inv, edge_coef, state, edge, more, part = call(
        first_kernel, "first_sweeps",
        (
            struct(components + 6, axial, wide, pitch), struct(wide, pitch), struct(components + 7, wide, pitch),
            state_shape, edge_shape,
            struct((axial - 1) * span + EDGE, pitch), struct(span, pitch),
        ),
        [(vmem, jac)] + [(vmem, x) for x in (state, coef, inv, edges, from_span, inner, outer, table)],
        aliases={1: 3, 2: 0, 3: 1},
        groups=groups,
    )

    more_shape = struct(axial * span + EDGE, pitch)
    more = call(
        late_kernel, "late_modes", more_shape,
        [(vmem, x) for x in (jac, coef, inv, part, more, modes_b, modes_a, synth, table)],
    )
    state, edge, sent = call(
        between_kernel, "between_sweeps", (state_shape, edge_shape, more_shape),
        [(vmem, x) for x in (jac, coef, inv, edge_coef, state, edge, modes_b, modes_a, synth, more)],
        aliases={4: 0, 5: 1},
    )
    state, edge = call(
        beside_kernel, "beside_sweeps", (state_shape, edge_shape),
        [(vmem, x) for x in (jac, coef, edge_coef, state, edge)],
        aliases={3: 0, 4: 1},
    )
    for step in steps:
        got = moved(more, lambda r, s, p: (r, s, p ^ step))
        more, sent = sent + got, sent + got
    more_b = far(more)
    more_a = near(more)
    return call(
        second_kernel, "second_sweeps", (state_shape, edge_shape, struct(components, axial, span, pitch)),
        [(vmem, x) for x in (jac, coef, inv, edge_coef, state, edge, more_a, more_b, synth)],
        aliases={4: 0, 5: 1},
        scratch=[pltpu.VMEM((axial + 1, components, wide, pitch), jnp.float32)],
    )[2]


def solution(mesh):
    placed = (
        P(None, "row", "span", "pitch"),
        P(None, "row", "span", "pitch"),
        P(None, "row", "span", "pitch"),
        P("row", "span", "pitch"),
        P("row", None, None, None),
        P(),
        P(),
        P(),
        P(),
        P("row", None),
    )
    return jax.shard_map(
        on_device,
        mesh=mesh,
        in_specs=placed,
        out_specs=P(None, "row", "span", "pitch"),
        check_vma=False,
    )
```

```python
import functools
import math

import jax
import jax.numpy as jnp
from jax import lax
from jax.experimental import pallas as pl
from jax.experimental.pallas import tpu as pltpu
from jax.sharding import PartitionSpec as P

ITERS = 5
AXES = ("row", "span", "pitch")

ORDER_MAX = 2
BASE = 2 * ORDER_MAX + 1
COSINES = (BASE * BASE + 1) // 2
WAVES = 2 * COSINES - 1
COMPONENTS = 5
EDGE = 8
HALF = EDGE // 2
SEGMENT_LANES = 4 * EDGE
EXACT = lax.Precision.HIGHEST
MIB = 1024 * 1024


def params(limit):
    return pltpu.CompilerParams(vmem_limit_bytes=limit)


def lanes(shape):
    return lax.broadcasted_iota(jnp.int32, shape, len(shape) - 1)


def rows(shape):
    return lax.broadcasted_iota(jnp.int32, shape, len(shape) - 2)


def column(j):
    component = (j * 41) >> 10
    wave = j - WAVES * component
    sine = wave >= COSINES
    return component, jnp.where(sine, wave - (COSINES - 1), wave), sine


def mode_number(mode, blades):
    high = ((mode + ORDER_MAX) * 13) >> 6
    low = mode - BASE * high
    return high * blades[0] + low * blades[1]


def waves(products, length):
    if length & (length - 1) == 0:
        phase = products & (length - 1)
    else:
        phase = jnp.mod(products, length)
    turn = phase.astype(jnp.float32) * (1.0 / length)
    quarter = jnp.floor(4.0 * turn + 0.5)
    x = (turn - 0.25 * quarter) * (2.0 * math.pi)
    y = x * x
    sine = x * (1.0 + y * (-1.0 / 6 + y * (1.0 / 120 + y * (-1.0 / 5040 + y * (1.0 / 362880)))))
    cosine = 1.0 + y * (-0.5 + y * (1.0 / 24 + y * (-1.0 / 720 + y * (1.0 / 40320 - y * (1.0 / 3628800)))))
    quarter = quarter.astype(jnp.int32) & 3
    odd = (quarter & 1) == 1
    cos_out = jnp.where(odd, sine, cosine)
    sin_out = jnp.where(odd, cosine, sine)
    cos_out = jnp.where((quarter == 1) | (quarter == 2), -cos_out, cos_out)
    sin_out = jnp.where(quarter >= 2, -sin_out, sin_out)
    return cos_out, sin_out


def to_edges(layers, pitch):
    lane = lanes(layers[-1].shape)
    block = jnp.zeros_like(layers[-1])
    for a, layer in enumerate(layers):
        if layer is None:
            continue
        start = a * SEGMENT_LANES
        first = pltpu.roll(layer, (start + EDGE) % pitch, layer.ndim - 1)
        last = pltpu.roll(layer, (start + 3 * EDGE) % pitch, layer.ndim - 1)
        block = jnp.where((lane >= start + EDGE) & (lane < start + 2 * EDGE), first, block)
        block = jnp.where((lane >= start + 2 * EDGE) & (lane < start + 3 * EDGE), last, block)
    return block


def half_rows(side):
    return jnp.where(side == 0, EDGE // 2, 0), jnp.where(side == 0, 0, EDGE // 2)


def slots(fields, components):
    per_group = SEGMENT_LANES // HALF
    near = [(f // per_group, f % per_group * HALF) for f in range(fields)]
    group, lane = near[-1]
    far = [(group, lane + HALF + c) for c in range(components)]
    return near, far


def packed_edges(blocks, place, components):
    near, far = slots(len(blocks), components)
    pitch = blocks[0].shape[1]
    lane = lanes(blocks[0].shape) % SEGMENT_LANES
    sides = []
    for near_at, far_at in ((3 * EDGE - HALF, 3 * EDGE - HALF - 1), (EDGE, EDGE + HALF)):
        packed = [jnp.zeros_like(blocks[0]) for _ in range(far[-1][0] + 1)]
        for f, (g, to) in enumerate(near):
            value = pltpu.roll(blocks[f], (to - near_at) % pitch, 1)
            packed[g] = jnp.where((lane >= to) & (lane < to + HALF), value, packed[g])
        for f, (g, to) in enumerate(far):
            packed[g] = jnp.where(lane == to, pltpu.roll(blocks[f], (to - far_at) % pitch, 1), packed[g])
        sides.append(packed)
    even = lax.rem(place, 2) == 0
    inner = [jnp.where(even, right, left) for right, left in zip(*sides)]
    outer = [jnp.where(even, left, right) for right, left in zip(*sides)]
    return inner, outer


def edge_blocks(state_ref, coef_ref, inv_ref, at):
    components, axial, pitch = state_ref.shape[1], state_ref.shape[2], state_ref.shape[4]
    blocks = [to_edges([state_ref[0, c, a, at, :] for a in range(axial)], pitch) for c in range(components)]
    blocks += [to_edges([coef_ref[f, a, at, :] for a in range(axial)], pitch) for f in range(components + 6)]
    return blocks + [to_edges([None] * (axial - 1) + [inv_ref[at, :]], pitch)]


def start_kernel(
    adjoint_hbm, source_hbm, couplings_hbm, damping_hbm, blades_hbm, *refs, groups, length,
):
    state_ref, coef_ref, inv_ref, span_ref, small_ref, modes_ref, table_ref, blades_ref = refs[5:13]
    source_ref, couplings_ref, damping_ref, sems = refs[18:]
    components, axial, span, pitch = source_ref.shape
    adjoint_ref = state_ref.at[0, :, :, pl.ds(0, span), :]
    copies = [
        pltpu.make_async_copy(src, dst, sems.at[n])
        for n, (src, dst) in enumerate((
            (couplings_hbm, couplings_ref), (damping_hbm, damping_ref), (source_hbm, source_ref),
            (adjoint_hbm, adjoint_ref), (blades_hbm, blades_ref), *zip(refs[:5], refs[13:18]),
        ))
    ]
    for copy in copies:
        copy.start()
    row, side, place = (lax.axis_index(name) for name in AXES)
    copies[4].wait()
    face = jnp.maximum(row - 1, 0)
    component, mode, sine = column(lanes((pitch, pitch)))
    number = mode_number(mode, [picked(blades_ref[...], face + n) for n in range(2)])
    cos_table, sin_table = waves(number * (place * pitch + rows((pitch, pitch))), length)
    table = jnp.where(component < components, jnp.where(sine, sin_table, cos_table), 0.0)
    for c in range(components):
        for n, value in enumerate(split(jnp.where(component == c, table, 0.0))):
            table_ref[n, pl.ds(c * pitch, pitch), :] = value
    copies[0].wait()
    copies[1].wait()
    diag = damping_ref[...]
    for d in range(6):
        diag = diag + couplings_ref[d]
    inverse = 1.0 / diag
    for d in range(6):
        coef_ref[components + d, :, :span] = couplings_ref[d] * inverse
    inv_ref[:span] = inverse[axial - 1]
    copies[2].wait()
    for c in range(components):
        coef_ref[c, :, :span] = source_ref[c] * inverse
    copies[3].wait()
    edge_row = pl.multiple_of(jnp.where(side == 0, span - EDGE, 0), EDGE)
    blocks = edge_blocks(state_ref, coef_ref, inv_ref, pl.ds(edge_row, EDGE))
    for n, packed in enumerate(packed_edges(blocks, place, components)):
        for g, value in enumerate(packed):
            small_ref[pl.ds((n * (groups + 1) + g) * EDGE, EDGE), :] = value
    modes_ref[:span] = projected([adjoint_ref[c, 0] for c in range(components)], table_ref)
    modes_ref[span:] = modes_ref[pl.ds(edge_row, EDGE), :]

    to_low, to_high = half_rows(side)
    line = rows((EDGE, pitch))
    tiles = [state_ref[0, c, a, pl.ds(edge_row, EDGE), :] for c in range(components) for a in range(axial)]
    tiles += [coef_ref[f, a, pl.ds(edge_row, EDGE), :] for f in range(components + 6) for a in range(axial)]
    tiles += [inv_ref[pl.ds(edge_row, EDGE), :]]
    pairs = -(-len(tiles) // 2)
    for n in range(pairs):
        value = pltpu.roll(tiles[2 * n], to_low, 0)
        if 2 * n + 1 < len(tiles):
            value = jnp.where(line < HALF, value, pltpu.roll(tiles[2 * n + 1], to_high, 0))
        span_ref[n] = value
    fifth = jnp.where(side == 0, HALF - 1, HALF)
    for n in range(span_ref.shape[0] - pairs):
        value = jnp.zeros((EDGE, pitch), jnp.float32)
        for k in range(min(EDGE, components * axial - n * EDGE)):
            value = jnp.where(line == k, pltpu.roll(tiles[n * EDGE + k], lax.rem(k + EDGE - fifth, EDGE), 0), value)
        span_ref[pairs + n] = value
    for copy in copies[5:]:
        copy.wait()


def pack_kernel(state_ref, coef_ref, inv_ref, edges_ref, inner_ref, outer_ref):
    _, components, axial, wide, pitch = state_ref.shape
    span = wide - EDGE
    place = lax.axis_index("pitch")
    blocks = edge_blocks(state_ref, coef_ref, inv_ref, pl.ds(0, span))
    for f, block in enumerate(blocks):
        edges_ref[f] = block
    for out_ref, packed in zip((inner_ref, outer_ref), packed_edges(blocks, place, components)):
        for g, value in enumerate(packed):
            out_ref[pl.ds(g * span, span), :] = value


def picked(values, at):
    chosen = jnp.where(lanes(values.shape) == at, values.astype(jnp.float32), 0.0)
    return jnp.sum(chosen, axis=1, keepdims=True).astype(jnp.int32)


def split(x):
    high = x.astype(jnp.bfloat16)
    return high, (x - high.astype(jnp.float32)).astype(jnp.bfloat16)


def product(x, table, dims):
    x_high, x_low = split(x)
    table_high, table_low = table
    dot = functools.partial(lax.dot_general, dimension_numbers=(dims, ((), ())), preferred_element_type=jnp.float32)
    return dot(x_high, table_high) + (dot(x_low, table_high) + dot(x_high, table_low))


def projected(strips, table_ref):
    return product(jnp.concatenate(strips, 1), (table_ref[0], table_ref[1]), ((1,), (0,)))


def synthesised(modes, synth_ref, count):
    return product(modes, (synth_ref[0, :count], synth_ref[1, :count]), ((1,), (1,)))


def synth_kernel(
    blades_ref, jacobians_ref, giles_re_ref, giles_im_ref, orders_ref, cells_ref, synth_ref, rows_ref, sums_ref,
    *, row_count, place_count, components, pitch, length, axial,
):
    row, place = lax.axis_index("row"), lax.axis_index("pitch")
    face = jnp.minimum(row, row_count - 2)
    for b in range(components):
        for c in range(components):
            entries = jacobians_ref[b, c]
            for d in range(6):
                at = (b * components + c) * 6 + d
                rows_ref[pl.ds(at, 1), :] = jnp.broadcast_to(entries[:, d:d + 1], (1, pitch))
    modes = orders_ref.shape[2]
    orders = orders_ref[face]
    tag = BASE * orders[0:1] + orders[1:2]
    component, mode, _ = column(rows((pitch, modes)))
    same = (jnp.abs(tag) == mode) & (component < components)
    plain = jnp.where(same, 1.0, 0.0)
    signed = jnp.where(tag < 0, -plain, plain)
    dims = (((1,), (1,)), ((), ()))
    for n, ref in enumerate((giles_re_ref, giles_im_ref)):
        for b in range(components):
            for c in range(components):
                sums_ref[n, pl.ds(b * components + c, 1), :] = ref[b, c, pl.ds(face, 1), :]
    sums_re = lax.dot_general(sums_ref[0], plain, dims, precision=EXACT, preferred_element_type=jnp.float32)
    sums_im = lax.dot_general(sums_ref[1], signed, dims, precision=EXACT, preferred_element_type=jnp.float32)
    component, mode, sine = column(lanes(sums_re.shape))
    scale = 2.0 / length
    with_cos = jnp.where(sine, sums_im, sums_re) * scale
    with_sin = jnp.where(sine, sums_re, -sums_im) * scale
    component = component[0:1]

    def chunk(at):
        start = pl.multiple_of(lax.rem(place + at + place_count, place_count) * pitch, pitch)
        return cells_ref[:, pl.ds(start, pitch)]

    own = chunk(0)
    lane = lanes((1, pitch))
    first = (axial - 1) * SEGMENT_LANES
    edge = jnp.where(lane < first + EDGE, pltpu.roll(chunk(-1), (first + EDGE) % pitch, 1), pltpu.roll(own, (first + EDGE) % pitch, 1))
    edge = jnp.where(lane < first + 2 * EDGE, edge, pltpu.roll(own, (first + 3 * EDGE) % pitch, 1))
    edge = jnp.where(lane < first + 3 * EDGE, edge, pltpu.roll(chunk(1), (first + 3 * EDGE) % pitch, 1))

    def upright(cells):
        wide = jnp.broadcast_to(cells.astype(jnp.float32), (pitch, pitch))
        return jnp.transpose(wide).astype(jnp.int32)

    edge_cells = upright(edge)[first:first + SEGMENT_LANES]
    at_cells = jnp.concatenate([upright(own), edge_cells], 0)
    _, mode, _ = column(lanes(at_cells.shape))
    blades = [picked(blades_ref[...], face + n) for n in range(2)]
    cos_table, sin_table = waves(mode_number(mode, blades) * at_cells, length)
    for c in range(components):
        row_cos = jnp.zeros((1, pitch), jnp.float32)
        row_sin = jnp.zeros((1, pitch), jnp.float32)
        for b in range(components):
            at = b * components + c
            row_cos = jnp.where(component == b, with_cos[at:at + 1], row_cos)
            row_sin = jnp.where(component == b, with_sin[at:at + 1], row_sin)
        part = row_cos * cos_table + row_sin * sin_table
        for n, value in enumerate(split(part)):
            synth_ref[n, pl.ds(c * pitch, pitch), :] = value[:pitch]
            synth_ref[n, pl.ds(components * pitch + c * SEGMENT_LANES, SEGMENT_LANES), :] = value[pitch:]
    used = components * (pitch + SEGMENT_LANES)
    rest = synth_ref.shape[1] - used
    if rest:
        synth_ref[:, pl.ds(used, rest), :] = jnp.zeros((2, rest, pitch), jnp.bfloat16)


def jacobian(jac_ref, components, b, c, d):
    return jac_ref[pl.ds((b * components + c) * 6 + d, 1), :]


def mixed(jac_ref, source, couplings, neighbours):
    total = list(source)
    jac = functools.partial(jacobian, jac_ref, len(total))
    for d, neighbour in enumerate(neighbours):
        if neighbour is None:
            continue
        for c in range(len(total)):
            term = jac(0, c, d) * neighbour[0]
            for b in range(1, len(total)):
                term = term + jac(b, c, d) * neighbour[b]
            total[c] = total[c] + couplings[d] * term
    return total


def layer_update(jac_ref, state_ref, edge_ref, coef_ref, t, a, height):
    _, components, axial, wide, pitch = state_ref.shape
    lane = lanes((height, pitch))
    start = a * SEGMENT_LANES
    own = [state_ref[t, c, a] for c in range(components)]
    above = [state_ref[t, c, a + 1, :height] for c in range(components)] if a < axial - 1 else None
    below = [state_ref[t, c, a - 1, :height] for c in range(components)] if a else None
    edge = [edge_ref[t, c, :height] for c in range(components)]
    span_next = [pltpu.roll(x, wide - 1, 0)[:height] for x in own]
    span_prev = [pltpu.roll(x, 1, 0)[:height] for x in own]
    own = [x[:height] for x in own]
    to_end = (pitch - 1 - (start + 3 * EDGE)) % pitch
    to_begin = (pitch - (start + EDGE - 1)) % pitch
    pitch_next = [
        jnp.where(lane == pitch - 1, pltpu.roll(e, to_end, 1), pltpu.roll(x, pitch - 1, 1))
        for e, x in zip(edge, own)
    ]
    pitch_prev = [
        jnp.where(lane == 0, pltpu.roll(e, to_begin, 1), pltpu.roll(x, 1, 1))
        for e, x in zip(edge, own)
    ]
    source = [coef_ref[c, a, :height] for c in range(components)]
    couplings = [coef_ref[components + d, a, :height] for d in range(6)]
    return mixed(jac_ref, source, couplings, (above, below, span_next, span_prev, pitch_next, pitch_prev))


def edge_update(jac_ref, edge_ref, edge_coef_ref, t, axial):
    components, wide, pitch = edge_ref.shape[1:]
    lane = lanes((wide, pitch))
    own = [edge_ref[t, c] for c in range(components)]
    above = [jnp.where(lane < (axial - 1) * SEGMENT_LANES, pltpu.roll(x, pitch - SEGMENT_LANES, 1), 0.0) for x in own]
    below = [jnp.where(lane >= SEGMENT_LANES, pltpu.roll(x, SEGMENT_LANES, 1), 0.0) for x in own]
    span_next = [pltpu.roll(x, wide - 1, 0) for x in own]
    span_prev = [pltpu.roll(x, 1, 0) for x in own]
    pitch_next = [pltpu.roll(x, pitch - 1, 1) for x in own]
    pitch_prev = [pltpu.roll(x, 1, 1) for x in own]
    source = [edge_coef_ref[c] for c in range(components)]
    couplings = [edge_coef_ref[components + d] for d in range(6)]
    return mixed(jac_ref, source, couplings, (above, below, span_next, span_prev, pitch_next, pitch_prev))


def edge_boundary(field, c, components, pitch, axial):
    at = components * pitch + c * SEGMENT_LANES
    tile = field[:, (at // pitch) * pitch:(at // pitch + 1) * pitch]
    return pltpu.roll(tile, ((axial - 1) * SEGMENT_LANES - at % pitch) % pitch, 1)


def advance(refs, t, a, height=None):
    state_ref = refs[1]
    height = height or state_ref.shape[3]
    for c, value in enumerate(layer_update(*refs, t, a, height)):
        state_ref[t + 1, c, a, :height] = value


def first_kernel(
    jac_ref, state_in_ref, coef_in_ref, inv_in_ref, edges_ref, span_ref, inner_ref, outer_ref, table_ref,
    coef_ref, inv_ref, edge_coef_ref, state_ref, edge_ref, modes_ref, part_ref, *, groups,
):
    _, components, axial, wide, pitch = state_ref.shape
    span = wide - EDGE
    side = lax.axis_index("span")
    fields = 2 * components + 6
    line = rows((EDGE, pitch))
    keep_half = jnp.where(side == 0, line, EDGE - 1 - line) < HALF
    fifth = jnp.where(side == 0, HALF, HALF - 1)
    from_low, from_high = half_rows(1 - side)
    pairs = -(-(fields * axial + 1) // 2)

    def ghost(n):
        value = pltpu.roll(span_ref[n // 2], from_high if n % 2 else from_low, 0)
        value = jnp.where(keep_half, value, 0.0)
        if n < components * axial:
            extra = pltpu.roll(span_ref[pairs + n // EDGE], lax.rem(fifth + EDGE - n % EDGE, EDGE), 0)
            value = jnp.where(line == fifth, extra, value)
        return value

    even = lax.rem(lax.axis_index("pitch"), 2) == 0

    def group(ref, g):
        corner = ref[pl.ds(groups * span + g * EDGE, EDGE), :]
        return jnp.concatenate([ref[pl.ds(g * span, span), :], corner], 0)

    halves = [(group(inner_ref, g), group(outer_ref, g)) for g in range(groups)]
    from_left = [jnp.where(even, outer, inner) for inner, outer in halves]
    from_right = [jnp.where(even, inner, outer) for inner, outer in halves]
    near, far = slots(fields + 1, components)
    keep_five = keep_half | (line == fifth)
    for f in range(fields + 1):
        if f < fields:
            layers = [ghost(f * axial + a) for a in range(axial)]
        else:
            layers = [jnp.zeros((EDGE, pitch), jnp.float32)] * (axial - 1) + [ghost(fields * axial)]
        if f < components:
            for a in range(axial):
                state_ref[0, f, a, span:] = layers[a]
        elif f < fields:
            for a in range(axial):
                coef_ref[f - components, a, span:] = layers[a]
        else:
            inv_ref[span:] = layers[-1]
        g, at = near[f]
        value = jnp.concatenate([edges_ref[f], to_edges(layers, pitch)], 0)
        lane = lanes((wide, pitch)) % SEGMENT_LANES
        value = jnp.where((lane >= HALF) & (lane < EDGE), pltpu.roll(from_left[g], (HALF - at) % pitch, 1), value)
        value = jnp.where(
            (lane >= 3 * EDGE) & (lane < 3 * EDGE + HALF),
            pltpu.roll(from_right[g], (3 * EDGE - at) % pitch, 1), value,
        )
        if f < components:
            g, at = far[f]
            value = jnp.where(lane == HALF - 1, pltpu.roll(from_left[g], (HALF - 1 - at) % pitch, 1), value)
            value = jnp.where(
                lane == 3 * EDGE + HALF, pltpu.roll(from_right[g], (3 * EDGE + HALF - at) % pitch, 1), value,
            )
        target, at = (edge_ref.at[0], f) if f < components else (edge_coef_ref, f - components)
        target[at, :span] = value[:span]
        target[at, span:] = jnp.where(keep_five if f < components else keep_half, value[span:], 0.0)
    refs = (jac_ref, state_ref, edge_ref, coef_ref)
    for t in range(axial):
        for a in range(axial - t):
            advance(refs, t, a)
        if t < axial - 1:
            for c, value in enumerate(edge_update(jac_ref, edge_ref, edge_coef_ref, t, axial)):
                edge_ref[t + 1, c] = value
    strips = [
        jnp.concatenate([state_ref[t, c, 0] for t in range(1, axial)] + [state_ref[axial, c, 0, :span]], 0)
        for c in range(components)
    ]
    total = projected(strips, table_ref)
    ghosts = jnp.zeros((EDGE, pitch), jnp.float32)
    for t in range(1, axial):
        part = total[(t - 1) * wide:t * wide]
        modes_ref[pl.ds((t - 1) * span, span), :] = part[:span]
        keep, to_packed, _ = ghost_rows(side, t, axial)
        ghosts = jnp.where(keep, pltpu.roll(part[span:], to_packed, 0), ghosts)
    modes_ref[pl.ds((axial - 1) * span, EDGE), :] = ghosts
    part_ref[...] = total[(axial - 1) * wide:]


def ghost_rows(side, t, axial):
    line = rows((EDGE, 1))
    distance = jnp.where(side == 0, line, EDGE - 1 - line)
    start = sum(axial - n for n in range(1, t))
    to_packed = jnp.where(side == 0, start, (EDGE - start) % EDGE)
    from_packed = jnp.where(side == 0, (EDGE - start) % EDGE, start)
    return (distance >= start) & (distance < start + axial - t), to_packed, from_packed


def along_axis(jac_ref, coef_ref, delta, a, height):
    components = len(delta)
    out = []
    for c in range(components):
        term = jacobian(jac_ref, components, 0, c, 0) * delta[0]
        for b in range(1, components):
            term = term + jacobian(jac_ref, components, b, c, 0) * delta[b]
        out.append(coef_ref[components, a, :height] * term)
    return out


def late_kernel(
    jac_ref, coef_ref, inv_ref, part_ref, more_ref, modes_b_ref, modes_a_ref, synth_ref, table_ref, modes_ref,
):
    span, pitch = part_ref.shape
    components, axial = coef_ref.shape[0] - 6, coef_ref.shape[1]
    field = synthesised(modes_a_ref[EDGE:] + modes_b_ref[EDGE:], synth_ref, components * pitch)
    delta = [inv_ref[:span] * field[:, c * pitch:(c + 1) * pitch] for c in range(components)]
    for a in range(axial - 2, -1, -1):
        delta = along_axis(jac_ref, coef_ref, delta, a, span)
    before = more_ref.shape[0]
    modes_ref[:before] = more_ref[...]
    modes_ref[before:] = part_ref[...] + projected(delta, table_ref)


def between_kernel(
    jac_ref, coef_ref, inv_ref, edge_coef_ref, state_in_ref, edge_in_ref, modes_b_ref, modes_a_ref, synth_ref, more_ref,
    state_ref, edge_ref, sent_ref,
):
    sent_ref[...] = more_ref[...]
    components, axial = state_ref.shape[1], state_ref.shape[2]
    wide, pitch = state_ref.shape[3:]
    modes = modes_a_ref[...] + modes_b_ref[...]
    field = synthesised(jnp.concatenate([modes[EDGE:], modes[:EDGE]], 0), synth_ref, synth_ref.shape[1])
    delta = [inv_ref[...] * field[:, c * pitch:(c + 1) * pitch] for c in range(components)]
    for t in range(1, axial + 1):
        for c in range(components):
            state_ref[t, c, axial - t] += delta[c]
        if t < axial:
            delta = along_axis(jac_ref, coef_ref, delta, axial - 1 - t, wide)
    for c in range(components):
        edge_ref[1, c] += edge_coef_ref[components + 6] * edge_boundary(field, c, components, pitch, axial)
    diagonal_sweeps(jac_ref, state_ref, edge_ref, coef_ref, edge_coef_ref, 1, axial // 2 + 1)


def beside_kernel(jac_ref, coef_ref, edge_coef_ref, state_in_ref, edge_in_ref, state_ref, edge_ref):
    axial, span = state_ref.shape[2], state_ref.shape[3] - EDGE
    diagonal_sweeps(jac_ref, state_ref, edge_ref, coef_ref, edge_coef_ref, axial // 2 + 1, axial)
    advance((jac_ref, state_ref, edge_ref, coef_ref), axial, 0, span)


def diagonal_sweeps(jac_ref, state_ref, edge_ref, coef_ref, edge_coef_ref, first, last):
    axial = state_ref.shape[2]
    for t in range(first, last):
        advance((jac_ref, state_ref, edge_ref, coef_ref), t, axial - t)
        for c, value in enumerate(edge_update(jac_ref, edge_ref, edge_coef_ref, t, axial)):
            edge_ref[t + 1, c] = value


def second_kernel(
    jac_ref, coef_ref, inv_ref, edge_coef_ref, state_in_ref, edge_in_ref, more_a_ref, more_b_ref, synth_ref,
    state_ref, edge_ref, out_ref, bound_ref,
):
    components, axial, span, pitch = out_ref.shape
    wide = span + EDGE
    side = lax.axis_index("span")
    more = more_a_ref[...] + more_b_ref[...]
    start = (axial - 1) * span
    parts = []
    for t in range(1, axial):
        _, _, from_packed = ghost_rows(side, t, axial)
        parts += [more[(t - 1) * span:t * span], pltpu.roll(more[start:start + EDGE], from_packed, 0)]
    field = synthesised(jnp.concatenate(parts + [more[start + EDGE:]], 0), synth_ref, synth_ref.shape[1])
    for t in range(1, axial):
        part = field[(t - 1) * wide:t * wide]
        for c in range(components):
            bound_ref[t, c] = inv_ref[...] * part[:, c * pitch:(c + 1) * pitch]
    for c in range(components):
        bound_ref[axial, c, :span] = inv_ref[:span] * field[(axial - 1) * wide:, c * pitch:(c + 1) * pitch]
    delta = [bound_ref[1, c] for c in range(components)]
    for t in range(2, axial + 2):
        height = wide if t <= axial else span
        for c in range(components):
            state_ref[t, c, axial + 1 - t, :height] += delta[c][:height]
        if t < axial + 1:
            delta = along_axis(jac_ref, coef_ref, delta, axial - t, wide)
    for t in range(1, axial):
        if t > 1:
            for c, value in enumerate(edge_update(jac_ref, edge_ref, edge_coef_ref, t, axial)):
                edge_ref[t + 1, c] = value
        part = field[(t - 1) * wide:t * wide]
        for c in range(components):
            edge_ref[t + 1, c] += edge_coef_ref[components + 6] * edge_boundary(part, c, components, pitch, axial)
    refs = (jac_ref, state_ref, edge_ref, coef_ref)

    for t in range(2, axial):
        for a in range(axial + 1 - t, axial):
            advance(refs, t, a)
        for c in range(components):
            state_ref[t + 1, c, axial - 1] += bound_ref[t, c]
    for a in range(1, axial):
        for c, value in enumerate(layer_update(*refs, axial, a, span)):
            out_ref[c, a] = value + bound_ref[axial, c, :span] if a == axial - 1 else value
    for c in range(components):
        out_ref[c, 0] = state_ref[axial + 1, c, 0, :span]


def moved(x, to):
    sizes = [lax.axis_size(name) for name in AXES]
    pairs = []
    for r in range(sizes[0]):
        for s in range(sizes[1]):
            for p in range(sizes[2]):
                target = to(r, s, p)
                if all(0 <= at < size for at, size in zip(target, sizes)):
                    number = lambda at: (at[0] * sizes[1] + at[1]) * sizes[2] + at[2]
                    pairs.append((number((r, s, p)), number(target)))
    return lax.ppermute(x, AXES, pairs)


def struct(*shape):
    return jax.ShapeDtypeStruct(shape, jnp.float32)


def on_device(
    adjoint_start, source, couplings, damping, jacobians, giles_real, giles_imag, blades, mode_orders, cell_map,
):
    components, axial, span, pitch = adjoint_start.shape
    row_count, span_count, place_count = (lax.axis_size(name) for name in AXES)
    length = pitch * place_count
    assert sum(axial - t for t in range(1, axial)) <= EDGE
    assert components == COMPONENTS and components * WAVES <= pitch
    assert axial == ITERS - 1 and ITERS <= EDGE and axial * SEGMENT_LANES == pitch
    assert span_count == 2 and place_count > 2 and place_count & (place_count - 1) == 0
    wide = span + EDGE
    fields = 2 * components + 6
    groups = slots(fields + 1, components)[1][-1][0] + 1
    pairs = -(-(fields * axial + 1) // 2)
    span_tiles = pairs + -(-components * axial // EDGE)
    vmem = pl.BlockSpec(memory_space=pltpu.VMEM)
    hbm = pl.BlockSpec(memory_space=pltpu.HBM)

    def in_hbm(x):
        return pltpu.with_memory_space_constraint(x, pltpu.HBM)

    def call(kernel, name, outs, ins, aliases=None, scratch=(), limit=40 * MIB, **fixed):
        specs = [spec for spec, _ in ins]
        return pl.pallas_call(
            functools.partial(kernel, **fixed),
            out_shape=outs,
            in_specs=specs,
            out_specs=jax.tree.map(lambda _: vmem, outs),
            scratch_shapes=scratch,
            input_output_aliases=aliases or {},
            compiler_params=params(limit),
            name=name,
        )(*[value for _, value in ins])

    tables = (
        jacobians.transpose(2, 3, 0, 1), giles_real.transpose(2, 3, 0, 1), giles_imag.transpose(2, 3, 0, 1),
        mode_orders.transpose(0, 2, 1), cell_map,
    )
    blades = blades.reshape(1, -1)
    corner_rows = groups * EDGE
    state_shape = struct(axial + 2, components, axial, wide, pitch)
    state, coef, inv, span_out, small, modes, table, blades, *tables = call(
        start_kernel, "start",
        (
            state_shape, struct(components + 6, axial, wide, pitch), struct(wide, pitch),
            struct(span_tiles, EDGE, pitch), struct(2 * corner_rows + EDGE, pitch), struct(wide, pitch),
            jax.ShapeDtypeStruct((2, components * pitch, pitch), jnp.bfloat16),
            *(jax.ShapeDtypeStruct(x.shape, x.dtype) for x in (blades, *tables)),
        ),
        [(hbm, in_hbm(x)) for x in (adjoint_start, source, couplings, damping, blades, *tables)],
        scratch=[
            pltpu.VMEM(source.shape, jnp.float32), pltpu.VMEM(couplings.shape, jnp.float32),
            pltpu.VMEM(damping.shape, jnp.float32), pltpu.SemaphoreType.DMA((5 + len(tables),)),
        ],
        groups=groups, length=length,
    )
    edges, inner, outer = call(
        pack_kernel, "pack",
        (struct(fields + 1, span, pitch), struct((groups + 1) * wide, pitch), struct(groups * wide, pitch)),
        [(vmem, x) for x in (state, coef, inv)],
    )
    steps = [1 << n for n in range(place_count.bit_length() - 2)]
    last_step = place_count // 2

    def near(x):
        return moved(x, lambda r, s, p: (r - 1, s, p))

    def far(x):
        return moved(x, lambda r, s, p: (r - 1, s, p ^ last_step))

    modes, edges = lax.optimization_barrier((near(modes), edges))
    small = lax.dynamic_update_slice(small, modes[span:], (corner_rows, 0))
    small, span_out = lax.optimization_barrier((small, span_out))
    small = moved(small, lambda r, s, p: (r, 1 - s, p))
    from_span = moved(span_out, lambda r, s, p: (r, 1 - s, p))
    inner = lax.dynamic_update_slice(inner, modes[:span], (groups * wide + EDGE, 0))
    synth, jac = call(
        synth_kernel, "synth",
        (
            jax.ShapeDtypeStruct(
                (2, -(-components * (pitch + SEGMENT_LANES) // pitch) * pitch, pitch), jnp.bfloat16
            ),
            struct(-(-6 * components * components // EDGE) * EDGE, pitch),
        ),
        [(vmem, x) for x in (blades, *tables)],
        scratch=[pltpu.VMEM((2, components * components, mode_orders.shape[1]), jnp.float32)],
        row_count=row_count, place_count=place_count, components=components, pitch=pitch, length=length, axial=axial,
    )
    edge_shape = struct(axial + 1, components, wide, pitch)
    inner = lax.dynamic_update_slice(inner, small[:corner_rows + EDGE], (groups * span, 0))
    outer = lax.dynamic_update_slice(outer, small[corner_rows + EDGE:], (groups * span, 0))
    modes = inner[groups * span + corner_rows:]
    outer = moved(outer, lambda r, s, p: (r, s, (p - 1 + 2 * (p % 2)) % place_count))
    inner = moved(inner, lambda r, s, p: (r, s, p ^ 1))
    modes = modes + inner[groups * span + corner_rows:]
    for step in steps[1:]:
        modes = modes + moved(modes, lambda r, s, p: (r, s, p ^ step))
    modes_a, modes_b = modes, moved(modes, lambda r, s, p: (r, s, p ^ last_step))

    coef, inv, edge_coef, state, edge, more, part = call(
        first_kernel, "first_sweeps",
        (
            struct(components + 6, axial, wide, pitch), struct(wide, pitch), struct(components + 7, wide, pitch),
            state_shape, edge_shape,
            struct((axial - 1) * span + EDGE, pitch), struct(span, pitch),
        ),
        [(vmem, jac)] + [(vmem, x) for x in (state, coef, inv, edges, from_span, inner, outer, table)],
        aliases={1: 3, 2: 0, 3: 1},
        groups=groups,
    )

    more_shape = struct(axial * span + EDGE, pitch)
    more = call(
        late_kernel, "late_modes", more_shape,
        [(vmem, x) for x in (jac, coef, inv, part, more, modes_b, modes_a, synth, table)],
    )
    state, edge, sent = call(
        between_kernel, "between_sweeps", (state_shape, edge_shape, more_shape),
        [(vmem, x) for x in (jac, coef, inv, edge_coef, state, edge, modes_b, modes_a, synth, more)],
        aliases={4: 0, 5: 1},
    )
    state, edge = call(
        beside_kernel, "beside_sweeps", (state_shape, edge_shape),
        [(vmem, x) for x in (jac, coef, edge_coef, state, edge)],
        aliases={3: 0, 4: 1},
    )
    for step in steps:
        got = moved(more, lambda r, s, p: (r, s, p ^ step))
        more, sent = sent + got, sent + got
    more_b = far(more)
    more_a = near(more)
    return call(
        second_kernel, "second_sweeps", (state_shape, edge_shape, struct(components, axial, span, pitch)),
        [(vmem, x) for x in (jac, coef, inv, edge_coef, state, edge, more_a, more_b, synth)],
        aliases={4: 0, 5: 1},
        scratch=[pltpu.VMEM((axial + 1, components, wide, pitch), jnp.float32)],
    )[2]


def solution(mesh):
    placed = (
        P(None, "row", "span", "pitch"),
        P(None, "row", "span", "pitch"),
        P(None, "row", "span", "pitch"),
        P("row", "span", "pitch"),
        P("row", None, None, None),
        P(),
        P(),
        P(),
        P(),
        P("row", None),
    )
    return jax.shard_map(
        on_device,
        mesh=mesh,
        in_specs=placed,
        out_specs=P(None, "row", "span", "pitch"),
        check_vma=False,
    )
```

```python
import functools
import math

import jax
import jax.numpy as jnp
from jax import lax
from jax.experimental import pallas as pl
from jax.experimental.pallas import tpu as pltpu
from jax.sharding import PartitionSpec as P

ITERS = 5
AXES = ("row", "span", "pitch")

ORDER_MAX = 2
BASE = 2 * ORDER_MAX + 1
COSINES = (BASE * BASE + 1) // 2
WAVES = 2 * COSINES - 1
COMPONENTS = 5
EDGE = 8
HALF = EDGE // 2
SEGMENT_LANES = 4 * EDGE
EXACT = lax.Precision.HIGHEST
MIB = 1024 * 1024


def params(limit):
    return pltpu.CompilerParams(vmem_limit_bytes=limit)


def lanes(shape):
    return lax.broadcasted_iota(jnp.int32, shape, len(shape) - 1)


def rows(shape):
    return lax.broadcasted_iota(jnp.int32, shape, len(shape) - 2)


def column(j):
    component = (j * 41) >> 10
    wave = j - WAVES * component
    sine = wave >= COSINES
    return component, jnp.where(sine, wave - (COSINES - 1), wave), sine


def mode_number(mode, blades):
    high = ((mode + ORDER_MAX) * 13) >> 6
    low = mode - BASE * high
    return high * blades[0] + low * blades[1]


def waves(products, length):
    if length & (length - 1) == 0:
        phase = products & (length - 1)
    else:
        phase = jnp.mod(products, length)
    turn = phase.astype(jnp.float32) * (1.0 / length)
    quarter = jnp.floor(4.0 * turn + 0.5)
    x = (turn - 0.25 * quarter) * (2.0 * math.pi)
    y = x * x
    sine = x * (1.0 + y * (-1.0 / 6 + y * (1.0 / 120 + y * (-1.0 / 5040 + y * (1.0 / 362880)))))
    cosine = 1.0 + y * (-0.5 + y * (1.0 / 24 + y * (-1.0 / 720 + y * (1.0 / 40320 - y * (1.0 / 3628800)))))
    quarter = quarter.astype(jnp.int32) & 3
    odd = (quarter & 1) == 1
    cos_out = jnp.where(odd, sine, cosine)
    sin_out = jnp.where(odd, cosine, sine)
    cos_out = jnp.where((quarter == 1) | (quarter == 2), -cos_out, cos_out)
    sin_out = jnp.where(quarter >= 2, -sin_out, sin_out)
    return cos_out, sin_out


def to_edges(layers, pitch):
    lane = lanes(layers[-1].shape)
    block = jnp.zeros_like(layers[-1])
    for a, layer in enumerate(layers):
        if layer is None:
            continue
        start = a * SEGMENT_LANES
        first = pltpu.roll(layer, (start + EDGE) % pitch, layer.ndim - 1)
        last = pltpu.roll(layer, (start + 3 * EDGE) % pitch, layer.ndim - 1)
        block = jnp.where((lane >= start + EDGE) & (lane < start + 2 * EDGE), first, block)
        block = jnp.where((lane >= start + 2 * EDGE) & (lane < start + 3 * EDGE), last, block)
    return block


def half_rows(side):
    return jnp.where(side == 0, EDGE // 2, 0), jnp.where(side == 0, 0, EDGE // 2)


def slots(fields, components):
    per_group = SEGMENT_LANES // HALF
    near = [(f // per_group, f % per_group * HALF) for f in range(fields)]
    group, lane = near[-1]
    far = [(group, lane + HALF + c) for c in range(components)]
    return near, far


def packed_edges(blocks, place, components):
    near, far = slots(len(blocks), components)
    pitch = blocks[0].shape[1]
    lane = lanes(blocks[0].shape) % SEGMENT_LANES
    sides = []
    for near_at, far_at in ((3 * EDGE - HALF, 3 * EDGE - HALF - 1), (EDGE, EDGE + HALF)):
        packed = [jnp.zeros_like(blocks[0]) for _ in range(far[-1][0] + 1)]
        for f, (g, to) in enumerate(near):
            value = pltpu.roll(blocks[f], (to - near_at) % pitch, 1)
            packed[g] = jnp.where((lane >= to) & (lane < to + HALF), value, packed[g])
        for f, (g, to) in enumerate(far):
            packed[g] = jnp.where(lane == to, pltpu.roll(blocks[f], (to - far_at) % pitch, 1), packed[g])
        sides.append(packed)
    even = lax.rem(place, 2) == 0
    inner = [jnp.where(even, right, left) for right, left in zip(*sides)]
    outer = [jnp.where(even, left, right) for right, left in zip(*sides)]
    return inner, outer


def edge_blocks(state_ref, coef_ref, inv_ref, at):
    components, axial, pitch = state_ref.shape[1], state_ref.shape[2], state_ref.shape[4]
    blocks = [to_edges([state_ref[0, c, a, at, :] for a in range(axial)], pitch) for c in range(components)]
    blocks += [to_edges([coef_ref[f, a, at, :] for a in range(axial)], pitch) for f in range(components + 6)]
    return blocks + [to_edges([None] * (axial - 1) + [inv_ref[at, :]], pitch)]


def start_kernel(
    adjoint_hbm, source_hbm, couplings_hbm, damping_hbm, blades_hbm, *refs, groups, length,
):
    state_ref, coef_ref, inv_ref, span_ref, small_ref, modes_ref, table_ref, blades_ref = refs[5:13]
    source_ref, couplings_ref, damping_ref, sems = refs[18:]
    components, axial, span, pitch = source_ref.shape
    adjoint_ref = state_ref.at[0, :, :, pl.ds(0, span), :]
    copies = [
        pltpu.make_async_copy(src, dst, sems.at[n])
        for n, (src, dst) in enumerate((
            (couplings_hbm, couplings_ref), (damping_hbm, damping_ref), (source_hbm, source_ref),
            (adjoint_hbm, adjoint_ref), (blades_hbm, blades_ref), *zip(refs[:5], refs[13:18]),
        ))
    ]
    for copy in copies:
        copy.start()
    row, side, place = (lax.axis_index(name) for name in AXES)
    copies[4].wait()
    face = jnp.maximum(row - 1, 0)
    component, mode, sine = column(lanes((pitch, pitch)))
    number = mode_number(mode, [picked(blades_ref[...], face + n) for n in range(2)])
    cos_table, sin_table = waves(number * (place * pitch + rows((pitch, pitch))), length)
    table = jnp.where(component < components, jnp.where(sine, sin_table, cos_table), 0.0)
    for c in range(components):
        for n, value in enumerate(split(jnp.where(component == c, table, 0.0))):
            table_ref[n, pl.ds(c * pitch, pitch), :] = value
    copies[0].wait()
    copies[1].wait()
    diag = damping_ref[...]
    for d in range(6):
        diag = diag + couplings_ref[d]
    inverse = 1.0 / diag
    for d in range(6):
        coef_ref[components + d, :, :span] = couplings_ref[d] * inverse
    inv_ref[:span] = inverse[axial - 1]
    copies[2].wait()
    for c in range(components):
        coef_ref[c, :, :span] = source_ref[c] * inverse
    copies[3].wait()
    edge_row = pl.multiple_of(jnp.where(side == 0, span - EDGE, 0), EDGE)
    blocks = edge_blocks(state_ref, coef_ref, inv_ref, pl.ds(edge_row, EDGE))
    for n, packed in enumerate(packed_edges(blocks, place, components)):
        for g, value in enumerate(packed):
            small_ref[pl.ds((n * (groups + 1) + g) * EDGE, EDGE), :] = value
    modes_ref[...] = projected([adjoint_ref[c, 0] for c in range(components)], table_ref)
    small_ref[pl.ds(groups * EDGE, EDGE), :] = modes_ref[pl.ds(edge_row, EDGE), :]

    to_low, to_high = half_rows(side)
    line = rows((EDGE, pitch))
    tiles = [state_ref[0, c, a, pl.ds(edge_row, EDGE), :] for c in range(components) for a in range(axial)]
    tiles += [coef_ref[f, a, pl.ds(edge_row, EDGE), :] for f in range(components + 6) for a in range(axial)]
    tiles += [inv_ref[pl.ds(edge_row, EDGE), :]]
    pairs = -(-len(tiles) // 2)
    for n in range(pairs):
        value = pltpu.roll(tiles[2 * n], to_low, 0)
        if 2 * n + 1 < len(tiles):
            value = jnp.where(line < HALF, value, pltpu.roll(tiles[2 * n + 1], to_high, 0))
        span_ref[n] = value
    fifth = jnp.where(side == 0, HALF - 1, HALF)
    for n in range(span_ref.shape[0] - pairs):
        value = jnp.zeros((EDGE, pitch), jnp.float32)
        for k in range(min(EDGE, components * axial - n * EDGE)):
            value = jnp.where(line == k, pltpu.roll(tiles[n * EDGE + k], lax.rem(k + EDGE - fifth, EDGE), 0), value)
        span_ref[pairs + n] = value
    for copy in copies[5:]:
        copy.wait()


def pack_kernel(state_ref, coef_ref, inv_ref, modes_ref, edges_ref, inner_ref, outer_ref, *, groups):
    _, components, axial, wide, pitch = state_ref.shape
    span = wide - EDGE
    place = lax.axis_index("pitch")
    blocks = edge_blocks(state_ref, coef_ref, inv_ref, pl.ds(0, span))
    for f, block in enumerate(blocks):
        edges_ref[f] = block
    for out_ref, packed in zip((inner_ref, outer_ref), packed_edges(blocks, place, components)):
        for g, value in enumerate(packed):
            out_ref[pl.ds(g * span, span), :] = value
    start = groups * span + (groups + 1) * EDGE
    inner_ref[pl.ds(start, span), :] = modes_ref[...]


def picked(values, at):
    chosen = jnp.where(lanes(values.shape) == at, values.astype(jnp.float32), 0.0)
    return jnp.sum(chosen, axis=1, keepdims=True).astype(jnp.int32)


def split(x):
    high = x.astype(jnp.bfloat16)
    return high, (x - high.astype(jnp.float32)).astype(jnp.bfloat16)


def product(x, table, dims):
    x_high, x_low = split(x)
    table_high, table_low = table
    dot = functools.partial(lax.dot_general, dimension_numbers=(dims, ((), ())), preferred_element_type=jnp.float32)
    return dot(x_high, table_high) + (dot(x_low, table_high) + dot(x_high, table_low))


def projected(strips, table_ref):
    return product(jnp.concatenate(strips, 1), (table_ref[0], table_ref[1]), ((1,), (0,)))


def synthesised(modes, synth_ref, count):
    return product(modes, (synth_ref[0, :count], synth_ref[1, :count]), ((1,), (1,)))


def synth_kernel(
    blades_ref, jacobians_ref, giles_re_ref, giles_im_ref, orders_ref, cells_ref, synth_ref, rows_ref, sums_ref,
    *, row_count, place_count, components, pitch, length, axial,
):
    row, place = lax.axis_index("row"), lax.axis_index("pitch")
    face = jnp.minimum(row, row_count - 2)
    for b in range(components):
        for c in range(components):
            entries = jacobians_ref[b, c]
            for d in range(6):
                at = (b * components + c) * 6 + d
                rows_ref[pl.ds(at, 1), :] = jnp.broadcast_to(entries[:, d:d + 1], (1, pitch))
    modes = orders_ref.shape[2]
    orders = orders_ref[face]
    tag = BASE * orders[0:1] + orders[1:2]
    component, mode, _ = column(rows((pitch, modes)))
    same = (jnp.abs(tag) == mode) & (component < components)
    plain = jnp.where(same, 1.0, 0.0)
    signed = jnp.where(tag < 0, -plain, plain)
    dims = (((1,), (1,)), ((), ()))
    for n, ref in enumerate((giles_re_ref, giles_im_ref)):
        for b in range(components):
            for c in range(components):
                sums_ref[n, pl.ds(b * components + c, 1), :] = ref[b, c, pl.ds(face, 1), :]
    sums_re = lax.dot_general(sums_ref[0], plain, dims, precision=EXACT, preferred_element_type=jnp.float32)
    sums_im = lax.dot_general(sums_ref[1], signed, dims, precision=EXACT, preferred_element_type=jnp.float32)
    component, mode, sine = column(lanes(sums_re.shape))
    scale = 2.0 / length
    with_cos = jnp.where(sine, sums_im, sums_re) * scale
    with_sin = jnp.where(sine, sums_re, -sums_im) * scale
    component = component[0:1]

    def chunk(at):
        start = pl.multiple_of(lax.rem(place + at + place_count, place_count) * pitch, pitch)
        return cells_ref[:, pl.ds(start, pitch)]

    own = chunk(0)
    lane = lanes((1, pitch))
    first = (axial - 1) * SEGMENT_LANES
    edge = jnp.where(lane < first + EDGE, pltpu.roll(chunk(-1), (first + EDGE) % pitch, 1), pltpu.roll(own, (first + EDGE) % pitch, 1))
    edge = jnp.where(lane < first + 2 * EDGE, edge, pltpu.roll(own, (first + 3 * EDGE) % pitch, 1))
    edge = jnp.where(lane < first + 3 * EDGE, edge, pltpu.roll(chunk(1), (first + 3 * EDGE) % pitch, 1))

    def upright(cells):
        wide = jnp.broadcast_to(cells.astype(jnp.float32), (pitch, pitch))
        return jnp.transpose(wide).astype(jnp.int32)

    edge_cells = upright(edge)[first:first + SEGMENT_LANES]
    at_cells = jnp.concatenate([upright(own), edge_cells], 0)
    _, mode, _ = column(lanes(at_cells.shape))
    blades = [picked(blades_ref[...], face + n) for n in range(2)]
    cos_table, sin_table = waves(mode_number(mode, blades) * at_cells, length)
    for c in range(components):
        row_cos = jnp.zeros((1, pitch), jnp.float32)
        row_sin = jnp.zeros((1, pitch), jnp.float32)
        for b in range(components):
            at = b * components + c
            row_cos = jnp.where(component == b, with_cos[at:at + 1], row_cos)
            row_sin = jnp.where(component == b, with_sin[at:at + 1], row_sin)
        part = row_cos * cos_table + row_sin * sin_table
        for n, value in enumerate(split(part)):
            synth_ref[n, pl.ds(c * pitch, pitch), :] = value[:pitch]
            synth_ref[n, pl.ds(components * pitch + c * SEGMENT_LANES, SEGMENT_LANES), :] = value[pitch:]
    used = components * (pitch + SEGMENT_LANES)
    rest = synth_ref.shape[1] - used
    if rest:
        synth_ref[:, pl.ds(used, rest), :] = jnp.zeros((2, rest, pitch), jnp.bfloat16)


def jacobian(jac_ref, components, b, c, d):
    return jac_ref[pl.ds((b * components + c) * 6 + d, 1), :]


def mixed(jac_ref, source, couplings, neighbours):
    total = list(source)
    jac = functools.partial(jacobian, jac_ref, len(total))
    for d, neighbour in enumerate(neighbours):
        if neighbour is None:
            continue
        for c in range(len(total)):
            term = jac(0, c, d) * neighbour[0]
            for b in range(1, len(total)):
                term = term + jac(b, c, d) * neighbour[b]
            total[c] = total[c] + couplings[d] * term
    return total


def layer_update(jac_ref, state_ref, edge_ref, coef_ref, t, a, height):
    _, components, axial, wide, pitch = state_ref.shape
    lane = lanes((height, pitch))
    start = a * SEGMENT_LANES
    own = [state_ref[t, c, a] for c in range(components)]
    above = [state_ref[t, c, a + 1, :height] for c in range(components)] if a < axial - 1 else None
    below = [state_ref[t, c, a - 1, :height] for c in range(components)] if a else None
    edge = [edge_ref[t, c, :height] for c in range(components)]
    span_next = [pltpu.roll(x, wide - 1, 0)[:height] for x in own]
    span_prev = [pltpu.roll(x, 1, 0)[:height] for x in own]
    own = [x[:height] for x in own]
    to_end = (pitch - 1 - (start + 3 * EDGE)) % pitch
    to_begin = (pitch - (start + EDGE - 1)) % pitch
    pitch_next = [
        jnp.where(lane == pitch - 1, pltpu.roll(e, to_end, 1), pltpu.roll(x, pitch - 1, 1))
        for e, x in zip(edge, own)
    ]
    pitch_prev = [
        jnp.where(lane == 0, pltpu.roll(e, to_begin, 1), pltpu.roll(x, 1, 1))
        for e, x in zip(edge, own)
    ]
    source = [coef_ref[c, a, :height] for c in range(components)]
    couplings = [coef_ref[components + d, a, :height] for d in range(6)]
    return mixed(jac_ref, source, couplings, (above, below, span_next, span_prev, pitch_next, pitch_prev))


def edge_update(jac_ref, edge_ref, edge_coef_ref, t, axial):
    components, wide, pitch = edge_ref.shape[1:]
    lane = lanes((wide, pitch))
    own = [edge_ref[t, c] for c in range(components)]
    above = [jnp.where(lane < (axial - 1) * SEGMENT_LANES, pltpu.roll(x, pitch - SEGMENT_LANES, 1), 0.0) for x in own]
    below = [jnp.where(lane >= SEGMENT_LANES, pltpu.roll(x, SEGMENT_LANES, 1), 0.0) for x in own]
    span_next = [pltpu.roll(x, wide - 1, 0) for x in own]
    span_prev = [pltpu.roll(x, 1, 0) for x in own]
    pitch_next = [pltpu.roll(x, pitch - 1, 1) for x in own]
    pitch_prev = [pltpu.roll(x, 1, 1) for x in own]
    source = [edge_coef_ref[c] for c in range(components)]
    couplings = [edge_coef_ref[components + d] for d in range(6)]
    return mixed(jac_ref, source, couplings, (above, below, span_next, span_prev, pitch_next, pitch_prev))


def edge_boundary(field, c, components, pitch, axial):
    at = components * pitch + c * SEGMENT_LANES
    tile = field[:, (at // pitch) * pitch:(at // pitch + 1) * pitch]
    return pltpu.roll(tile, ((axial - 1) * SEGMENT_LANES - at % pitch) % pitch, 1)


def advance(refs, t, a, height=None):
    state_ref = refs[1]
    height = height or state_ref.shape[3]
    for c, value in enumerate(layer_update(*refs, t, a, height)):
        state_ref[t + 1, c, a, :height] = value


def first_kernel(
    jac_ref, state_in_ref, coef_in_ref, inv_in_ref, edges_ref, span_ref, inner_ref, outer_ref,
    coef_ref, inv_ref, edge_coef_ref, state_ref, edge_ref, *, groups,
):
    _, components, axial, wide, pitch = state_ref.shape
    span = wide - EDGE
    side = lax.axis_index("span")
    fields = 2 * components + 6
    line = rows((EDGE, pitch))
    keep_half = jnp.where(side == 0, line, EDGE - 1 - line) < HALF
    fifth = jnp.where(side == 0, HALF, HALF - 1)
    from_low, from_high = half_rows(1 - side)
    pairs = -(-(fields * axial + 1) // 2)

    def ghost(n):
        value = pltpu.roll(span_ref[n // 2], from_high if n % 2 else from_low, 0)
        value = jnp.where(keep_half, value, 0.0)
        if n < components * axial:
            extra = pltpu.roll(span_ref[pairs + n // EDGE], lax.rem(fifth + EDGE - n % EDGE, EDGE), 0)
            value = jnp.where(line == fifth, extra, value)
        return value

    even = lax.rem(lax.axis_index("pitch"), 2) == 0

    def group(ref, g):
        corner = ref[pl.ds(groups * span + g * EDGE, EDGE), :]
        return jnp.concatenate([ref[pl.ds(g * span, span), :], corner], 0)

    halves = [(group(inner_ref, g), group(outer_ref, g)) for g in range(groups)]
    from_left = [jnp.where(even, outer, inner) for inner, outer in halves]
    from_right = [jnp.where(even, inner, outer) for inner, outer in halves]
    near, far = slots(fields + 1, components)
    keep_five = keep_half | (line == fifth)
    for f in range(fields + 1):
        if f < fields:
            layers = [ghost(f * axial + a) for a in range(axial)]
        else:
            layers = [jnp.zeros((EDGE, pitch), jnp.float32)] * (axial - 1) + [ghost(fields * axial)]
        if f < components:
            for a in range(axial):
                state_ref[0, f, a, span:] = layers[a]
        elif f < fields:
            for a in range(axial):
                coef_ref[f - components, a, span:] = layers[a]
        else:
            inv_ref[span:] = layers[-1]
        g, at = near[f]
        value = jnp.concatenate([edges_ref[f], to_edges(layers, pitch)], 0)
        lane = lanes((wide, pitch)) % SEGMENT_LANES
        value = jnp.where((lane >= HALF) & (lane < EDGE), pltpu.roll(from_left[g], (HALF - at) % pitch, 1), value)
        value = jnp.where(
            (lane >= 3 * EDGE) & (lane < 3 * EDGE + HALF),
            pltpu.roll(from_right[g], (3 * EDGE - at) % pitch, 1), value,
        )
        if f < components:
            g, at = far[f]
            value = jnp.where(lane == HALF - 1, pltpu.roll(from_left[g], (HALF - 1 - at) % pitch, 1), value)
            value = jnp.where(
                lane == 3 * EDGE + HALF, pltpu.roll(from_right[g], (3 * EDGE + HALF - at) % pitch, 1), value,
            )
        target, at = (edge_ref.at[0], f) if f < components else (edge_coef_ref, f - components)
        target[at, :span] = value[:span]
        target[at, span:] = jnp.where(keep_five if f < components else keep_half, value[span:], 0.0)
    sweeps_without_boundaries(jac_ref, state_ref, edge_ref, coef_ref, edge_coef_ref, 0, 1)


def sweeps_without_boundaries(jac_ref, state_ref, edge_ref, coef_ref, edge_coef_ref, first, last):
    axial = state_ref.shape[2]
    for t in range(first, last):
        for a in range(axial - t):
            advance((jac_ref, state_ref, edge_ref, coef_ref), t, a)
        if t < axial - 1:
            for c, value in enumerate(edge_update(jac_ref, edge_ref, edge_coef_ref, t, axial)):
                edge_ref[t + 1, c] = value


def more_kernel(
    jac_ref, coef_ref, edge_coef_ref, state_in_ref, edge_in_ref, table_ref, state_ref, edge_ref, modes_ref, part_ref,
):
    _, components, axial, wide, pitch = state_ref.shape
    span = wide - EDGE
    side = lax.axis_index("span")
    sweeps_without_boundaries(jac_ref, state_ref, edge_ref, coef_ref, edge_coef_ref, 1, axial)
    strips = [
        jnp.concatenate([state_ref[t, c, 0] for t in range(1, axial)] + [state_ref[axial, c, 0, :span]], 0)
        for c in range(components)
    ]
    total = projected(strips, table_ref)
    ghosts = jnp.zeros((EDGE, pitch), jnp.float32)
    for t in range(1, axial):
        part = total[(t - 1) * wide:t * wide]
        modes_ref[pl.ds((t - 1) * span, span), :] = part[:span]
        keep, to_packed, _ = ghost_rows(side, t, axial)
        ghosts = jnp.where(keep, pltpu.roll(part[span:], to_packed, 0), ghosts)
    modes_ref[pl.ds((axial - 1) * span, EDGE), :] = ghosts
    part_ref[...] = total[(axial - 1) * wide:]


def ghost_rows(side, t, axial):
    line = rows((EDGE, 1))
    distance = jnp.where(side == 0, line, EDGE - 1 - line)
    start = sum(axial - n for n in range(1, t))
    to_packed = jnp.where(side == 0, start, (EDGE - start) % EDGE)
    from_packed = jnp.where(side == 0, (EDGE - start) % EDGE, start)
    return (distance >= start) & (distance < start + axial - t), to_packed, from_packed


def along_axis(jac_ref, coef_ref, delta, a, height):
    components = len(delta)
    out = []
    for c in range(components):
        term = jacobian(jac_ref, components, 0, c, 0) * delta[0]
        for b in range(1, components):
            term = term + jacobian(jac_ref, components, b, c, 0) * delta[b]
        out.append(coef_ref[components, a, :height] * term)
    return out


def late_kernel(
    jac_ref, coef_ref, inv_ref, part_ref, more_ref, first_ref, synth_ref, table_ref, modes_ref,
):
    span, pitch = part_ref.shape
    components, axial = coef_ref.shape[0] - 6, coef_ref.shape[1]
    field = synthesised(first_ref[EDGE:], synth_ref, components * pitch)
    delta = [inv_ref[:span] * field[:, c * pitch:(c + 1) * pitch] for c in range(components)]
    for a in range(axial - 2, -1, -1):
        delta = along_axis(jac_ref, coef_ref, delta, a, span)
    before = more_ref.shape[0]
    modes_ref[:before] = more_ref[...]
    modes_ref[before:] = part_ref[...] + projected(delta, table_ref)


def between_kernel(
    jac_ref, coef_ref, inv_ref, edge_coef_ref, state_in_ref, edge_in_ref, modes_ref, synth_ref, more_ref,
    state_ref, edge_ref, sent_ref,
):
    sent_ref[...] = more_ref[...]
    components, axial = state_ref.shape[1], state_ref.shape[2]
    wide, pitch = state_ref.shape[3:]
    modes = modes_ref[...]
    field = synthesised(jnp.concatenate([modes[EDGE:], modes[:EDGE]], 0), synth_ref, synth_ref.shape[1])
    delta = [inv_ref[...] * field[:, c * pitch:(c + 1) * pitch] for c in range(components)]
    for t in range(1, axial + 1):
        for c in range(components):
            state_ref[t, c, axial - t] += delta[c]
        if t < axial:
            delta = along_axis(jac_ref, coef_ref, delta, axial - 1 - t, wide)
    for c in range(components):
        edge_ref[1, c] += edge_coef_ref[components + 6] * edge_boundary(field, c, components, pitch, axial)
    diagonal_sweeps(jac_ref, state_ref, edge_ref, coef_ref, edge_coef_ref, 1, axial // 2 + 1)


def beside_kernel(jac_ref, coef_ref, edge_coef_ref, state_in_ref, edge_in_ref, state_ref, edge_ref):
    axial, span = state_ref.shape[2], state_ref.shape[3] - EDGE
    diagonal_sweeps(jac_ref, state_ref, edge_ref, coef_ref, edge_coef_ref, axial // 2 + 1, axial)
    advance((jac_ref, state_ref, edge_ref, coef_ref), axial, 0, span)


def diagonal_sweeps(jac_ref, state_ref, edge_ref, coef_ref, edge_coef_ref, first, last):
    axial = state_ref.shape[2]
    for t in range(first, last):
        advance((jac_ref, state_ref, edge_ref, coef_ref), t, axial - t)
        for c, value in enumerate(edge_update(jac_ref, edge_ref, edge_coef_ref, t, axial)):
            edge_ref[t + 1, c] = value


def second_kernel(
    jac_ref, coef_ref, inv_ref, edge_coef_ref, state_in_ref, edge_in_ref, more_a_ref, more_b_ref, synth_ref,
    state_ref, edge_ref, out_ref, bound_ref,
):
    components, axial, span, pitch = out_ref.shape
    wide = span + EDGE
    side = lax.axis_index("span")
    more = more_a_ref[...] + more_b_ref[...]
    start = (axial - 1) * span
    parts = []
    for t in range(1, axial):
        _, _, from_packed = ghost_rows(side, t, axial)
        parts += [more[(t - 1) * span:t * span], pltpu.roll(more[start:start + EDGE], from_packed, 0)]
    field = synthesised(jnp.concatenate(parts + [more[start + EDGE:]], 0), synth_ref, synth_ref.shape[1])
    for t in range(1, axial):
        part = field[(t - 1) * wide:t * wide]
        for c in range(components):
            bound_ref[t, c] = inv_ref[...] * part[:, c * pitch:(c + 1) * pitch]
    for c in range(components):
        bound_ref[axial, c, :span] = inv_ref[:span] * field[(axial - 1) * wide:, c * pitch:(c + 1) * pitch]
    delta = [bound_ref[1, c] for c in range(components)]
    for t in range(2, axial + 2):
        height = wide if t <= axial else span
        for c in range(components):
            state_ref[t, c, axial + 1 - t, :height] += delta[c][:height]
        if t < axial + 1:
            delta = along_axis(jac_ref, coef_ref, delta, axial - t, wide)
    for t in range(1, axial):
        if t > 1:
            for c, value in enumerate(edge_update(jac_ref, edge_ref, edge_coef_ref, t, axial)):
                edge_ref[t + 1, c] = value
        part = field[(t - 1) * wide:t * wide]
        for c in range(components):
            edge_ref[t + 1, c] += edge_coef_ref[components + 6] * edge_boundary(part, c, components, pitch, axial)
    refs = (jac_ref, state_ref, edge_ref, coef_ref)

    for t in range(2, axial):
        for a in range(axial + 1 - t, axial):
            advance(refs, t, a)
        for c in range(components):
            state_ref[t + 1, c, axial - 1] += bound_ref[t, c]
    for a in range(1, axial):
        for c, value in enumerate(layer_update(*refs, axial, a, span)):
            out_ref[c, a] = value + bound_ref[axial, c, :span] if a == axial - 1 else value
    for c in range(components):
        out_ref[c, 0] = state_ref[axial + 1, c, 0, :span]


def moved(x, to):
    sizes = [lax.axis_size(name) for name in AXES]
    pairs = []
    for r in range(sizes[0]):
        for s in range(sizes[1]):
            for p in range(sizes[2]):
                target = to(r, s, p)
                if all(0 <= at < size for at, size in zip(target, sizes)):
                    number = lambda at: (at[0] * sizes[1] + at[1]) * sizes[2] + at[2]
                    pairs.append((number((r, s, p)), number(target)))
    return lax.ppermute(x, AXES, pairs)


def struct(*shape):
    return jax.ShapeDtypeStruct(shape, jnp.float32)


def on_device(
    adjoint_start, source, couplings, damping, jacobians, giles_real, giles_imag, blades, mode_orders, cell_map,
):
    components, axial, span, pitch = adjoint_start.shape
    row_count, span_count, place_count = (lax.axis_size(name) for name in AXES)
    length = pitch * place_count
    assert sum(axial - t for t in range(1, axial)) <= EDGE
    assert components == COMPONENTS and components * WAVES <= pitch
    assert axial == ITERS - 1 and ITERS <= EDGE and axial * SEGMENT_LANES == pitch
    assert span_count == 2 and place_count > 2 and place_count & (place_count - 1) == 0
    wide = span + EDGE
    fields = 2 * components + 6
    groups = slots(fields + 1, components)[1][-1][0] + 1
    pairs = -(-(fields * axial + 1) // 2)
    span_tiles = pairs + -(-components * axial // EDGE)
    vmem = pl.BlockSpec(memory_space=pltpu.VMEM)
    hbm = pl.BlockSpec(memory_space=pltpu.HBM)

    def in_hbm(x):
        return pltpu.with_memory_space_constraint(x, pltpu.HBM)

    def call(kernel, name, outs, ins, aliases=None, scratch=(), limit=40 * MIB, **fixed):
        specs = [spec for spec, _ in ins]
        return pl.pallas_call(
            functools.partial(kernel, **fixed),
            out_shape=outs,
            in_specs=specs,
            out_specs=jax.tree.map(lambda _: vmem, outs),
            scratch_shapes=scratch,
            input_output_aliases=aliases or {},
            compiler_params=params(limit),
            name=name,
        )(*[value for _, value in ins])

    tables = (
        jacobians.transpose(2, 3, 0, 1), giles_real.transpose(2, 3, 0, 1), giles_imag.transpose(2, 3, 0, 1),
        mode_orders.transpose(0, 2, 1), cell_map,
    )
    blades = blades.reshape(1, -1)
    corner_rows = groups * EDGE
    state_shape = struct(axial + 2, components, axial, wide, pitch)
    state, coef, inv, span_out, small, modes, table, blades, *tables = call(
        start_kernel, "start",
        (
            state_shape, struct(components + 6, axial, wide, pitch), struct(wide, pitch),
            struct(span_tiles, EDGE, pitch), struct(2 * corner_rows + EDGE, pitch), struct(span, pitch),
            jax.ShapeDtypeStruct((2, components * pitch, pitch), jnp.bfloat16),
            *(jax.ShapeDtypeStruct(x.shape, x.dtype) for x in (blades, *tables)),
        ),
        [(hbm, in_hbm(x)) for x in (adjoint_start, source, couplings, damping, blades, *tables)],
        scratch=[
            pltpu.VMEM(source.shape, jnp.float32), pltpu.VMEM(couplings.shape, jnp.float32),
            pltpu.VMEM(damping.shape, jnp.float32), pltpu.SemaphoreType.DMA((5 + len(tables),)),
        ],
        groups=groups, length=length,
    )
    edges, inner, outer = call(
        pack_kernel, "pack",
        (struct(fields + 1, span, pitch), struct((groups + 1) * wide, pitch), struct(groups * wide, pitch)),
        [(vmem, x) for x in (state, coef, inv, modes)],
        groups=groups,
    )
    steps = [1 << n for n in range(place_count.bit_length() - 2)]
    last_step = place_count // 2

    def near(x):
        return moved(x, lambda r, s, p: (r - 1, s, p))

    def far(x):
        return moved(x, lambda r, s, p: (r - 1, s, p ^ last_step))

    small, edges = lax.optimization_barrier((moved(small, lambda r, s, p: (r, 1 - s, p)), edges))
    from_span = moved(span_out, lambda r, s, p: (r, 1 - s, p))
    synth, jac = call(
        synth_kernel, "synth",
        (
            jax.ShapeDtypeStruct(
                (2, -(-components * (pitch + SEGMENT_LANES) // pitch) * pitch, pitch), jnp.bfloat16
            ),
            struct(-(-6 * components * components // EDGE) * EDGE, pitch),
        ),
        [(vmem, x) for x in (blades, *tables)],
        scratch=[pltpu.VMEM((2, components * components, mode_orders.shape[1]), jnp.float32)],
        row_count=row_count, place_count=place_count, components=components, pitch=pitch, length=length, axial=axial,
    )
    edge_shape = struct(axial + 1, components, wide, pitch)
    inner = lax.dynamic_update_slice(inner, small[:corner_rows + EDGE], (groups * span, 0))
    outer = lax.dynamic_update_slice(outer, small[corner_rows + EDGE:], (groups * span, 0))
    modes = inner[groups * span + corner_rows:]
    outer = moved(outer, lambda r, s, p: (r, s, (p - 1 + 2 * (p % 2)) % place_count))
    inner = moved(inner, lambda r, s, p: (r, s, p ^ 1))
    modes = modes + inner[groups * span + corner_rows:]
    for step in steps[1:]:
        modes = modes + moved(modes, lambda r, s, p: (r, s, p ^ step))
    got = moved(modes, lambda r, s, p: (r, s, p ^ last_step))
    coef, inv, edge_coef, state, edge = call(
        first_kernel, "first_sweep",
        (
            struct(components + 6, axial, wide, pitch), struct(wide, pitch), struct(components + 7, wide, pitch),
            state_shape, edge_shape,
        ),
        [(vmem, x) for x in (jac, state, coef, inv, edges, from_span, inner, outer)],
        aliases={1: 3, 2: 0, 3: 1},
        groups=groups,
    )
    got, inv = lax.optimization_barrier((got, inv))
    modes = near(modes + got)
    state, edge, more, part = call(
        more_kernel, "more_sweeps",
        (state_shape, edge_shape, struct((axial - 1) * span + EDGE, pitch), struct(span, pitch)),
        [(vmem, x) for x in (jac, coef, edge_coef, state, edge, table)],
        aliases={3: 0, 4: 1},
    )
    more_shape = struct(axial * span + EDGE, pitch)
    more = call(
        late_kernel, "late_modes", more_shape,
        [(vmem, x) for x in (jac, coef, inv, part, more, modes, synth, table)],
    )
    state, edge, sent = call(
        between_kernel, "between_sweeps", (state_shape, edge_shape, more_shape),
        [(vmem, x) for x in (jac, coef, inv, edge_coef, state, edge, modes, synth, more)],
        aliases={4: 0, 5: 1},
    )
    state, edge = call(
        beside_kernel, "beside_sweeps", (state_shape, edge_shape),
        [(vmem, x) for x in (jac, coef, edge_coef, state, edge)],
        aliases={3: 0, 4: 1},
    )
    for step in steps:
        got = moved(more, lambda r, s, p: (r, s, p ^ step))
        more, sent = sent + got, sent + got
    more_b = far(more)
    more_a = near(more)
    return call(
        second_kernel, "second_sweeps", (state_shape, edge_shape, struct(components, axial, span, pitch)),
        [(vmem, x) for x in (jac, coef, inv, edge_coef, state, edge, more_a, more_b, synth)],
        aliases={4: 0, 5: 1},
        scratch=[pltpu.VMEM((axial + 1, components, wide, pitch), jnp.float32)],
    )[2]


def solution(mesh):
    placed = (
        P(None, "row", "span", "pitch"),
        P(None, "row", "span", "pitch"),
        P(None, "row", "span", "pitch"),
        P("row", "span", "pitch"),
        P("row", None, None, None),
        P(),
        P(),
        P(),
        P(),
        P("row", None),
    )
    return jax.shard_map(
        on_device,
        mesh=mesh,
        in_specs=placed,
        out_specs=P(None, "row", "span", "pitch"),
        check_vma=False,
    )
```

```python
import functools
import math

import jax
import jax.numpy as jnp
from jax import lax
from jax.experimental import pallas as pl
from jax.experimental.pallas import tpu as pltpu
from jax.sharding import PartitionSpec as P

ITERS = 5
AXES = ("row", "span", "pitch")

ORDER_MAX = 2
BASE = 2 * ORDER_MAX + 1
COSINES = (BASE * BASE + 1) // 2
WAVES = 2 * COSINES - 1
COMPONENTS = 5
EDGE = 8
HALF = EDGE // 2
SEGMENT_LANES = 4 * EDGE
EXACT = lax.Precision.HIGHEST
MIB = 1024 * 1024


def params(limit):
    return pltpu.CompilerParams(vmem_limit_bytes=limit)


def lanes(shape):
    return lax.broadcasted_iota(jnp.int32, shape, len(shape) - 1)


def rows(shape):
    return lax.broadcasted_iota(jnp.int32, shape, len(shape) - 2)


def column(j):
    component = (j * 41) >> 10
    wave = j - WAVES * component
    sine = wave >= COSINES
    return component, jnp.where(sine, wave - (COSINES - 1), wave), sine


def mode_number(mode, blades):
    high = ((mode + ORDER_MAX) * 13) >> 6
    low = mode - BASE * high
    return high * blades[0] + low * blades[1]


def waves(products, length):
    if length & (length - 1) == 0:
        phase = products & (length - 1)
    else:
        phase = jnp.mod(products, length)
    turn = phase.astype(jnp.float32) * (1.0 / length)
    quarter = jnp.floor(4.0 * turn + 0.5)
    x = (turn - 0.25 * quarter) * (2.0 * math.pi)
    y = x * x
    sine = x * (1.0 + y * (-1.0 / 6 + y * (1.0 / 120 + y * (-1.0 / 5040 + y * (1.0 / 362880)))))
    cosine = 1.0 + y * (-0.5 + y * (1.0 / 24 + y * (-1.0 / 720 + y * (1.0 / 40320 - y * (1.0 / 3628800)))))
    quarter = quarter.astype(jnp.int32) & 3
    odd = (quarter & 1) == 1
    cos_out = jnp.where(odd, sine, cosine)
    sin_out = jnp.where(odd, cosine, sine)
    cos_out = jnp.where((quarter == 1) | (quarter == 2), -cos_out, cos_out)
    sin_out = jnp.where(quarter >= 2, -sin_out, sin_out)
    return cos_out, sin_out


def to_edges(layers, pitch):
    lane = lanes(layers[-1].shape)
    block = jnp.zeros_like(layers[-1])
    for a, layer in enumerate(layers):
        if layer is None:
            continue
        start = a * SEGMENT_LANES
        first = pltpu.roll(layer, (start + EDGE) % pitch, layer.ndim - 1)
        last = pltpu.roll(layer, (start + 3 * EDGE) % pitch, layer.ndim - 1)
        block = jnp.where((lane >= start + EDGE) & (lane < start + 2 * EDGE), first, block)
        block = jnp.where((lane >= start + 2 * EDGE) & (lane < start + 3 * EDGE), last, block)
    return block


def half_rows(side):
    return jnp.where(side == 0, EDGE // 2, 0), jnp.where(side == 0, 0, EDGE // 2)


def slots(fields, components):
    per_group = SEGMENT_LANES // HALF
    near = [(f // per_group, f % per_group * HALF) for f in range(fields)]
    group, lane = near[-1]
    far = [(group, lane + HALF + c) for c in range(components)]
    return near, far


def packed_edges(blocks, place, components):
    near, far = slots(len(blocks), components)
    pitch = blocks[0].shape[1]
    lane = lanes(blocks[0].shape) % SEGMENT_LANES
    sides = []
    for near_at, far_at in ((3 * EDGE - HALF, 3 * EDGE - HALF - 1), (EDGE, EDGE + HALF)):
        packed = [jnp.zeros_like(blocks[0]) for _ in range(far[-1][0] + 1)]
        for f, (g, to) in enumerate(near):
            value = pltpu.roll(blocks[f], (to - near_at) % pitch, 1)
            packed[g] = jnp.where((lane >= to) & (lane < to + HALF), value, packed[g])
        for f, (g, to) in enumerate(far):
            packed[g] = jnp.where(lane == to, pltpu.roll(blocks[f], (to - far_at) % pitch, 1), packed[g])
        sides.append(packed)
    even = lax.rem(place, 2) == 0
    inner = [jnp.where(even, right, left) for right, left in zip(*sides)]
    outer = [jnp.where(even, left, right) for right, left in zip(*sides)]
    return inner, outer


def edge_blocks(state_ref, coef_ref, inv_ref, at):
    components, axial, pitch = state_ref.shape[1], state_ref.shape[2], state_ref.shape[4]
    blocks = [to_edges([state_ref[0, c, a, at, :] for a in range(axial)], pitch) for c in range(components)]
    blocks += [to_edges([coef_ref[f, a, at, :] for a in range(axial)], pitch) for f in range(components + 6)]
    return blocks + [to_edges([None] * (axial - 1) + [inv_ref[at, :]], pitch)]


def start_kernel(
    adjoint_hbm, source_hbm, couplings_hbm, damping_hbm, blades_hbm, *refs, groups, length,
):
    state_ref, coef_ref, inv_ref, span_ref, small_ref, modes_ref, table_ref, blades_ref = refs[5:13]
    source_ref, couplings_ref, damping_ref, sems = refs[18:]
    components, axial, span, pitch = source_ref.shape
    adjoint_ref = state_ref.at[0, :, :, pl.ds(0, span), :]
    copies = [
        pltpu.make_async_copy(src, dst, sems.at[n])
        for n, (src, dst) in enumerate((
            (couplings_hbm, couplings_ref), (damping_hbm, damping_ref), (source_hbm, source_ref),
            (adjoint_hbm, adjoint_ref), (blades_hbm, blades_ref), *zip(refs[:5], refs[13:18]),
        ))
    ]
    for copy in copies:
        copy.start()
    row, side, place = (lax.axis_index(name) for name in AXES)
    copies[4].wait()
    face = jnp.maximum(row - 1, 0)
    component, mode, sine = column(lanes((pitch, pitch)))
    number = mode_number(mode, [picked(blades_ref[...], face + n) for n in range(2)])
    cos_table, sin_table = waves(number * (place * pitch + rows((pitch, pitch))), length)
    table = jnp.where(component < components, jnp.where(sine, sin_table, cos_table), 0.0)
    for c in range(components):
        for n, value in enumerate(split(jnp.where(component == c, table, 0.0))):
            table_ref[n, pl.ds(c * pitch, pitch), :] = value
    copies[0].wait()
    copies[1].wait()
    diag = damping_ref[...]
    for d in range(6):
        diag = diag + couplings_ref[d]
    inverse = 1.0 / diag
    for d in range(6):
        coef_ref[components + d, :, :span] = couplings_ref[d] * inverse
    inv_ref[:span] = inverse[axial - 1]
    copies[2].wait()
    for c in range(components):
        coef_ref[c, :, :span] = source_ref[c] * inverse
    copies[3].wait()
    edge_row = pl.multiple_of(jnp.where(side == 0, span - EDGE, 0), EDGE)
    blocks = edge_blocks(state_ref, coef_ref, inv_ref, pl.ds(edge_row, EDGE))
    for n, packed in enumerate(packed_edges(blocks, place, components)):
        for g, value in enumerate(packed):
            small_ref[pl.ds((n * (groups + 1) + g) * EDGE, EDGE), :] = value
    modes_ref[...] = projected([adjoint_ref[c, 0] for c in range(components)], table_ref)
    small_ref[pl.ds(groups * EDGE, EDGE), :] = modes_ref[pl.ds(edge_row, EDGE), :]

    to_low, to_high = half_rows(side)
    line = rows((EDGE, pitch))
    tiles = [state_ref[0, c, a, pl.ds(edge_row, EDGE), :] for c in range(components) for a in range(axial)]
    tiles += [coef_ref[f, a, pl.ds(edge_row, EDGE), :] for f in range(components + 6) for a in range(axial)]
    tiles += [inv_ref[pl.ds(edge_row, EDGE), :]]
    pairs = -(-len(tiles) // 2)
    for n in range(pairs):
        value = pltpu.roll(tiles[2 * n], to_low, 0)
        if 2 * n + 1 < len(tiles):
            value = jnp.where(line < HALF, value, pltpu.roll(tiles[2 * n + 1], to_high, 0))
        span_ref[n] = value
    fifth = jnp.where(side == 0, HALF - 1, HALF)
    for n in range(span_ref.shape[0] - pairs):
        value = jnp.zeros((EDGE, pitch), jnp.float32)
        for k in range(min(EDGE, components * axial - n * EDGE)):
            value = jnp.where(line == k, pltpu.roll(tiles[n * EDGE + k], lax.rem(k + EDGE - fifth, EDGE), 0), value)
        span_ref[pairs + n] = value
    for copy in copies[5:]:
        copy.wait()


def pack_kernel(state_ref, coef_ref, inv_ref, modes_ref, edges_ref, inner_ref, outer_ref, *, groups):
    _, components, axial, wide, pitch = state_ref.shape
    span = wide - EDGE
    place = lax.axis_index("pitch")
    blocks = edge_blocks(state_ref, coef_ref, inv_ref, pl.ds(0, span))
    for f, block in enumerate(blocks):
        edges_ref[f] = block
    for out_ref, packed in zip((inner_ref, outer_ref), packed_edges(blocks, place, components)):
        for g, value in enumerate(packed):
            out_ref[pl.ds(g * span, span), :] = value
    start = groups * span + (groups + 1) * EDGE
    inner_ref[pl.ds(start, span), :] = modes_ref[...]


def picked(values, at):
    chosen = jnp.where(lanes(values.shape) == at, values.astype(jnp.float32), 0.0)
    return jnp.sum(chosen, axis=1, keepdims=True).astype(jnp.int32)


def split(x):
    high = x.astype(jnp.bfloat16)
    return high, (x - high.astype(jnp.float32)).astype(jnp.bfloat16)


def product(x, table, dims):
    x_high, x_low = split(x)
    table_high, table_low = table
    dot = functools.partial(lax.dot_general, dimension_numbers=(dims, ((), ())), preferred_element_type=jnp.float32)
    return dot(x_high, table_high) + (dot(x_low, table_high) + dot(x_high, table_low))


def projected(strips, table_ref):
    return product(jnp.concatenate(strips, 1), (table_ref[0], table_ref[1]), ((1,), (0,)))


def synthesised(modes, synth_ref, count):
    return product(modes, (synth_ref[0, :count], synth_ref[1, :count]), ((1,), (1,)))


def synth_kernel(
    blades_ref, jacobians_ref, giles_re_ref, giles_im_ref, orders_ref, cells_ref, synth_ref, rows_ref, sums_ref,
    *, row_count, place_count, components, pitch, length, axial,
):
    row, place = lax.axis_index("row"), lax.axis_index("pitch")
    face = jnp.minimum(row, row_count - 2)
    for b in range(components):
        for c in range(components):
            entries = jacobians_ref[b, c]
            for d in range(6):
                at = (b * components + c) * 6 + d
                rows_ref[pl.ds(at, 1), :] = jnp.broadcast_to(entries[:, d:d + 1], (1, pitch))
    modes = orders_ref.shape[2]
    orders = orders_ref[face]
    tag = BASE * orders[0:1] + orders[1:2]
    component, mode, _ = column(rows((pitch, modes)))
    same = (jnp.abs(tag) == mode) & (component < components)
    plain = jnp.where(same, 1.0, 0.0)
    signed = jnp.where(tag < 0, -plain, plain)
    dims = (((1,), (1,)), ((), ()))
    for n, ref in enumerate((giles_re_ref, giles_im_ref)):
        for b in range(components):
            for c in range(components):
                sums_ref[n, pl.ds(b * components + c, 1), :] = ref[b, c, pl.ds(face, 1), :]
    sums_re = lax.dot_general(sums_ref[0], plain, dims, precision=EXACT, preferred_element_type=jnp.float32)
    sums_im = lax.dot_general(sums_ref[1], signed, dims, precision=EXACT, preferred_element_type=jnp.float32)
    component, mode, sine = column(lanes(sums_re.shape))
    scale = 2.0 / length
    with_cos = jnp.where(sine, sums_im, sums_re) * scale
    with_sin = jnp.where(sine, sums_re, -sums_im) * scale
    component = component[0:1]

    def chunk(at):
        start = pl.multiple_of(lax.rem(place + at + place_count, place_count) * pitch, pitch)
        return cells_ref[:, pl.ds(start, pitch)]

    own = chunk(0)
    lane = lanes((1, pitch))
    first = (axial - 1) * SEGMENT_LANES
    edge = jnp.where(lane < first + EDGE, pltpu.roll(chunk(-1), (first + EDGE) % pitch, 1), pltpu.roll(own, (first + EDGE) % pitch, 1))
    edge = jnp.where(lane < first + 2 * EDGE, edge, pltpu.roll(own, (first + 3 * EDGE) % pitch, 1))
    edge = jnp.where(lane < first + 3 * EDGE, edge, pltpu.roll(chunk(1), (first + 3 * EDGE) % pitch, 1))

    def upright(cells):
        wide = jnp.broadcast_to(cells.astype(jnp.float32), (pitch, pitch))
        return jnp.transpose(wide).astype(jnp.int32)

    edge_cells = upright(edge)[first:first + SEGMENT_LANES]
    at_cells = jnp.concatenate([upright(own), edge_cells], 0)
    _, mode, _ = column(lanes(at_cells.shape))
    blades = [picked(blades_ref[...], face + n) for n in range(2)]
    cos_table, sin_table = waves(mode_number(mode, blades) * at_cells, length)
    for c in range(components):
        row_cos = jnp.zeros((1, pitch), jnp.float32)
        row_sin = jnp.zeros((1, pitch), jnp.float32)
        for b in range(components):
            at = b * components + c
            row_cos = jnp.where(component == b, with_cos[at:at + 1], row_cos)
            row_sin = jnp.where(component == b, with_sin[at:at + 1], row_sin)
        part = row_cos * cos_table + row_sin * sin_table
        for n, value in enumerate(split(part)):
            synth_ref[n, pl.ds(c * pitch, pitch), :] = value[:pitch]
            synth_ref[n, pl.ds(components * pitch + c * SEGMENT_LANES, SEGMENT_LANES), :] = value[pitch:]
    used = components * (pitch + SEGMENT_LANES)
    rest = synth_ref.shape[1] - used
    if rest:
        synth_ref[:, pl.ds(used, rest), :] = jnp.zeros((2, rest, pitch), jnp.bfloat16)


def jacobian(jac_ref, components, b, c, d):
    return jac_ref[pl.ds((b * components + c) * 6 + d, 1), :]


def mixed(jac_ref, source, couplings, neighbours):
    total = list(source)
    jac = functools.partial(jacobian, jac_ref, len(total))
    for d, neighbour in enumerate(neighbours):
        if neighbour is None:
            continue
        for c in range(len(total)):
            term = jac(0, c, d) * neighbour[0]
            for b in range(1, len(total)):
                term = term + jac(b, c, d) * neighbour[b]
            total[c] = total[c] + couplings[d] * term
    return total


def layer_update(jac_ref, state_ref, edge_ref, coef_ref, t, a, height):
    _, components, axial, wide, pitch = state_ref.shape
    lane = lanes((height, pitch))
    start = a * SEGMENT_LANES
    own = [state_ref[t, c, a] for c in range(components)]
    above = [state_ref[t, c, a + 1, :height] for c in range(components)] if a < axial - 1 else None
    below = [state_ref[t, c, a - 1, :height] for c in range(components)] if a else None
    edge = [edge_ref[t, c, :height] for c in range(components)]
    span_next = [pltpu.roll(x, wide - 1, 0)[:height] for x in own]
    span_prev = [pltpu.roll(x, 1, 0)[:height] for x in own]
    own = [x[:height] for x in own]
    to_end = (pitch - 1 - (start + 3 * EDGE)) % pitch
    to_begin = (pitch - (start + EDGE - 1)) % pitch
    pitch_next = [
        jnp.where(lane == pitch - 1, pltpu.roll(e, to_end, 1), pltpu.roll(x, pitch - 1, 1))
        for e, x in zip(edge, own)
    ]
    pitch_prev = [
        jnp.where(lane == 0, pltpu.roll(e, to_begin, 1), pltpu.roll(x, 1, 1))
        for e, x in zip(edge, own)
    ]
    source = [coef_ref[c, a, :height] for c in range(components)]
    couplings = [coef_ref[components + d, a, :height] for d in range(6)]
    return mixed(jac_ref, source, couplings, (above, below, span_next, span_prev, pitch_next, pitch_prev))


def edge_update(jac_ref, edge_ref, edge_coef_ref, t, axial):
    components, wide, pitch = edge_ref.shape[1:]
    lane = lanes((wide, pitch))
    own = [edge_ref[t, c] for c in range(components)]
    above = [jnp.where(lane < (axial - 1) * SEGMENT_LANES, pltpu.roll(x, pitch - SEGMENT_LANES, 1), 0.0) for x in own]
    below = [jnp.where(lane >= SEGMENT_LANES, pltpu.roll(x, SEGMENT_LANES, 1), 0.0) for x in own]
    span_next = [pltpu.roll(x, wide - 1, 0) for x in own]
    span_prev = [pltpu.roll(x, 1, 0) for x in own]
    pitch_next = [pltpu.roll(x, pitch - 1, 1) for x in own]
    pitch_prev = [pltpu.roll(x, 1, 1) for x in own]
    source = [edge_coef_ref[c] for c in range(components)]
    couplings = [edge_coef_ref[components + d] for d in range(6)]
    return mixed(jac_ref, source, couplings, (above, below, span_next, span_prev, pitch_next, pitch_prev))


def edge_boundary(field, c, components, pitch, axial):
    at = components * pitch + c * SEGMENT_LANES
    tile = field[:, (at // pitch) * pitch:(at // pitch + 1) * pitch]
    return pltpu.roll(tile, ((axial - 1) * SEGMENT_LANES - at % pitch) % pitch, 1)


def advance(refs, t, a, height=None):
    state_ref = refs[1]
    height = height or state_ref.shape[3]
    for c, value in enumerate(layer_update(*refs, t, a, height)):
        state_ref[t + 1, c, a, :height] = value


def first_kernel(
    jac_ref, state_in_ref, coef_in_ref, inv_in_ref, edges_ref, span_ref, inner_ref, outer_ref,
    coef_ref, inv_ref, edge_coef_ref, state_ref, edge_ref, *, groups,
):
    _, components, axial, wide, pitch = state_ref.shape
    span = wide - EDGE
    side = lax.axis_index("span")
    fields = 2 * components + 6
    line = rows((EDGE, pitch))
    keep_half = jnp.where(side == 0, line, EDGE - 1 - line) < HALF
    fifth = jnp.where(side == 0, HALF, HALF - 1)
    from_low, from_high = half_rows(1 - side)
    pairs = -(-(fields * axial + 1) // 2)

    def ghost(n):
        value = pltpu.roll(span_ref[n // 2], from_high if n % 2 else from_low, 0)
        value = jnp.where(keep_half, value, 0.0)
        if n < components * axial:
            extra = pltpu.roll(span_ref[pairs + n // EDGE], lax.rem(fifth + EDGE - n % EDGE, EDGE), 0)
            value = jnp.where(line == fifth, extra, value)
        return value

    even = lax.rem(lax.axis_index("pitch"), 2) == 0

    def group(ref, g):
        corner = ref[pl.ds(groups * span + g * EDGE, EDGE), :]
        return jnp.concatenate([ref[pl.ds(g * span, span), :], corner], 0)

    halves = [(group(inner_ref, g), group(outer_ref, g)) for g in range(groups)]
    from_left = [jnp.where(even, outer, inner) for inner, outer in halves]
    from_right = [jnp.where(even, inner, outer) for inner, outer in halves]
    near, far = slots(fields + 1, components)
    keep_five = keep_half | (line == fifth)
    for f in range(fields + 1):
        if f < fields:
            layers = [ghost(f * axial + a) for a in range(axial)]
        else:
            layers = [jnp.zeros((EDGE, pitch), jnp.float32)] * (axial - 1) + [ghost(fields * axial)]
        if f < components:
            for a in range(axial):
                state_ref[0, f, a, span:] = layers[a]
        elif f < fields:
            for a in range(axial):
                coef_ref[f - components, a, span:] = layers[a]
        else:
            inv_ref[span:] = layers[-1]
        g, at = near[f]
        value = jnp.concatenate([edges_ref[f], to_edges(layers, pitch)], 0)
        lane = lanes((wide, pitch)) % SEGMENT_LANES
        value = jnp.where((lane >= HALF) & (lane < EDGE), pltpu.roll(from_left[g], (HALF - at) % pitch, 1), value)
        value = jnp.where(
            (lane >= 3 * EDGE) & (lane < 3 * EDGE + HALF),
            pltpu.roll(from_right[g], (3 * EDGE - at) % pitch, 1), value,
        )
        if f < components:
            g, at = far[f]
            value = jnp.where(lane == HALF - 1, pltpu.roll(from_left[g], (HALF - 1 - at) % pitch, 1), value)
            value = jnp.where(
                lane == 3 * EDGE + HALF, pltpu.roll(from_right[g], (3 * EDGE + HALF - at) % pitch, 1), value,
            )
        target, at = (edge_ref.at[0], f) if f < components else (edge_coef_ref, f - components)
        target[at, :span] = value[:span]
        target[at, span:] = jnp.where(keep_five if f < components else keep_half, value[span:], 0.0)
    sweeps_without_boundaries(jac_ref, state_ref, edge_ref, coef_ref, edge_coef_ref, 0, 1)


def sweeps_without_boundaries(jac_ref, state_ref, edge_ref, coef_ref, edge_coef_ref, first, last):
    axial = state_ref.shape[2]
    for t in range(first, last):
        for a in range(axial - t):
            advance((jac_ref, state_ref, edge_ref, coef_ref), t, a)
        if t < axial - 1:
            for c, value in enumerate(edge_update(jac_ref, edge_ref, edge_coef_ref, t, axial)):
                edge_ref[t + 1, c] = value


def more_kernel(
    jac_ref, coef_ref, edge_coef_ref, state_in_ref, edge_in_ref, table_ref, state_ref, edge_ref, modes_ref, part_ref,
):
    _, components, axial, wide, pitch = state_ref.shape
    span = wide - EDGE
    side = lax.axis_index("span")
    sweeps_without_boundaries(jac_ref, state_ref, edge_ref, coef_ref, edge_coef_ref, 1, axial)
    strips = [
        jnp.concatenate([state_ref[t, c, 0] for t in range(1, axial)] + [state_ref[axial, c, 0, :span]], 0)
        for c in range(components)
    ]
    total = projected(strips, table_ref)
    ghosts = jnp.zeros((EDGE, pitch), jnp.float32)
    for t in range(1, axial):
        part = total[(t - 1) * wide:t * wide]
        modes_ref[pl.ds((t - 1) * span, span), :] = part[:span]
        keep, to_packed, _ = ghost_rows(side, t, axial)
        ghosts = jnp.where(keep, pltpu.roll(part[span:], to_packed, 0), ghosts)
    modes_ref[pl.ds((axial - 1) * span, EDGE), :] = ghosts
    part_ref[...] = total[(axial - 1) * wide:]


def ghost_rows(side, t, axial):
    line = rows((EDGE, 1))
    distance = jnp.where(side == 0, line, EDGE - 1 - line)
    start = sum(axial - n for n in range(1, t))
    to_packed = jnp.where(side == 0, start, (EDGE - start) % EDGE)
    from_packed = jnp.where(side == 0, (EDGE - start) % EDGE, start)
    return (distance >= start) & (distance < start + axial - t), to_packed, from_packed


def along_axis(jac_ref, coef_ref, delta, a, height):
    components = len(delta)
    out = []
    for c in range(components):
        term = jacobian(jac_ref, components, 0, c, 0) * delta[0]
        for b in range(1, components):
            term = term + jacobian(jac_ref, components, b, c, 0) * delta[b]
        out.append(coef_ref[components, a, :height] * term)
    return out


def late_kernel(
    jac_ref, coef_ref, inv_ref, part_ref, more_ref, first_ref, synth_ref, table_ref, modes_ref,
):
    span, pitch = part_ref.shape
    components, axial = coef_ref.shape[0] - 6, coef_ref.shape[1]
    field = synthesised(first_ref[EDGE:], synth_ref, components * pitch)
    delta = [inv_ref[:span] * field[:, c * pitch:(c + 1) * pitch] for c in range(components)]
    for a in range(axial - 2, -1, -1):
        delta = along_axis(jac_ref, coef_ref, delta, a, span)
    before = more_ref.shape[0]
    modes_ref[:before] = more_ref[...]
    modes_ref[before:] = part_ref[...] + projected(delta, table_ref)


def between_kernel(
    jac_ref, coef_ref, inv_ref, edge_coef_ref, state_in_ref, edge_in_ref, modes_ref, synth_ref, more_ref,
    state_ref, edge_ref, sent_ref,
):
    sent_ref[...] = more_ref[...]
    components, axial = state_ref.shape[1], state_ref.shape[2]
    wide, pitch = state_ref.shape[3:]
    modes = modes_ref[...]
    field = synthesised(jnp.concatenate([modes[EDGE:], modes[:EDGE]], 0), synth_ref, synth_ref.shape[1])
    delta = [inv_ref[...] * field[:, c * pitch:(c + 1) * pitch] for c in range(components)]
    for t in range(1, axial + 1):
        for c in range(components):
            state_ref[t, c, axial - t] += delta[c]
        if t < axial:
            delta = along_axis(jac_ref, coef_ref, delta, axial - 1 - t, wide)
    for c in range(components):
        edge_ref[1, c] += edge_coef_ref[components + 6] * edge_boundary(field, c, components, pitch, axial)
    diagonal_sweeps(jac_ref, state_ref, edge_ref, coef_ref, edge_coef_ref, 1, axial // 2 + 1)


def beside_kernel(jac_ref, coef_ref, edge_coef_ref, state_in_ref, edge_in_ref, state_ref, edge_ref):
    axial, span = state_ref.shape[2], state_ref.shape[3] - EDGE
    diagonal_sweeps(jac_ref, state_ref, edge_ref, coef_ref, edge_coef_ref, axial // 2 + 1, axial)
    advance((jac_ref, state_ref, edge_ref, coef_ref), axial, 0, span)


def diagonal_sweeps(jac_ref, state_ref, edge_ref, coef_ref, edge_coef_ref, first, last):
    axial = state_ref.shape[2]
    for t in range(first, last):
        advance((jac_ref, state_ref, edge_ref, coef_ref), t, axial - t)
        for c, value in enumerate(edge_update(jac_ref, edge_ref, edge_coef_ref, t, axial)):
            edge_ref[t + 1, c] = value


def second_kernel(
    jac_ref, coef_ref, inv_ref, edge_coef_ref, state_in_ref, edge_in_ref, more_a_ref, more_b_ref, synth_ref,
    state_ref, edge_ref, out_hbm, bound_ref, out_ref, sems,
):
    axial, components, span, pitch = out_ref.shape
    copies = [pltpu.make_async_copy(out_ref.at[a], out_hbm.at[:, a], sems.at[a]) for a in range(axial)]
    wide = span + EDGE
    side = lax.axis_index("span")
    more = more_a_ref[...] + more_b_ref[...]
    start = (axial - 1) * span
    parts = []
    for t in range(1, axial):
        _, _, from_packed = ghost_rows(side, t, axial)
        parts += [more[(t - 1) * span:t * span], pltpu.roll(more[start:start + EDGE], from_packed, 0)]
    field = synthesised(jnp.concatenate(parts + [more[start + EDGE:]], 0), synth_ref, synth_ref.shape[1])
    for t in range(1, axial):
        part = field[(t - 1) * wide:t * wide]
        for c in range(components):
            bound_ref[t, c] = inv_ref[...] * part[:, c * pitch:(c + 1) * pitch]
    for c in range(components):
        bound_ref[axial, c, :span] = inv_ref[:span] * field[(axial - 1) * wide:, c * pitch:(c + 1) * pitch]
    delta = [bound_ref[1, c] for c in range(components)]
    for t in range(2, axial + 2):
        height = wide if t <= axial else span
        for c in range(components):
            state_ref[t, c, axial + 1 - t, :height] += delta[c][:height]
        if t < axial + 1:
            delta = along_axis(jac_ref, coef_ref, delta, axial - t, wide)
    for c in range(components):
        out_ref[0, c] = state_ref[axial + 1, c, 0, :span]
    copies[0].start()
    for t in range(1, axial):
        if t > 1:
            for c, value in enumerate(edge_update(jac_ref, edge_ref, edge_coef_ref, t, axial)):
                edge_ref[t + 1, c] = value
        part = field[(t - 1) * wide:t * wide]
        for c in range(components):
            edge_ref[t + 1, c] += edge_coef_ref[components + 6] * edge_boundary(part, c, components, pitch, axial)
    refs = (jac_ref, state_ref, edge_ref, coef_ref)

    for t in range(2, axial):
        for a in range(axial + 1 - t, axial):
            advance(refs, t, a)
        for c in range(components):
            state_ref[t + 1, c, axial - 1] += bound_ref[t, c]
    for a in range(1, axial):
        for c, value in enumerate(layer_update(*refs, axial, a, span)):
            out_ref[a, c] = value + bound_ref[axial, c, :span] if a == axial - 1 else value
        copies[a].start()
    for copy in copies:
        copy.wait()


def moved(x, to):
    sizes = [lax.axis_size(name) for name in AXES]
    pairs = []
    for r in range(sizes[0]):
        for s in range(sizes[1]):
            for p in range(sizes[2]):
                target = to(r, s, p)
                if all(0 <= at < size for at, size in zip(target, sizes)):
                    number = lambda at: (at[0] * sizes[1] + at[1]) * sizes[2] + at[2]
                    pairs.append((number((r, s, p)), number(target)))
    return lax.ppermute(x, AXES, pairs)


def struct(*shape):
    return jax.ShapeDtypeStruct(shape, jnp.float32)


def on_device(
    adjoint_start, source, couplings, damping, jacobians, giles_real, giles_imag, blades, mode_orders, cell_map,
):
    components, axial, span, pitch = adjoint_start.shape
    row_count, span_count, place_count = (lax.axis_size(name) for name in AXES)
    length = pitch * place_count
    assert sum(axial - t for t in range(1, axial)) <= EDGE
    assert components == COMPONENTS and components * WAVES <= pitch
    assert axial == ITERS - 1 and ITERS <= EDGE and axial * SEGMENT_LANES == pitch
    assert span_count == 2 and place_count > 2 and place_count & (place_count - 1) == 0
    wide = span + EDGE
    fields = 2 * components + 6
    groups = slots(fields + 1, components)[1][-1][0] + 1
    pairs = -(-(fields * axial + 1) // 2)
    span_tiles = pairs + -(-components * axial // EDGE)
    vmem = pl.BlockSpec(memory_space=pltpu.VMEM)
    hbm = pl.BlockSpec(memory_space=pltpu.HBM)

    def in_hbm(x):
        return pltpu.with_memory_space_constraint(x, pltpu.HBM)

    def call(kernel, name, outs, ins, aliases=None, scratch=(), limit=40 * MIB, out_specs=None, **fixed):
        specs = [spec for spec, _ in ins]
        return pl.pallas_call(
            functools.partial(kernel, **fixed),
            out_shape=outs,
            in_specs=specs,
            out_specs=out_specs or jax.tree.map(lambda _: vmem, outs),
            scratch_shapes=scratch,
            input_output_aliases=aliases or {},
            compiler_params=params(limit),
            name=name,
        )(*[value for _, value in ins])

    tables = (
        jacobians.transpose(2, 3, 0, 1), giles_real.transpose(2, 3, 0, 1), giles_imag.transpose(2, 3, 0, 1),
        mode_orders.transpose(0, 2, 1), cell_map,
    )
    blades = blades.reshape(1, -1)
    corner_rows = groups * EDGE
    state_shape = struct(axial + 2, components, axial, wide, pitch)
    state, coef, inv, span_out, small, modes, table, blades, *tables = call(
        start_kernel, "start",
        (
            state_shape, struct(components + 6, axial, wide, pitch), struct(wide, pitch),
            struct(span_tiles, EDGE, pitch), struct(2 * corner_rows + EDGE, pitch), struct(span, pitch),
            jax.ShapeDtypeStruct((2, components * pitch, pitch), jnp.bfloat16),
            *(jax.ShapeDtypeStruct(x.shape, x.dtype) for x in (blades, *tables)),
        ),
        [(hbm, in_hbm(x)) for x in (adjoint_start, source, couplings, damping, blades, *tables)],
        scratch=[
            pltpu.VMEM(source.shape, jnp.float32), pltpu.VMEM(couplings.shape, jnp.float32),
            pltpu.VMEM(damping.shape, jnp.float32), pltpu.SemaphoreType.DMA((5 + len(tables),)),
        ],
        groups=groups, length=length,
    )
    edges, inner, outer = call(
        pack_kernel, "pack",
        (struct(fields + 1, span, pitch), struct((groups + 1) * wide, pitch), struct(groups * wide, pitch)),
        [(vmem, x) for x in (state, coef, inv, modes)],
        groups=groups,
    )
    steps = [1 << n for n in range(place_count.bit_length() - 2)]
    last_step = place_count // 2

    def near(x):
        return moved(x, lambda r, s, p: (r - 1, s, p))

    def far(x):
        return moved(x, lambda r, s, p: (r - 1, s, p ^ last_step))

    synth, jac = call(
        synth_kernel, "synth",
        (
            jax.ShapeDtypeStruct(
                (2, -(-components * (pitch + SEGMENT_LANES) // pitch) * pitch, pitch), jnp.bfloat16
            ),
            struct(-(-6 * components * components // EDGE) * EDGE, pitch),
        ),
        [(vmem, x) for x in (blades, *tables)],
        scratch=[pltpu.VMEM((2, components * components, mode_orders.shape[1]), jnp.float32)],
        row_count=row_count, place_count=place_count, components=components, pitch=pitch, length=length, axial=axial,
    )
    small, edges, jac = lax.optimization_barrier((moved(small, lambda r, s, p: (r, 1 - s, p)), edges, jac))
    from_span = moved(span_out, lambda r, s, p: (r, 1 - s, p))
    edge_shape = struct(axial + 1, components, wide, pitch)
    inner = lax.dynamic_update_slice(inner, small[:corner_rows + EDGE], (groups * span, 0))
    outer = lax.dynamic_update_slice(outer, small[corner_rows + EDGE:], (groups * span, 0))
    modes = inner[groups * span + corner_rows:]
    outer = moved(outer, lambda r, s, p: (r, s, (p - 1 + 2 * (p % 2)) % place_count))
    inner = moved(inner, lambda r, s, p: (r, s, p ^ 1))
    modes = modes + inner[groups * span + corner_rows:]
    for step in steps[1:]:
        modes = modes + moved(modes, lambda r, s, p: (r, s, p ^ step))
    got = moved(modes, lambda r, s, p: (r, s, p ^ last_step))
    coef, inv, edge_coef, state, edge = call(
        first_kernel, "first_sweep",
        (
            struct(components + 6, axial, wide, pitch), struct(wide, pitch), struct(components + 7, wide, pitch),
            state_shape, edge_shape,
        ),
        [(vmem, x) for x in (jac, state, coef, inv, edges, from_span, inner, outer)],
        aliases={1: 3, 2: 0, 3: 1},
        groups=groups,
    )
    got, inv = lax.optimization_barrier((got, inv))
    modes = near(modes + got)
    state, edge, more, part = call(
        more_kernel, "more_sweeps",
        (state_shape, edge_shape, struct((axial - 1) * span + EDGE, pitch), struct(span, pitch)),
        [(vmem, x) for x in (jac, coef, edge_coef, state, edge, table)],
        aliases={3: 0, 4: 1},
    )
    more_shape = struct(axial * span + EDGE, pitch)
    more = call(
        late_kernel, "late_modes", more_shape,
        [(vmem, x) for x in (jac, coef, inv, part, more, modes, synth, table)],
    )
    state, edge, sent = call(
        between_kernel, "between_sweeps", (state_shape, edge_shape, more_shape),
        [(vmem, x) for x in (jac, coef, inv, edge_coef, state, edge, modes, synth, more)],
        aliases={4: 0, 5: 1},
    )
    state, edge = call(
        beside_kernel, "beside_sweeps", (state_shape, edge_shape),
        [(vmem, x) for x in (jac, coef, edge_coef, state, edge)],
        aliases={3: 0, 4: 1},
    )
    for step in steps:
        got = moved(more, lambda r, s, p: (r, s, p ^ step))
        more, sent = sent + got, sent + got
    more_b = far(more)
    more_a = near(more)
    return call(
        second_kernel, "second_sweeps", (state_shape, edge_shape, struct(components, axial, span, pitch)),
        [(vmem, x) for x in (jac, coef, inv, edge_coef, state, edge, more_a, more_b, synth)],
        aliases={4: 0, 5: 1},
        scratch=[
            pltpu.VMEM((axial + 1, components, wide, pitch), jnp.float32),
            pltpu.VMEM((axial, components, span, pitch), jnp.float32), pltpu.SemaphoreType.DMA((axial,)),
        ],
        out_specs=(vmem, vmem, hbm),
    )[2]


def solution(mesh):
    placed = (
        P(None, "row", "span", "pitch"),
        P(None, "row", "span", "pitch"),
        P(None, "row", "span", "pitch"),
        P("row", "span", "pitch"),
        P("row", None, None, None),
        P(),
        P(),
        P(),
        P(),
        P("row", None),
    )
    return jax.shard_map(
        on_device,
        mesh=mesh,
        in_specs=placed,
        out_specs=P(None, "row", "span", "pitch"),
        check_vma=False,
    )
```

```python
import functools
import math

import jax
import jax.numpy as jnp
from jax import lax
from jax.experimental import pallas as pl
from jax.experimental.pallas import tpu as pltpu
from jax.sharding import PartitionSpec as P

ITERS = 5
AXES = ("row", "span", "pitch")

ORDER_MAX = 2
BASE = 2 * ORDER_MAX + 1
COSINES = (BASE * BASE + 1) // 2
WAVES = 2 * COSINES - 1
COMPONENTS = 5
EDGE = 8
HALF = EDGE // 2
SEGMENT_LANES = 4 * EDGE
EXACT = lax.Precision.HIGHEST
MIB = 1024 * 1024


def params(limit):
    return pltpu.CompilerParams(vmem_limit_bytes=limit)


def lanes(shape):
    return lax.broadcasted_iota(jnp.int32, shape, len(shape) - 1)


def rows(shape):
    return lax.broadcasted_iota(jnp.int32, shape, len(shape) - 2)


def column(j):
    component = (j * 41) >> 10
    wave = j - WAVES * component
    sine = wave >= COSINES
    return component, jnp.where(sine, wave - (COSINES - 1), wave), sine


def mode_number(mode, blades):
    high = ((mode + ORDER_MAX) * 13) >> 6
    low = mode - BASE * high
    return high * blades[0] + low * blades[1]


def waves(products, length):
    if length & (length - 1) == 0:
        phase = products & (length - 1)
    else:
        phase = jnp.mod(products, length)
    turn = phase.astype(jnp.float32) * (1.0 / length)
    quarter = jnp.floor(4.0 * turn + 0.5)
    x = (turn - 0.25 * quarter) * (2.0 * math.pi)
    y = x * x
    sine = x * (1.0 + y * (-1.0 / 6 + y * (1.0 / 120 + y * (-1.0 / 5040 + y * (1.0 / 362880)))))
    cosine = 1.0 + y * (-0.5 + y * (1.0 / 24 + y * (-1.0 / 720 + y * (1.0 / 40320 - y * (1.0 / 3628800)))))
    quarter = quarter.astype(jnp.int32) & 3
    odd = (quarter & 1) == 1
    cos_out = jnp.where(odd, sine, cosine)
    sin_out = jnp.where(odd, cosine, sine)
    cos_out = jnp.where((quarter == 1) | (quarter == 2), -cos_out, cos_out)
    sin_out = jnp.where(quarter >= 2, -sin_out, sin_out)
    return cos_out, sin_out


def to_edges(layers, pitch):
    lane = lanes(layers[-1].shape)
    block = jnp.zeros_like(layers[-1])
    for a, layer in enumerate(layers):
        if layer is None:
            continue
        start = a * SEGMENT_LANES
        first = pltpu.roll(layer, (start + EDGE) % pitch, layer.ndim - 1)
        last = pltpu.roll(layer, (start + 3 * EDGE) % pitch, layer.ndim - 1)
        block = jnp.where((lane >= start + EDGE) & (lane < start + 2 * EDGE), first, block)
        block = jnp.where((lane >= start + 2 * EDGE) & (lane < start + 3 * EDGE), last, block)
    return block


def half_rows(side):
    return jnp.where(side == 0, EDGE // 2, 0), jnp.where(side == 0, 0, EDGE // 2)


def slots(fields, components):
    per_group = SEGMENT_LANES // HALF
    near = [(f // per_group, f % per_group * HALF) for f in range(fields)]
    group, lane = near[-1]
    far = [(group, lane + HALF + c) for c in range(components)]
    return near, far


def packed_edges(blocks, place, components):
    near, far = slots(len(blocks), components)
    pitch = blocks[0].shape[1]
    lane = lanes(blocks[0].shape) % SEGMENT_LANES
    sides = []
    for near_at, far_at in ((3 * EDGE - HALF, 3 * EDGE - HALF - 1), (EDGE, EDGE + HALF)):
        packed = [jnp.zeros_like(blocks[0]) for _ in range(far[-1][0] + 1)]
        for f, (g, to) in enumerate(near):
            value = pltpu.roll(blocks[f], (to - near_at) % pitch, 1)
            packed[g] = jnp.where((lane >= to) & (lane < to + HALF), value, packed[g])
        for f, (g, to) in enumerate(far):
            packed[g] = jnp.where(lane == to, pltpu.roll(blocks[f], (to - far_at) % pitch, 1), packed[g])
        sides.append(packed)
    even = lax.rem(place, 2) == 0
    inner = [jnp.where(even, right, left) for right, left in zip(*sides)]
    outer = [jnp.where(even, left, right) for right, left in zip(*sides)]
    return inner, outer


def edge_blocks(state_ref, coef_ref, inv_ref, at):
    components, axial, pitch = state_ref.shape[1], state_ref.shape[2], state_ref.shape[4]
    blocks = [to_edges([state_ref[0, c, a, at, :] for a in range(axial)], pitch) for c in range(components)]
    blocks += [to_edges([coef_ref[f, a, at, :] for a in range(axial)], pitch) for f in range(components + 6)]
    return blocks + [to_edges([None] * (axial - 1) + [inv_ref[at, :]], pitch)]


def start_kernel(
    adjoint_hbm, source_hbm, couplings_hbm, damping_hbm, blades_hbm, *refs, groups, length,
):
    state_ref, coef_ref, inv_ref, span_ref, small_ref, modes_ref, table_ref, blades_ref = refs[5:13]
    source_ref, couplings_ref, damping_ref, sems = refs[18:]
    components, axial, span, pitch = source_ref.shape
    adjoint_ref = state_ref.at[0, :, :, pl.ds(0, span), :]
    copies = [
        pltpu.make_async_copy(src, dst, sems.at[n])
        for n, (src, dst) in enumerate((
            (couplings_hbm, couplings_ref), (damping_hbm, damping_ref), (source_hbm, source_ref),
            (adjoint_hbm, adjoint_ref), (blades_hbm, blades_ref), *zip(refs[:5], refs[13:18]),
        ))
    ]
    for copy in copies:
        copy.start()
    row, side, place = (lax.axis_index(name) for name in AXES)
    copies[4].wait()
    face = jnp.maximum(row - 1, 0)
    component, mode, sine = column(lanes((pitch, pitch)))
    number = mode_number(mode, [picked(blades_ref[...], face + n) for n in range(2)])
    cos_table, sin_table = waves(number * (place * pitch + rows((pitch, pitch))), length)
    table = jnp.where(component < components, jnp.where(sine, sin_table, cos_table), 0.0)
    for c in range(components):
        for n, value in enumerate(split(jnp.where(component == c, table, 0.0))):
            table_ref[n, pl.ds(c * pitch, pitch), :] = value
    copies[0].wait()
    copies[1].wait()
    diag = damping_ref[...]
    for d in range(6):
        diag = diag + couplings_ref[d]
    inverse = 1.0 / diag
    for d in range(6):
        coef_ref[components + d, :, :span] = couplings_ref[d] * inverse
    inv_ref[:span] = inverse[axial - 1]
    copies[2].wait()
    for c in range(components):
        coef_ref[c, :, :span] = source_ref[c] * inverse
    copies[3].wait()
    edge_row = pl.multiple_of(jnp.where(side == 0, span - EDGE, 0), EDGE)
    blocks = edge_blocks(state_ref, coef_ref, inv_ref, pl.ds(edge_row, EDGE))
    for n, packed in enumerate(packed_edges(blocks, place, components)):
        for g, value in enumerate(packed):
            small_ref[pl.ds((n * (groups + 1) + g) * EDGE, EDGE), :] = value
    modes_ref[...] = projected([adjoint_ref[c, 0] for c in range(components)], table_ref)
    small_ref[pl.ds(groups * EDGE, EDGE), :] = modes_ref[pl.ds(edge_row, EDGE), :]

    to_low, to_high = half_rows(side)
    line = rows((EDGE, pitch))
    tiles = [state_ref[0, c, a, pl.ds(edge_row, EDGE), :] for c in range(components) for a in range(axial)]
    tiles += [coef_ref[f, a, pl.ds(edge_row, EDGE), :] for f in range(components + 6) for a in range(axial)]
    tiles += [inv_ref[pl.ds(edge_row, EDGE), :]]
    pairs = -(-len(tiles) // 2)
    for n in range(pairs):
        value = pltpu.roll(tiles[2 * n], to_low, 0)
        if 2 * n + 1 < len(tiles):
            value = jnp.where(line < HALF, value, pltpu.roll(tiles[2 * n + 1], to_high, 0))
        span_ref[n] = value
    fifth = jnp.where(side == 0, HALF - 1, HALF)
    for n in range(span_ref.shape[0] - pairs):
        value = jnp.zeros((EDGE, pitch), jnp.float32)
        for k in range(min(EDGE, components * axial - n * EDGE)):
            value = jnp.where(line == k, pltpu.roll(tiles[n * EDGE + k], lax.rem(k + EDGE - fifth, EDGE), 0), value)
        span_ref[pairs + n] = value
    for copy in copies[5:]:
        copy.wait()


def pack_kernel(state_ref, coef_ref, inv_ref, modes_ref, edges_ref, inner_ref, outer_ref, *, groups):
    _, components, axial, wide, pitch = state_ref.shape
    span = wide - EDGE
    place = lax.axis_index("pitch")
    blocks = edge_blocks(state_ref, coef_ref, inv_ref, pl.ds(0, span))
    for f, block in enumerate(blocks):
        edges_ref[f] = block
    for out_ref, packed in zip((inner_ref, outer_ref), packed_edges(blocks, place, components)):
        for g, value in enumerate(packed):
            out_ref[pl.ds(g * span, span), :] = value
    start = groups * span + (groups + 1) * EDGE
    inner_ref[pl.ds(start, span), :] = modes_ref[...]


def picked(values, at):
    chosen = jnp.where(lanes(values.shape) == at, values.astype(jnp.float32), 0.0)
    return jnp.sum(chosen, axis=1, keepdims=True).astype(jnp.int32)


def split(x):
    high = x.astype(jnp.bfloat16)
    return high, (x - high.astype(jnp.float32)).astype(jnp.bfloat16)


def product(x, table, dims):
    x_high, x_low = split(x)
    table_high, table_low = table
    dot = functools.partial(lax.dot_general, dimension_numbers=(dims, ((), ())), preferred_element_type=jnp.float32)
    return dot(x_high, table_high) + (dot(x_low, table_high) + dot(x_high, table_low))


def projected(strips, table_ref):
    return product(jnp.concatenate(strips, 1), (table_ref[0], table_ref[1]), ((1,), (0,)))


def synthesised(modes, synth_ref, count):
    return product(modes, (synth_ref[0, :count], synth_ref[1, :count]), ((1,), (1,)))


def synth_kernel(
    blades_ref, jacobians_ref, giles_re_ref, giles_im_ref, orders_ref, cells_ref, synth_ref, rows_ref, sums_ref,
    *, row_count, place_count, components, pitch, length, axial,
):
    row, place = lax.axis_index("row"), lax.axis_index("pitch")
    face = jnp.minimum(row, row_count - 2)
    for b in range(components):
        for c in range(components):
            entries = jacobians_ref[b, c]
            for d in range(6):
                at = (b * components + c) * 6 + d
                rows_ref[pl.ds(at, 1), :] = jnp.broadcast_to(entries[:, d:d + 1], (1, pitch))
    modes = orders_ref.shape[2]
    orders = orders_ref[face]
    tag = BASE * orders[0:1] + orders[1:2]
    component, mode, _ = column(rows((pitch, modes)))
    same = (jnp.abs(tag) == mode) & (component < components)
    plain = jnp.where(same, 1.0, 0.0)
    signed = jnp.where(tag < 0, -plain, plain)
    dims = (((1,), (1,)), ((), ()))
    for n, ref in enumerate((giles_re_ref, giles_im_ref)):
        for b in range(components):
            for c in range(components):
                sums_ref[n, pl.ds(b * components + c, 1), :] = ref[b, c, pl.ds(face, 1), :]
    sums_re = lax.dot_general(sums_ref[0], plain, dims, precision=EXACT, preferred_element_type=jnp.float32)
    sums_im = lax.dot_general(sums_ref[1], signed, dims, precision=EXACT, preferred_element_type=jnp.float32)
    component, mode, sine = column(lanes(sums_re.shape))
    scale = 2.0 / length
    with_cos = jnp.where(sine, sums_im, sums_re) * scale
    with_sin = jnp.where(sine, sums_re, -sums_im) * scale
    component = component[0:1]

    def chunk(at):
        start = pl.multiple_of(lax.rem(place + at + place_count, place_count) * pitch, pitch)
        return cells_ref[:, pl.ds(start, pitch)]

    own = chunk(0)
    lane = lanes((1, pitch))
    first = (axial - 1) * SEGMENT_LANES
    edge = jnp.where(lane < first + EDGE, pltpu.roll(chunk(-1), (first + EDGE) % pitch, 1), pltpu.roll(own, (first + EDGE) % pitch, 1))
    edge = jnp.where(lane < first + 2 * EDGE, edge, pltpu.roll(own, (first + 3 * EDGE) % pitch, 1))
    edge = jnp.where(lane < first + 3 * EDGE, edge, pltpu.roll(chunk(1), (first + 3 * EDGE) % pitch, 1))

    def upright(cells):
        wide = jnp.broadcast_to(cells.astype(jnp.float32), (pitch, pitch))
        return jnp.transpose(wide).astype(jnp.int32)

    edge_cells = upright(edge)[first:first + SEGMENT_LANES]
    at_cells = jnp.concatenate([upright(own), edge_cells], 0)
    _, mode, _ = column(lanes(at_cells.shape))
    blades = [picked(blades_ref[...], face + n) for n in range(2)]
    cos_table, sin_table = waves(mode_number(mode, blades) * at_cells, length)
    for c in range(components):
        row_cos = jnp.zeros((1, pitch), jnp.float32)
        row_sin = jnp.zeros((1, pitch), jnp.float32)
        for b in range(components):
            at = b * components + c
            row_cos = jnp.where(component == b, with_cos[at:at + 1], row_cos)
            row_sin = jnp.where(component == b, with_sin[at:at + 1], row_sin)
        part = row_cos * cos_table + row_sin * sin_table
        for n, value in enumerate(split(part)):
            synth_ref[n, pl.ds(c * pitch, pitch), :] = value[:pitch]
            synth_ref[n, pl.ds(components * pitch + c * SEGMENT_LANES, SEGMENT_LANES), :] = value[pitch:]
    used = components * (pitch + SEGMENT_LANES)
    rest = synth_ref.shape[1] - used
    if rest:
        synth_ref[:, pl.ds(used, rest), :] = jnp.zeros((2, rest, pitch), jnp.bfloat16)


def jacobian(jac_ref, components, b, c, d):
    return jac_ref[pl.ds((b * components + c) * 6 + d, 1), :]


def mixed(jac_ref, source, couplings, neighbours):
    total = list(source)
    jac = functools.partial(jacobian, jac_ref, len(total))
    for d, neighbour in enumerate(neighbours):
        if neighbour is None:
            continue
        for c in range(len(total)):
            term = jac(0, c, d) * neighbour[0]
            for b in range(1, len(total)):
                term = term + jac(b, c, d) * neighbour[b]
            total[c] = total[c] + couplings[d] * term
    return total


def layer_update(jac_ref, state_ref, edge_ref, coef_ref, t, a, height):
    _, components, axial, wide, pitch = state_ref.shape
    lane = lanes((height, pitch))
    start = a * SEGMENT_LANES
    own = [state_ref[t, c, a] for c in range(components)]
    above = [state_ref[t, c, a + 1, :height] for c in range(components)] if a < axial - 1 else None
    below = [state_ref[t, c, a - 1, :height] for c in range(components)] if a else None
    edge = [edge_ref[t, c, :height] for c in range(components)]
    span_next = [pltpu.roll(x, wide - 1, 0)[:height] for x in own]
    span_prev = [pltpu.roll(x, 1, 0)[:height] for x in own]
    own = [x[:height] for x in own]
    to_end = (pitch - 1 - (start + 3 * EDGE)) % pitch
    to_begin = (pitch - (start + EDGE - 1)) % pitch
    pitch_next = [
        jnp.where(lane == pitch - 1, pltpu.roll(e, to_end, 1), pltpu.roll(x, pitch - 1, 1))
        for e, x in zip(edge, own)
    ]
    pitch_prev = [
        jnp.where(lane == 0, pltpu.roll(e, to_begin, 1), pltpu.roll(x, 1, 1))
        for e, x in zip(edge, own)
    ]
    source = [coef_ref[c, a, :height] for c in range(components)]
    couplings = [coef_ref[components + d, a, :height] for d in range(6)]
    return mixed(jac_ref, source, couplings, (above, below, span_next, span_prev, pitch_next, pitch_prev))


def edge_update(jac_ref, edge_ref, edge_coef_ref, t, axial):
    components, wide, pitch = edge_ref.shape[1:]
    lane = lanes((wide, pitch))
    own = [edge_ref[t, c] for c in range(components)]
    above = [jnp.where(lane < (axial - 1) * SEGMENT_LANES, pltpu.roll(x, pitch - SEGMENT_LANES, 1), 0.0) for x in own]
    below = [jnp.where(lane >= SEGMENT_LANES, pltpu.roll(x, SEGMENT_LANES, 1), 0.0) for x in own]
    span_next = [pltpu.roll(x, wide - 1, 0) for x in own]
    span_prev = [pltpu.roll(x, 1, 0) for x in own]
    pitch_next = [pltpu.roll(x, pitch - 1, 1) for x in own]
    pitch_prev = [pltpu.roll(x, 1, 1) for x in own]
    source = [edge_coef_ref[c] for c in range(components)]
    couplings = [edge_coef_ref[components + d] for d in range(6)]
    return mixed(jac_ref, source, couplings, (above, below, span_next, span_prev, pitch_next, pitch_prev))


def edge_boundary(field, c, components, pitch, axial):
    at = components * pitch + c * SEGMENT_LANES
    tile = field[:, (at // pitch) * pitch:(at // pitch + 1) * pitch]
    return pltpu.roll(tile, ((axial - 1) * SEGMENT_LANES - at % pitch) % pitch, 1)


def advance(refs, t, a, height=None):
    state_ref = refs[1]
    height = height or state_ref.shape[3]
    for c, value in enumerate(layer_update(*refs, t, a, height)):
        state_ref[t + 1, c, a, :height] = value


def first_kernel(
    jac_ref, state_in_ref, coef_in_ref, inv_in_ref, edges_ref, span_ref, inner_ref, outer_ref,
    coef_ref, inv_ref, edge_coef_ref, state_ref, edge_ref, *, groups,
):
    _, components, axial, wide, pitch = state_ref.shape
    span = wide - EDGE
    side = lax.axis_index("span")
    fields = 2 * components + 6
    line = rows((EDGE, pitch))
    keep_half = jnp.where(side == 0, line, EDGE - 1 - line) < HALF
    fifth = jnp.where(side == 0, HALF, HALF - 1)
    from_low, from_high = half_rows(1 - side)
    pairs = -(-(fields * axial + 1) // 2)

    def ghost(n):
        value = pltpu.roll(span_ref[n // 2], from_high if n % 2 else from_low, 0)
        value = jnp.where(keep_half, value, 0.0)
        if n < components * axial:
            extra = pltpu.roll(span_ref[pairs + n // EDGE], lax.rem(fifth + EDGE - n % EDGE, EDGE), 0)
            value = jnp.where(line == fifth, extra, value)
        return value

    even = lax.rem(lax.axis_index("pitch"), 2) == 0

    def group(ref, g):
        corner = ref[pl.ds(groups * span + g * EDGE, EDGE), :]
        return jnp.concatenate([ref[pl.ds(g * span, span), :], corner], 0)

    halves = [(group(inner_ref, g), group(outer_ref, g)) for g in range(groups)]
    from_left = [jnp.where(even, outer, inner) for inner, outer in halves]
    from_right = [jnp.where(even, inner, outer) for inner, outer in halves]
    near, far = slots(fields + 1, components)
    keep_five = keep_half | (line == fifth)
    for f in range(fields + 1):
        if f < fields:
            layers = [ghost(f * axial + a) for a in range(axial)]
        else:
            layers = [jnp.zeros((EDGE, pitch), jnp.float32)] * (axial - 1) + [ghost(fields * axial)]
        if f < components:
            for a in range(axial):
                state_ref[0, f, a, span:] = layers[a]
        elif f < fields:
            for a in range(axial):
                coef_ref[f - components, a, span:] = layers[a]
        else:
            inv_ref[span:] = layers[-1]
        g, at = near[f]
        value = jnp.concatenate([edges_ref[f], to_edges(layers, pitch)], 0)
        lane = lanes((wide, pitch)) % SEGMENT_LANES
        value = jnp.where((lane >= HALF) & (lane < EDGE), pltpu.roll(from_left[g], (HALF - at) % pitch, 1), value)
        value = jnp.where(
            (lane >= 3 * EDGE) & (lane < 3 * EDGE + HALF),
            pltpu.roll(from_right[g], (3 * EDGE - at) % pitch, 1), value,
        )
        if f < components:
            g, at = far[f]
            value = jnp.where(lane == HALF - 1, pltpu.roll(from_left[g], (HALF - 1 - at) % pitch, 1), value)
            value = jnp.where(
                lane == 3 * EDGE + HALF, pltpu.roll(from_right[g], (3 * EDGE + HALF - at) % pitch, 1), value,
            )
        target, at = (edge_ref.at[0], f) if f < components else (edge_coef_ref, f - components)
        target[at, :span] = value[:span]
        target[at, span:] = jnp.where(keep_five if f < components else keep_half, value[span:], 0.0)
    sweeps_without_boundaries(jac_ref, state_ref, edge_ref, coef_ref, edge_coef_ref, 0, 1)


def sweeps_without_boundaries(jac_ref, state_ref, edge_ref, coef_ref, edge_coef_ref, first, last):
    axial = state_ref.shape[2]
    for t in range(first, last):
        for a in range(axial - t):
            advance((jac_ref, state_ref, edge_ref, coef_ref), t, a)
        if t < axial - 1:
            for c, value in enumerate(edge_update(jac_ref, edge_ref, edge_coef_ref, t, axial)):
                edge_ref[t + 1, c] = value


def more_kernel(
    jac_ref, coef_ref, edge_coef_ref, state_in_ref, edge_in_ref, table_ref, state_ref, edge_ref, modes_ref, part_ref,
):
    _, components, axial, wide, pitch = state_ref.shape
    span = wide - EDGE
    side = lax.axis_index("span")
    sweeps_without_boundaries(jac_ref, state_ref, edge_ref, coef_ref, edge_coef_ref, 1, axial)
    strips = [
        jnp.concatenate([state_ref[t, c, 0] for t in range(1, axial)] + [state_ref[axial, c, 0, :span]], 0)
        for c in range(components)
    ]
    total = projected(strips, table_ref)
    ghosts = jnp.zeros((EDGE, pitch), jnp.float32)
    for t in range(1, axial):
        part = total[(t - 1) * wide:t * wide]
        modes_ref[pl.ds((t - 1) * span, span), :] = part[:span]
        keep, to_packed, _ = ghost_rows(side, t, axial)
        ghosts = jnp.where(keep, pltpu.roll(part[span:], to_packed, 0), ghosts)
    modes_ref[pl.ds((axial - 1) * span, EDGE), :] = ghosts
    part_ref[...] = total[(axial - 1) * wide:]


def ghost_rows(side, t, axial):
    line = rows((EDGE, 1))
    distance = jnp.where(side == 0, line, EDGE - 1 - line)
    start = sum(axial - n for n in range(1, t))
    to_packed = jnp.where(side == 0, start, (EDGE - start) % EDGE)
    from_packed = jnp.where(side == 0, (EDGE - start) % EDGE, start)
    return (distance >= start) & (distance < start + axial - t), to_packed, from_packed


def along_axis(jac_ref, coef_ref, delta, a, height):
    components = len(delta)
    out = []
    for c in range(components):
        term = jacobian(jac_ref, components, 0, c, 0) * delta[0]
        for b in range(1, components):
            term = term + jacobian(jac_ref, components, b, c, 0) * delta[b]
        out.append(coef_ref[components, a, :height] * term)
    return out


def late_kernel(
    jac_ref, coef_ref, inv_ref, part_ref, more_ref, first_ref, synth_ref, table_ref, modes_ref,
):
    span, pitch = part_ref.shape
    components, axial = coef_ref.shape[0] - 6, coef_ref.shape[1]
    field = synthesised(first_ref[EDGE:], synth_ref, components * pitch)
    delta = [inv_ref[:span] * field[:, c * pitch:(c + 1) * pitch] for c in range(components)]
    for a in range(axial - 2, -1, -1):
        delta = along_axis(jac_ref, coef_ref, delta, a, span)
    before = more_ref.shape[0]
    modes_ref[:before] = more_ref[...]
    modes_ref[before:] = part_ref[...] + projected(delta, table_ref)


def between_kernel(
    jac_ref, coef_ref, inv_ref, edge_coef_ref, state_in_ref, edge_in_ref, modes_ref, synth_ref, more_ref,
    state_ref, edge_ref,
):
    components, axial = state_ref.shape[1], state_ref.shape[2]
    wide, pitch = state_ref.shape[3:]
    modes = modes_ref[...]
    field = synthesised(jnp.concatenate([modes[EDGE:], modes[:EDGE]], 0), synth_ref, synth_ref.shape[1])
    delta = [inv_ref[...] * field[:, c * pitch:(c + 1) * pitch] for c in range(components)]
    for t in range(1, axial + 1):
        for c in range(components):
            state_ref[t, c, axial - t] += delta[c]
        if t < axial:
            delta = along_axis(jac_ref, coef_ref, delta, axial - 1 - t, wide)
    for c in range(components):
        edge_ref[1, c] += edge_coef_ref[components + 6] * edge_boundary(field, c, components, pitch, axial)
    diagonal_sweeps(jac_ref, state_ref, edge_ref, coef_ref, edge_coef_ref, 1, axial // 2 + 1)


def beside_kernel(jac_ref, coef_ref, edge_coef_ref, state_in_ref, edge_in_ref, state_ref, edge_ref):
    axial, span = state_ref.shape[2], state_ref.shape[3] - EDGE
    diagonal_sweeps(jac_ref, state_ref, edge_ref, coef_ref, edge_coef_ref, axial // 2 + 1, axial)
    advance((jac_ref, state_ref, edge_ref, coef_ref), axial, 0, span)


def diagonal_sweeps(jac_ref, state_ref, edge_ref, coef_ref, edge_coef_ref, first, last):
    axial = state_ref.shape[2]
    for t in range(first, last):
        advance((jac_ref, state_ref, edge_ref, coef_ref), t, axial - t)
        for c, value in enumerate(edge_update(jac_ref, edge_ref, edge_coef_ref, t, axial)):
            edge_ref[t + 1, c] = value


def second_kernel(
    jac_ref, coef_ref, inv_ref, edge_coef_ref, state_in_ref, edge_in_ref, more_a_ref, more_b_ref, synth_ref,
    state_ref, edge_ref, out_hbm, bound_ref, out_ref, sems,
):
    axial, components, span, pitch = out_ref.shape
    copies = [pltpu.make_async_copy(out_ref.at[a], out_hbm.at[:, a], sems.at[a]) for a in range(axial)]
    wide = span + EDGE
    side = lax.axis_index("span")
    more = more_a_ref[...] + more_b_ref[...]
    start = (axial - 1) * span
    parts = []
    for t in range(1, axial):
        _, _, from_packed = ghost_rows(side, t, axial)
        parts += [more[(t - 1) * span:t * span], pltpu.roll(more[start:start + EDGE], from_packed, 0)]
    field = synthesised(jnp.concatenate(parts + [more[start + EDGE:]], 0), synth_ref, synth_ref.shape[1])
    for t in range(1, axial):
        part = field[(t - 1) * wide:t * wide]
        for c in range(components):
            bound_ref[t, c] = inv_ref[...] * part[:, c * pitch:(c + 1) * pitch]
    for c in range(components):
        bound_ref[axial, c, :span] = inv_ref[:span] * field[(axial - 1) * wide:, c * pitch:(c + 1) * pitch]
    delta = [bound_ref[1, c] for c in range(components)]
    for t in range(2, axial + 2):
        height = wide if t <= axial else span
        for c in range(components):
            state_ref[t, c, axial + 1 - t, :height] += delta[c][:height]
        if t < axial + 1:
            delta = along_axis(jac_ref, coef_ref, delta, axial - t, wide)
    for c in range(components):
        out_ref[0, c] = state_ref[axial + 1, c, 0, :span]
    copies[0].start()
    for t in range(1, axial):
        if t > 1:
            for c, value in enumerate(edge_update(jac_ref, edge_ref, edge_coef_ref, t, axial)):
                edge_ref[t + 1, c] = value
        part = field[(t - 1) * wide:t * wide]
        for c in range(components):
            edge_ref[t + 1, c] += edge_coef_ref[components + 6] * edge_boundary(part, c, components, pitch, axial)
    refs = (jac_ref, state_ref, edge_ref, coef_ref)

    for t in range(2, axial):
        for a in range(axial + 1 - t, axial):
            advance(refs, t, a)
        for c in range(components):
            state_ref[t + 1, c, axial - 1] += bound_ref[t, c]
    for a in range(1, axial):
        for c, value in enumerate(layer_update(*refs, axial, a, span)):
            out_ref[a, c] = value + bound_ref[axial, c, :span] if a == axial - 1 else value
        copies[a].start()
    for copy in copies:
        copy.wait()


def moved(x, to):
    sizes = [lax.axis_size(name) for name in AXES]
    pairs = []
    for r in range(sizes[0]):
        for s in range(sizes[1]):
            for p in range(sizes[2]):
                target = to(r, s, p)
                if all(0 <= at < size for at, size in zip(target, sizes)):
                    number = lambda at: (at[0] * sizes[1] + at[1]) * sizes[2] + at[2]
                    pairs.append((number((r, s, p)), number(target)))
    return lax.ppermute(x, AXES, pairs)


def struct(*shape):
    return jax.ShapeDtypeStruct(shape, jnp.float32)


def on_device(
    adjoint_start, source, couplings, damping, jacobians, giles_real, giles_imag, blades, mode_orders, cell_map,
):
    components, axial, span, pitch = adjoint_start.shape
    row_count, span_count, place_count = (lax.axis_size(name) for name in AXES)
    length = pitch * place_count
    assert sum(axial - t for t in range(1, axial)) <= EDGE
    assert components == COMPONENTS and components * WAVES <= pitch
    assert axial == ITERS - 1 and ITERS <= EDGE and axial * SEGMENT_LANES == pitch
    assert span_count == 2 and place_count > 2 and place_count & (place_count - 1) == 0
    wide = span + EDGE
    fields = 2 * components + 6
    groups = slots(fields + 1, components)[1][-1][0] + 1
    pairs = -(-(fields * axial + 1) // 2)
    span_tiles = pairs + -(-components * axial // EDGE)
    vmem = pl.BlockSpec(memory_space=pltpu.VMEM)
    hbm = pl.BlockSpec(memory_space=pltpu.HBM)

    def in_hbm(x):
        return pltpu.with_memory_space_constraint(x, pltpu.HBM)

    def call(kernel, name, outs, ins, aliases=None, scratch=(), limit=40 * MIB, out_specs=None, **fixed):
        specs = [spec for spec, _ in ins]
        return pl.pallas_call(
            functools.partial(kernel, **fixed),
            out_shape=outs,
            in_specs=specs,
            out_specs=out_specs or jax.tree.map(lambda _: vmem, outs),
            scratch_shapes=scratch,
            input_output_aliases=aliases or {},
            compiler_params=params(limit),
            name=name,
        )(*[value for _, value in ins])

    tables = (
        jacobians.transpose(2, 3, 0, 1), giles_real.transpose(2, 3, 0, 1), giles_imag.transpose(2, 3, 0, 1),
        mode_orders.transpose(0, 2, 1), cell_map,
    )
    blades = blades.reshape(1, -1)
    corner_rows = groups * EDGE
    state_shape = struct(axial + 2, components, axial, wide, pitch)
    state, coef, inv, span_out, small, modes, table, blades, *tables = call(
        start_kernel, "start",
        (
            state_shape, struct(components + 6, axial, wide, pitch), struct(wide, pitch),
            struct(span_tiles, EDGE, pitch), struct(2 * corner_rows + EDGE, pitch), struct(span, pitch),
            jax.ShapeDtypeStruct((2, components * pitch, pitch), jnp.bfloat16),
            *(jax.ShapeDtypeStruct(x.shape, x.dtype) for x in (blades, *tables)),
        ),
        [(hbm, in_hbm(x)) for x in (adjoint_start, source, couplings, damping, blades, *tables)],
        scratch=[
            pltpu.VMEM(source.shape, jnp.float32), pltpu.VMEM(couplings.shape, jnp.float32),
            pltpu.VMEM(damping.shape, jnp.float32), pltpu.SemaphoreType.DMA((5 + len(tables),)),
        ],
        groups=groups, length=length,
    )
    edges, inner, outer = call(
        pack_kernel, "pack",
        (struct(fields + 1, span, pitch), struct((groups + 1) * wide, pitch), struct(groups * wide, pitch)),
        [(vmem, x) for x in (state, coef, inv, modes)],
        groups=groups,
    )
    steps = [1 << n for n in range(place_count.bit_length() - 2)]
    last_step = place_count // 2

    def near(x):
        return moved(x, lambda r, s, p: (r - 1, s, p))

    synth, jac = call(
        synth_kernel, "synth",
        (
            jax.ShapeDtypeStruct(
                (2, -(-components * (pitch + SEGMENT_LANES) // pitch) * pitch, pitch), jnp.bfloat16
            ),
            struct(-(-6 * components * components // EDGE) * EDGE, pitch),
        ),
        [(vmem, x) for x in (blades, *tables)],
        scratch=[pltpu.VMEM((2, components * components, mode_orders.shape[1]), jnp.float32)],
        row_count=row_count, place_count=place_count, components=components, pitch=pitch, length=length, axial=axial,
    )
    small, edges, jac = lax.optimization_barrier((moved(small, lambda r, s, p: (r, 1 - s, p)), edges, jac))
    from_span = moved(span_out, lambda r, s, p: (r, 1 - s, p))
    edge_shape = struct(axial + 1, components, wide, pitch)
    inner = lax.dynamic_update_slice(inner, small[:corner_rows + EDGE], (groups * span, 0))
    outer = lax.dynamic_update_slice(outer, small[corner_rows + EDGE:], (groups * span, 0))
    modes = inner[groups * span + corner_rows:]
    outer = moved(outer, lambda r, s, p: (r, s, (p - 1 + 2 * (p % 2)) % place_count))
    inner = moved(inner, lambda r, s, p: (r, s, p ^ 1))
    modes = modes + inner[groups * span + corner_rows:]
    for step in steps[1:]:
        modes = modes + moved(modes, lambda r, s, p: (r, s, p ^ step))
    got = moved(modes, lambda r, s, p: (r, s, p ^ last_step))
    coef, inv, edge_coef, state, edge = call(
        first_kernel, "first_sweep",
        (
            struct(components + 6, axial, wide, pitch), struct(wide, pitch), struct(components + 7, wide, pitch),
            state_shape, edge_shape,
        ),
        [(vmem, x) for x in (jac, state, coef, inv, edges, from_span, inner, outer)],
        aliases={1: 3, 2: 0, 3: 1},
        groups=groups,
    )
    got, inv = lax.optimization_barrier((got, inv))
    modes = near(modes + got)
    state, edge, more, part = call(
        more_kernel, "more_sweeps",
        (state_shape, edge_shape, struct((axial - 1) * span + EDGE, pitch), struct(span, pitch)),
        [(vmem, x) for x in (jac, coef, edge_coef, state, edge, table)],
        aliases={3: 0, 4: 1},
    )
    more_shape = struct(axial * span + EDGE, pitch)
    more = call(
        late_kernel, "late_modes", more_shape,
        [(vmem, x) for x in (jac, coef, inv, part, more, modes, synth, table)],
    )
    up, up_across = near(more), moved(more, lambda r, s, p: (r - 1, s, p ^ 1))
    state, edge = call(
        between_kernel, "between_sweeps", (state_shape, edge_shape),
        [(vmem, x) for x in (jac, coef, inv, edge_coef, state, edge, modes, synth, more)],
        aliases={4: 0, 5: 1},
    )
    up, edge = lax.optimization_barrier((up, edge))
    more_a = up + up_across
    state, edge = call(
        beside_kernel, "beside_sweeps", (state_shape, edge_shape),
        [(vmem, x) for x in (jac, coef, edge_coef, state, edge)],
        aliases={3: 0, 4: 1},
    )
    for step in steps[1:]:
        more_a = more_a + moved(more_a, lambda r, s, p: (r, s, p ^ step))
    more_b = moved(more_a, lambda r, s, p: (r, s, p ^ last_step))
    return call(
        second_kernel, "second_sweeps", (state_shape, edge_shape, struct(components, axial, span, pitch)),
        [(vmem, x) for x in (jac, coef, inv, edge_coef, state, edge, more_a, more_b, synth)],
        aliases={4: 0, 5: 1},
        scratch=[
            pltpu.VMEM((axial + 1, components, wide, pitch), jnp.float32),
            pltpu.VMEM((axial, components, span, pitch), jnp.float32), pltpu.SemaphoreType.DMA((axial,)),
        ],
        out_specs=(vmem, vmem, hbm),
    )[2]


def solution(mesh):
    placed = (
        P(None, "row", "span", "pitch"),
        P(None, "row", "span", "pitch"),
        P(None, "row", "span", "pitch"),
        P("row", "span", "pitch"),
        P("row", None, None, None),
        P(),
        P(),
        P(),
        P(),
        P("row", None),
    )
    return jax.shard_map(
        on_device,
        mesh=mesh,
        in_specs=placed,
        out_specs=P(None, "row", "span", "pitch"),
        check_vma=False,
    )
```

```python
import functools
import math

import jax
import jax.numpy as jnp
from jax import lax
from jax.experimental import pallas as pl
from jax.experimental.pallas import tpu as pltpu
from jax.sharding import PartitionSpec as P

ITERS = 5
AXES = ("row", "span", "pitch")

ORDER_MAX = 2
BASE = 2 * ORDER_MAX + 1
COSINES = (BASE * BASE + 1) // 2
WAVES = 2 * COSINES - 1
COMPONENTS = 5
EDGE = 8
HALF = EDGE // 2
SEGMENT_LANES = 4 * EDGE
EXACT = lax.Precision.HIGHEST
MIB = 1024 * 1024


def params(limit):
    return pltpu.CompilerParams(vmem_limit_bytes=limit)


def lanes(shape):
    return lax.broadcasted_iota(jnp.int32, shape, len(shape) - 1)


def rows(shape):
    return lax.broadcasted_iota(jnp.int32, shape, len(shape) - 2)


def column(j):
    component = (j * 41) >> 10
    wave = j - WAVES * component
    sine = wave >= COSINES
    return component, jnp.where(sine, wave - (COSINES - 1), wave), sine


def mode_number(mode, blades):
    high = ((mode + ORDER_MAX) * 13) >> 6
    low = mode - BASE * high
    return high * blades[0] + low * blades[1]


def waves(products, length):
    if length & (length - 1) == 0:
        phase = products & (length - 1)
    else:
        phase = jnp.mod(products, length)
    turn = phase.astype(jnp.float32) * (1.0 / length)
    quarter = jnp.floor(4.0 * turn + 0.5)
    x = (turn - 0.25 * quarter) * (2.0 * math.pi)
    y = x * x
    sine = x * (1.0 + y * (-1.0 / 6 + y * (1.0 / 120 + y * (-1.0 / 5040 + y * (1.0 / 362880)))))
    cosine = 1.0 + y * (-0.5 + y * (1.0 / 24 + y * (-1.0 / 720 + y * (1.0 / 40320 - y * (1.0 / 3628800)))))
    quarter = quarter.astype(jnp.int32) & 3
    odd = (quarter & 1) == 1
    cos_out = jnp.where(odd, sine, cosine)
    sin_out = jnp.where(odd, cosine, sine)
    cos_out = jnp.where((quarter == 1) | (quarter == 2), -cos_out, cos_out)
    sin_out = jnp.where(quarter >= 2, -sin_out, sin_out)
    return cos_out, sin_out


def to_edges(layers, pitch):
    lane = lanes(layers[-1].shape)
    block = jnp.zeros_like(layers[-1])
    for a, layer in enumerate(layers):
        if layer is None:
            continue
        start = a * SEGMENT_LANES
        first = pltpu.roll(layer, (start + EDGE) % pitch, layer.ndim - 1)
        last = pltpu.roll(layer, (start + 3 * EDGE) % pitch, layer.ndim - 1)
        block = jnp.where((lane >= start + EDGE) & (lane < start + 2 * EDGE), first, block)
        block = jnp.where((lane >= start + 2 * EDGE) & (lane < start + 3 * EDGE), last, block)
    return block


def half_rows(side):
    return jnp.where(side == 0, EDGE // 2, 0), jnp.where(side == 0, 0, EDGE // 2)


def slots(fields, components):
    per_group = SEGMENT_LANES // HALF
    near = [(f // per_group, f % per_group * HALF) for f in range(fields)]
    group, lane = near[-1]
    far = [(group, lane + HALF + c) for c in range(components)]
    return near, far


def packed_edges(blocks, place, components):
    near, far = slots(len(blocks), components)
    pitch = blocks[0].shape[1]
    lane = lanes(blocks[0].shape) % SEGMENT_LANES
    sides = []
    for near_at, far_at in ((3 * EDGE - HALF, 3 * EDGE - HALF - 1), (EDGE, EDGE + HALF)):
        packed = [jnp.zeros_like(blocks[0]) for _ in range(far[-1][0] + 1)]
        for f, (g, to) in enumerate(near):
            value = pltpu.roll(blocks[f], (to - near_at) % pitch, 1)
            packed[g] = jnp.where((lane >= to) & (lane < to + HALF), value, packed[g])
        for f, (g, to) in enumerate(far):
            packed[g] = jnp.where(lane == to, pltpu.roll(blocks[f], (to - far_at) % pitch, 1), packed[g])
        sides.append(packed)
    even = lax.rem(place, 2) == 0
    inner = [jnp.where(even, right, left) for right, left in zip(*sides)]
    outer = [jnp.where(even, left, right) for right, left in zip(*sides)]
    return inner, outer


def edge_blocks(state_ref, coef_ref, inv_ref, at):
    components, axial, pitch = state_ref.shape[1], state_ref.shape[2], state_ref.shape[4]
    blocks = [to_edges([state_ref[0, c, a, at, :] for a in range(axial)], pitch) for c in range(components)]
    blocks += [to_edges([coef_ref[f, a, at, :] for a in range(axial)], pitch) for f in range(components + 6)]
    return blocks + [to_edges([None] * (axial - 1) + [inv_ref[at, :]], pitch)]


def start_kernel(
    adjoint_hbm, source_hbm, couplings_hbm, damping_hbm, blades_hbm, *refs, groups, length,
):
    state_ref, coef_ref, inv_ref, span_ref, small_ref, modes_ref, table_ref, blades_ref = refs[5:13]
    source_ref, couplings_ref, damping_ref, sems = refs[18:]
    components, axial, span, pitch = source_ref.shape
    adjoint_ref = state_ref.at[0, :, :, pl.ds(0, span), :]
    copies = [
        pltpu.make_async_copy(src, dst, sems.at[n])
        for n, (src, dst) in enumerate((
            (couplings_hbm, couplings_ref), (damping_hbm, damping_ref), (source_hbm, source_ref),
            (adjoint_hbm, adjoint_ref), (blades_hbm, blades_ref), *zip(refs[:5], refs[13:18]),
        ))
    ]
    for copy in copies:
        copy.start()
    row, side, place = (lax.axis_index(name) for name in AXES)
    copies[4].wait()
    face = jnp.maximum(row - 1, 0)
    component, mode, sine = column(lanes((pitch, pitch)))
    number = mode_number(mode, [picked(blades_ref[...], face + n) for n in range(2)])
    cos_table, sin_table = waves(number * (place * pitch + rows((pitch, pitch))), length)
    table = jnp.where(component < components, jnp.where(sine, sin_table, cos_table), 0.0)
    for c in range(components):
        for n, value in enumerate(split(jnp.where(component == c, table, 0.0))):
            table_ref[n, pl.ds(c * pitch, pitch), :] = value
    copies[0].wait()
    copies[1].wait()
    diag = damping_ref[...]
    for d in range(6):
        diag = diag + couplings_ref[d]
    inverse = 1.0 / diag
    for d in range(6):
        coef_ref[components + d, :, :span] = couplings_ref[d] * inverse
    inv_ref[:span] = inverse[axial - 1]
    copies[2].wait()
    for c in range(components):
        coef_ref[c, :, :span] = source_ref[c] * inverse
    copies[3].wait()
    edge_row = pl.multiple_of(jnp.where(side == 0, span - EDGE, 0), EDGE)
    blocks = edge_blocks(state_ref, coef_ref, inv_ref, pl.ds(edge_row, EDGE))
    for n, packed in enumerate(packed_edges(blocks, place, components)):
        for g, value in enumerate(packed):
            small_ref[pl.ds((n * (groups + 1) + g) * EDGE, EDGE), :] = value
    modes_ref[...] = projected([adjoint_ref[c, 0] for c in range(components)], table_ref)
    small_ref[pl.ds(groups * EDGE, EDGE), :] = modes_ref[pl.ds(edge_row, EDGE), :]

    to_low, to_high = half_rows(side)
    line = rows((EDGE, pitch))
    tiles = [state_ref[0, c, a, pl.ds(edge_row, EDGE), :] for c in range(components) for a in range(axial)]
    tiles += [coef_ref[f, a, pl.ds(edge_row, EDGE), :] for f in range(components + 6) for a in range(axial)]
    tiles += [inv_ref[pl.ds(edge_row, EDGE), :]]
    pairs = -(-len(tiles) // 2)
    for n in range(pairs):
        value = pltpu.roll(tiles[2 * n], to_low, 0)
        if 2 * n + 1 < len(tiles):
            value = jnp.where(line < HALF, value, pltpu.roll(tiles[2 * n + 1], to_high, 0))
        span_ref[n] = value
    fifth = jnp.where(side == 0, HALF - 1, HALF)
    for n in range(span_ref.shape[0] - pairs):
        value = jnp.zeros((EDGE, pitch), jnp.float32)
        for k in range(min(EDGE, components * axial - n * EDGE)):
            value = jnp.where(line == k, pltpu.roll(tiles[n * EDGE + k], lax.rem(k + EDGE - fifth, EDGE), 0), value)
        span_ref[pairs + n] = value
    for copy in copies[5:]:
        copy.wait()


def pack_kernel(state_ref, coef_ref, inv_ref, modes_ref, edges_ref, inner_ref, outer_ref, *, groups):
    _, components, axial, wide, pitch = state_ref.shape
    span = wide - EDGE
    place = lax.axis_index("pitch")
    blocks = edge_blocks(state_ref, coef_ref, inv_ref, pl.ds(0, span))
    for f, block in enumerate(blocks):
        edges_ref[f] = block
    for out_ref, packed in zip((inner_ref, outer_ref), packed_edges(blocks, place, components)):
        for g, value in enumerate(packed):
            out_ref[pl.ds(g * span, span), :] = value
    start = groups * span + (groups + 1) * EDGE
    inner_ref[pl.ds(start, span), :] = modes_ref[...]


def picked(values, at):
    chosen = jnp.where(lanes(values.shape) == at, values.astype(jnp.float32), 0.0)
    return jnp.sum(chosen, axis=1, keepdims=True).astype(jnp.int32)


def split(x):
    high = x.astype(jnp.bfloat16)
    return high, (x - high.astype(jnp.float32)).astype(jnp.bfloat16)


def product(x, table, dims):
    x_high, x_low = split(x)
    table_high, table_low = table
    dot = functools.partial(lax.dot_general, dimension_numbers=(dims, ((), ())), preferred_element_type=jnp.float32)
    return dot(x_high, table_high) + (dot(x_low, table_high) + dot(x_high, table_low))


def projected(strips, table_ref):
    return product(jnp.concatenate(strips, 1), (table_ref[0], table_ref[1]), ((1,), (0,)))


def synthesised(modes, synth_ref, count):
    return product(modes, (synth_ref[0, :count], synth_ref[1, :count]), ((1,), (1,)))


def synth_kernel(
    blades_ref, jacobians_ref, giles_re_ref, giles_im_ref, orders_ref, cells_ref, synth_ref, rows_ref, sums_ref,
    *, row_count, place_count, components, pitch, length, axial,
):
    row, place = lax.axis_index("row"), lax.axis_index("pitch")
    face = jnp.minimum(row, row_count - 2)
    for b in range(components):
        for c in range(components):
            entries = jacobians_ref[b, c]
            for d in range(6):
                at = (b * components + c) * 6 + d
                rows_ref[pl.ds(at, 1), :] = jnp.broadcast_to(entries[:, d:d + 1], (1, pitch))
    modes = orders_ref.shape[2]
    orders = orders_ref[face]
    tag = BASE * orders[0:1] + orders[1:2]
    component, mode, _ = column(rows((pitch, modes)))
    same = (jnp.abs(tag) == mode) & (component < components)
    plain = jnp.where(same, 1.0, 0.0)
    signed = jnp.where(tag < 0, -plain, plain)
    dims = (((1,), (1,)), ((), ()))
    for n, ref in enumerate((giles_re_ref, giles_im_ref)):
        for b in range(components):
            for c in range(components):
                sums_ref[n, pl.ds(b * components + c, 1), :] = ref[b, c, pl.ds(face, 1), :]
    sums_re = lax.dot_general(sums_ref[0], plain, dims, precision=EXACT, preferred_element_type=jnp.float32)
    sums_im = lax.dot_general(sums_ref[1], signed, dims, precision=EXACT, preferred_element_type=jnp.float32)
    component, mode, sine = column(lanes(sums_re.shape))
    scale = 2.0 / length
    with_cos = jnp.where(sine, sums_im, sums_re) * scale
    with_sin = jnp.where(sine, sums_re, -sums_im) * scale
    component = component[0:1]

    def chunk(at):
        start = pl.multiple_of(lax.rem(place + at + place_count, place_count) * pitch, pitch)
        return cells_ref[:, pl.ds(start, pitch)]

    own = chunk(0)
    lane = lanes((1, pitch))
    first = (axial - 1) * SEGMENT_LANES
    edge = jnp.where(lane < first + EDGE, pltpu.roll(chunk(-1), (first + EDGE) % pitch, 1), pltpu.roll(own, (first + EDGE) % pitch, 1))
    edge = jnp.where(lane < first + 2 * EDGE, edge, pltpu.roll(own, (first + 3 * EDGE) % pitch, 1))
    edge = jnp.where(lane < first + 3 * EDGE, edge, pltpu.roll(chunk(1), (first + 3 * EDGE) % pitch, 1))

    def upright(cells):
        wide = jnp.broadcast_to(cells.astype(jnp.float32), (pitch, pitch))
        return jnp.transpose(wide).astype(jnp.int32)

    edge_cells = upright(edge)[first:first + SEGMENT_LANES]
    at_cells = jnp.concatenate([upright(own), edge_cells], 0)
    _, mode, _ = column(lanes(at_cells.shape))
    blades = [picked(blades_ref[...], face + n) for n in range(2)]
    cos_table, sin_table = waves(mode_number(mode, blades) * at_cells, length)
    for c in range(components):
        row_cos = jnp.zeros((1, pitch), jnp.float32)
        row_sin = jnp.zeros((1, pitch), jnp.float32)
        for b in range(components):
            at = b * components + c
            row_cos = jnp.where(component == b, with_cos[at:at + 1], row_cos)
            row_sin = jnp.where(component == b, with_sin[at:at + 1], row_sin)
        part = row_cos * cos_table + row_sin * sin_table
        for n, value in enumerate(split(part)):
            synth_ref[n, pl.ds(c * pitch, pitch), :] = value[:pitch]
            synth_ref[n, pl.ds(components * pitch + c * SEGMENT_LANES, SEGMENT_LANES), :] = value[pitch:]
    used = components * (pitch + SEGMENT_LANES)
    rest = synth_ref.shape[1] - used
    if rest:
        synth_ref[:, pl.ds(used, rest), :] = jnp.zeros((2, rest, pitch), jnp.bfloat16)


def jacobian(jac_ref, components, b, c, d):
    return jac_ref[pl.ds((b * components + c) * 6 + d, 1), :]


def mixed(jac_ref, source, couplings, neighbours):
    total = list(source)
    jac = functools.partial(jacobian, jac_ref, len(total))
    for d, neighbour in enumerate(neighbours):
        if neighbour is None:
            continue
        for c in range(len(total)):
            term = jac(0, c, d) * neighbour[0]
            for b in range(1, len(total)):
                term = term + jac(b, c, d) * neighbour[b]
            total[c] = total[c] + couplings[d] * term
    return total


def layer_update(jac_ref, state_ref, edge_ref, coef_ref, t, a, height):
    _, components, axial, wide, pitch = state_ref.shape
    lane = lanes((height, pitch))
    start = a * SEGMENT_LANES
    own = [state_ref[t, c, a] for c in range(components)]
    above = [state_ref[t, c, a + 1, :height] for c in range(components)] if a < axial - 1 else None
    below = [state_ref[t, c, a - 1, :height] for c in range(components)] if a else None
    edge = [edge_ref[t, c, :height] for c in range(components)]
    span_next = [pltpu.roll(x, wide - 1, 0)[:height] for x in own]
    span_prev = [pltpu.roll(x, 1, 0)[:height] for x in own]
    own = [x[:height] for x in own]
    to_end = (pitch - 1 - (start + 3 * EDGE)) % pitch
    to_begin = (pitch - (start + EDGE - 1)) % pitch
    pitch_next = [
        jnp.where(lane == pitch - 1, pltpu.roll(e, to_end, 1), pltpu.roll(x, pitch - 1, 1))
        for e, x in zip(edge, own)
    ]
    pitch_prev = [
        jnp.where(lane == 0, pltpu.roll(e, to_begin, 1), pltpu.roll(x, 1, 1))
        for e, x in zip(edge, own)
    ]
    source = [coef_ref[c, a, :height] for c in range(components)]
    couplings = [coef_ref[components + d, a, :height] for d in range(6)]
    return mixed(jac_ref, source, couplings, (above, below, span_next, span_prev, pitch_next, pitch_prev))


def edge_update(jac_ref, edge_ref, edge_coef_ref, t, axial):
    components, wide, pitch = edge_ref.shape[1:]
    lane = lanes((wide, pitch))
    own = [edge_ref[t, c] for c in range(components)]
    above = [jnp.where(lane < (axial - 1) * SEGMENT_LANES, pltpu.roll(x, pitch - SEGMENT_LANES, 1), 0.0) for x in own]
    below = [jnp.where(lane >= SEGMENT_LANES, pltpu.roll(x, SEGMENT_LANES, 1), 0.0) for x in own]
    span_next = [pltpu.roll(x, wide - 1, 0) for x in own]
    span_prev = [pltpu.roll(x, 1, 0) for x in own]
    pitch_next = [pltpu.roll(x, pitch - 1, 1) for x in own]
    pitch_prev = [pltpu.roll(x, 1, 1) for x in own]
    source = [edge_coef_ref[c] for c in range(components)]
    couplings = [edge_coef_ref[components + d] for d in range(6)]
    return mixed(jac_ref, source, couplings, (above, below, span_next, span_prev, pitch_next, pitch_prev))


def edge_boundary(field, c, components, pitch, axial):
    at = components * pitch + c * SEGMENT_LANES
    tile = field[:, (at // pitch) * pitch:(at // pitch + 1) * pitch]
    return pltpu.roll(tile, ((axial - 1) * SEGMENT_LANES - at % pitch) % pitch, 1)


def advance(refs, t, a, height=None):
    state_ref = refs[1]
    height = height or state_ref.shape[3]
    for c, value in enumerate(layer_update(*refs, t, a, height)):
        state_ref[t + 1, c, a, :height] = value


def first_kernel(
    jac_ref, state_in_ref, coef_in_ref, inv_in_ref, edges_ref, span_ref, inner_ref, outer_ref,
    coef_ref, inv_ref, edge_coef_ref, state_ref, edge_ref, *, groups,
):
    _, components, axial, wide, pitch = state_ref.shape
    span = wide - EDGE
    side = lax.axis_index("span")
    fields = 2 * components + 6
    line = rows((EDGE, pitch))
    keep_half = jnp.where(side == 0, line, EDGE - 1 - line) < HALF
    fifth = jnp.where(side == 0, HALF, HALF - 1)
    from_low, from_high = half_rows(1 - side)
    pairs = -(-(fields * axial + 1) // 2)

    def ghost(n):
        value = pltpu.roll(span_ref[n // 2], from_high if n % 2 else from_low, 0)
        value = jnp.where(keep_half, value, 0.0)
        if n < components * axial:
            extra = pltpu.roll(span_ref[pairs + n // EDGE], lax.rem(fifth + EDGE - n % EDGE, EDGE), 0)
            value = jnp.where(line == fifth, extra, value)
        return value

    even = lax.rem(lax.axis_index("pitch"), 2) == 0

    def group(ref, g):
        corner = ref[pl.ds(groups * span + g * EDGE, EDGE), :]
        return jnp.concatenate([ref[pl.ds(g * span, span), :], corner], 0)

    halves = [(group(inner_ref, g), group(outer_ref, g)) for g in range(groups)]
    from_left = [jnp.where(even, outer, inner) for inner, outer in halves]
    from_right = [jnp.where(even, inner, outer) for inner, outer in halves]
    near, far = slots(fields + 1, components)
    keep_five = keep_half | (line == fifth)
    for f in range(fields + 1):
        if f < fields:
            layers = [ghost(f * axial + a) for a in range(axial)]
        else:
            layers = [jnp.zeros((EDGE, pitch), jnp.float32)] * (axial - 1) + [ghost(fields * axial)]
        if f < components:
            for a in range(axial):
                state_ref[0, f, a, span:] = layers[a]
        elif f < fields:
            for a in range(axial):
                coef_ref[f - components, a, span:] = layers[a]
        else:
            inv_ref[span:] = layers[-1]
        g, at = near[f]
        value = jnp.concatenate([edges_ref[f], to_edges(layers, pitch)], 0)
        lane = lanes((wide, pitch)) % SEGMENT_LANES
        value = jnp.where((lane >= HALF) & (lane < EDGE), pltpu.roll(from_left[g], (HALF - at) % pitch, 1), value)
        value = jnp.where(
            (lane >= 3 * EDGE) & (lane < 3 * EDGE + HALF),
            pltpu.roll(from_right[g], (3 * EDGE - at) % pitch, 1), value,
        )
        if f < components:
            g, at = far[f]
            value = jnp.where(lane == HALF - 1, pltpu.roll(from_left[g], (HALF - 1 - at) % pitch, 1), value)
            value = jnp.where(
                lane == 3 * EDGE + HALF, pltpu.roll(from_right[g], (3 * EDGE + HALF - at) % pitch, 1), value,
            )
        target, at = (edge_ref.at[0], f) if f < components else (edge_coef_ref, f - components)
        target[at, :span] = value[:span]
        target[at, span:] = jnp.where(keep_five if f < components else keep_half, value[span:], 0.0)
    sweeps_without_boundaries(jac_ref, state_ref, edge_ref, coef_ref, edge_coef_ref, 0, 1)


def sweeps_without_boundaries(jac_ref, state_ref, edge_ref, coef_ref, edge_coef_ref, first, last):
    axial = state_ref.shape[2]
    for t in range(first, last):
        for a in range(axial - t):
            advance((jac_ref, state_ref, edge_ref, coef_ref), t, a)
        if t < axial - 1:
            for c, value in enumerate(edge_update(jac_ref, edge_ref, edge_coef_ref, t, axial)):
                edge_ref[t + 1, c] = value


def more_kernel(
    jac_ref, coef_ref, edge_coef_ref, state_in_ref, edge_in_ref, table_ref, state_ref, edge_ref, modes_ref, part_ref,
):
    _, components, axial, wide, pitch = state_ref.shape
    span = wide - EDGE
    side = lax.axis_index("span")
    sweeps_without_boundaries(jac_ref, state_ref, edge_ref, coef_ref, edge_coef_ref, 1, axial)
    strips = [
        jnp.concatenate([state_ref[t, c, 0] for t in range(1, axial)] + [state_ref[axial, c, 0, :span]], 0)
        for c in range(components)
    ]
    total = projected(strips, table_ref)
    ghosts = jnp.zeros((EDGE, pitch), jnp.float32)
    for t in range(1, axial):
        part = total[(t - 1) * wide:t * wide]
        modes_ref[pl.ds((t - 1) * span, span), :] = part[:span]
        keep, to_packed, _ = ghost_rows(side, t, axial)
        ghosts = jnp.where(keep, pltpu.roll(part[span:], to_packed, 0), ghosts)
    modes_ref[pl.ds((axial - 1) * span, EDGE), :] = ghosts
    part_ref[...] = total[(axial - 1) * wide:]


def ghost_rows(side, t, axial):
    line = rows((EDGE, 1))
    distance = jnp.where(side == 0, line, EDGE - 1 - line)
    start = sum(axial - n for n in range(1, t))
    to_packed = jnp.where(side == 0, start, (EDGE - start) % EDGE)
    from_packed = jnp.where(side == 0, (EDGE - start) % EDGE, start)
    return (distance >= start) & (distance < start + axial - t), to_packed, from_packed


def along_axis(jac_ref, coef_ref, delta, a, height):
    components = len(delta)
    out = []
    for c in range(components):
        term = jacobian(jac_ref, components, 0, c, 0) * delta[0]
        for b in range(1, components):
            term = term + jacobian(jac_ref, components, b, c, 0) * delta[b]
        out.append(coef_ref[components, a, :height] * term)
    return out


def late_kernel(
    jac_ref, coef_ref, inv_ref, part_ref, more_ref, first_ref, synth_ref, table_ref, modes_ref,
):
    span, pitch = part_ref.shape
    components, axial = coef_ref.shape[0] - 6, coef_ref.shape[1]
    field = synthesised(first_ref[EDGE:], synth_ref, components * pitch)
    delta = [inv_ref[:span] * field[:, c * pitch:(c + 1) * pitch] for c in range(components)]
    for a in range(axial - 2, -1, -1):
        delta = along_axis(jac_ref, coef_ref, delta, a, span)
    before = more_ref.shape[0]
    modes_ref[:before] = more_ref[...]
    modes_ref[before:] = part_ref[...] + projected(delta, table_ref)


def between_kernel(
    jac_ref, coef_ref, inv_ref, edge_coef_ref, state_in_ref, edge_in_ref, modes_ref, synth_ref, more_ref,
    state_ref, edge_ref,
):
    components, axial = state_ref.shape[1], state_ref.shape[2]
    wide, pitch = state_ref.shape[3:]
    modes = modes_ref[...]
    field = synthesised(jnp.concatenate([modes[EDGE:], modes[:EDGE]], 0), synth_ref, synth_ref.shape[1])
    delta = [inv_ref[...] * field[:, c * pitch:(c + 1) * pitch] for c in range(components)]
    for t in range(1, axial + 1):
        for c in range(components):
            state_ref[t, c, axial - t] += delta[c]
        if t < axial:
            delta = along_axis(jac_ref, coef_ref, delta, axial - 1 - t, wide)
    for c in range(components):
        edge_ref[1, c] += edge_coef_ref[components + 6] * edge_boundary(field, c, components, pitch, axial)
    diagonal_sweeps(jac_ref, state_ref, edge_ref, coef_ref, edge_coef_ref, 1, axial // 2 + 1)


def beside_kernel(jac_ref, coef_ref, edge_coef_ref, state_in_ref, edge_in_ref, state_ref, edge_ref):
    axial, span = state_ref.shape[2], state_ref.shape[3] - EDGE
    diagonal_sweeps(jac_ref, state_ref, edge_ref, coef_ref, edge_coef_ref, axial // 2 + 1, axial)
    advance((jac_ref, state_ref, edge_ref, coef_ref), axial, 0, span)


def diagonal_sweeps(jac_ref, state_ref, edge_ref, coef_ref, edge_coef_ref, first, last):
    axial = state_ref.shape[2]
    for t in range(first, last):
        advance((jac_ref, state_ref, edge_ref, coef_ref), t, axial - t)
        for c, value in enumerate(edge_update(jac_ref, edge_ref, edge_coef_ref, t, axial)):
            edge_ref[t + 1, c] = value


def second_kernel(
    jac_ref, coef_ref, inv_ref, edge_coef_ref, state_in_ref, edge_in_ref, more_a_ref, more_b_ref, synth_ref,
    state_ref, edge_ref, out_hbm, bound_ref, out_ref, sems,
):
    axial, components, span, pitch = out_ref.shape
    copies = [pltpu.make_async_copy(out_ref.at[a], out_hbm.at[:, a], sems.at[a]) for a in range(axial)]
    wide = span + EDGE
    side = lax.axis_index("span")
    more = more_a_ref[...] + more_b_ref[...]
    start = (axial - 1) * span
    parts = []
    for t in range(1, axial):
        _, _, from_packed = ghost_rows(side, t, axial)
        parts += [more[(t - 1) * span:t * span], pltpu.roll(more[start:start + EDGE], from_packed, 0)]
    field = synthesised(jnp.concatenate(parts + [more[start + EDGE:]], 0), synth_ref, synth_ref.shape[1])
    for t in range(1, axial):
        part = field[(t - 1) * wide:t * wide]
        for c in range(components):
            bound_ref[t, c] = inv_ref[...] * part[:, c * pitch:(c + 1) * pitch]
    for c in range(components):
        bound_ref[axial, c, :span] = inv_ref[:span] * field[(axial - 1) * wide:, c * pitch:(c + 1) * pitch]
    delta = [bound_ref[1, c] for c in range(components)]
    for t in range(2, axial + 2):
        height = wide if t <= axial else span
        for c in range(components):
            state_ref[t, c, axial + 1 - t, :height] += delta[c][:height]
        if t < axial + 1:
            delta = along_axis(jac_ref, coef_ref, delta, axial - t, wide)
    for c in range(components):
        out_ref[0, c] = state_ref[axial + 1, c, 0, :span]
    copies[0].start()
    for t in range(1, axial):
        if t > 1:
            for c, value in enumerate(edge_update(jac_ref, edge_ref, edge_coef_ref, t, axial)):
                edge_ref[t + 1, c] = value
        part = field[(t - 1) * wide:t * wide]
        for c in range(components):
            edge_ref[t + 1, c] += edge_coef_ref[components + 6] * edge_boundary(part, c, components, pitch, axial)
    refs = (jac_ref, state_ref, edge_ref, coef_ref)

    for t in range(2, axial):
        for a in range(axial + 1 - t, axial):
            advance(refs, t, a)
        for c in range(components):
            state_ref[t + 1, c, axial - 1] += bound_ref[t, c]
    for a in range(1, axial):
        for c, value in enumerate(layer_update(*refs, axial, a, span)):
            out_ref[a, c] = value + bound_ref[axial, c, :span] if a == axial - 1 else value
        copies[a].start()
    for copy in copies:
        copy.wait()


def moved(x, to):
    sizes = [lax.axis_size(name) for name in AXES]
    pairs = []
    for r in range(sizes[0]):
        for s in range(sizes[1]):
            for p in range(sizes[2]):
                target = to(r, s, p)
                if all(0 <= at < size for at, size in zip(target, sizes)):
                    number = lambda at: (at[0] * sizes[1] + at[1]) * sizes[2] + at[2]
                    pairs.append((number((r, s, p)), number(target)))
    return lax.ppermute(x, AXES, pairs)


def struct(*shape):
    return jax.ShapeDtypeStruct(shape, jnp.float32)


def on_device(
    adjoint_start, source, couplings, damping, jacobians, giles_real, giles_imag, blades, mode_orders, cell_map,
):
    components, axial, span, pitch = adjoint_start.shape
    row_count, span_count, place_count = (lax.axis_size(name) for name in AXES)
    length = pitch * place_count
    assert sum(axial - t for t in range(1, axial)) <= EDGE
    assert components == COMPONENTS and components * WAVES <= pitch
    assert axial == ITERS - 1 and ITERS <= EDGE and axial * SEGMENT_LANES == pitch
    assert span_count == 2 and place_count > 2 and place_count & (place_count - 1) == 0
    wide = span + EDGE
    fields = 2 * components + 6
    groups = slots(fields + 1, components)[1][-1][0] + 1
    pairs = -(-(fields * axial + 1) // 2)
    span_tiles = pairs + -(-components * axial // EDGE)
    vmem = pl.BlockSpec(memory_space=pltpu.VMEM)
    hbm = pl.BlockSpec(memory_space=pltpu.HBM)

    def in_hbm(x):
        return pltpu.with_memory_space_constraint(x, pltpu.HBM)

    def call(kernel, name, outs, ins, aliases=None, scratch=(), limit=40 * MIB, out_specs=None, **fixed):
        specs = [spec for spec, _ in ins]
        return pl.pallas_call(
            functools.partial(kernel, **fixed),
            out_shape=outs,
            in_specs=specs,
            out_specs=out_specs or jax.tree.map(lambda _: vmem, outs),
            scratch_shapes=scratch,
            input_output_aliases=aliases or {},
            compiler_params=params(limit),
            name=name,
        )(*[value for _, value in ins])

    tables = (
        jacobians.transpose(2, 3, 0, 1), giles_real.transpose(2, 3, 0, 1), giles_imag.transpose(2, 3, 0, 1),
        mode_orders.transpose(0, 2, 1), cell_map,
    )
    blades = blades.reshape(1, -1)
    corner_rows = groups * EDGE
    state_shape = struct(axial + 2, components, axial, wide, pitch)
    state, coef, inv, span_out, small, modes, table, blades, *tables = call(
        start_kernel, "start",
        (
            state_shape, struct(components + 6, axial, wide, pitch), struct(wide, pitch),
            struct(span_tiles, EDGE, pitch), struct(2 * corner_rows + EDGE, pitch), struct(span, pitch),
            jax.ShapeDtypeStruct((2, components * pitch, pitch), jnp.bfloat16),
            *(jax.ShapeDtypeStruct(x.shape, x.dtype) for x in (blades, *tables)),
        ),
        [(hbm, in_hbm(x)) for x in (adjoint_start, source, couplings, damping, blades, *tables)],
        scratch=[
            pltpu.VMEM(source.shape, jnp.float32), pltpu.VMEM(couplings.shape, jnp.float32),
            pltpu.VMEM(damping.shape, jnp.float32), pltpu.SemaphoreType.DMA((5 + len(tables),)),
        ],
        groups=groups, length=length,
    )
    edges, inner, outer = call(
        pack_kernel, "pack",
        (struct(fields + 1, span, pitch), struct((groups + 1) * wide, pitch), struct(groups * wide, pitch)),
        [(vmem, x) for x in (state, coef, inv, modes)],
        groups=groups,
    )
    steps = [1 << n for n in range(place_count.bit_length() - 2)]
    last_step = place_count // 2

    def near(x):
        return moved(x, lambda r, s, p: (r - 1, s, p))

    synth, jac = call(
        synth_kernel, "synth",
        (
            jax.ShapeDtypeStruct(
                (2, -(-components * (pitch + SEGMENT_LANES) // pitch) * pitch, pitch), jnp.bfloat16
            ),
            struct(-(-6 * components * components // EDGE) * EDGE, pitch),
        ),
        [(vmem, x) for x in (blades, *tables)],
        scratch=[pltpu.VMEM((2, components * components, mode_orders.shape[1]), jnp.float32)],
        row_count=row_count, place_count=place_count, components=components, pitch=pitch, length=length, axial=axial,
    )
    small, edges, jac = lax.optimization_barrier((moved(small, lambda r, s, p: (r, 1 - s, p)), edges, jac))
    from_span = moved(span_out, lambda r, s, p: (r, 1 - s, p))
    edge_shape = struct(axial + 1, components, wide, pitch)
    inner = lax.dynamic_update_slice(inner, small[:corner_rows + EDGE], (groups * span, 0))
    outer = lax.dynamic_update_slice(outer, small[corner_rows + EDGE:], (groups * span, 0))
    modes = inner[groups * span + corner_rows:]
    outer = moved(outer, lambda r, s, p: (r, s, (p - 1 + 2 * (p % 2)) % place_count))
    inner = moved(inner, lambda r, s, p: (r, s, p ^ 1))
    modes = modes + inner[groups * span + corner_rows:]
    for step in steps[1:]:
        modes = modes + moved(modes, lambda r, s, p: (r, s, p ^ step))
    got = moved(modes, lambda r, s, p: (r, s, p ^ last_step))
    coef, inv, edge_coef, state, edge = call(
        first_kernel, "first_sweep",
        (
            struct(components + 6, axial, wide, pitch), struct(wide, pitch), struct(components + 7, wide, pitch),
            state_shape, edge_shape,
        ),
        [(vmem, x) for x in (jac, state, coef, inv, edges, from_span, inner, outer)],
        aliases={1: 3, 2: 0, 3: 1},
        groups=groups,
    )
    got, inv = lax.optimization_barrier((got, inv))
    modes = near(modes + got)
    state, edge, more, part = call(
        more_kernel, "more_sweeps",
        (state_shape, edge_shape, struct((axial - 1) * span + EDGE, pitch), struct(span, pitch)),
        [(vmem, x) for x in (jac, coef, edge_coef, state, edge, table)],
        aliases={3: 0, 4: 1},
    )
    more_shape = struct(axial * span + EDGE, pitch)
    more = call(
        late_kernel, "late_modes", more_shape,
        [(vmem, x) for x in (jac, coef, inv, part, more, modes, synth, table)],
    )
    up_across, up = moved(more, lambda r, s, p: (r - 1, s, p ^ 1)), near(more)
    state, edge = call(
        between_kernel, "between_sweeps", (state_shape, edge_shape),
        [(vmem, x) for x in (jac, coef, inv, edge_coef, state, edge, modes, synth, more)],
        aliases={4: 0, 5: 1},
    )
    up_across, edge = lax.optimization_barrier((up_across, edge))
    more_a = up_across + up
    state, edge = call(
        beside_kernel, "beside_sweeps", (state_shape, edge_shape),
        [(vmem, x) for x in (jac, coef, edge_coef, state, edge)],
        aliases={3: 0, 4: 1},
    )
    for step in steps[1:]:
        more_a = more_a + moved(more_a, lambda r, s, p: (r, s, p ^ step))
    more_b = moved(more_a, lambda r, s, p: (r, s, p ^ last_step))
    return call(
        second_kernel, "second_sweeps", (state_shape, edge_shape, struct(components, axial, span, pitch)),
        [(vmem, x) for x in (jac, coef, inv, edge_coef, state, edge, more_a, more_b, synth)],
        aliases={4: 0, 5: 1},
        scratch=[
            pltpu.VMEM((axial + 1, components, wide, pitch), jnp.float32),
            pltpu.VMEM((axial, components, span, pitch), jnp.float32), pltpu.SemaphoreType.DMA((axial,)),
        ],
        out_specs=(vmem, vmem, hbm),
    )[2]


def solution(mesh):
    placed = (
        P(None, "row", "span", "pitch"),
        P(None, "row", "span", "pitch"),
        P(None, "row", "span", "pitch"),
        P("row", "span", "pitch"),
        P("row", None, None, None),
        P(),
        P(),
        P(),
        P(),
        P("row", None),
    )
    return jax.shard_map(
        on_device,
        mesh=mesh,
        in_specs=placed,
        out_specs=P(None, "row", "span", "pitch"),
        check_vma=False,
    )
```

```python
import functools
import math

import jax
import jax.numpy as jnp
from jax import lax
from jax.experimental import pallas as pl
from jax.experimental.pallas import tpu as pltpu
from jax.sharding import PartitionSpec as P

ITERS = 5
AXES = ("row", "span", "pitch")

ORDER_MAX = 2
BASE = 2 * ORDER_MAX + 1
COSINES = (BASE * BASE + 1) // 2
WAVES = 2 * COSINES - 1
COMPONENTS = 5
EDGE = 8
HALF = EDGE // 2
SEGMENT_LANES = 4 * EDGE
EXACT = lax.Precision.HIGHEST
MIB = 1024 * 1024


def params(limit):
    return pltpu.CompilerParams(vmem_limit_bytes=limit)


def lanes(shape):
    return lax.broadcasted_iota(jnp.int32, shape, len(shape) - 1)


def rows(shape):
    return lax.broadcasted_iota(jnp.int32, shape, len(shape) - 2)


def column(j):
    component = (j * 41) >> 10
    wave = j - WAVES * component
    sine = wave >= COSINES
    return component, jnp.where(sine, wave - (COSINES - 1), wave), sine


def mode_number(mode, blades):
    high = ((mode + ORDER_MAX) * 13) >> 6
    low = mode - BASE * high
    return high * blades[0] + low * blades[1]


def waves(products, length):
    if length & (length - 1) == 0:
        phase = products & (length - 1)
    else:
        phase = jnp.mod(products, length)
    turn = phase.astype(jnp.float32) * (1.0 / length)
    quarter = jnp.floor(4.0 * turn + 0.5)
    x = (turn - 0.25 * quarter) * (2.0 * math.pi)
    y = x * x
    sine = x * (1.0 + y * (-1.0 / 6 + y * (1.0 / 120 + y * (-1.0 / 5040 + y * (1.0 / 362880)))))
    cosine = 1.0 + y * (-0.5 + y * (1.0 / 24 + y * (-1.0 / 720 + y * (1.0 / 40320 - y * (1.0 / 3628800)))))
    quarter = quarter.astype(jnp.int32) & 3
    odd = (quarter & 1) == 1
    cos_out = jnp.where(odd, sine, cosine)
    sin_out = jnp.where(odd, cosine, sine)
    cos_out = jnp.where((quarter == 1) | (quarter == 2), -cos_out, cos_out)
    sin_out = jnp.where(quarter >= 2, -sin_out, sin_out)
    return cos_out, sin_out


def to_edges(layers, pitch):
    lane = lanes(layers[-1].shape)
    block = jnp.zeros_like(layers[-1])
    for a, layer in enumerate(layers):
        if layer is None:
            continue
        start = a * SEGMENT_LANES
        first = pltpu.roll(layer, (start + EDGE) % pitch, layer.ndim - 1)
        last = pltpu.roll(layer, (start + 3 * EDGE) % pitch, layer.ndim - 1)
        block = jnp.where((lane >= start + EDGE) & (lane < start + 2 * EDGE), first, block)
        block = jnp.where((lane >= start + 2 * EDGE) & (lane < start + 3 * EDGE), last, block)
    return block


def half_rows(side):
    return jnp.where(side == 0, EDGE // 2, 0), jnp.where(side == 0, 0, EDGE // 2)


def slots(fields, components):
    per_group = SEGMENT_LANES // HALF
    near = [(f // per_group, f % per_group * HALF) for f in range(fields)]
    group, lane = near[-1]
    far = [(group, lane + HALF + c) for c in range(components)]
    return near, far


def packed_edges(blocks, place, components):
    near, far = slots(len(blocks), components)
    pitch = blocks[0].shape[1]
    lane = lanes(blocks[0].shape) % SEGMENT_LANES
    sides = []
    for near_at, far_at in ((3 * EDGE - HALF, 3 * EDGE - HALF - 1), (EDGE, EDGE + HALF)):
        packed = [jnp.zeros_like(blocks[0]) for _ in range(far[-1][0] + 1)]
        for f, (g, to) in enumerate(near):
            value = pltpu.roll(blocks[f], (to - near_at) % pitch, 1)
            packed[g] = jnp.where((lane >= to) & (lane < to + HALF), value, packed[g])
        for f, (g, to) in enumerate(far):
            packed[g] = jnp.where(lane == to, pltpu.roll(blocks[f], (to - far_at) % pitch, 1), packed[g])
        sides.append(packed)
    even = lax.rem(place, 2) == 0
    inner = [jnp.where(even, right, left) for right, left in zip(*sides)]
    outer = [jnp.where(even, left, right) for right, left in zip(*sides)]
    return inner, outer


def edge_blocks(state_ref, coef_ref, inv_ref, at):
    components, axial, pitch = state_ref.shape[1], state_ref.shape[2], state_ref.shape[4]
    blocks = [to_edges([state_ref[0, c, a, at, :] for a in range(axial)], pitch) for c in range(components)]
    blocks += [to_edges([coef_ref[f, a, at, :] for a in range(axial)], pitch) for f in range(components + 6)]
    return blocks + [to_edges([None] * (axial - 1) + [inv_ref[at, :]], pitch)]


def start_kernel(
    adjoint_hbm, source_hbm, couplings_hbm, damping_hbm, blades_hbm, *refs, groups, length,
):
    state_ref, coef_ref, inv_ref, span_ref, small_ref, modes_ref, table_ref, blades_ref = refs[5:13]
    source_ref, couplings_ref, damping_ref, sems = refs[18:]
    components, axial, span, pitch = source_ref.shape
    adjoint_ref = state_ref.at[0, :, :, pl.ds(0, span), :]
    copies = [
        pltpu.make_async_copy(src, dst, sems.at[n])
        for n, (src, dst) in enumerate((
            (couplings_hbm, couplings_ref), (damping_hbm, damping_ref), (source_hbm, source_ref),
            (adjoint_hbm, adjoint_ref), (blades_hbm, blades_ref), *zip(refs[:5], refs[13:18]),
        ))
    ]
    for copy in copies:
        copy.start()
    row, side, place = (lax.axis_index(name) for name in AXES)
    copies[4].wait()
    face = jnp.maximum(row - 1, 0)
    component, mode, sine = column(lanes((pitch, pitch)))
    number = mode_number(mode, [picked(blades_ref[...], face + n) for n in range(2)])
    cos_table, sin_table = waves(number * (place * pitch + rows((pitch, pitch))), length)
    table = jnp.where(component < components, jnp.where(sine, sin_table, cos_table), 0.0)
    for c in range(components):
        high, low = split(jnp.where(component == c, table, 0.0))
        for n, value in enumerate((high, high, low)):
            table_ref[pl.ds((n * components + c) * pitch, pitch), :] = value
    copies[0].wait()
    copies[1].wait()
    diag = damping_ref[...]
    for d in range(6):
        diag = diag + couplings_ref[d]
    inverse = 1.0 / diag
    for d in range(6):
        coef_ref[components + d, :, :span] = couplings_ref[d] * inverse
    inv_ref[:span] = inverse[axial - 1]
    copies[2].wait()
    for c in range(components):
        coef_ref[c, :, :span] = source_ref[c] * inverse
    copies[3].wait()
    edge_row = pl.multiple_of(jnp.where(side == 0, span - EDGE, 0), EDGE)
    blocks = edge_blocks(state_ref, coef_ref, inv_ref, pl.ds(edge_row, EDGE))
    for n, packed in enumerate(packed_edges(blocks, place, components)):
        for g, value in enumerate(packed):
            small_ref[pl.ds((n * (groups + 1) + g) * EDGE, EDGE), :] = value
    modes_ref[...] = projected([adjoint_ref[c, 0] for c in range(components)], table_ref)
    small_ref[pl.ds(groups * EDGE, EDGE), :] = modes_ref[pl.ds(edge_row, EDGE), :]

    to_low, to_high = half_rows(side)
    line = rows((EDGE, pitch))
    tiles = [state_ref[0, c, a, pl.ds(edge_row, EDGE), :] for c in range(components) for a in range(axial)]
    tiles += [coef_ref[f, a, pl.ds(edge_row, EDGE), :] for f in range(components + 6) for a in range(axial)]
    tiles += [inv_ref[pl.ds(edge_row, EDGE), :]]
    pairs = -(-len(tiles) // 2)
    for n in range(pairs):
        value = pltpu.roll(tiles[2 * n], to_low, 0)
        if 2 * n + 1 < len(tiles):
            value = jnp.where(line < HALF, value, pltpu.roll(tiles[2 * n + 1], to_high, 0))
        span_ref[n] = value
    fifth = jnp.where(side == 0, HALF - 1, HALF)
    for n in range(span_ref.shape[0] - pairs):
        value = jnp.zeros((EDGE, pitch), jnp.float32)
        for k in range(min(EDGE, components * axial - n * EDGE)):
            value = jnp.where(line == k, pltpu.roll(tiles[n * EDGE + k], lax.rem(k + EDGE - fifth, EDGE), 0), value)
        span_ref[pairs + n] = value
    for copy in copies[5:]:
        copy.wait()


def pack_kernel(state_ref, coef_ref, inv_ref, modes_ref, edges_ref, inner_ref, outer_ref, *, groups):
    _, components, axial, wide, pitch = state_ref.shape
    span = wide - EDGE
    place = lax.axis_index("pitch")
    blocks = edge_blocks(state_ref, coef_ref, inv_ref, pl.ds(0, span))
    for f, block in enumerate(blocks):
        edges_ref[f] = block
    for out_ref, packed in zip((inner_ref, outer_ref), packed_edges(blocks, place, components)):
        for g, value in enumerate(packed):
            out_ref[pl.ds(g * span, span), :] = value
    start = groups * span + (groups + 1) * EDGE
    inner_ref[pl.ds(start, span), :] = modes_ref[...]


def picked(values, at):
    chosen = jnp.where(lanes(values.shape) == at, values.astype(jnp.float32), 0.0)
    return jnp.sum(chosen, axis=1, keepdims=True).astype(jnp.int32)


def split(x):
    high = x.astype(jnp.bfloat16)
    return high, (x - high.astype(jnp.float32)).astype(jnp.bfloat16)


def thrice(x):
    high, low = split(x)
    return jnp.concatenate([high, low, high], 1)


def projected(strips, table_ref):
    return jnp.dot(thrice(jnp.concatenate(strips, 1)), table_ref[...], preferred_element_type=jnp.float32)


def synthesised(modes, synth_ref, count):
    dims = (((1,), (1,)), ((), ()))
    return lax.dot_general(thrice(modes), synth_ref[:count], dims, preferred_element_type=jnp.float32)


def synth_kernel(
    blades_ref, jacobians_ref, giles_re_ref, giles_im_ref, orders_ref, cells_ref, synth_ref, rows_ref, sums_ref,
    *, row_count, place_count, components, pitch, length, axial,
):
    row, place = lax.axis_index("row"), lax.axis_index("pitch")
    face = jnp.minimum(row, row_count - 2)
    for b in range(components):
        for c in range(components):
            entries = jacobians_ref[b, c]
            for d in range(6):
                at = (b * components + c) * 6 + d
                rows_ref[pl.ds(at, 1), :] = jnp.broadcast_to(entries[:, d:d + 1], (1, pitch))
    modes = orders_ref.shape[2]
    orders = orders_ref[face]
    tag = BASE * orders[0:1] + orders[1:2]
    component, mode, _ = column(rows((pitch, modes)))
    same = (jnp.abs(tag) == mode) & (component < components)
    plain = jnp.where(same, 1.0, 0.0)
    signed = jnp.where(tag < 0, -plain, plain)
    dims = (((1,), (1,)), ((), ()))
    for n, ref in enumerate((giles_re_ref, giles_im_ref)):
        for b in range(components):
            for c in range(components):
                sums_ref[n, pl.ds(b * components + c, 1), :] = ref[b, c, pl.ds(face, 1), :]
    sums_re = lax.dot_general(sums_ref[0], plain, dims, precision=EXACT, preferred_element_type=jnp.float32)
    sums_im = lax.dot_general(sums_ref[1], signed, dims, precision=EXACT, preferred_element_type=jnp.float32)
    component, mode, sine = column(lanes(sums_re.shape))
    scale = 2.0 / length
    with_cos = jnp.where(sine, sums_im, sums_re) * scale
    with_sin = jnp.where(sine, sums_re, -sums_im) * scale
    component = component[0:1]

    def chunk(at):
        start = pl.multiple_of(lax.rem(place + at + place_count, place_count) * pitch, pitch)
        return cells_ref[:, pl.ds(start, pitch)]

    own = chunk(0)
    lane = lanes((1, pitch))
    first = (axial - 1) * SEGMENT_LANES
    edge = jnp.where(lane < first + EDGE, pltpu.roll(chunk(-1), (first + EDGE) % pitch, 1), pltpu.roll(own, (first + EDGE) % pitch, 1))
    edge = jnp.where(lane < first + 2 * EDGE, edge, pltpu.roll(own, (first + 3 * EDGE) % pitch, 1))
    edge = jnp.where(lane < first + 3 * EDGE, edge, pltpu.roll(chunk(1), (first + 3 * EDGE) % pitch, 1))

    def upright(cells):
        wide = jnp.broadcast_to(cells.astype(jnp.float32), (pitch, pitch))
        return jnp.transpose(wide).astype(jnp.int32)

    edge_cells = upright(edge)[first:first + SEGMENT_LANES]
    at_cells = jnp.concatenate([upright(own), edge_cells], 0)
    _, mode, _ = column(lanes(at_cells.shape))
    blades = [picked(blades_ref[...], face + n) for n in range(2)]
    cos_table, sin_table = waves(mode_number(mode, blades) * at_cells, length)
    for c in range(components):
        row_cos = jnp.zeros((1, pitch), jnp.float32)
        row_sin = jnp.zeros((1, pitch), jnp.float32)
        for b in range(components):
            at = b * components + c
            row_cos = jnp.where(component == b, with_cos[at:at + 1], row_cos)
            row_sin = jnp.where(component == b, with_sin[at:at + 1], row_sin)
        part = row_cos * cos_table + row_sin * sin_table
        high, low = split(part)
        value = jnp.concatenate([high, high, low], 1)
        synth_ref[pl.ds(c * pitch, pitch), :] = value[:pitch]
        synth_ref[pl.ds(components * pitch + c * SEGMENT_LANES, SEGMENT_LANES), :] = value[pitch:]
    used = components * (pitch + SEGMENT_LANES)
    rest = synth_ref.shape[0] - used
    if rest:
        synth_ref[pl.ds(used, rest), :] = jnp.zeros((rest, 3 * pitch), jnp.bfloat16)


def jacobian(jac_ref, components, b, c, d):
    return jac_ref[pl.ds((b * components + c) * 6 + d, 1), :]


def mixed(jac_ref, source, couplings, neighbours):
    total = list(source)
    jac = functools.partial(jacobian, jac_ref, len(total))
    for d, neighbour in enumerate(neighbours):
        if neighbour is None:
            continue
        for c in range(len(total)):
            term = jac(0, c, d) * neighbour[0]
            for b in range(1, len(total)):
                term = term + jac(b, c, d) * neighbour[b]
            total[c] = total[c] + couplings[d] * term
    return total


def layer_update(jac_ref, state_ref, edge_ref, coef_ref, t, a, height):
    _, components, axial, wide, pitch = state_ref.shape
    lane = lanes((height, pitch))
    start = a * SEGMENT_LANES
    own = [state_ref[t, c, a] for c in range(components)]
    above = [state_ref[t, c, a + 1, :height] for c in range(components)] if a < axial - 1 else None
    below = [state_ref[t, c, a - 1, :height] for c in range(components)] if a else None
    edge = [edge_ref[t, c, :height] for c in range(components)]
    span_next = [pltpu.roll(x, wide - 1, 0)[:height] for x in own]
    span_prev = [pltpu.roll(x, 1, 0)[:height] for x in own]
    own = [x[:height] for x in own]
    to_end = (pitch - 1 - (start + 3 * EDGE)) % pitch
    to_begin = (pitch - (start + EDGE - 1)) % pitch
    pitch_next = [
        jnp.where(lane == pitch - 1, pltpu.roll(e, to_end, 1), pltpu.roll(x, pitch - 1, 1))
        for e, x in zip(edge, own)
    ]
    pitch_prev = [
        jnp.where(lane == 0, pltpu.roll(e, to_begin, 1), pltpu.roll(x, 1, 1))
        for e, x in zip(edge, own)
    ]
    source = [coef_ref[c, a, :height] for c in range(components)]
    couplings = [coef_ref[components + d, a, :height] for d in range(6)]
    return mixed(jac_ref, source, couplings, (above, below, span_next, span_prev, pitch_next, pitch_prev))


def edge_update(jac_ref, edge_ref, edge_coef_ref, t, axial):
    components, wide, pitch = edge_ref.shape[1:]
    lane = lanes((wide, pitch))
    own = [edge_ref[t, c] for c in range(components)]
    above = [jnp.where(lane < (axial - 1) * SEGMENT_LANES, pltpu.roll(x, pitch - SEGMENT_LANES, 1), 0.0) for x in own]
    below = [jnp.where(lane >= SEGMENT_LANES, pltpu.roll(x, SEGMENT_LANES, 1), 0.0) for x in own]
    span_next = [pltpu.roll(x, wide - 1, 0) for x in own]
    span_prev = [pltpu.roll(x, 1, 0) for x in own]
    pitch_next = [pltpu.roll(x, pitch - 1, 1) for x in own]
    pitch_prev = [pltpu.roll(x, 1, 1) for x in own]
    source = [edge_coef_ref[c] for c in range(components)]
    couplings = [edge_coef_ref[components + d] for d in range(6)]
    return mixed(jac_ref, source, couplings, (above, below, span_next, span_prev, pitch_next, pitch_prev))


def edge_boundary(field, c, components, pitch, axial):
    at = components * pitch + c * SEGMENT_LANES
    tile = field[:, (at // pitch) * pitch:(at // pitch + 1) * pitch]
    return pltpu.roll(tile, ((axial - 1) * SEGMENT_LANES - at % pitch) % pitch, 1)


def advance(refs, t, a, height=None):
    state_ref = refs[1]
    height = height or state_ref.shape[3]
    for c, value in enumerate(layer_update(*refs, t, a, height)):
        state_ref[t + 1, c, a, :height] = value


def first_kernel(
    jac_ref, state_in_ref, coef_in_ref, inv_in_ref, edges_ref, span_ref, inner_ref, outer_ref,
    coef_ref, inv_ref, edge_coef_ref, state_ref, edge_ref, *, groups,
):
    _, components, axial, wide, pitch = state_ref.shape
    span = wide - EDGE
    side = lax.axis_index("span")
    fields = 2 * components + 6
    line = rows((EDGE, pitch))
    keep_half = jnp.where(side == 0, line, EDGE - 1 - line) < HALF
    fifth = jnp.where(side == 0, HALF, HALF - 1)
    from_low, from_high = half_rows(1 - side)
    pairs = -(-(fields * axial + 1) // 2)

    def ghost(n):
        value = pltpu.roll(span_ref[n // 2], from_high if n % 2 else from_low, 0)
        value = jnp.where(keep_half, value, 0.0)
        if n < components * axial:
            extra = pltpu.roll(span_ref[pairs + n // EDGE], lax.rem(fifth + EDGE - n % EDGE, EDGE), 0)
            value = jnp.where(line == fifth, extra, value)
        return value

    even = lax.rem(lax.axis_index("pitch"), 2) == 0

    def group(ref, g):
        corner = ref[pl.ds(groups * span + g * EDGE, EDGE), :]
        return jnp.concatenate([ref[pl.ds(g * span, span), :], corner], 0)

    halves = [(group(inner_ref, g), group(outer_ref, g)) for g in range(groups)]
    from_left = [jnp.where(even, outer, inner) for inner, outer in halves]
    from_right = [jnp.where(even, inner, outer) for inner, outer in halves]
    near, far = slots(fields + 1, components)
    keep_five = keep_half | (line == fifth)
    for f in range(fields + 1):
        if f < fields:
            layers = [ghost(f * axial + a) for a in range(axial)]
        else:
            layers = [jnp.zeros((EDGE, pitch), jnp.float32)] * (axial - 1) + [ghost(fields * axial)]
        if f < components:
            for a in range(axial):
                state_ref[0, f, a, span:] = layers[a]
        elif f < fields:
            for a in range(axial):
                coef_ref[f - components, a, span:] = layers[a]
        else:
            inv_ref[span:] = layers[-1]
        g, at = near[f]
        value = jnp.concatenate([edges_ref[f], to_edges(layers, pitch)], 0)
        lane = lanes((wide, pitch)) % SEGMENT_LANES
        value = jnp.where((lane >= HALF) & (lane < EDGE), pltpu.roll(from_left[g], (HALF - at) % pitch, 1), value)
        value = jnp.where(
            (lane >= 3 * EDGE) & (lane < 3 * EDGE + HALF),
            pltpu.roll(from_right[g], (3 * EDGE - at) % pitch, 1), value,
        )
        if f < components:
            g, at = far[f]
            value = jnp.where(lane == HALF - 1, pltpu.roll(from_left[g], (HALF - 1 - at) % pitch, 1), value)
            value = jnp.where(
                lane == 3 * EDGE + HALF, pltpu.roll(from_right[g], (3 * EDGE + HALF - at) % pitch, 1), value,
            )
        target, at = (edge_ref.at[0], f) if f < components else (edge_coef_ref, f - components)
        target[at, :span] = value[:span]
        target[at, span:] = jnp.where(keep_five if f < components else keep_half, value[span:], 0.0)
    sweeps_without_boundaries(jac_ref, state_ref, edge_ref, coef_ref, edge_coef_ref, 0, 1)


def sweeps_without_boundaries(jac_ref, state_ref, edge_ref, coef_ref, edge_coef_ref, first, last):
    axial = state_ref.shape[2]
    for t in range(first, last):
        for a in range(axial - t):
            advance((jac_ref, state_ref, edge_ref, coef_ref), t, a)
        if t < axial - 1:
            for c, value in enumerate(edge_update(jac_ref, edge_ref, edge_coef_ref, t, axial)):
                edge_ref[t + 1, c] = value


def more_kernel(
    jac_ref, coef_ref, edge_coef_ref, state_in_ref, edge_in_ref, table_ref, state_ref, edge_ref, modes_ref, part_ref,
):
    _, components, axial, wide, pitch = state_ref.shape
    span = wide - EDGE
    side = lax.axis_index("span")
    sweeps_without_boundaries(jac_ref, state_ref, edge_ref, coef_ref, edge_coef_ref, 1, axial)
    strips = [
        jnp.concatenate([state_ref[t, c, 0] for t in range(1, axial)] + [state_ref[axial, c, 0, :span]], 0)
        for c in range(components)
    ]
    total = projected(strips, table_ref)
    ghosts = jnp.zeros((EDGE, pitch), jnp.float32)
    for t in range(1, axial):
        part = total[(t - 1) * wide:t * wide]
        modes_ref[pl.ds((t - 1) * span, span), :] = part[:span]
        keep, to_packed, _ = ghost_rows(side, t, axial)
        ghosts = jnp.where(keep, pltpu.roll(part[span:], to_packed, 0), ghosts)
    modes_ref[pl.ds((axial - 1) * span, EDGE), :] = ghosts
    part_ref[...] = total[(axial - 1) * wide:]


def ghost_rows(side, t, axial):
    line = rows((EDGE, 1))
    distance = jnp.where(side == 0, line, EDGE - 1 - line)
    start = sum(axial - n for n in range(1, t))
    to_packed = jnp.where(side == 0, start, (EDGE - start) % EDGE)
    from_packed = jnp.where(side == 0, (EDGE - start) % EDGE, start)
    return (distance >= start) & (distance < start + axial - t), to_packed, from_packed


def along_axis(jac_ref, coef_ref, delta, a, height):
    components = len(delta)
    out = []
    for c in range(components):
        term = jacobian(jac_ref, components, 0, c, 0) * delta[0]
        for b in range(1, components):
            term = term + jacobian(jac_ref, components, b, c, 0) * delta[b]
        out.append(coef_ref[components, a, :height] * term)
    return out


def late_kernel(
    jac_ref, coef_ref, inv_ref, part_ref, more_ref, first_ref, synth_ref, table_ref, modes_ref,
):
    span, pitch = part_ref.shape
    components, axial = coef_ref.shape[0] - 6, coef_ref.shape[1]
    field = synthesised(first_ref[EDGE:], synth_ref, components * pitch)
    delta = [inv_ref[:span] * field[:, c * pitch:(c + 1) * pitch] for c in range(components)]
    for a in range(axial - 2, -1, -1):
        delta = along_axis(jac_ref, coef_ref, delta, a, span)
    before = more_ref.shape[0]
    modes_ref[:before] = more_ref[...]
    modes_ref[before:] = part_ref[...] + projected(delta, table_ref)


def between_kernel(
    jac_ref, coef_ref, inv_ref, edge_coef_ref, state_in_ref, edge_in_ref, modes_ref, synth_ref, more_ref,
    state_ref, edge_ref, sent_ref,
):
    sent_ref[...] = more_ref[...]
    components, axial = state_ref.shape[1], state_ref.shape[2]
    wide, pitch = state_ref.shape[3:]
    modes = modes_ref[...]
    field = synthesised(jnp.concatenate([modes[EDGE:], modes[:EDGE]], 0), synth_ref, synth_ref.shape[0])
    delta = [inv_ref[...] * field[:, c * pitch:(c + 1) * pitch] for c in range(components)]
    for t in range(1, axial + 1):
        for c in range(components):
            state_ref[t, c, axial - t] += delta[c]
        if t < axial:
            delta = along_axis(jac_ref, coef_ref, delta, axial - 1 - t, wide)
    for c in range(components):
        edge_ref[1, c] += edge_coef_ref[components + 6] * edge_boundary(field, c, components, pitch, axial)
    diagonal_sweeps(jac_ref, state_ref, edge_ref, coef_ref, edge_coef_ref, 1, axial // 2 + 1)


def beside_kernel(jac_ref, coef_ref, edge_coef_ref, state_in_ref, edge_in_ref, state_ref, edge_ref):
    axial, span = state_ref.shape[2], state_ref.shape[3] - EDGE
    diagonal_sweeps(jac_ref, state_ref, edge_ref, coef_ref, edge_coef_ref, axial // 2 + 1, axial)
    advance((jac_ref, state_ref, edge_ref, coef_ref), axial, 0, span)


def diagonal_sweeps(jac_ref, state_ref, edge_ref, coef_ref, edge_coef_ref, first, last):
    axial = state_ref.shape[2]
    for t in range(first, last):
        advance((jac_ref, state_ref, edge_ref, coef_ref), t, axial - t)
        for c, value in enumerate(edge_update(jac_ref, edge_ref, edge_coef_ref, t, axial)):
            edge_ref[t + 1, c] = value


def second_kernel(
    jac_ref, coef_ref, inv_ref, edge_coef_ref, state_in_ref, edge_in_ref, more_a_ref, more_b_ref, synth_ref,
    state_ref, edge_ref, out_hbm, bound_ref, out_ref, sems,
):
    axial, components, span, pitch = out_ref.shape
    copies = [pltpu.make_async_copy(out_ref.at[a], out_hbm.at[:, a], sems.at[a]) for a in range(axial)]
    wide = span + EDGE
    side = lax.axis_index("span")
    more = more_a_ref[...] + more_b_ref[...]
    start = (axial - 1) * span
    parts = []
    for t in range(1, axial):
        _, _, from_packed = ghost_rows(side, t, axial)
        parts += [more[(t - 1) * span:t * span], pltpu.roll(more[start:start + EDGE], from_packed, 0)]
    field = synthesised(jnp.concatenate(parts + [more[start + EDGE:]], 0), synth_ref, synth_ref.shape[0])
    for t in range(1, axial):
        part = field[(t - 1) * wide:t * wide]
        for c in range(components):
            bound_ref[t, c] = inv_ref[...] * part[:, c * pitch:(c + 1) * pitch]
    for c in range(components):
        bound_ref[axial, c, :span] = inv_ref[:span] * field[(axial - 1) * wide:, c * pitch:(c + 1) * pitch]
    delta = [bound_ref[1, c] for c in range(components)]
    for t in range(2, axial + 2):
        height = wide if t <= axial else span
        for c in range(components):
            state_ref[t, c, axial + 1 - t, :height] += delta[c][:height]
        if t < axial + 1:
            delta = along_axis(jac_ref, coef_ref, delta, axial - t, wide)
    for c in range(components):
        out_ref[0, c] = state_ref[axial + 1, c, 0, :span]
    copies[0].start()
    for t in range(1, axial):
        if t > 1:
            for c, value in enumerate(edge_update(jac_ref, edge_ref, edge_coef_ref, t, axial)):
                edge_ref[t + 1, c] = value
        part = field[(t - 1) * wide:t * wide]
        for c in range(components):
            edge_ref[t + 1, c] += edge_coef_ref[components + 6] * edge_boundary(part, c, components, pitch, axial)
    refs = (jac_ref, state_ref, edge_ref, coef_ref)

    for t in range(2, axial):
        for a in range(axial + 1 - t, axial):
            advance(refs, t, a)
        for c in range(components):
            state_ref[t + 1, c, axial - 1] += bound_ref[t, c]
    for a in range(1, axial):
        for c, value in enumerate(layer_update(*refs, axial, a, span)):
            out_ref[a, c] = value + bound_ref[axial, c, :span] if a == axial - 1 else value
        copies[a].start()
    for copy in copies:
        copy.wait()


def moved(x, to):
    sizes = [lax.axis_size(name) for name in AXES]
    pairs = []
    for r in range(sizes[0]):
        for s in range(sizes[1]):
            for p in range(sizes[2]):
                target = to(r, s, p)
                if all(0 <= at < size for at, size in zip(target, sizes)):
                    number = lambda at: (at[0] * sizes[1] + at[1]) * sizes[2] + at[2]
                    pairs.append((number((r, s, p)), number(target)))
    return lax.ppermute(x, AXES, pairs)


def struct(*shape):
    return jax.ShapeDtypeStruct(shape, jnp.float32)


def on_device(
    adjoint_start, source, couplings, damping, jacobians, giles_real, giles_imag, blades, mode_orders, cell_map,
):
    components, axial, span, pitch = adjoint_start.shape
    row_count, span_count, place_count = (lax.axis_size(name) for name in AXES)
    length = pitch * place_count
    assert sum(axial - t for t in range(1, axial)) <= EDGE
    assert components == COMPONENTS and components * WAVES <= pitch
    assert axial == ITERS - 1 and ITERS <= EDGE and axial * SEGMENT_LANES == pitch
    assert span_count == 2 and place_count > 2 and place_count & (place_count - 1) == 0
    wide = span + EDGE
    fields = 2 * components + 6
    groups = slots(fields + 1, components)[1][-1][0] + 1
    pairs = -(-(fields * axial + 1) // 2)
    span_tiles = pairs + -(-components * axial // EDGE)
    vmem = pl.BlockSpec(memory_space=pltpu.VMEM)
    hbm = pl.BlockSpec(memory_space=pltpu.HBM)

    def in_hbm(x):
        return pltpu.with_memory_space_constraint(x, pltpu.HBM)

    def call(kernel, name, outs, ins, aliases=None, scratch=(), limit=40 * MIB, out_specs=None, **fixed):
        specs = [spec for spec, _ in ins]
        return pl.pallas_call(
            functools.partial(kernel, **fixed),
            out_shape=outs,
            in_specs=specs,
            out_specs=out_specs or jax.tree.map(lambda _: vmem, outs),
            scratch_shapes=scratch,
            input_output_aliases=aliases or {},
            compiler_params=params(limit),
            name=name,
        )(*[value for _, value in ins])

    tables = (
        jacobians.transpose(2, 3, 0, 1), giles_real.transpose(2, 3, 0, 1), giles_imag.transpose(2, 3, 0, 1),
        mode_orders.transpose(0, 2, 1), cell_map,
    )
    blades = blades.reshape(1, -1)
    corner_rows = groups * EDGE
    state_shape = struct(axial + 2, components, axial, wide, pitch)
    state, coef, inv, span_out, small, modes, table, blades, *tables = call(
        start_kernel, "start",
        (
            state_shape, struct(components + 6, axial, wide, pitch), struct(wide, pitch),
            struct(span_tiles, EDGE, pitch), struct(2 * corner_rows + EDGE, pitch), struct(span, pitch),
            jax.ShapeDtypeStruct((3 * components * pitch, pitch), jnp.bfloat16),
            *(jax.ShapeDtypeStruct(x.shape, x.dtype) for x in (blades, *tables)),
        ),
        [(hbm, in_hbm(x)) for x in (adjoint_start, source, couplings, damping, blades, *tables)],
        scratch=[
            pltpu.VMEM(source.shape, jnp.float32), pltpu.VMEM(couplings.shape, jnp.float32),
            pltpu.VMEM(damping.shape, jnp.float32), pltpu.SemaphoreType.DMA((5 + len(tables),)),
        ],
        groups=groups, length=length,
    )
    edges, inner, outer = call(
        pack_kernel, "pack",
        (struct(fields + 1, span, pitch), struct((groups + 1) * wide, pitch), struct(groups * wide, pitch)),
        [(vmem, x) for x in (state, coef, inv, modes)],
        groups=groups,
    )
    steps = [1 << n for n in range(place_count.bit_length() - 2)]
    last_step = place_count // 2

    def near(x):
        return moved(x, lambda r, s, p: (r - 1, s, p))

    def far(x):
        return moved(x, lambda r, s, p: (r - 1, s, p ^ last_step))

    synth, jac = call(
        synth_kernel, "synth",
        (
            jax.ShapeDtypeStruct(
                (-(-components * (pitch + SEGMENT_LANES) // pitch) * pitch, 3 * pitch), jnp.bfloat16
            ),
            struct(-(-6 * components * components // EDGE) * EDGE, pitch),
        ),
        [(vmem, x) for x in (blades, *tables)],
        scratch=[pltpu.VMEM((2, components * components, mode_orders.shape[1]), jnp.float32)],
        row_count=row_count, place_count=place_count, components=components, pitch=pitch, length=length, axial=axial,
    )
    small, edges, jac = lax.optimization_barrier((moved(small, lambda r, s, p: (r, 1 - s, p)), edges, jac))
    from_span = moved(span_out, lambda r, s, p: (r, 1 - s, p))
    edge_shape = struct(axial + 1, components, wide, pitch)
    inner = lax.dynamic_update_slice(inner, small[:corner_rows + EDGE], (groups * span, 0))
    outer = lax.dynamic_update_slice(outer, small[corner_rows + EDGE:], (groups * span, 0))
    modes = inner[groups * span + corner_rows:]
    outer = moved(outer, lambda r, s, p: (r, s, (p - 1 + 2 * (p % 2)) % place_count))
    inner = moved(inner, lambda r, s, p: (r, s, p ^ 1))
    modes = modes + inner[groups * span + corner_rows:]
    for step in steps[1:]:
        modes = modes + moved(modes, lambda r, s, p: (r, s, p ^ step))
    got = moved(modes, lambda r, s, p: (r, s, p ^ last_step))
    coef, inv, edge_coef, state, edge = call(
        first_kernel, "first_sweep",
        (
            struct(components + 6, axial, wide, pitch), struct(wide, pitch), struct(components + 7, wide, pitch),
            state_shape, edge_shape,
        ),
        [(vmem, x) for x in (jac, state, coef, inv, edges, from_span, inner, outer)],
        aliases={1: 3, 2: 0, 3: 1},
        groups=groups,
    )
    got, inv = lax.optimization_barrier((got, inv))
    modes = near(modes + got)
    state, edge, more, part = call(
        more_kernel, "more_sweeps",
        (state_shape, edge_shape, struct((axial - 1) * span + EDGE, pitch), struct(span, pitch)),
        [(vmem, x) for x in (jac, coef, edge_coef, state, edge, table)],
        aliases={3: 0, 4: 1},
    )
    more_shape = struct(axial * span + EDGE, pitch)
    more = call(
        late_kernel, "late_modes", more_shape,
        [(vmem, x) for x in (jac, coef, inv, part, more, modes, synth, table)],
    )
    state, edge, sent = call(
        between_kernel, "between_sweeps", (state_shape, edge_shape, more_shape),
        [(vmem, x) for x in (jac, coef, inv, edge_coef, state, edge, modes, synth, more)],
        aliases={4: 0, 5: 1},
    )
    state, edge = call(
        beside_kernel, "beside_sweeps", (state_shape, edge_shape),
        [(vmem, x) for x in (jac, coef, edge_coef, state, edge)],
        aliases={3: 0, 4: 1},
    )
    for step in steps:
        got = moved(more, lambda r, s, p: (r, s, p ^ step))
        more, sent = sent + got, sent + got
    more_b = far(more)
    more_a = near(more)
    return call(
        second_kernel, "second_sweeps", (state_shape, edge_shape, struct(components, axial, span, pitch)),
        [(vmem, x) for x in (jac, coef, inv, edge_coef, state, edge, more_a, more_b, synth)],
        aliases={4: 0, 5: 1},
        scratch=[
            pltpu.VMEM((axial + 1, components, wide, pitch), jnp.float32),
            pltpu.VMEM((axial, components, span, pitch), jnp.float32), pltpu.SemaphoreType.DMA((axial,)),
        ],
        out_specs=(vmem, vmem, hbm),
    )[2]


def solution(mesh):
    placed = (
        P(None, "row", "span", "pitch"),
        P(None, "row", "span", "pitch"),
        P(None, "row", "span", "pitch"),
        P("row", "span", "pitch"),
        P("row", None, None, None),
        P(),
        P(),
        P(),
        P(),
        P("row", None),
    )
    return jax.shard_map(
        on_device,
        mesh=mesh,
        in_specs=placed,
        out_specs=P(None, "row", "span", "pitch"),
        check_vma=False,
    )
```

```python
import functools
import math

import jax
import jax.numpy as jnp
from jax import lax
from jax.experimental import pallas as pl
from jax.experimental.pallas import tpu as pltpu
from jax.sharding import PartitionSpec as P

ITERS = 5
AXES = ("row", "span", "pitch")

ORDER_MAX = 2
BASE = 2 * ORDER_MAX + 1
COSINES = (BASE * BASE + 1) // 2
WAVES = 2 * COSINES - 1
COMPONENTS = 5
EDGE = 8
HALF = EDGE // 2
SEGMENT_LANES = 4 * EDGE
SHARED_LANES = SEGMENT_LANES // 2
EXACT = lax.Precision.HIGHEST
MIB = 1024 * 1024


def params(limit):
    return pltpu.CompilerParams(vmem_limit_bytes=limit)


def lanes(shape):
    return lax.broadcasted_iota(jnp.int32, shape, len(shape) - 1)


def rows(shape):
    return lax.broadcasted_iota(jnp.int32, shape, len(shape) - 2)


def column(j):
    component = (j * 41) >> 10
    wave = j - WAVES * component
    sine = wave >= COSINES
    return component, jnp.where(sine, wave - (COSINES - 1), wave), sine


def mode_number(mode, blades):
    high = ((mode + ORDER_MAX) * 13) >> 6
    low = mode - BASE * high
    return high * blades[0] + low * blades[1]


def waves(products, length):
    if length & (length - 1) == 0:
        phase = products & (length - 1)
    else:
        phase = jnp.mod(products, length)
    turn = phase.astype(jnp.float32) * (1.0 / length)
    quarter = jnp.floor(4.0 * turn + 0.5)
    x = (turn - 0.25 * quarter) * (2.0 * math.pi)
    y = x * x
    sine = x * (1.0 + y * (-1.0 / 6 + y * (1.0 / 120 + y * (-1.0 / 5040 + y * (1.0 / 362880)))))
    cosine = 1.0 + y * (-0.5 + y * (1.0 / 24 + y * (-1.0 / 720 + y * (1.0 / 40320 - y * (1.0 / 3628800)))))
    quarter = quarter.astype(jnp.int32) & 3
    odd = (quarter & 1) == 1
    cos_out = jnp.where(odd, sine, cosine)
    sin_out = jnp.where(odd, cosine, sine)
    cos_out = jnp.where((quarter == 1) | (quarter == 2), -cos_out, cos_out)
    sin_out = jnp.where(quarter >= 2, -sin_out, sin_out)
    return cos_out, sin_out


def to_edges(layers, pitch):
    lane = lanes(layers[-1].shape)
    block = jnp.zeros_like(layers[-1])
    for a, layer in enumerate(layers):
        if layer is None:
            continue
        start = a * SEGMENT_LANES
        first = pltpu.roll(layer, (start + EDGE) % pitch, layer.ndim - 1)
        last = pltpu.roll(layer, (start + 3 * EDGE) % pitch, layer.ndim - 1)
        block = jnp.where((lane >= start + EDGE) & (lane < start + 2 * EDGE), first, block)
        block = jnp.where((lane >= start + 2 * EDGE) & (lane < start + 3 * EDGE), last, block)
    return block


def half_rows(side):
    return jnp.where(side == 0, EDGE // 2, 0), jnp.where(side == 0, 0, EDGE // 2)


def slots(fields, components):
    per_group = SEGMENT_LANES // HALF
    near = [(f // per_group, f % per_group * HALF) for f in range(fields)]
    group, lane = near[-1]
    far = [(group, lane + HALF + c) for c in range(components)]
    return near, far


def packed_edges(blocks, place, components):
    near, far = slots(len(blocks), components)
    pitch = blocks[0].shape[1]
    lane = lanes(blocks[0].shape) % SEGMENT_LANES
    sides = []
    for near_at, far_at in ((3 * EDGE - HALF, 3 * EDGE - HALF - 1), (EDGE, EDGE + HALF)):
        packed = [jnp.zeros_like(blocks[0]) for _ in range(far[-1][0] + 1)]
        for f, (g, to) in enumerate(near):
            value = pltpu.roll(blocks[f], (to - near_at) % pitch, 1)
            packed[g] = jnp.where((lane >= to) & (lane < to + HALF), value, packed[g])
        for f, (g, to) in enumerate(far):
            packed[g] = jnp.where(lane == to, pltpu.roll(blocks[f], (to - far_at) % pitch, 1), packed[g])
        sides.append(packed)
    even = lax.rem(place, 2) == 0
    inner = [jnp.where(even, right, left) for right, left in zip(*sides)]
    outer = [jnp.where(even, left, right) for right, left in zip(*sides)]
    return inner, outer


def edge_blocks(state_ref, coef_ref, inv_ref, at):
    components, axial, pitch = state_ref.shape[1], state_ref.shape[2], state_ref.shape[4]
    blocks = [to_edges([state_ref[0, c, a, at, :] for a in range(axial)], pitch) for c in range(components)]
    blocks += [to_edges([coef_ref[f, a, at, :] for a in range(axial)], pitch) for f in range(components + 6)]
    return blocks + [to_edges([None] * (axial - 1) + [inv_ref[at, :]], pitch)]


def start_kernel(
    adjoint_hbm, source_hbm, couplings_hbm, damping_hbm, blades_hbm, *refs, groups, length,
):
    state_ref, coef_ref, inv_ref, span_ref, small_ref, modes_ref, table_ref, blades_ref = refs[5:13]
    source_ref, couplings_ref, damping_ref, sems = refs[18:]
    components, axial, span, pitch = source_ref.shape
    adjoint_ref = state_ref.at[0, :, :, pl.ds(0, span), :]
    copies = [
        pltpu.make_async_copy(src, dst, sems.at[n])
        for n, (src, dst) in enumerate((
            (couplings_hbm, couplings_ref), (damping_hbm, damping_ref), (source_hbm, source_ref),
            (adjoint_hbm, adjoint_ref), (blades_hbm, blades_ref), *zip(refs[:5], refs[13:18]),
        ))
    ]
    for copy in copies:
        copy.start()
    row, side, place = (lax.axis_index(name) for name in AXES)
    copies[4].wait()
    face = jnp.maximum(row - 1, 0)
    component, mode, sine = column(lanes((pitch, pitch)))
    number = mode_number(mode, [picked(blades_ref[...], face + n) for n in range(2)])
    cos_table, sin_table = waves(number * (place * pitch + rows((pitch, pitch))), length)
    table = jnp.where(component < components, jnp.where(sine, sin_table, cos_table), 0.0)
    for c in range(components):
        high, low = split(jnp.where(component == c, table, 0.0))
        for n, value in enumerate((high, high, low)):
            table_ref[pl.ds((n * components + c) * pitch, pitch), :] = value
    copies[0].wait()
    copies[1].wait()
    diag = damping_ref[...]
    for d in range(6):
        diag = diag + couplings_ref[d]
    inverse = 1.0 / diag
    for d in range(6):
        coef_ref[components + d, :, :span] = couplings_ref[d] * inverse
    inv_ref[:span] = inverse[axial - 1]
    copies[2].wait()
    for c in range(components):
        coef_ref[c, :, :span] = source_ref[c] * inverse
    copies[3].wait()
    edge_row = pl.multiple_of(jnp.where(side == 0, span - EDGE, 0), EDGE)
    blocks = edge_blocks(state_ref, coef_ref, inv_ref, pl.ds(edge_row, EDGE))
    for n, packed in enumerate(packed_edges(blocks, place, components)):
        for g, value in enumerate(packed):
            small_ref[pl.ds((n * (groups + 1) + g) * EDGE, EDGE), :] = value
    modes_ref[...] = projected([adjoint_ref[c, 0] for c in range(components)], table_ref)
    small_ref[pl.ds(groups * EDGE, EDGE), :] = modes_ref[pl.ds(edge_row, EDGE), :]

    to_low, to_high = half_rows(side)
    line = rows((EDGE, pitch))
    tiles = [state_ref[0, c, a, pl.ds(edge_row, EDGE), :] for c in range(components) for a in range(axial)]
    tiles += [coef_ref[f, a, pl.ds(edge_row, EDGE), :] for f in range(components + 6) for a in range(axial)]
    tiles += [inv_ref[pl.ds(edge_row, EDGE), :]]
    pairs = -(-len(tiles) // 2)
    for n in range(pairs):
        value = pltpu.roll(tiles[2 * n], to_low, 0)
        if 2 * n + 1 < len(tiles):
            value = jnp.where(line < HALF, value, pltpu.roll(tiles[2 * n + 1], to_high, 0))
        span_ref[n] = value
    fifth = jnp.where(side == 0, HALF - 1, HALF)
    for n in range(span_ref.shape[0] - pairs):
        value = jnp.zeros((EDGE, pitch), jnp.float32)
        for k in range(min(EDGE, components * axial - n * EDGE)):
            value = jnp.where(line == k, pltpu.roll(tiles[n * EDGE + k], lax.rem(k + EDGE - fifth, EDGE), 0), value)
        span_ref[pairs + n] = value
    for copy in copies[5:]:
        copy.wait()


def pack_kernel(state_ref, coef_ref, inv_ref, modes_ref, edges_ref, inner_ref, outer_ref, *, groups):
    _, components, axial, wide, pitch = state_ref.shape
    span = wide - EDGE
    place = lax.axis_index("pitch")
    blocks = edge_blocks(state_ref, coef_ref, inv_ref, pl.ds(0, span))
    for f, block in enumerate(blocks):
        edges_ref[f] = block
    for out_ref, packed in zip((inner_ref, outer_ref), packed_edges(blocks, place, components)):
        for g, value in enumerate(packed[:-1]):
            out_ref[pl.ds(g * span, span), :] = value
        low, high = packed[-1][:span // 2], packed[-1][span // 2:]
        shared = jnp.where(lanes(low.shape) % SEGMENT_LANES < SHARED_LANES, low, pltpu.roll(high, SHARED_LANES, 1))
        out_ref[pl.ds((len(packed) - 1) * span, span // 2), :] = shared
    start = (groups - 1) * span + span // 2 + (groups + 1) * EDGE
    inner_ref[pl.ds(start, span), :] = modes_ref[...]


def picked(values, at):
    chosen = jnp.where(lanes(values.shape) == at, values.astype(jnp.float32), 0.0)
    return jnp.sum(chosen, axis=1, keepdims=True).astype(jnp.int32)


def split(x):
    high = x.astype(jnp.bfloat16)
    return high, (x - high.astype(jnp.float32)).astype(jnp.bfloat16)


def thrice(x):
    high, low = split(x)
    return jnp.concatenate([high, low, high], 1)


def projected(strips, table_ref):
    return jnp.dot(thrice(jnp.concatenate(strips, 1)), table_ref[...], preferred_element_type=jnp.float32)


def synthesised(modes, synth_ref, count):
    dims = (((1,), (1,)), ((), ()))
    return lax.dot_general(thrice(modes), synth_ref[:count], dims, preferred_element_type=jnp.float32)


def synth_kernel(
    blades_ref, jacobians_ref, giles_re_ref, giles_im_ref, orders_ref, cells_ref, synth_ref, rows_ref, sums_ref,
    *, row_count, place_count, components, pitch, length, axial,
):
    row, place = lax.axis_index("row"), lax.axis_index("pitch")
    face = jnp.minimum(row, row_count - 2)
    for b in range(components):
        for c in range(components):
            entries = jacobians_ref[b, c]
            for d in range(6):
                at = (b * components + c) * 6 + d
                rows_ref[pl.ds(at, 1), :] = jnp.broadcast_to(entries[:, d:d + 1], (1, pitch))
    modes = orders_ref.shape[2]
    orders = orders_ref[face]
    tag = BASE * orders[0:1] + orders[1:2]
    component, mode, _ = column(rows((pitch, modes)))
    same = (jnp.abs(tag) == mode) & (component < components)
    plain = jnp.where(same, 1.0, 0.0)
    signed = jnp.where(tag < 0, -plain, plain)
    dims = (((1,), (1,)), ((), ()))
    for n, ref in enumerate((giles_re_ref, giles_im_ref)):
        for b in range(components):
            for c in range(components):
                sums_ref[n, pl.ds(b * components + c, 1), :] = ref[b, c, pl.ds(face, 1), :]
    sums_re = lax.dot_general(sums_ref[0], plain, dims, precision=EXACT, preferred_element_type=jnp.float32)
    sums_im = lax.dot_general(sums_ref[1], signed, dims, precision=EXACT, preferred_element_type=jnp.float32)
    component, mode, sine = column(lanes(sums_re.shape))
    scale = 2.0 / length
    with_cos = jnp.where(sine, sums_im, sums_re) * scale
    with_sin = jnp.where(sine, sums_re, -sums_im) * scale
    component = component[0:1]

    def chunk(at):
        start = pl.multiple_of(lax.rem(place + at + place_count, place_count) * pitch, pitch)
        return cells_ref[:, pl.ds(start, pitch)]

    own = chunk(0)
    lane = lanes((1, pitch))
    first = (axial - 1) * SEGMENT_LANES
    edge = jnp.where(lane < first + EDGE, pltpu.roll(chunk(-1), (first + EDGE) % pitch, 1), pltpu.roll(own, (first + EDGE) % pitch, 1))
    edge = jnp.where(lane < first + 2 * EDGE, edge, pltpu.roll(own, (first + 3 * EDGE) % pitch, 1))
    edge = jnp.where(lane < first + 3 * EDGE, edge, pltpu.roll(chunk(1), (first + 3 * EDGE) % pitch, 1))

    def upright(cells):
        wide = jnp.broadcast_to(cells.astype(jnp.float32), (pitch, pitch))
        return jnp.transpose(wide).astype(jnp.int32)

    edge_cells = upright(edge)[first:first + SEGMENT_LANES]
    at_cells = jnp.concatenate([upright(own), edge_cells], 0)
    _, mode, _ = column(lanes(at_cells.shape))
    blades = [picked(blades_ref[...], face + n) for n in range(2)]
    cos_table, sin_table = waves(mode_number(mode, blades) * at_cells, length)
    for c in range(components):
        row_cos = jnp.zeros((1, pitch), jnp.float32)
        row_sin = jnp.zeros((1, pitch), jnp.float32)
        for b in range(components):
            at = b * components + c
            row_cos = jnp.where(component == b, with_cos[at:at + 1], row_cos)
            row_sin = jnp.where(component == b, with_sin[at:at + 1], row_sin)
        part = row_cos * cos_table + row_sin * sin_table
        high, low = split(part)
        value = jnp.concatenate([high, high, low], 1)
        synth_ref[pl.ds(c * pitch, pitch), :] = value[:pitch]
        synth_ref[pl.ds(components * pitch + c * SEGMENT_LANES, SEGMENT_LANES), :] = value[pitch:]
    used = components * (pitch + SEGMENT_LANES)
    rest = synth_ref.shape[0] - used
    if rest:
        synth_ref[pl.ds(used, rest), :] = jnp.zeros((rest, 3 * pitch), jnp.bfloat16)


def jacobian(jac_ref, components, b, c, d):
    return jac_ref[pl.ds((b * components + c) * 6 + d, 1), :]


def mixed(jac_ref, source, couplings, neighbours):
    total = list(source)
    jac = functools.partial(jacobian, jac_ref, len(total))
    for d, neighbour in enumerate(neighbours):
        if neighbour is None:
            continue
        for c in range(len(total)):
            term = jac(0, c, d) * neighbour[0]
            for b in range(1, len(total)):
                term = term + jac(b, c, d) * neighbour[b]
            total[c] = total[c] + couplings[d] * term
    return total


def layer_update(jac_ref, state_ref, edge_ref, coef_ref, t, a, height):
    _, components, axial, wide, pitch = state_ref.shape
    lane = lanes((height, pitch))
    start = a * SEGMENT_LANES
    own = [state_ref[t, c, a] for c in range(components)]
    above = [state_ref[t, c, a + 1, :height] for c in range(components)] if a < axial - 1 else None
    below = [state_ref[t, c, a - 1, :height] for c in range(components)] if a else None
    edge = [edge_ref[t, c, :height] for c in range(components)]
    span_next = [pltpu.roll(x, wide - 1, 0)[:height] for x in own]
    span_prev = [pltpu.roll(x, 1, 0)[:height] for x in own]
    own = [x[:height] for x in own]
    to_end = (pitch - 1 - (start + 3 * EDGE)) % pitch
    to_begin = (pitch - (start + EDGE - 1)) % pitch
    pitch_next = [
        jnp.where(lane == pitch - 1, pltpu.roll(e, to_end, 1), pltpu.roll(x, pitch - 1, 1))
        for e, x in zip(edge, own)
    ]
    pitch_prev = [
        jnp.where(lane == 0, pltpu.roll(e, to_begin, 1), pltpu.roll(x, 1, 1))
        for e, x in zip(edge, own)
    ]
    source = [coef_ref[c, a, :height] for c in range(components)]
    couplings = [coef_ref[components + d, a, :height] for d in range(6)]
    return mixed(jac_ref, source, couplings, (above, below, span_next, span_prev, pitch_next, pitch_prev))


def edge_update(jac_ref, edge_ref, edge_coef_ref, t, axial):
    components, wide, pitch = edge_ref.shape[1:]
    lane = lanes((wide, pitch))
    own = [edge_ref[t, c] for c in range(components)]
    above = [jnp.where(lane < (axial - 1) * SEGMENT_LANES, pltpu.roll(x, pitch - SEGMENT_LANES, 1), 0.0) for x in own]
    below = [jnp.where(lane >= SEGMENT_LANES, pltpu.roll(x, SEGMENT_LANES, 1), 0.0) for x in own]
    span_next = [pltpu.roll(x, wide - 1, 0) for x in own]
    span_prev = [pltpu.roll(x, 1, 0) for x in own]
    pitch_next = [pltpu.roll(x, pitch - 1, 1) for x in own]
    pitch_prev = [pltpu.roll(x, 1, 1) for x in own]
    source = [edge_coef_ref[c] for c in range(components)]
    couplings = [edge_coef_ref[components + d] for d in range(6)]
    return mixed(jac_ref, source, couplings, (above, below, span_next, span_prev, pitch_next, pitch_prev))


def edge_boundary(field, c, components, pitch, axial):
    at = components * pitch + c * SEGMENT_LANES
    tile = field[:, (at // pitch) * pitch:(at // pitch + 1) * pitch]
    return pltpu.roll(tile, ((axial - 1) * SEGMENT_LANES - at % pitch) % pitch, 1)


def advance(refs, t, a, height=None):
    state_ref = refs[1]
    height = height or state_ref.shape[3]
    for c, value in enumerate(layer_update(*refs, t, a, height)):
        state_ref[t + 1, c, a, :height] = value


def first_kernel(
    jac_ref, state_in_ref, coef_in_ref, inv_in_ref, edges_ref, span_ref, inner_ref, outer_ref,
    coef_ref, inv_ref, edge_coef_ref, state_ref, edge_ref, *, groups,
):
    _, components, axial, wide, pitch = state_ref.shape
    span = wide - EDGE
    side = lax.axis_index("span")
    fields = 2 * components + 6
    line = rows((EDGE, pitch))
    keep_half = jnp.where(side == 0, line, EDGE - 1 - line) < HALF
    fifth = jnp.where(side == 0, HALF, HALF - 1)
    from_low, from_high = half_rows(1 - side)
    pairs = -(-(fields * axial + 1) // 2)

    def ghost(n):
        value = pltpu.roll(span_ref[n // 2], from_high if n % 2 else from_low, 0)
        value = jnp.where(keep_half, value, 0.0)
        if n < components * axial:
            extra = pltpu.roll(span_ref[pairs + n // EDGE], lax.rem(fifth + EDGE - n % EDGE, EDGE), 0)
            value = jnp.where(line == fifth, extra, value)
        return value

    even = lax.rem(lax.axis_index("pitch"), 2) == 0

    def group(ref, g):
        corner = ref[pl.ds((groups - 1) * span + span // 2 + g * EDGE, EDGE), :]
        if g < groups - 1:
            return jnp.concatenate([ref[pl.ds(g * span, span), :], corner], 0)
        shared = ref[pl.ds(g * span, span // 2), :]
        return jnp.concatenate([shared, pltpu.roll(shared, pitch - SHARED_LANES, 1), corner], 0)

    halves = [(group(inner_ref, g), group(outer_ref, g)) for g in range(groups)]
    from_left = [jnp.where(even, outer, inner) for inner, outer in halves]
    from_right = [jnp.where(even, inner, outer) for inner, outer in halves]
    near, far = slots(fields + 1, components)
    keep_five = keep_half | (line == fifth)
    for f in range(fields + 1):
        if f < fields:
            layers = [ghost(f * axial + a) for a in range(axial)]
        else:
            layers = [jnp.zeros((EDGE, pitch), jnp.float32)] * (axial - 1) + [ghost(fields * axial)]
        if f < components:
            for a in range(axial):
                state_ref[0, f, a, span:] = layers[a]
        elif f < fields:
            for a in range(axial):
                coef_ref[f - components, a, span:] = layers[a]
        else:
            inv_ref[span:] = layers[-1]
        g, at = near[f]
        value = jnp.concatenate([edges_ref[f], to_edges(layers, pitch)], 0)
        lane = lanes((wide, pitch)) % SEGMENT_LANES
        value = jnp.where((lane >= HALF) & (lane < EDGE), pltpu.roll(from_left[g], (HALF - at) % pitch, 1), value)
        value = jnp.where(
            (lane >= 3 * EDGE) & (lane < 3 * EDGE + HALF),
            pltpu.roll(from_right[g], (3 * EDGE - at) % pitch, 1), value,
        )
        if f < components:
            g, at = far[f]
            value = jnp.where(lane == HALF - 1, pltpu.roll(from_left[g], (HALF - 1 - at) % pitch, 1), value)
            value = jnp.where(
                lane == 3 * EDGE + HALF, pltpu.roll(from_right[g], (3 * EDGE + HALF - at) % pitch, 1), value,
            )
        target, at = (edge_ref.at[0], f) if f < components else (edge_coef_ref, f - components)
        target[at, :span] = value[:span]
        target[at, span:] = jnp.where(keep_five if f < components else keep_half, value[span:], 0.0)
    sweeps_without_boundaries(jac_ref, state_ref, edge_ref, coef_ref, edge_coef_ref, 0, 1)


def sweeps_without_boundaries(jac_ref, state_ref, edge_ref, coef_ref, edge_coef_ref, first, last):
    axial = state_ref.shape[2]
    for t in range(first, last):
        for a in range(axial - t):
            advance((jac_ref, state_ref, edge_ref, coef_ref), t, a)
        if t < axial - 1:
            for c, value in enumerate(edge_update(jac_ref, edge_ref, edge_coef_ref, t, axial)):
                edge_ref[t + 1, c] = value


def more_kernel(
    jac_ref, coef_ref, edge_coef_ref, state_in_ref, edge_in_ref, table_ref, state_ref, edge_ref, modes_ref, part_ref,
):
    _, components, axial, wide, pitch = state_ref.shape
    span = wide - EDGE
    side = lax.axis_index("span")
    sweeps_without_boundaries(jac_ref, state_ref, edge_ref, coef_ref, edge_coef_ref, 1, axial)
    strips = [
        jnp.concatenate([state_ref[t, c, 0] for t in range(1, axial)] + [state_ref[axial, c, 0, :span]], 0)
        for c in range(components)
    ]
    total = projected(strips, table_ref)
    ghosts = jnp.zeros((EDGE, pitch), jnp.float32)
    for t in range(1, axial):
        part = total[(t - 1) * wide:t * wide]
        modes_ref[pl.ds((t - 1) * span, span), :] = part[:span]
        keep, to_packed, _ = ghost_rows(side, t, axial)
        ghosts = jnp.where(keep, pltpu.roll(part[span:], to_packed, 0), ghosts)
    modes_ref[pl.ds((axial - 1) * span, EDGE), :] = ghosts
    part_ref[...] = total[(axial - 1) * wide:]


def ghost_rows(side, t, axial):
    line = rows((EDGE, 1))
    distance = jnp.where(side == 0, line, EDGE - 1 - line)
    start = sum(axial - n for n in range(1, t))
    to_packed = jnp.where(side == 0, start, (EDGE - start) % EDGE)
    from_packed = jnp.where(side == 0, (EDGE - start) % EDGE, start)
    return (distance >= start) & (distance < start + axial - t), to_packed, from_packed


def along_axis(jac_ref, coef_ref, delta, a, height):
    components = len(delta)
    out = []
    for c in range(components):
        term = jacobian(jac_ref, components, 0, c, 0) * delta[0]
        for b in range(1, components):
            term = term + jacobian(jac_ref, components, b, c, 0) * delta[b]
        out.append(coef_ref[components, a, :height] * term)
    return out


def late_kernel(
    jac_ref, coef_ref, inv_ref, part_ref, more_ref, first_ref, synth_ref, table_ref, modes_ref,
):
    span, pitch = part_ref.shape
    components, axial = coef_ref.shape[0] - 6, coef_ref.shape[1]
    field = synthesised(first_ref[EDGE:], synth_ref, components * pitch)
    delta = [inv_ref[:span] * field[:, c * pitch:(c + 1) * pitch] for c in range(components)]
    for a in range(axial - 2, -1, -1):
        delta = along_axis(jac_ref, coef_ref, delta, a, span)
    before = more_ref.shape[0]
    modes_ref[:before] = more_ref[...]
    modes_ref[before:] = part_ref[...] + projected(delta, table_ref)


def between_kernel(
    jac_ref, coef_ref, inv_ref, edge_coef_ref, state_in_ref, edge_in_ref, modes_ref, synth_ref, more_ref,
    state_ref, edge_ref, sent_ref,
):
    sent_ref[...] = more_ref[...]
    components, axial = state_ref.shape[1], state_ref.shape[2]
    wide, pitch = state_ref.shape[3:]
    modes = modes_ref[...]
    field = synthesised(jnp.concatenate([modes[EDGE:], modes[:EDGE]], 0), synth_ref, synth_ref.shape[0])
    delta = [inv_ref[...] * field[:, c * pitch:(c + 1) * pitch] for c in range(components)]
    for t in range(1, axial + 1):
        for c in range(components):
            state_ref[t, c, axial - t] += delta[c]
        if t < axial:
            delta = along_axis(jac_ref, coef_ref, delta, axial - 1 - t, wide)
    for c in range(components):
        edge_ref[1, c] += edge_coef_ref[components + 6] * edge_boundary(field, c, components, pitch, axial)
    diagonal_sweeps(jac_ref, state_ref, edge_ref, coef_ref, edge_coef_ref, 1, axial // 2 + 1)


def beside_kernel(jac_ref, coef_ref, edge_coef_ref, state_in_ref, edge_in_ref, state_ref, edge_ref):
    axial, span = state_ref.shape[2], state_ref.shape[3] - EDGE
    diagonal_sweeps(jac_ref, state_ref, edge_ref, coef_ref, edge_coef_ref, axial // 2 + 1, axial)
    advance((jac_ref, state_ref, edge_ref, coef_ref), axial, 0, span)


def diagonal_sweeps(jac_ref, state_ref, edge_ref, coef_ref, edge_coef_ref, first, last):
    axial = state_ref.shape[2]
    for t in range(first, last):
        advance((jac_ref, state_ref, edge_ref, coef_ref), t, axial - t)
        for c, value in enumerate(edge_update(jac_ref, edge_ref, edge_coef_ref, t, axial)):
            edge_ref[t + 1, c] = value


def second_kernel(
    jac_ref, coef_ref, inv_ref, edge_coef_ref, state_in_ref, edge_in_ref, more_a_ref, more_b_ref, synth_ref,
    state_ref, edge_ref, out_hbm, bound_ref, out_ref, sems,
):
    axial, components, span, pitch = out_ref.shape
    copies = [pltpu.make_async_copy(out_ref.at[a], out_hbm.at[:, a], sems.at[a]) for a in range(axial)]
    wide = span + EDGE
    side = lax.axis_index("span")
    more = more_a_ref[...] + more_b_ref[...]
    start = (axial - 1) * span
    parts = []
    for t in range(1, axial):
        _, _, from_packed = ghost_rows(side, t, axial)
        parts += [more[(t - 1) * span:t * span], pltpu.roll(more[start:start + EDGE], from_packed, 0)]
    field = synthesised(jnp.concatenate(parts + [more[start + EDGE:]], 0), synth_ref, synth_ref.shape[0])
    for t in range(1, axial):
        part = field[(t - 1) * wide:t * wide]
        for c in range(components):
            bound_ref[t, c] = inv_ref[...] * part[:, c * pitch:(c + 1) * pitch]
    for c in range(components):
        bound_ref[axial, c, :span] = inv_ref[:span] * field[(axial - 1) * wide:, c * pitch:(c + 1) * pitch]
    delta = [bound_ref[1, c] for c in range(components)]
    for t in range(2, axial + 2):
        height = wide if t <= axial else span
        for c in range(components):
            state_ref[t, c, axial + 1 - t, :height] += delta[c][:height]
        if t < axial + 1:
            delta = along_axis(jac_ref, coef_ref, delta, axial - t, wide)
    for c in range(components):
        out_ref[0, c] = state_ref[axial + 1, c, 0, :span]
    copies[0].start()
    for t in range(1, axial):
        if t > 1:
            for c, value in enumerate(edge_update(jac_ref, edge_ref, edge_coef_ref, t, axial)):
                edge_ref[t + 1, c] = value
        part = field[(t - 1) * wide:t * wide]
        for c in range(components):
            edge_ref[t + 1, c] += edge_coef_ref[components + 6] * edge_boundary(part, c, components, pitch, axial)
    refs = (jac_ref, state_ref, edge_ref, coef_ref)

    for t in range(2, axial):
        for a in range(axial + 1 - t, axial):
            advance(refs, t, a)
        for c in range(components):
            state_ref[t + 1, c, axial - 1] += bound_ref[t, c]
    for a in range(1, axial):
        for c, value in enumerate(layer_update(*refs, axial, a, span)):
            out_ref[a, c] = value + bound_ref[axial, c, :span] if a == axial - 1 else value
        copies[a].start()
    for copy in copies:
        copy.wait()


def moved(x, to):
    sizes = [lax.axis_size(name) for name in AXES]
    pairs = []
    for r in range(sizes[0]):
        for s in range(sizes[1]):
            for p in range(sizes[2]):
                target = to(r, s, p)
                if all(0 <= at < size for at, size in zip(target, sizes)):
                    number = lambda at: (at[0] * sizes[1] + at[1]) * sizes[2] + at[2]
                    pairs.append((number((r, s, p)), number(target)))
    return lax.ppermute(x, AXES, pairs)


def struct(*shape):
    return jax.ShapeDtypeStruct(shape, jnp.float32)


def on_device(
    adjoint_start, source, couplings, damping, jacobians, giles_real, giles_imag, blades, mode_orders, cell_map,
):
    components, axial, span, pitch = adjoint_start.shape
    row_count, span_count, place_count = (lax.axis_size(name) for name in AXES)
    length = pitch * place_count
    assert sum(axial - t for t in range(1, axial)) <= EDGE
    assert components == COMPONENTS and components * WAVES <= pitch
    assert axial == ITERS - 1 and ITERS <= EDGE and axial * SEGMENT_LANES == pitch
    assert span_count == 2 and place_count > 2 and place_count & (place_count - 1) == 0
    wide = span + EDGE
    fields = 2 * components + 6
    groups = slots(fields + 1, components)[1][-1][0] + 1
    pairs = -(-(fields * axial + 1) // 2)
    span_tiles = pairs + -(-components * axial // EDGE)
    vmem = pl.BlockSpec(memory_space=pltpu.VMEM)
    hbm = pl.BlockSpec(memory_space=pltpu.HBM)

    def in_hbm(x):
        return pltpu.with_memory_space_constraint(x, pltpu.HBM)

    def call(kernel, name, outs, ins, aliases=None, scratch=(), limit=40 * MIB, out_specs=None, **fixed):
        specs = [spec for spec, _ in ins]
        return pl.pallas_call(
            functools.partial(kernel, **fixed),
            out_shape=outs,
            in_specs=specs,
            out_specs=out_specs or jax.tree.map(lambda _: vmem, outs),
            scratch_shapes=scratch,
            input_output_aliases=aliases or {},
            compiler_params=params(limit),
            name=name,
        )(*[value for _, value in ins])

    tables = (
        jacobians.transpose(2, 3, 0, 1), giles_real.transpose(2, 3, 0, 1), giles_imag.transpose(2, 3, 0, 1),
        mode_orders.transpose(0, 2, 1), cell_map,
    )
    blades = blades.reshape(1, -1)
    corner_rows = groups * EDGE
    own_rows = (groups - 1) * span + span // 2
    assert slots(fields + 1, components)[1][-1][1] < SHARED_LANES
    state_shape = struct(axial + 2, components, axial, wide, pitch)
    state, coef, inv, span_out, small, modes, table, blades, *tables = call(
        start_kernel, "start",
        (
            state_shape, struct(components + 6, axial, wide, pitch), struct(wide, pitch),
            struct(span_tiles, EDGE, pitch), struct(2 * corner_rows + EDGE, pitch), struct(span, pitch),
            jax.ShapeDtypeStruct((3 * components * pitch, pitch), jnp.bfloat16),
            *(jax.ShapeDtypeStruct(x.shape, x.dtype) for x in (blades, *tables)),
        ),
        [(hbm, in_hbm(x)) for x in (adjoint_start, source, couplings, damping, blades, *tables)],
        scratch=[
            pltpu.VMEM(source.shape, jnp.float32), pltpu.VMEM(couplings.shape, jnp.float32),
            pltpu.VMEM(damping.shape, jnp.float32), pltpu.SemaphoreType.DMA((5 + len(tables),)),
        ],
        groups=groups, length=length,
    )
    edges, inner, outer = call(
        pack_kernel, "pack",
        (struct(fields + 1, span, pitch), struct(own_rows + corner_rows + wide, pitch), struct(own_rows + corner_rows, pitch)),
        [(vmem, x) for x in (state, coef, inv, modes)],
        groups=groups,
    )
    steps = [1 << n for n in range(place_count.bit_length() - 2)]
    last_step = place_count // 2

    def near(x):
        return moved(x, lambda r, s, p: (r - 1, s, p))

    def far(x):
        return moved(x, lambda r, s, p: (r - 1, s, p ^ last_step))

    synth, jac = call(
        synth_kernel, "synth",
        (
            jax.ShapeDtypeStruct(
                (-(-components * (pitch + SEGMENT_LANES) // pitch) * pitch, 3 * pitch), jnp.bfloat16
            ),
            struct(-(-6 * components * components // EDGE) * EDGE, pitch),
        ),
        [(vmem, x) for x in (blades, *tables)],
        scratch=[pltpu.VMEM((2, components * components, mode_orders.shape[1]), jnp.float32)],
        row_count=row_count, place_count=place_count, components=components, pitch=pitch, length=length, axial=axial,
    )
    small, edges, jac = lax.optimization_barrier((moved(small, lambda r, s, p: (r, 1 - s, p)), edges, jac))
    from_span = moved(span_out, lambda r, s, p: (r, 1 - s, p))
    edge_shape = struct(axial + 1, components, wide, pitch)
    inner = lax.dynamic_update_slice(inner, small[:corner_rows + EDGE], (own_rows, 0))
    outer = lax.dynamic_update_slice(outer, small[corner_rows + EDGE:], (own_rows, 0))
    modes = inner[own_rows + corner_rows:]
    outer = moved(outer, lambda r, s, p: (r, s, (p - 1 + 2 * (p % 2)) % place_count))
    inner = moved(inner, lambda r, s, p: (r, s, p ^ 1))
    modes = modes + inner[own_rows + corner_rows:]
    for step in steps[1:]:
        modes = modes + moved(modes, lambda r, s, p: (r, s, p ^ step))
    got = moved(modes, lambda r, s, p: (r, s, p ^ last_step))
    coef, inv, edge_coef, state, edge = call(
        first_kernel, "first_sweep",
        (
            struct(components + 6, axial, wide, pitch), struct(wide, pitch), struct(components + 7, wide, pitch),
            state_shape, edge_shape,
        ),
        [(vmem, x) for x in (jac, state, coef, inv, edges, from_span, inner, outer)],
        aliases={1: 3, 2: 0, 3: 1},
        groups=groups,
    )
    got, inv = lax.optimization_barrier((got, inv))
    modes = near(modes + got)
    state, edge, more, part = call(
        more_kernel, "more_sweeps",
        (state_shape, edge_shape, struct((axial - 1) * span + EDGE, pitch), struct(span, pitch)),
        [(vmem, x) for x in (jac, coef, edge_coef, state, edge, table)],
        aliases={3: 0, 4: 1},
    )
    more_shape = struct(axial * span + EDGE, pitch)
    more = call(
        late_kernel, "late_modes", more_shape,
        [(vmem, x) for x in (jac, coef, inv, part, more, modes, synth, table)],
    )
    state, edge, sent = call(
        between_kernel, "between_sweeps", (state_shape, edge_shape, more_shape),
        [(vmem, x) for x in (jac, coef, inv, edge_coef, state, edge, modes, synth, more)],
        aliases={4: 0, 5: 1},
    )
    state, edge = call(
        beside_kernel, "beside_sweeps", (state_shape, edge_shape),
        [(vmem, x) for x in (jac, coef, edge_coef, state, edge)],
        aliases={3: 0, 4: 1},
    )
    for step in steps:
        got = moved(more, lambda r, s, p: (r, s, p ^ step))
        more, sent = sent + got, sent + got
    more_b = far(more)
    more_a = near(more)
    return call(
        second_kernel, "second_sweeps", (state_shape, edge_shape, struct(components, axial, span, pitch)),
        [(vmem, x) for x in (jac, coef, inv, edge_coef, state, edge, more_a, more_b, synth)],
        aliases={4: 0, 5: 1},
        scratch=[
            pltpu.VMEM((axial + 1, components, wide, pitch), jnp.float32),
            pltpu.VMEM((axial, components, span, pitch), jnp.float32), pltpu.SemaphoreType.DMA((axial,)),
        ],
        out_specs=(vmem, vmem, hbm),
    )[2]


def solution(mesh):
    placed = (
        P(None, "row", "span", "pitch"),
        P(None, "row", "span", "pitch"),
        P(None, "row", "span", "pitch"),
        P("row", "span", "pitch"),
        P("row", None, None, None),
        P(),
        P(),
        P(),
        P(),
        P("row", None),
    )
    return jax.shard_map(
        on_device,
        mesh=mesh,
        in_specs=placed,
        out_specs=P(None, "row", "span", "pitch"),
        check_vma=False,
    )
```

```python
import functools
import math

import jax
import jax.numpy as jnp
from jax import lax
from jax.experimental import pallas as pl
from jax.experimental.pallas import tpu as pltpu
from jax.sharding import PartitionSpec as P

ITERS = 5
AXES = ("row", "span", "pitch")

ORDER_MAX = 2
BASE = 2 * ORDER_MAX + 1
COSINES = (BASE * BASE + 1) // 2
WAVES = 2 * COSINES - 1
COMPONENTS = 5
EDGE = 8
HALF = EDGE // 2
SEGMENT_LANES = 4 * EDGE
SHARED_LANES = SEGMENT_LANES // 2
EXACT = lax.Precision.HIGHEST
MIB = 1024 * 1024


def params(limit):
    return pltpu.CompilerParams(vmem_limit_bytes=limit)


def lanes(shape):
    return lax.broadcasted_iota(jnp.int32, shape, len(shape) - 1)


def rows(shape):
    return lax.broadcasted_iota(jnp.int32, shape, len(shape) - 2)


def column(j):
    component = (j * 41) >> 10
    wave = j - WAVES * component
    sine = wave >= COSINES
    return component, jnp.where(sine, wave - (COSINES - 1), wave), sine


def mode_number(mode, blades):
    high = ((mode + ORDER_MAX) * 13) >> 6
    low = mode - BASE * high
    return high * blades[0] + low * blades[1]


def waves(products, length):
    if length & (length - 1) == 0:
        phase = products & (length - 1)
    else:
        phase = jnp.mod(products, length)
    turn = phase.astype(jnp.float32) * (1.0 / length)
    quarter = jnp.floor(4.0 * turn + 0.5)
    x = (turn - 0.25 * quarter) * (2.0 * math.pi)
    y = x * x
    sine = x * (1.0 + y * (-1.0 / 6 + y * (1.0 / 120 + y * (-1.0 / 5040 + y * (1.0 / 362880)))))
    cosine = 1.0 + y * (-0.5 + y * (1.0 / 24 + y * (-1.0 / 720 + y * (1.0 / 40320 - y * (1.0 / 3628800)))))
    quarter = quarter.astype(jnp.int32) & 3
    odd = (quarter & 1) == 1
    cos_out = jnp.where(odd, sine, cosine)
    sin_out = jnp.where(odd, cosine, sine)
    cos_out = jnp.where((quarter == 1) | (quarter == 2), -cos_out, cos_out)
    sin_out = jnp.where(quarter >= 2, -sin_out, sin_out)
    return cos_out, sin_out


def to_edges(layers, pitch):
    lane = lanes(layers[-1].shape)
    block = jnp.zeros_like(layers[-1])
    for a, layer in enumerate(layers):
        if layer is None:
            continue
        start = a * SEGMENT_LANES
        first = pltpu.roll(layer, (start + EDGE) % pitch, layer.ndim - 1)
        last = pltpu.roll(layer, (start + 3 * EDGE) % pitch, layer.ndim - 1)
        block = jnp.where((lane >= start + EDGE) & (lane < start + 2 * EDGE), first, block)
        block = jnp.where((lane >= start + 2 * EDGE) & (lane < start + 3 * EDGE), last, block)
    return block


def half_rows(side):
    return jnp.where(side == 0, EDGE // 2, 0), jnp.where(side == 0, 0, EDGE // 2)


def slots(fields, components):
    per_group = SEGMENT_LANES // HALF
    near = [(f // per_group, f % per_group * HALF) for f in range(fields)]
    group, lane = near[-1]
    far = [(group, lane + HALF + c) for c in range(components)]
    return near, far


def packed_edges(blocks, place, components):
    near, far = slots(len(blocks), components)
    pitch = blocks[0].shape[1]
    lane = lanes(blocks[0].shape) % SEGMENT_LANES
    sides = []
    for near_at, far_at in ((3 * EDGE - HALF, 3 * EDGE - HALF - 1), (EDGE, EDGE + HALF)):
        packed = [jnp.zeros_like(blocks[0]) for _ in range(far[-1][0] + 1)]
        for f, (g, to) in enumerate(near):
            value = pltpu.roll(blocks[f], (to - near_at) % pitch, 1)
            packed[g] = jnp.where((lane >= to) & (lane < to + HALF), value, packed[g])
        for f, (g, to) in enumerate(far):
            packed[g] = jnp.where(lane == to, pltpu.roll(blocks[f], (to - far_at) % pitch, 1), packed[g])
        sides.append(packed)
    even = lax.rem(place, 2) == 0
    inner = [jnp.where(even, right, left) for right, left in zip(*sides)]
    outer = [jnp.where(even, left, right) for right, left in zip(*sides)]
    return inner, outer


def edge_blocks(state_ref, coef_ref, inv_ref, at):
    components, axial, pitch = state_ref.shape[1], state_ref.shape[2], state_ref.shape[4]
    blocks = [to_edges([state_ref[0, c, a, at, :] for a in range(axial)], pitch) for c in range(components)]
    blocks += [to_edges([coef_ref[f, a, at, :] for a in range(axial)], pitch) for f in range(components + 6)]
    return blocks + [to_edges([None] * (axial - 1) + [inv_ref[at, :]], pitch)]


def start_kernel(
    adjoint_hbm, source_hbm, couplings_hbm, damping_hbm, blades_hbm, *refs, groups, length,
):
    state_ref, coef_ref, inv_ref, span_ref, small_ref, modes_ref, table_ref, blades_ref = refs[5:13]
    source_ref, couplings_ref, damping_ref, sems = refs[18:]
    components, axial, span, pitch = source_ref.shape
    adjoint_ref = state_ref.at[0, :, :, pl.ds(0, span), :]
    copies = [
        pltpu.make_async_copy(src, dst, sems.at[n])
        for n, (src, dst) in enumerate((
            (couplings_hbm, couplings_ref), (damping_hbm, damping_ref), (source_hbm, source_ref),
            (adjoint_hbm, adjoint_ref), (blades_hbm, blades_ref), *zip(refs[:5], refs[13:18]),
        ))
    ]
    for copy in copies:
        copy.start()
    row, side, place = (lax.axis_index(name) for name in AXES)
    copies[4].wait()
    face = jnp.maximum(row - 1, 0)
    component, mode, sine = column(lanes((pitch, pitch)))
    number = mode_number(mode, [picked(blades_ref[...], face + n) for n in range(2)])
    cos_table, sin_table = waves(number * (place * pitch + rows((pitch, pitch))), length)
    table = jnp.where(component < components, jnp.where(sine, sin_table, cos_table), 0.0)
    for c in range(components):
        high, low = split(jnp.where(component == c, table, 0.0))
        for n, value in enumerate((high, high, low)):
            table_ref[pl.ds((n * components + c) * pitch, pitch), :] = value
    copies[0].wait()
    copies[1].wait()
    diag = damping_ref[...]
    for d in range(6):
        diag = diag + couplings_ref[d]
    inverse = 1.0 / diag
    for d in range(6):
        coef_ref[components + d, :, :span] = couplings_ref[d] * inverse
    inv_ref[:span] = inverse[axial - 1]
    copies[2].wait()
    for c in range(components):
        coef_ref[c, :, :span] = source_ref[c] * inverse
    copies[3].wait()
    edge_row = pl.multiple_of(jnp.where(side == 0, span - EDGE, 0), EDGE)
    blocks = edge_blocks(state_ref, coef_ref, inv_ref, pl.ds(edge_row, EDGE))
    for n, packed in enumerate(packed_edges(blocks, place, components)):
        for g, value in enumerate(packed):
            small_ref[pl.ds((n * (groups + 1) + g) * EDGE, EDGE), :] = value
    modes_ref[...] = projected([adjoint_ref[c, 0] for c in range(components)], table_ref)
    small_ref[pl.ds(groups * EDGE, EDGE), :] = modes_ref[pl.ds(edge_row, EDGE), :]

    to_low, to_high = half_rows(side)
    line = rows((EDGE, pitch))
    tiles = [state_ref[0, c, a, pl.ds(edge_row, EDGE), :] for c in range(components) for a in range(axial)]
    tiles += [coef_ref[f, a, pl.ds(edge_row, EDGE), :] for f in range(components + 6) for a in range(axial)]
    tiles += [inv_ref[pl.ds(edge_row, EDGE), :]]
    pairs = -(-len(tiles) // 2)
    for n in range(pairs):
        value = pltpu.roll(tiles[2 * n], to_low, 0)
        if 2 * n + 1 < len(tiles):
            value = jnp.where(line < HALF, value, pltpu.roll(tiles[2 * n + 1], to_high, 0))
        span_ref[n] = value
    fifth = jnp.where(side == 0, HALF - 1, HALF)
    for n in range(span_ref.shape[0] - pairs):
        value = jnp.zeros((EDGE, pitch), jnp.float32)
        for k in range(min(EDGE, components * axial - n * EDGE)):
            value = jnp.where(line == k, pltpu.roll(tiles[n * EDGE + k], lax.rem(k + EDGE - fifth, EDGE), 0), value)
        span_ref[pairs + n] = value
    for copy in copies[5:]:
        copy.wait()


def pack_kernel(state_ref, coef_ref, inv_ref, modes_ref, edges_ref, inner_ref, outer_ref, *, groups):
    _, components, axial, wide, pitch = state_ref.shape
    span = wide - EDGE
    place = lax.axis_index("pitch")
    blocks = edge_blocks(state_ref, coef_ref, inv_ref, pl.ds(0, span))
    for f, block in enumerate(blocks):
        edges_ref[f] = block
    for out_ref, packed in zip((inner_ref, outer_ref), packed_edges(blocks, place, components)):
        for g, value in enumerate(packed[:-1]):
            out_ref[pl.ds(g * span, span), :] = value
        low, high = packed[-1][:span // 2], packed[-1][span // 2:]
        shared = jnp.where(lanes(low.shape) % SEGMENT_LANES < SHARED_LANES, low, pltpu.roll(high, SHARED_LANES, 1))
        out_ref[pl.ds((len(packed) - 1) * span, span // 2), :] = shared
    start = (groups - 1) * span + span // 2 + (groups + 1) * EDGE
    inner_ref[pl.ds(start, span), :] = modes_ref[...]


def picked(values, at):
    chosen = jnp.where(lanes(values.shape) == at, values.astype(jnp.float32), 0.0)
    return jnp.sum(chosen, axis=1, keepdims=True).astype(jnp.int32)


def split(x):
    high = x.astype(jnp.bfloat16)
    return high, (x - high.astype(jnp.float32)).astype(jnp.bfloat16)


def thrice(x):
    high, low = split(x)
    return jnp.concatenate([high, low, high], 1)


def projected(strips, table_ref):
    return jnp.dot(thrice(jnp.concatenate(strips, 1)), table_ref[...], preferred_element_type=jnp.float32)


def synthesised(modes, synth_ref, count):
    dims = (((1,), (1,)), ((), ()))
    return lax.dot_general(thrice(modes), synth_ref[:count], dims, preferred_element_type=jnp.float32)


def synth_kernel(
    blades_ref, jacobians_ref, giles_re_ref, giles_im_ref, orders_ref, cells_ref, synth_ref, rows_ref, sums_ref,
    *, row_count, place_count, components, pitch, length, axial,
):
    row, place = lax.axis_index("row"), lax.axis_index("pitch")
    face = jnp.minimum(row, row_count - 2)
    for b in range(components):
        for c in range(components):
            entries = jacobians_ref[b, c]
            for d in range(6):
                at = (b * components + c) * 6 + d
                rows_ref[pl.ds(at, 1), :] = jnp.broadcast_to(entries[:, d:d + 1], (1, pitch))
    modes = orders_ref.shape[2]
    orders = orders_ref[face]
    tag = BASE * orders[0:1] + orders[1:2]
    component, mode, _ = column(rows((pitch, modes)))
    same = (jnp.abs(tag) == mode) & (component < components)
    plain = jnp.where(same, 1.0, 0.0)
    signed = jnp.where(tag < 0, -plain, plain)
    dims = (((1,), (1,)), ((), ()))
    for n, ref in enumerate((giles_re_ref, giles_im_ref)):
        for b in range(components):
            for c in range(components):
                sums_ref[n, pl.ds(b * components + c, 1), :] = ref[b, c, pl.ds(face, 1), :]
    sums_re = lax.dot_general(sums_ref[0], plain, dims, precision=EXACT, preferred_element_type=jnp.float32)
    sums_im = lax.dot_general(sums_ref[1], signed, dims, precision=EXACT, preferred_element_type=jnp.float32)
    component, mode, sine = column(lanes(sums_re.shape))
    scale = 2.0 / length
    with_cos = jnp.where(sine, sums_im, sums_re) * scale
    with_sin = jnp.where(sine, sums_re, -sums_im) * scale
    component = component[0:1]

    def chunk(at):
        start = pl.multiple_of(lax.rem(place + at + place_count, place_count) * pitch, pitch)
        return cells_ref[:, pl.ds(start, pitch)]

    own = chunk(0)
    lane = lanes((1, pitch))
    first = (axial - 1) * SEGMENT_LANES
    edge = jnp.where(lane < first + EDGE, pltpu.roll(chunk(-1), (first + EDGE) % pitch, 1), pltpu.roll(own, (first + EDGE) % pitch, 1))
    edge = jnp.where(lane < first + 2 * EDGE, edge, pltpu.roll(own, (first + 3 * EDGE) % pitch, 1))
    edge = jnp.where(lane < first + 3 * EDGE, edge, pltpu.roll(chunk(1), (first + 3 * EDGE) % pitch, 1))

    def upright(cells):
        wide = jnp.broadcast_to(cells.astype(jnp.float32), (pitch, pitch))
        return jnp.transpose(wide).astype(jnp.int32)

    edge_cells = upright(edge)[first:first + SEGMENT_LANES]
    at_cells = jnp.concatenate([upright(own), edge_cells], 0)
    _, mode, _ = column(lanes(at_cells.shape))
    blades = [picked(blades_ref[...], face + n) for n in range(2)]
    cos_table, sin_table = waves(mode_number(mode, blades) * at_cells, length)
    for c in range(components):
        row_cos = jnp.zeros((1, pitch), jnp.float32)
        row_sin = jnp.zeros((1, pitch), jnp.float32)
        for b in range(components):
            at = b * components + c
            row_cos = jnp.where(component == b, with_cos[at:at + 1], row_cos)
            row_sin = jnp.where(component == b, with_sin[at:at + 1], row_sin)
        part = row_cos * cos_table + row_sin * sin_table
        high, low = split(part)
        value = jnp.concatenate([high, high, low], 1)
        synth_ref[pl.ds(c * pitch, pitch), :] = value[:pitch]
        synth_ref[pl.ds(components * pitch + c * SEGMENT_LANES, SEGMENT_LANES), :] = value[pitch:]
    used = components * (pitch + SEGMENT_LANES)
    rest = synth_ref.shape[0] - used
    if rest:
        synth_ref[pl.ds(used, rest), :] = jnp.zeros((rest, 3 * pitch), jnp.bfloat16)


def jacobian(jac_ref, components, b, c, d):
    return jac_ref[pl.ds((b * components + c) * 6 + d, 1), :]


def mixed(jac_ref, source, couplings, neighbours):
    total = list(source)
    jac = functools.partial(jacobian, jac_ref, len(total))
    for d, neighbour in enumerate(neighbours):
        if neighbour is None:
            continue
        for c in range(len(total)):
            term = jac(0, c, d) * neighbour[0]
            for b in range(1, len(total)):
                term = term + jac(b, c, d) * neighbour[b]
            total[c] = total[c] + couplings[d] * term
    return total


def layer_update(jac_ref, state_ref, edge_ref, coef_ref, t, a, height):
    _, components, axial, wide, pitch = state_ref.shape
    lane = lanes((height, pitch))
    start = a * SEGMENT_LANES
    own = [state_ref[t, c, a] for c in range(components)]
    above = [state_ref[t, c, a + 1, :height] for c in range(components)] if a < axial - 1 else None
    below = [state_ref[t, c, a - 1, :height] for c in range(components)] if a else None
    edge = [edge_ref[t, c, :height] for c in range(components)]
    span_next = [pltpu.roll(x, wide - 1, 0)[:height] for x in own]
    span_prev = [pltpu.roll(x, 1, 0)[:height] for x in own]
    own = [x[:height] for x in own]
    to_end = (pitch - 1 - (start + 3 * EDGE)) % pitch
    to_begin = (pitch - (start + EDGE - 1)) % pitch
    pitch_next = [
        jnp.where(lane == pitch - 1, pltpu.roll(e, to_end, 1), pltpu.roll(x, pitch - 1, 1))
        for e, x in zip(edge, own)
    ]
    pitch_prev = [
        jnp.where(lane == 0, pltpu.roll(e, to_begin, 1), pltpu.roll(x, 1, 1))
        for e, x in zip(edge, own)
    ]
    source = [coef_ref[c, a, :height] for c in range(components)]
    couplings = [coef_ref[components + d, a, :height] for d in range(6)]
    return mixed(jac_ref, source, couplings, (above, below, span_next, span_prev, pitch_next, pitch_prev))


def edge_update(jac_ref, edge_ref, edge_coef_ref, t, axial):
    components, wide, pitch = edge_ref.shape[1:]
    lane = lanes((wide, pitch))
    own = [edge_ref[t, c] for c in range(components)]
    above = [jnp.where(lane < (axial - 1) * SEGMENT_LANES, pltpu.roll(x, pitch - SEGMENT_LANES, 1), 0.0) for x in own]
    below = [jnp.where(lane >= SEGMENT_LANES, pltpu.roll(x, SEGMENT_LANES, 1), 0.0) for x in own]
    span_next = [pltpu.roll(x, wide - 1, 0) for x in own]
    span_prev = [pltpu.roll(x, 1, 0) for x in own]
    pitch_next = [pltpu.roll(x, pitch - 1, 1) for x in own]
    pitch_prev = [pltpu.roll(x, 1, 1) for x in own]
    source = [edge_coef_ref[c] for c in range(components)]
    couplings = [edge_coef_ref[components + d] for d in range(6)]
    return mixed(jac_ref, source, couplings, (above, below, span_next, span_prev, pitch_next, pitch_prev))


def edge_boundary(field, c, components, pitch, axial):
    at = components * pitch + c * SEGMENT_LANES
    tile = field[:, (at // pitch) * pitch:(at // pitch + 1) * pitch]
    return pltpu.roll(tile, ((axial - 1) * SEGMENT_LANES - at % pitch) % pitch, 1)


def advance(refs, t, a, height=None):
    state_ref = refs[1]
    height = height or state_ref.shape[3]
    for c, value in enumerate(layer_update(*refs, t, a, height)):
        state_ref[t + 1, c, a, :height] = value


def first_kernel(
    jac_ref, state_in_ref, coef_in_ref, inv_in_ref, edges_ref, span_ref, inner_ref, outer_ref,
    coef_ref, inv_ref, edge_coef_ref, state_ref, edge_ref, *, groups,
):
    _, components, axial, wide, pitch = state_ref.shape
    span = wide - EDGE
    side = lax.axis_index("span")
    fields = 2 * components + 6
    line = rows((EDGE, pitch))
    keep_half = jnp.where(side == 0, line, EDGE - 1 - line) < HALF
    fifth = jnp.where(side == 0, HALF, HALF - 1)
    from_low, from_high = half_rows(1 - side)
    pairs = -(-(fields * axial + 1) // 2)

    def ghost(n):
        value = pltpu.roll(span_ref[n // 2], from_high if n % 2 else from_low, 0)
        value = jnp.where(keep_half, value, 0.0)
        if n < components * axial:
            extra = pltpu.roll(span_ref[pairs + n // EDGE], lax.rem(fifth + EDGE - n % EDGE, EDGE), 0)
            value = jnp.where(line == fifth, extra, value)
        return value

    even = lax.rem(lax.axis_index("pitch"), 2) == 0

    def group(ref, g):
        corner = ref[pl.ds((groups - 1) * span + span // 2 + g * EDGE, EDGE), :]
        if g < groups - 1:
            return jnp.concatenate([ref[pl.ds(g * span, span), :], corner], 0)
        shared = ref[pl.ds(g * span, span // 2), :]
        return jnp.concatenate([shared, pltpu.roll(shared, pitch - SHARED_LANES, 1), corner], 0)

    halves = [(group(inner_ref, g), group(outer_ref, g)) for g in range(groups)]
    from_left = [jnp.where(even, outer, inner) for inner, outer in halves]
    from_right = [jnp.where(even, inner, outer) for inner, outer in halves]
    near, far = slots(fields + 1, components)
    keep_five = keep_half | (line == fifth)
    for f in range(fields + 1):
        if f < fields:
            layers = [ghost(f * axial + a) for a in range(axial)]
        else:
            layers = [jnp.zeros((EDGE, pitch), jnp.float32)] * (axial - 1) + [ghost(fields * axial)]
        if f < components:
            for a in range(axial):
                state_ref[0, f, a, span:] = layers[a]
        elif f < fields:
            for a in range(axial):
                coef_ref[f - components, a, span:] = layers[a]
        else:
            inv_ref[span:] = layers[-1]
        g, at = near[f]
        value = jnp.concatenate([edges_ref[f], to_edges(layers, pitch)], 0)
        lane = lanes((wide, pitch)) % SEGMENT_LANES
        value = jnp.where((lane >= HALF) & (lane < EDGE), pltpu.roll(from_left[g], (HALF - at) % pitch, 1), value)
        value = jnp.where(
            (lane >= 3 * EDGE) & (lane < 3 * EDGE + HALF),
            pltpu.roll(from_right[g], (3 * EDGE - at) % pitch, 1), value,
        )
        if f < components:
            g, at = far[f]
            value = jnp.where(lane == HALF - 1, pltpu.roll(from_left[g], (HALF - 1 - at) % pitch, 1), value)
            value = jnp.where(
                lane == 3 * EDGE + HALF, pltpu.roll(from_right[g], (3 * EDGE + HALF - at) % pitch, 1), value,
            )
        target, at = (edge_ref.at[0], f) if f < components else (edge_coef_ref, f - components)
        target[at, :span] = value[:span]
        target[at, span:] = jnp.where(keep_five if f < components else keep_half, value[span:], 0.0)
    sweeps_without_boundaries(jac_ref, state_ref, edge_ref, coef_ref, edge_coef_ref, 0, 1)


def sweeps_without_boundaries(jac_ref, state_ref, edge_ref, coef_ref, edge_coef_ref, first, last):
    axial = state_ref.shape[2]
    for t in range(first, last):
        for a in range(axial - t):
            advance((jac_ref, state_ref, edge_ref, coef_ref), t, a)
        if t < axial - 1:
            for c, value in enumerate(edge_update(jac_ref, edge_ref, edge_coef_ref, t, axial)):
                edge_ref[t + 1, c] = value


def more_kernel(
    jac_ref, coef_ref, edge_coef_ref, state_in_ref, edge_in_ref, table_ref, state_ref, edge_ref, modes_ref, part_ref,
):
    _, components, axial, wide, pitch = state_ref.shape
    span = wide - EDGE
    side = lax.axis_index("span")
    sweeps_without_boundaries(jac_ref, state_ref, edge_ref, coef_ref, edge_coef_ref, 1, axial)
    strips = [
        jnp.concatenate([state_ref[t, c, 0] for t in range(1, axial)] + [state_ref[axial, c, 0, :span]], 0)
        for c in range(components)
    ]
    total = projected(strips, table_ref)
    ghosts = jnp.zeros((EDGE, pitch), jnp.float32)
    for t in range(1, axial):
        part = total[(t - 1) * wide:t * wide]
        modes_ref[pl.ds((t - 1) * span, span), :] = part[:span]
        keep, to_packed, _ = ghost_rows(side, t, axial)
        ghosts = jnp.where(keep, pltpu.roll(part[span:], to_packed, 0), ghosts)
    modes_ref[pl.ds((axial - 1) * span, EDGE), :] = ghosts
    part_ref[...] = total[(axial - 1) * wide:]


def ghost_rows(side, t, axial):
    line = rows((EDGE, 1))
    distance = jnp.where(side == 0, line, EDGE - 1 - line)
    start = sum(axial - n for n in range(1, t))
    to_packed = jnp.where(side == 0, start, (EDGE - start) % EDGE)
    from_packed = jnp.where(side == 0, (EDGE - start) % EDGE, start)
    return (distance >= start) & (distance < start + axial - t), to_packed, from_packed


def along_axis(jac_ref, coef_ref, delta, a, height):
    components = len(delta)
    out = []
    for c in range(components):
        term = jacobian(jac_ref, components, 0, c, 0) * delta[0]
        for b in range(1, components):
            term = term + jacobian(jac_ref, components, b, c, 0) * delta[b]
        out.append(coef_ref[components, a, :height] * term)
    return out


def late_kernel(
    jac_ref, coef_ref, inv_ref, part_ref, more_ref, first_ref, synth_ref, table_ref, modes_ref,
):
    span, pitch = part_ref.shape
    components, axial = coef_ref.shape[0] - 6, coef_ref.shape[1]
    field = synthesised(first_ref[EDGE:], synth_ref, components * pitch)
    delta = [inv_ref[:span] * field[:, c * pitch:(c + 1) * pitch] for c in range(components)]
    for a in range(axial - 2, -1, -1):
        delta = along_axis(jac_ref, coef_ref, delta, a, span)
    before = more_ref.shape[0]
    modes_ref[:before] = more_ref[...]
    modes_ref[before:] = part_ref[...] + projected(delta, table_ref)


def between_kernel(
    jac_ref, coef_ref, inv_ref, edge_coef_ref, state_in_ref, edge_in_ref, modes_ref, synth_ref, more_ref,
    state_ref, edge_ref, sent_ref,
):
    sent_ref[...] = more_ref[...]
    components, axial = state_ref.shape[1], state_ref.shape[2]
    wide, pitch = state_ref.shape[3:]
    modes = modes_ref[...]
    field = synthesised(jnp.concatenate([modes[EDGE:], modes[:EDGE]], 0), synth_ref, synth_ref.shape[0])
    delta = [inv_ref[...] * field[:, c * pitch:(c + 1) * pitch] for c in range(components)]
    for t in range(1, axial + 1):
        for c in range(components):
            state_ref[t, c, axial - t] += delta[c]
        if t < axial:
            delta = along_axis(jac_ref, coef_ref, delta, axial - 1 - t, wide)
    for c in range(components):
        edge_ref[1, c] += edge_coef_ref[components + 6] * edge_boundary(field, c, components, pitch, axial)
    diagonal_sweeps(jac_ref, state_ref, edge_ref, coef_ref, edge_coef_ref, 1, axial // 2 + 1)


def beside_kernel(jac_ref, coef_ref, edge_coef_ref, state_in_ref, edge_in_ref, state_ref, edge_ref):
    axial, span = state_ref.shape[2], state_ref.shape[3] - EDGE
    diagonal_sweeps(jac_ref, state_ref, edge_ref, coef_ref, edge_coef_ref, axial // 2 + 1, axial)
    advance((jac_ref, state_ref, edge_ref, coef_ref), axial, 0, span)


def diagonal_sweeps(jac_ref, state_ref, edge_ref, coef_ref, edge_coef_ref, first, last):
    axial = state_ref.shape[2]
    for t in range(first, last):
        advance((jac_ref, state_ref, edge_ref, coef_ref), t, axial - t)
        for c, value in enumerate(edge_update(jac_ref, edge_ref, edge_coef_ref, t, axial)):
            edge_ref[t + 1, c] = value


def second_kernel(
    jac_ref, coef_ref, inv_ref, edge_coef_ref, state_in_ref, edge_in_ref, more_b_ref, more_a_ref, synth_ref,
    state_ref, edge_ref, out_hbm, bound_ref, out_ref, sems,
):
    axial, components, span, pitch = out_ref.shape
    copies = [pltpu.make_async_copy(out_ref.at[a], out_hbm.at[:, a], sems.at[a]) for a in range(axial)]
    wide = span + EDGE
    side = lax.axis_index("span")
    more = more_a_ref[...] + more_b_ref[...]
    start = (axial - 1) * span
    parts = []
    for t in range(1, axial):
        _, _, from_packed = ghost_rows(side, t, axial)
        parts += [more[(t - 1) * span:t * span], pltpu.roll(more[start:start + EDGE], from_packed, 0)]
    field = synthesised(jnp.concatenate(parts + [more[start + EDGE:]], 0), synth_ref, synth_ref.shape[0])
    for t in range(1, axial):
        part = field[(t - 1) * wide:t * wide]
        for c in range(components):
            bound_ref[t, c] = inv_ref[...] * part[:, c * pitch:(c + 1) * pitch]
    for c in range(components):
        bound_ref[axial, c, :span] = inv_ref[:span] * field[(axial - 1) * wide:, c * pitch:(c + 1) * pitch]
    delta = [bound_ref[1, c] for c in range(components)]
    for t in range(2, axial + 2):
        height = wide if t <= axial else span
        for c in range(components):
            state_ref[t, c, axial + 1 - t, :height] += delta[c][:height]
        if t < axial + 1:
            delta = along_axis(jac_ref, coef_ref, delta, axial - t, wide)
    for c in range(components):
        out_ref[0, c] = state_ref[axial + 1, c, 0, :span]
    copies[0].start()
    for t in range(1, axial):
        if t > 1:
            for c, value in enumerate(edge_update(jac_ref, edge_ref, edge_coef_ref, t, axial)):
                edge_ref[t + 1, c] = value
        part = field[(t - 1) * wide:t * wide]
        for c in range(components):
            edge_ref[t + 1, c] += edge_coef_ref[components + 6] * edge_boundary(part, c, components, pitch, axial)
    refs = (jac_ref, state_ref, edge_ref, coef_ref)

    for t in range(2, axial):
        for a in range(axial + 1 - t, axial):
            advance(refs, t, a)
        for c in range(components):
            state_ref[t + 1, c, axial - 1] += bound_ref[t, c]
    for a in range(1, axial):
        for c, value in enumerate(layer_update(*refs, axial, a, span)):
            out_ref[a, c] = value + bound_ref[axial, c, :span] if a == axial - 1 else value
        copies[a].start()
    for copy in copies:
        copy.wait()


def moved(x, to):
    sizes = [lax.axis_size(name) for name in AXES]
    pairs = []
    for r in range(sizes[0]):
        for s in range(sizes[1]):
            for p in range(sizes[2]):
                target = to(r, s, p)
                if all(0 <= at < size for at, size in zip(target, sizes)):
                    number = lambda at: (at[0] * sizes[1] + at[1]) * sizes[2] + at[2]
                    pairs.append((number((r, s, p)), number(target)))
    return lax.ppermute(x, AXES, pairs)


def struct(*shape):
    return jax.ShapeDtypeStruct(shape, jnp.float32)


def on_device(
    adjoint_start, source, couplings, damping, jacobians, giles_real, giles_imag, blades, mode_orders, cell_map,
):
    components, axial, span, pitch = adjoint_start.shape
    row_count, span_count, place_count = (lax.axis_size(name) for name in AXES)
    length = pitch * place_count
    assert sum(axial - t for t in range(1, axial)) <= EDGE
    assert components == COMPONENTS and components * WAVES <= pitch
    assert axial == ITERS - 1 and ITERS <= EDGE and axial * SEGMENT_LANES == pitch
    assert span_count == 2 and place_count > 2 and place_count & (place_count - 1) == 0
    wide = span + EDGE
    fields = 2 * components + 6
    groups = slots(fields + 1, components)[1][-1][0] + 1
    pairs = -(-(fields * axial + 1) // 2)
    span_tiles = pairs + -(-components * axial // EDGE)
    vmem = pl.BlockSpec(memory_space=pltpu.VMEM)
    hbm = pl.BlockSpec(memory_space=pltpu.HBM)

    def in_hbm(x):
        return pltpu.with_memory_space_constraint(x, pltpu.HBM)

    def call(kernel, name, outs, ins, aliases=None, scratch=(), limit=40 * MIB, out_specs=None, **fixed):
        specs = [spec for spec, _ in ins]
        return pl.pallas_call(
            functools.partial(kernel, **fixed),
            out_shape=outs,
            in_specs=specs,
            out_specs=out_specs or jax.tree.map(lambda _: vmem, outs),
            scratch_shapes=scratch,
            input_output_aliases=aliases or {},
            compiler_params=params(limit),
            name=name,
        )(*[value for _, value in ins])

    tables = (
        jacobians.transpose(2, 3, 0, 1), giles_real.transpose(2, 3, 0, 1), giles_imag.transpose(2, 3, 0, 1),
        mode_orders.transpose(0, 2, 1), cell_map,
    )
    blades = blades.reshape(1, -1)
    corner_rows = groups * EDGE
    own_rows = (groups - 1) * span + span // 2
    assert slots(fields + 1, components)[1][-1][1] < SHARED_LANES
    state_shape = struct(axial + 2, components, axial, wide, pitch)
    state, coef, inv, span_out, small, modes, table, blades, *tables = call(
        start_kernel, "start",
        (
            state_shape, struct(components + 6, axial, wide, pitch), struct(wide, pitch),
            struct(span_tiles, EDGE, pitch), struct(2 * corner_rows + EDGE, pitch), struct(span, pitch),
            jax.ShapeDtypeStruct((3 * components * pitch, pitch), jnp.bfloat16),
            *(jax.ShapeDtypeStruct(x.shape, x.dtype) for x in (blades, *tables)),
        ),
        [(hbm, in_hbm(x)) for x in (adjoint_start, source, couplings, damping, blades, *tables)],
        scratch=[
            pltpu.VMEM(source.shape, jnp.float32), pltpu.VMEM(couplings.shape, jnp.float32),
            pltpu.VMEM(damping.shape, jnp.float32), pltpu.SemaphoreType.DMA((5 + len(tables),)),
        ],
        groups=groups, length=length,
    )
    edges, inner, outer = call(
        pack_kernel, "pack",
        (struct(fields + 1, span, pitch), struct(own_rows + corner_rows + wide, pitch), struct(own_rows + corner_rows, pitch)),
        [(vmem, x) for x in (state, coef, inv, modes)],
        groups=groups,
    )
    steps = [1 << n for n in range(place_count.bit_length() - 2)]
    last_step = place_count // 2

    def near(x):
        return moved(x, lambda r, s, p: (r - 1, s, p))

    def far(x):
        return moved(x, lambda r, s, p: (r - 1, s, p ^ last_step))

    synth, jac = call(
        synth_kernel, "synth",
        (
            jax.ShapeDtypeStruct(
                (-(-components * (pitch + SEGMENT_LANES) // pitch) * pitch, 3 * pitch), jnp.bfloat16
            ),
            struct(-(-6 * components * components // EDGE) * EDGE, pitch),
        ),
        [(vmem, x) for x in (blades, *tables)],
        scratch=[pltpu.VMEM((2, components * components, mode_orders.shape[1]), jnp.float32)],
        row_count=row_count, place_count=place_count, components=components, pitch=pitch, length=length, axial=axial,
    )
    small, edges, jac = lax.optimization_barrier((moved(small, lambda r, s, p: (r, 1 - s, p)), edges, jac))
    from_span = moved(span_out, lambda r, s, p: (r, 1 - s, p))
    edge_shape = struct(axial + 1, components, wide, pitch)
    inner = lax.dynamic_update_slice(inner, small[:corner_rows + EDGE], (own_rows, 0))
    outer = lax.dynamic_update_slice(outer, small[corner_rows + EDGE:], (own_rows, 0))
    modes = inner[own_rows + corner_rows:]
    outer = moved(outer, lambda r, s, p: (r, s, (p - 1 + 2 * (p % 2)) % place_count))
    inner = moved(inner, lambda r, s, p: (r, s, p ^ 1))
    modes = modes + inner[own_rows + corner_rows:]
    for step in steps[1:]:
        modes = modes + moved(modes, lambda r, s, p: (r, s, p ^ step))
    got = moved(modes, lambda r, s, p: (r, s, p ^ last_step))
    coef, inv, edge_coef, state, edge = call(
        first_kernel, "first_sweep",
        (
            struct(components + 6, axial, wide, pitch), struct(wide, pitch), struct(components + 7, wide, pitch),
            state_shape, edge_shape,
        ),
        [(vmem, x) for x in (jac, state, coef, inv, edges, from_span, inner, outer)],
        aliases={1: 3, 2: 0, 3: 1},
        groups=groups,
    )
    got, inv = lax.optimization_barrier((got, inv))
    modes = near(modes + got)
    state, edge, more, part = call(
        more_kernel, "more_sweeps",
        (state_shape, edge_shape, struct((axial - 1) * span + EDGE, pitch), struct(span, pitch)),
        [(vmem, x) for x in (jac, coef, edge_coef, state, edge, table)],
        aliases={3: 0, 4: 1},
    )
    more_shape = struct(axial * span + EDGE, pitch)
    more = call(
        late_kernel, "late_modes", more_shape,
        [(vmem, x) for x in (jac, coef, inv, part, more, modes, synth, table)],
    )
    state, edge, sent = call(
        between_kernel, "between_sweeps", (state_shape, edge_shape, more_shape),
        [(vmem, x) for x in (jac, coef, inv, edge_coef, state, edge, modes, synth, more)],
        aliases={4: 0, 5: 1},
    )
    state, edge = call(
        beside_kernel, "beside_sweeps", (state_shape, edge_shape),
        [(vmem, x) for x in (jac, coef, edge_coef, state, edge)],
        aliases={3: 0, 4: 1},
    )
    for step in steps:
        got = moved(more, lambda r, s, p: (r, s, p ^ step))
        more, sent = sent + got, sent + got
    more_b = far(more)
    more_a = near(more)
    return call(
        second_kernel, "second_sweeps", (state_shape, edge_shape, struct(components, axial, span, pitch)),
        [(vmem, x) for x in (jac, coef, inv, edge_coef, state, edge, more_b, more_a, synth)],
        aliases={4: 0, 5: 1},
        scratch=[
            pltpu.VMEM((axial + 1, components, wide, pitch), jnp.float32),
            pltpu.VMEM((axial, components, span, pitch), jnp.float32), pltpu.SemaphoreType.DMA((axial,)),
        ],
        out_specs=(vmem, vmem, hbm),
    )[2]


def solution(mesh):
    placed = (
        P(None, "row", "span", "pitch"),
        P(None, "row", "span", "pitch"),
        P(None, "row", "span", "pitch"),
        P("row", "span", "pitch"),
        P("row", None, None, None),
        P(),
        P(),
        P(),
        P(),
        P("row", None),
    )
    return jax.shard_map(
        on_device,
        mesh=mesh,
        in_specs=placed,
        out_specs=P(None, "row", "span", "pitch"),
        check_vma=False,
    )
```
